32 devices in a mesh: dp: 8 (over z, core), tensor: 4 (over y, x).
Axes of the slice: x: 2, y: 2, z: 4, core: 2. Of those that a mesh axis runs over, the one named last changes fastest.
Arguments:
- images_in: bfloat16 [64, 196, 512], P(('dp', 'tensor')), may hold values from -6 to 6
- ln1_gain: float32 [2, 512], replicated, may hold values from 0.5 to 1.5
- ln1_bias: float32 [2, 512], replicated, may hold values from -3 to 3
- qkv_weight: bfloat16 [2, 512, 1536], P(None, None, 'tensor'), may hold values from -0.25 to 0.25
- qv_bias: float32 [2, 1024], P(None, 'tensor'), may hold values from -3 to 3
- rel_table: float32 [2, 169, 16], P(None, None, 'tensor'), may hold values from -4 to 4
- proj_weight: bfloat16 [2, 512, 512], P(None, 'tensor'), may hold values from -1 to 1
- proj_bias: float32 [2, 512], replicated, may hold values from -3 to 3
- ln2_gain: float32 [2, 512], replicated, may hold values from 0.5 to 1.5
- ln2_bias: float32 [2, 512], replicated, may hold values from -3 to 3
- fc1_weight: bfloat16 [2, 512, 2048], P(None, None, 'tensor'), may hold values from -0.25 to 0.25
- fc1_bias: float32 [2, 2048], P(None, 'tensor'), may hold values from -3 to 3
- fc2_weight: bfloat16 [2, 2048, 512], P(None, 'tensor'), may hold values from -0.1875 to 0.1875
- fc2_bias: float32 [2, 512], replicated, may hold values from -3 to 3
- rel_index: int32 [49, 49], replicated, may hold values from 0 to 168
- region_ids: int32 [196], replicated, may hold values from 0 to 8
- out_cot: bfloat16 [64, 196, 512], P(('dp', 'tensor')), may hold values from -6 to 6
Outputs:
- output: bfloat16 [64, 196, 512], P(('dp', 'tensor'))
- grad_input: bfloat16 [64, 196, 512], P(('dp', 'tensor'))
- grad_ln1_gain: float32 [2, 512], replicated
- grad_ln1_bias: float32 [2, 512], replicated
- grad_qkv_weight: float32 [2, 512, 1536], P(None, None, 'tensor')
- grad_qv_bias: float32 [2, 1024], P(None, 'tensor')
- grad_rel_table: float32 [2, 169, 16], P(None, None, 'tensor')
- grad_proj_weight: float32 [2, 512, 512], P(None, 'tensor')
- grad_proj_bias: float32 [2, 512], replicated
- grad_ln2_gain: float32 [2, 512], replicated
- grad_ln2_bias: float32 [2, 512], replicated
- grad_fc1_weight: float32 [2, 512, 2048], P(None, None, 'tensor')
- grad_fc1_bias: float32 [2, 2048], P(None, 'tensor')
- grad_fc2_weight: float32 [2, 2048, 512], P(None, 'tensor')
- grad_fc2_bias: float32 [2, 512], replicated
The draws below stay inside these ranges and needn't reach their ends.
Inputs may be any that keep to these rules, and one draw needn't show every extreme that they name: `rel_index`: indexes rows of rel_table. `region_ids`: a key is masked in the shifted block where its region differs from the query's.
All inputs are finite; a program needn't handle non-finite values.
Results may differ from the reference program's by a relative error of at most 0.03.
Values may be sent and summed in bfloat16 or wider, within the bound.
No kernel may reach another device: no remote copies, remote signals or barrier semaphores. Data moves between devices by JAX's collectives and lax.ppermute only.
A program may use at most 192 MiB of HBM per device.

```python
import jax
import jax.numpy as jnp
from jax import lax

C = 512
HEADS = 16
HEAD_DIM = 32
FF = 2048
WIN = 7
GRID = 14
SHIFT = 3
LAYERS = 2
TOK = 196
WTOK = 49
TABLE = 169
IMAGES = 64


def set_ends(result, key, least, high):
    extent = result.shape
    index_at = [jax.random.randint(jax.random.fold_in(key, axis), (), 0, extent[axis]) for axis in range(len(extent))]
    result = result.at[tuple(index_at)].set(least)
    longest = extent.index(max(extent))
    index_at[longest] = (index_at[longest] + 1) % extent[longest]
    return result.at[tuple(index_at)].set(high)


def block_levels(rng, extent, pieces, low, largest):
    level = 1.0
    for axis_at, blocks in pieces:
        heights = jax.random.uniform(jax.random.fold_in(jax.random.fold_in(rng, 6), axis_at), (blocks,), jnp.float32, low / len(pieces), largest / len(pieces))
        level = level * jnp.repeat(jnp.exp(heights), extent[axis_at] // blocks).reshape((-1,) + (1,) * (len(extent) - 1 - axis_at))
    return level


def normal_values(key, dims, scale, reach, shards=(), held_as=jnp.bfloat16):
    entries = jax.random.normal(key, dims, jnp.float32) * scale
    if len(shards) > 0:
        entries = block_levels(key, dims, shards, -0.22, 0.18) * entries
    return jnp.clip(entries, min=-reach, max=reach).astype(held_as)


def setup_inputs(seed: int = 0) -> dict:
    keys = jax.random.split(jax.random.key(seed), 18)
    return {
        "images_in": normal_values(keys[0], (IMAGES, TOK, C), 1.0, 6.0, ((0, 32),)),
        "ln1_gain": jnp.clip(1.0 + 0.1 * jax.random.normal(keys[1], (LAYERS, C), jnp.float32), 0.5, 1.5),
        "ln1_bias": normal_values(keys[2], (LAYERS, C), 0.5, 3.0, (), jnp.float32),
        "qkv_weight": normal_values(keys[3], (LAYERS, C, 3 * C), C ** -0.5, 0.25, ((2, 4),)),
        "qv_bias": normal_values(keys[4], (LAYERS, 2 * C), 0.5, 3.0, ((1, 4),), jnp.float32),
        "rel_table": normal_values(keys[5], (LAYERS, TABLE, HEADS), 1.0, 4.0, ((2, 4),), jnp.float32),
        "proj_weight": normal_values(keys[6], (LAYERS, C, C), (C // 16) ** -0.5, 1.0, ((1, 4),)),
        "proj_bias": normal_values(keys[7], (LAYERS, C), 0.5, 3.0, (), jnp.float32),
        "ln2_gain": jnp.clip(1.0 + 0.1 * jax.random.normal(keys[8], (LAYERS, C), jnp.float32), 0.5, 1.5),
        "ln2_bias": normal_values(keys[9], (LAYERS, C), 0.5, 3.0, (), jnp.float32),
        "fc1_weight": normal_values(keys[10], (LAYERS, C, FF), C ** -0.5, 0.25, ((2, 4),)),
        "fc1_bias": normal_values(keys[11], (LAYERS, FF), 0.5, 3.0, ((1, 4),), jnp.float32),
        "fc2_weight": normal_values(keys[12], (LAYERS, FF, C), (FF // 2) ** -0.5, 0.1875, ((1, 4),)),
        "fc2_bias": normal_values(keys[13], (LAYERS, C), 0.5, 3.0, (), jnp.float32),
        "rel_index": set_ends(jax.random.randint(keys[14], (WTOK, WTOK), 0, TABLE), jax.random.fold_in(keys[14], 1), 0, TABLE - 1).astype(jnp.int32),
        "region_ids": set_ends(jax.random.randint(keys[15], (TOK,), 0, 9), jax.random.fold_in(keys[15], 1), 0, 8).astype(jnp.int32),
        "out_cot": normal_values(keys[16], (IMAGES, TOK, C), 1.0, 6.0, ((0, 32),)),
    }


@jax.custom_vjp
def low(v):
    return lax.optimization_barrier(v.astype(jnp.bfloat16)).astype(jnp.float32)

@jax.custom_vjp
def low_back(v):
    return v

def low_keep(v):
    return (low(v), None)

def low_pass(kept, grad):
    return (grad,)

def back_keep(v):
    return (v, None)

def back_low(kept, grad):
    return (low(grad),)
low.defvjp(low_keep, low_pass)
low_back.defvjp(back_keep, back_low)

def matmul_high(left, right):
    return jnp.matmul(left, right, precision=lax.Precision.HIGHEST)

def layer_norm(values, gain, offset_term):
    centre = values - lax.optimization_barrier(jnp.mean(values, -1, keepdims=True))
    spread = lax.optimization_barrier(jnp.mean(centre * centre, -1, keepdims=True))
    return centre * lax.rsqrt(spread + 1e-05) * gain + offset_term

def to_windows(values, offset):
    batch = values.shape[0]
    feats = values.shape[-1]
    across = GRID // WIN
    grid = values.reshape(batch, GRID, GRID, feats)
    if offset:
        grid = jnp.roll(grid, (-offset, -offset), (1, 2))
    grid = grid.reshape(batch, across, WIN, across, WIN, feats).transpose(0, 1, 3, 2, 4, 5)
    return grid.reshape(batch * across * across, WIN * WIN, feats)

def from_windows(values, offset):
    across = GRID // WIN
    feats = values.shape[-1]
    batch = values.shape[0] // (across * across)
    grid = values.reshape(batch, across, across, WIN, WIN, feats).transpose(0, 1, 3, 2, 4, 5)
    grid = grid.reshape(batch, GRID, GRID, feats)
    if offset:
        grid = jnp.roll(grid, (offset, offset), (1, 2))
    return grid.reshape(batch, GRID * GRID, feats)

def full_bias(qv_row, heads):
    parts = qv_row.reshape(heads, 2, HEAD_DIM)
    return jnp.stack([parts[:, 0], jnp.zeros_like(parts[:, 0]), parts[:, 1]], 1).reshape(-1)

def window_mask(region_ids):
    window_ids = to_windows(region_ids.reshape(1, TOK, 1), 0).reshape(-1, WTOK)
    return jnp.where(window_ids[:, :, None] != window_ids[:, None, :], -100.0, 0.0).astype(jnp.float32)

def network(values, params, rel_index, mask_term):
    ln1_gain, ln1_bias, qkv_weight, qv_bias, rel_table, proj_weight, proj_bias, ln2_gain, ln2_bias, fc1_weight, fc1_bias, fc2_weight, fc2_bias = params
    batch = values.shape[0]
    windows = mask_term.shape[0]
    scale = HEAD_DIM ** (-0.5)
    state = values
    for layer in range(LAYERS):
        offset = SHIFT if layer % 2 == 1 else 0
        normed1 = low(layer_norm(state, ln1_gain[layer], ln1_bias[layer]))
        triple = low_back(low(matmul_high(normed1, qkv_weight[layer]) + full_bias(qv_bias[layer], HEADS)))
        wins = to_windows(triple, offset).reshape(-1, WTOK, HEADS, 3, HEAD_DIM)
        query = wins[:, :, :, 0]
        key = wins[:, :, :, 1]
        value = wins[:, :, :, 2]
        raw = low_back(jnp.einsum('wihd,wjhd->whij', query, key, precision=lax.Precision.HIGHEST))
        table_bias = rel_table[layer][rel_index].transpose(2, 0, 1)
        scores = raw * scale + table_bias[None]
        if offset:
            scores = (scores.reshape(batch, windows, HEADS, WTOK, WTOK) + mask_term[None, :, None]).reshape(scores.shape)
        probs = low(jax.nn.softmax(scores, axis=-1))
        mixed = jnp.einsum('whij,wjhd->wihd', probs, value, precision=lax.Precision.HIGHEST)
        heads_out = low_back(low(from_windows(mixed.reshape(-1, WTOK, C), offset)))
        middle = state + low_back(matmul_high(heads_out, proj_weight[layer])) + proj_bias[layer]
        normed2 = low(layer_norm(middle, ln2_gain[layer], ln2_bias[layer]))
        pre = low_back(matmul_high(normed2, fc1_weight[layer]) + fc1_bias[layer])
        act = low(jax.nn.gelu(pre, approximate=False))
        state = middle + low_back(matmul_high(act, fc2_weight[layer])) + fc2_bias[layer]
    return state

def reference(images_in, ln1_gain, ln1_bias, qkv_weight, qv_bias, rel_table, proj_weight, proj_bias, ln2_gain, ln2_bias, fc1_weight, fc1_bias, fc2_weight, fc2_bias, rel_index, region_ids, out_cot):
    weights = tuple((w.astype(jnp.float32) for w in (ln1_gain, ln1_bias, qkv_weight, qv_bias, rel_table, proj_weight, proj_bias, ln2_gain, ln2_bias, fc1_weight, fc1_bias, fc2_weight, fc2_bias)))
    mask_term = window_mask(region_ids)
    groups = IMAGES // 8
    inputs = images_in.reshape(groups, 8, TOK, C)
    cotangents = out_cot.reshape(groups, 8, TOK, C)

    def forward(values, *params):
        return network(values, params, rel_index, mask_term)

    def step(totals, item):
        block_in, block_cot = item
        outputs, pull = jax.vjp(forward, block_in.astype(jnp.float32), *weights)
        grads = pull(block_cot.astype(jnp.float32))
        totals = tuple((total + grad for total, grad in zip(totals, grads[1:])))
        return (totals, (outputs.astype(jnp.bfloat16), grads[0].astype(jnp.bfloat16)))
    zeros = tuple((jnp.zeros_like(w) for w in weights))
    totals, (outputs, grad_in) = lax.scan(step, zeros, (inputs, cotangents))
    return (outputs.reshape(IMAGES, TOK, C), grad_in.reshape(IMAGES, TOK, C), totals[0], totals[1], totals[2], totals[3], totals[4], totals[5], totals[6], totals[7], totals[8], totals[9], totals[10], totals[11], totals[12])
```

```python
import functools

import jax
import jax.numpy as jnp
import numpy as np
from jax import lax
from jax.experimental import pallas as pl
from jax.experimental.pallas import tpu as pltpu
from jax.sharding import PartitionSpec as P

C = 512
HEADS = 16
HEAD_DIM = 32
FF = 2048
WIN = 7
GRID = 14
SHIFT = 3
LAYERS = 2
TOK = 196
WTOK = 49
TABLE = 169
PAIR = 112
LANES = 128
GROUPS = 4
GHEADS = HEADS // GROUPS
TRI = 3 * LANES
HID = FF // GROUPS
SCALE = HEAD_DIM ** (-0.5)
NEG = -1e30
F32 = jnp.float32
BF16 = jnp.bfloat16


def window_tokens(offset):
    cells = np.arange(TOK).reshape(GRID, GRID)
    cells = np.roll(cells, (-offset, -offset), (0, 1))
    cells = cells.reshape(2, WIN, 2, WIN).transpose(0, 2, 1, 3)
    return cells.reshape(4, WTOK)


def place_matrix(offset):
    tokens = window_tokens(offset).reshape(2, 2 * WTOK)
    out = np.zeros((2 * PAIR, TOK), np.float32)
    for pair in range(2):
        out[pair * PAIR + np.arange(2 * WTOK), tokens[pair]] = 1.0
    return out


PLACE = [place_matrix(SHIFT if layer % 2 == 1 else 0) for layer in range(LAYERS)]


def group_matrix():
    out = np.zeros((TRI, TRI), np.float32)
    for head in range(GHEADS):
        for part in range(3):
            for pos in range(HEAD_DIM):
                out[
                    (head * 3 + part) * HEAD_DIM + pos, (part * GHEADS + head) * HEAD_DIM + pos
                ] = 1.0
    return out


GROUP = group_matrix()


def pick_matrix():
    out = np.zeros((TRI, 2 * LANES), np.float32)
    for head in range(GHEADS):
        for to, part in enumerate((0, 2)):
            for pos in range(HEAD_DIM):
                out[(head * 3 + part) * HEAD_DIM + pos, (head * 2 + to) * HEAD_DIM + pos] = 1.0
    return out


PICK = pick_matrix()


def mm(a, b):
    return jnp.dot(a, b, preferred_element_type=F32)


def mm_nt(a, b):
    return lax.dot_general(a, b, (((1,), (1,)), ((), ())), preferred_element_type=F32)


def mm_tn(a, b):
    return lax.dot_general(a, b, (((0,), (0,)), ((), ())), preferred_element_type=F32)


def normalize(x):
    centre = x - jnp.mean(x, -1, keepdims=True)
    spread = jnp.mean(centre * centre, -1, keepdims=True)
    rstd = lax.rsqrt(spread + 1e-05)
    return centre * rstd, rstd


def norm_back(x, gain, grad):
    xhat, rstd = normalize(x)
    scaled = grad * gain
    m1 = jnp.mean(scaled, -1, keepdims=True)
    m2 = jnp.mean(scaled * xhat, -1, keepdims=True)
    dx = rstd * (scaled - m1 - xhat * m2)
    return dx, jnp.sum(grad * xhat, 0, keepdims=True), jnp.sum(grad, 0, keepdims=True)


def rows_of(pair):
    return pl.ds(pl.multiple_of(pair * PAIR, 16), PAIR)


def head_mask(head):
    lane = lax.broadcasted_iota(jnp.int32, (PAIR, LANES), 1)
    return (lane // HEAD_DIM) == head


def stack_heads(block, masks):
    zero = jnp.zeros_like(block)
    pad = jnp.zeros((LANES - PAIR, LANES), block.dtype)
    parts = []
    for mask in masks:
        parts += [jnp.where(mask, block, zero), pad]
    return jnp.concatenate(parts, 0)


def split_exact(x):
    high = x.astype(BF16)
    return high, (x - high.astype(F32)).astype(BF16)


def half_rows(core, half):
    mine = pl.ds(pl.multiple_of(core * half, 16), half)
    other = pl.ds(pl.multiple_of((1 - core) * half, 16), half)
    return mine, other


Q_ROWS, M_ROWS = 192, 576
PACK_Q = [(0, 0, Q_ROWS, TRI, 0, 0)] + [
    (Q_ROWS, j * LANES, 64, LANES, 64 * j, TRI) for j in range(3)
]
PACK_1 = [(0, 0, 256, C, 0, 0)]
PACK_P = [(0, 0, 64, C, 256, 0)]
PACK_2 = [(0, 0, 256, C, 320, 0)]
ONE_ROWS, TWO_ROWS = 320, 256
PACK_TWO = [(0, 0, 256, C, 0, 0)]


def moved_down(blocks, base):
    return [block[:4] + (block[4] + base, block[5]) for block in blocks]


class Fetch:
    def __init__(self, full, layer, pieces, blocks, dest, core, sems):
        half = dest.shape[1] // 2
        self.copies = [[pltpu.make_async_copy(full.at[layer], dest.at[0], sems.at[0])]]
        at = 1
        for r in range(1, GROUPS):
            group = []
            for side, piece in ((core, pieces[0].at[r - 1]), (1 - core, pieces[1].at[r - 1])):
                for row, lane, rows, lanes, to_row, to_lane in blocks:
                    target = dest.at[
                        r,
                        pl.ds(pl.multiple_of(side * half + row, 16), rows),
                        pl.ds(lane, lanes),
                    ]
                    source = piece.at[pl.ds(to_row, rows), pl.ds(to_lane, lanes)]
                    group.append(pltpu.make_async_copy(source, target, sems.at[at]))
                    at += 1
            self.copies.append(group)
        for group in self.copies:
            for copy in group:
                copy.start()

    def wait(self, r):
        for copy in self.copies[r]:
            copy.wait()


def bias_kernel(layer, table, index, ids_col, ids_row, place, lanes_place, bias_ref):
    cols = mm(place[...], ids_col[...])
    rows = mm_nt(ids_row[...], lanes_place[...])
    masks = []
    for pair in range(2):
        col = cols[pair * PAIR : (pair + 1) * PAIR]
        row = rows[:1, pair * LANES : (pair + 1) * LANES]
        masks.append(jnp.where(col != row, -100.0, 0.0))
    idx = index[...]
    at_low = jnp.clip(idx, 0, LANES - 1)
    at_high = jnp.clip(idx - LANES, 0, LANES - 1)

    def pick(row):
        entries = table[row]
        low = jnp.broadcast_to(entries[:, 0:LANES], (PAIR, LANES))
        high = jnp.broadcast_to(entries[:, LANES : 2 * LANES], (PAIR, LANES))
        low = jnp.take_along_axis(low, at_low, axis=1)
        high = jnp.take_along_axis(high, at_high, axis=1)
        return jnp.where(idx < 0, NEG, jnp.where(idx < LANES, low, high))

    def one_head(head, carry):
        picked = pick(layer * HEADS + head)
        if layer == 0:
            bias_ref[0, head] = picked
        else:
            bias_ref[0, head] = picked + masks[0]
            bias_ref[1, head] = picked + masks[1]
        return carry

    lax.fori_loop(0, HEADS, one_head, 0)


def attn_fwd_kernel(layer, pairs, base, *refs):
    first = layer == 0
    where, x_in, place, ln_g, ln_b, b_qkv, group, bias, full_qkv = refs[:9]
    p_qkv, outs = refs[9:11], refs[11:]
    if first:
        x_ref, outs = outs[0], outs[1:]
    else:
        x_ref = x_in
    n1_ref, tri_ref, e_ref, rinv_ref, ho_ref, w_qkv, sem_q = outs
    qkv = Fetch(full_qkv, layer, p_qkv, moved_down(PACK_Q, base), w_qkv, where[1], sem_q)
    if first:
        for image in range(pairs // 2):
            x_ref[pl.ds(image * 2 * PAIR, 2 * PAIR), :] = mm(place[...], x_in[image])

    def norm_rows(pair, carry):
        rows = rows_of(pair)
        xhat, _ = normalize(x_ref[rows, :])
        n1_ref[rows, :] = (xhat * ln_g[...] + ln_b[...]).astype(BF16)
        return carry

    lax.fori_loop(0, pairs, norm_rows, 0)
    masks = [head_mask(h) for h in range(GHEADS)]
    ones = jnp.ones((PAIR, LANES), BF16)
    for r in range(GROUPS):
        qkv.wait(r)
        tri = (mm(n1_ref[...], w_qkv[r]) + b_qkv[r]).astype(BF16)
        tri_ref[r] = mm(tri, group[...]).astype(BF16)
        ones_stack = stack_heads(ones, masks)

        def pair_step(pair, carry):
            rows = rows_of(pair)
            q4 = tri_ref[r, rows, 0:LANES]
            k4 = tri_ref[r, rows, LANES : 2 * LANES]
            v4 = tri_ref[r, rows, 2 * LANES : 3 * LANES]
            s4 = mm_nt(q4, stack_heads(k4, masks))
            kind = 0 if first else lax.rem(pair, 2)
            es = []
            for h in range(GHEADS):
                s = s4[:, h * LANES : (h + 1) * LANES] * SCALE + bias[kind, r * GHEADS + h]
                es.append(jnp.exp(s - jnp.max(s, -1, keepdims=True)).astype(BF16))
            e4 = jnp.concatenate(es, 1)
            e_ref[r, pair] = e4
            vm = jnp.concatenate([stack_heads(v4, masks), ones_stack], 1)
            out = mm(e4, vm)
            rinv = 1.0 / out[:, LANES:]
            rinv_ref[r, rows, :] = rinv
            ho_ref[rows, r * LANES : (r + 1) * LANES] = (out[:, :LANES] * rinv).astype(BF16)
            return carry

        lax.fori_loop(0, pairs, pair_step, 0, unroll=True)


def mlp_fwd_kernel(layer, pairs, *refs):
    last = layer == LAYERS - 1
    where, x, ho, b_proj, ln_g, ln_b, b1, b2, place = refs[:9]
    full_p, full_1, full_2 = refs[9:12]
    p_m = refs[12:14]
    out_ref, mid, n2_ref, act_ref, dact_ref, wp, w1, w2, sem_p, sem_1, sem_2, acc, pre_ref = refs[14:]
    core = where[1]
    f_p = Fetch(full_p, layer, p_m, PACK_P, wp, core, sem_p)
    f_1 = Fetch(full_1, layer, p_m, PACK_1, w1, core, sem_1)
    f_2 = Fetch(full_2, layer, p_m, PACK_2, w2, core, sem_2)
    for r in range(GROUPS):
        f_p.wait(r)
    weight = jnp.concatenate([wp[r] for r in range(GROUPS)], 0)
    mid[...] = x[...] + mm(ho[...], weight) + b_proj[...]

    def norm_rows(pair, carry):
        rows = rows_of(pair)
        xhat, _ = normalize(mid[rows, :])
        n2_ref[rows, :] = (xhat * ln_g[...] + ln_b[...]).astype(BF16)
        return carry

    lax.fori_loop(0, pairs, norm_rows, 0)
    for r in range(GROUPS):
        f_1.wait(r)
        pre_ref[...] = mm(n2_ref[...], w1[r])
        b1_row = b1[r]

        def gelu_rows(step, carry):
            rows = pl.ds(pl.multiple_of(step * 16, 16), 16)
            pre = pre_ref[rows, :] + b1_row
            cdf = 0.5 + 0.5 * lax.erf(pre * (0.5**0.5))
            act_ref[r, rows, :] = (pre * cdf).astype(BF16)
            pdf = jnp.exp(-0.5 * pre * pre) * 0.3989422804014327
            dact_ref[r, rows, :] = (cdf + pre * pdf).astype(BF16)
            return carry

        lax.fori_loop(0, pairs * (PAIR // 16), gelu_rows, 0, unroll=2)
        f_2.wait(r)
        part = mm(act_ref[r], w2[r])
        if r == 0:
            acc[...] = part
        else:
            acc[...] += part
    acc[...] = acc[...] + mid[...] + b2[...]
    for image in range(pairs // 2):
        state = acc[pl.ds(image * 2 * PAIR, 2 * PAIR), :]
        if last:
            out_ref[image] = mm_tn(place[...], state.astype(BF16)).astype(BF16)
        else:
            high, low = split_exact(state)
            out_ref[pl.ds(image * 2 * PAIR, 2 * PAIR), :] = mm(place[...], high) + mm(
                place[...], low
            )


X_FIRST = (0, 2, 1, 3)
Y_FIRST = (0, 1, 2, 3)
ORDERS = (X_FIRST, Y_FIRST)


def give(keep_ref, send_ref, tmp, r, core, blocks):
    half = tmp.shape[0] // 2
    size = keep_ref.shape[2]
    for ref, base in ((keep_ref, core * half), (send_ref, (1 - core) * half)):
        for row, lane, rows, lanes, to_row, to_lane in blocks:
            done = 0
            while done < rows:
                part, at = divmod(to_row + done, size)
                count = min(rows - done, size - at)
                ref[part, ORDERS[part].index(r), at : at + count, to_lane : to_lane + lanes] = tmp[
                    pl.ds(pl.multiple_of(base + row + done, 16), count), lane : lane + lanes
                ]
                done += count


def hidden_back(layer, pairs, where, g_in, place, act, dact, w2, g_ref, gb_ref, gp_ref, tmp, outs, blocks):
    keep, send = outs
    core = where[1]
    if layer == LAYERS - 1:
        for image in range(pairs // 2):
            rows = pl.ds(image * 2 * PAIR, 2 * PAIR)
            g = mm(place[...], g_in[image])
            g_ref[rows, :] = g
            gb_ref[rows, :] = g.astype(BF16)
    else:
        gb_ref[...] = g_ref[...].astype(BF16)
    for r in range(GROUPS):
        tmp[...] = mm_tn(act[r], gb_ref[...]).astype(BF16)
        give(keep, send, tmp, r, core, blocks)
        ga = mm_nt(gb_ref[...], w2[r])
        gp_ref[r] = (ga * dact[r].astype(F32)).astype(BF16)


def middle_back(layer, pairs, where, gp_ref, g_ref, mid, n2, ho, rinv, ln_g, w1, wp, gb_ref, acc, tmp, tmp_p, outs):
    keep, send, gmid_ref, dh_ref, u_ref, small_ref, db1_ref = outs
    tid, core = where[0], where[1]
    small_ref[...] = jnp.zeros_like(small_ref)
    for r in range(GROUPS):
        db1_ref[tid ^ r] = jnp.sum(gp_ref[r].astype(F32), 0, keepdims=True)
        tmp[...] = mm_tn(n2[...], gp_ref[r]).astype(BF16)
        give(keep, send, tmp, r, core, PACK_1)
        part = mm_nt(gp_ref[r], w1[r])
        if r == 0:
            acc[...] = part
        else:
            acc[...] += part

    def back_rows(pair, carry):
        rows = rows_of(pair)
        g_rows = g_ref[rows, :]
        dx, dg, db = norm_back(mid[rows, :], ln_g[...], acc[rows, :])
        gmid = g_rows + dx
        gmid_ref[rows, :] = gmid
        gb_ref[rows, :] = gmid.astype(BF16)
        small_ref[0:1, :] += jnp.sum(g_rows, 0, keepdims=True)
        small_ref[1:2, :] += dg
        small_ref[2:3, :] += db
        small_ref[3:4, :] += jnp.sum(gmid, 0, keepdims=True)
        return carry

    lax.fori_loop(0, pairs, back_rows, 0)
    for r in range(GROUPS):
        lanes = slice(r * LANES, (r + 1) * LANES)
        tmp_p[...] = mm_tn(ho[:, lanes], gb_ref[...]).astype(BF16)
        give(keep, send, tmp_p, r, core, PACK_P)
        gh = mm_nt(gb_ref[...], wp[r]) * rinv[r]
        dh_ref[r] = gh.astype(BF16)
        u_ref[r] = (gh * ho[:, lanes].astype(F32)).astype(BF16)


def mlp_bwd_kernel(layer, pairs, *refs):
    where, g_in, place, act, dact, mid, n2, ho, rinv, ln_g, wp, w1, w2 = refs[:13]
    outs = refs[13:20]
    g_ref, gb_ref, gp_ref, acc, tmp, tmp_p = refs[20:]
    if layer < LAYERS - 1:
        g_ref = g_in
    hidden_back(
        layer, pairs, where, g_in, place, act, dact, w2, g_ref, gb_ref, gp_ref, tmp, outs[:2], PACK_2
    )
    middle_back(
        layer, pairs, where, gp_ref, g_ref, mid, n2, ho, rinv, ln_g, w1, wp, gb_ref, acc, tmp, tmp_p,
        outs,
    )


def hidden_bwd_kernel(layer, pairs, *refs):
    where, g, act, dact, w2 = refs[:5]
    gp_ref, gb_ref, tmp = refs[7:]
    hidden_back(
        layer, pairs, where, g, None, act, dact, w2, g, gb_ref, gp_ref, tmp, refs[5:7], PACK_TWO
    )


def middle_bwd_kernel(layer, pairs, *refs):
    where, gp, g, mid, n2, ho, rinv, ln_g, wp, w1 = refs[:10]
    gb_ref, acc, tmp, tmp_p = refs[17:]
    middle_back(
        layer, pairs, where, gp, g, mid, n2, ho, rinv, ln_g, w1, wp, gb_ref, acc, tmp, tmp_p,
        refs[10:17],
    )


def attn_bwd_kernel(pairs, where, dh, u, tri, e, group, dtri_ref, rel_ref, low_ref):
    tid = where[0]
    masks = [head_mask(h) for h in range(GHEADS)]
    neg_ones = jnp.full((PAIR, LANES), -1.0, BF16)
    for r in range(GROUPS):
        sid = tid ^ r
        neg_stack = stack_heads(neg_ones, masks)

        def pair_step(pair, carry):
            rows = rows_of(pair)
            q4 = tri[r, rows, 0:LANES]
            k4 = tri[r, rows, LANES : 2 * LANES]
            v4 = tri[r, rows, 2 * LANES : 3 * LANES]
            dh4 = dh[r, rows, :]
            left = jnp.concatenate([dh4, u[r, rows, :]], 1)
            right = jnp.concatenate([stack_heads(v4, masks), neg_stack], 1)
            dsp = mm_nt(left, right)
            e4 = e[r, pair]
            ds4 = e4.astype(F32) * dsp
            for h in range(GHEADS):
                part = ds4[:, h * LANES : (h + 1) * LANES]
                head = sid * GHEADS + h
                rel_ref[head] = jnp.where(pair == 0, part, rel_ref[head] + part)
            dsb = (ds4 * SCALE).astype(BF16)
            dq4 = mm(dsb, stack_heads(k4, masks))
            pad = jnp.zeros((LANES - PAIR, GHEADS * LANES), BF16)
            dsb_p = jnp.concatenate([dsb, pad], 0)
            e4_p = jnp.concatenate([e4, pad], 0)

            def flip(block):
                return jnp.concatenate(
                    [block[:, h * LANES : (h + 1) * LANES].T for h in range(GHEADS)], 1
                )[:PAIR]

            dk4 = mm(flip(dsb_p), stack_heads(q4, masks))
            dv4 = mm(flip(e4_p), stack_heads(dh4, masks))
            low_ref[rows, :] = jnp.concatenate([dq4, dk4, dv4], 1).astype(BF16)
            return carry

        lax.fori_loop(0, pairs, pair_step, 0, unroll=True)
        dtri_ref[r] = mm_nt(low_ref[...], group[...]).astype(BF16)


def qkv_grad_kernel(pairs, where, n1, dtri, keep, send, small_ref, tmp):
    tid, core = where[0], where[1]
    for r in range(GROUPS):
        tmp[...] = mm_tn(n1[...], dtri[r]).astype(BF16)
        give(keep, send, tmp, r, core, PACK_Q)
        small_ref[tid ^ r] = jnp.sum(dtri[r].astype(F32), 0, keepdims=True)


def input_bwd_kernel(layer, pairs, where, gmid, x, dtri, ln_g, place, w_qkv, gout_ref, small_ref, acc):
    last = layer == 0
    for r in range(GROUPS):
        part = mm_nt(dtri[r], w_qkv[r])
        if r == 0:
            acc[...] = part
        else:
            acc[...] += part
    small_ref[...] = jnp.zeros_like(small_ref)

    def back_rows(pair, carry):
        rows = rows_of(pair)
        dx, dg, db = norm_back(x[rows, :], ln_g[...], acc[rows, :])
        acc[rows, :] = gmid[rows, :] + dx
        small_ref[0:1, :] += dg
        small_ref[1:2, :] += db
        return carry

    lax.fori_loop(0, pairs, back_rows, 0)
    for image in range(pairs // 2):
        grad = acc[pl.ds(image * 2 * PAIR, 2 * PAIR), :]
        if last:
            gout_ref[image] = mm_tn(place[...], grad.astype(BF16)).astype(BF16)
        else:
            high, low = split_exact(grad)
            gout_ref[pl.ds(image * 2 * PAIR, 2 * PAIR), :] = mm(place[...], high) + mm(
                place[...], low
            )


def pack_start(plan, halved, where, weights, outs, sems):
    core = where[1]
    moves = []
    for weight, layer, out, blocks in plan:
        weight, out = weights[weight], outs[out]
        half = weight.shape[1] // 2
        for row, lane, rows, lanes, to_row, to_lane in blocks:
            from_row = pl.multiple_of(core * half + row, 16)
            moves.append(
                (
                    weight.at[layer, pl.ds(from_row, rows), pl.ds(lane, lanes)],
                    out.at[pl.ds(to_row, rows), pl.ds(to_lane, lanes)],
                )
            )
    copies = [pltpu.make_async_copy(a, b, sems.at[i]) for i, (a, b) in enumerate(moves)]
    for copy in copies:
        copy.start()

    def end():
        for copy in copies:
            copy.wait()
        for full, half in halved:
            size = outs[half].shape[0]
            rows = pl.ds(pl.multiple_of((where[2] & 1) * size, 16), size)
            outs[half][...] = outs[full][rows, :]

    return end


def merge_kernel(where, *refs):
    pieces, out, sems = refs[:-2], refs[-2], refs[-1]
    plan = [(pieces[0], out.at[0]), (pieces[1], out.at[1])]
    if len(pieces) == 3:
        plan.append((pieces[2], out.at[2]))
    else:
        odd = where[2] & 1
        size = pieces[2].shape[0]
        for piece, part in ((pieces[2], odd), (pieces[3], 1 - odd)):
            plan.append((piece, out.at[2, pl.ds(pl.multiple_of(part * size, 16), size)]))
    copies = [pltpu.make_async_copy(a, b, sems.at[i]) for i, (a, b) in enumerate(plan)]
    for copy in copies:
        copy.start()
    for copy in copies:
        copy.wait()


def exact_pick(row, chosen):
    high = row.astype(BF16)
    rest = row - high.astype(F32)
    mid = rest.astype(BF16)
    low = (rest - mid.astype(F32)).astype(BF16)
    parts = jnp.concatenate([high, mid, low, jnp.zeros((13, row.shape[1]), BF16)], 0)
    got = mm(parts, chosen)
    return got[0:1] + got[1:2] + got[2:3]


def small_kernel(index, *refs):
    out, acc, folded = refs[-3:]
    out[...] = jnp.zeros_like(out)
    pick = refs[0]
    for layer in range(LAYERS):
        small2, db1, small_q, small1, rel = refs[5 * layer + 1 : 5 * layer + 6]
        base = 24 * layer
        out[base : base + 4, :] = small2[...]
        for r in range(GROUPS):
            out[base + 4 + r : base + 5 + r, :] = db1[r]
            out[base + 8 + r : base + 9 + r, 0 : 2 * LANES] = exact_pick(small_q[r], pick[...])
        out[base + 12 : base + 14, :] = small1[...]

        def fold(head, carry, layer=layer, rel=rel):
            second = pltpu.roll(rel[head, WTOK : 2 * WTOK, :], LANES - WTOK, 1)
            at = pl.multiple_of((layer * HEADS + head) * 56, 8)
            folded[pl.ds(at, WTOK), :] = rel[head, 0:WTOK, :] + second
            return carry

        lax.fori_loop(0, HEADS, fold, 0)
    entry = lax.broadcasted_iota(jnp.int32, (2 * LANES, LANES), 0)
    count = LAYERS * HEADS
    acc[...] = jnp.zeros_like(acc)

    def one_row(i, carry):
        onehot = jnp.where(entry == index[i], 1.0, 0.0).astype(BF16)
        high, low = split_exact(folded[pl.ds(i, count, stride=56), :])
        acc[...] += mm_nt(onehot, jnp.concatenate([high, low], 0))
        return carry

    lax.fori_loop(0, WTOK, one_row, 0, unroll=7)
    total = acc[...].T
    total = total[:count] + total[count:]
    for layer in range(LAYERS):
        for part in range(2):
            at = layer * HEADS + part * 8
            out[24 * layer + 16 : 24 * layer + 24, part * 2 * LANES : (part + 1) * 2 * LANES] = total[
                at : at + 8, :
            ]


def add_go_kernel(where, *refs):
    count = (len(refs) - 4) // 2
    go_a, go_b, stay_a, stay_b = refs[-4:]
    row = 0
    for i in range(count):
        keep, got = refs[2 * i], refs[2 * i + 1]
        size = keep.shape[2]
        rows = slice(row, row + size)
        for part, (stay, go) in enumerate(((stay_a, go_a), (stay_b, go_b))):
            stay[:, rows, :] = keep[part, :2] + got[part, :2]
            go[:, rows, :] = keep[part, 2:] + got[part, 2:]
        row += size


def add_next_kernel(where, stay_a, stay_b, got_a, got_b, next_a, next_b, keep_a, keep_b):
    next_a[...] = stay_a[1] + got_a[1]
    next_b[...] = stay_b[1] + got_b[1]
    keep_a[...] = stay_a[0] + got_a[0]
    keep_b[...] = stay_b[0] + got_b[0]


def add_whole_kernel(where, keep_a, keep_b, got_a, got_b, out):
    size = keep_a.shape[0]
    out[0:size, :] = keep_a[...] + got_a[...]
    out[size:, :] = keep_b[...] + got_b[...]


def choose_kernel(where, mine, got, out):
    end = jnp.logical_or(where[2] == 0, where[2] == 3)
    out[...] = jnp.where(end, got[...], mine[...])


def add_level_kernel(where, keep_a, keep_b, got_a, got_b, mine, send):
    odd = where[2] & 1
    a = keep_a[...] + got_a[...]
    b = keep_b[...] + got_b[...]
    mine[...] = jnp.where(odd == 1, b, a)
    send[...] = jnp.where(odd == 1, a, b)


def add_kernel(where, a, b, out):
    out[...] = a[...] + b[...]


FINISH = {"q": (0, PACK_Q), "p": (1, PACK_P), "1": (2, PACK_1), "2": (3, PACK_2), "two": (3, PACK_TWO)}


def finish_kernel(plan, count, made, where, *refs):
    pieces = refs[:made]
    scratch, sems = refs[count + 5 : -1], refs[-1]
    core, odd = where[1], where[2] & 1
    copies = []
    first, slot = 0, 0
    results = refs[count : count + 4]
    for total, layer, names in plan:
        size = total // 2
        for name in names:
            index, blocks = FINISH[name]
            out = scratch[slot]
            half = out.shape[0] // 2
            for at, piece in enumerate(pieces):
                c = core if at < len(pieces) // 2 else 1 - core
                if len(pieces) == 2:
                    for row, lane, rows, lanes, to_row, to_lane in blocks:
                        target = pl.multiple_of(c * half + row, 16)
                        out[pl.ds(target, rows), lane : lane + lanes] = piece[
                            first + to_row : first + to_row + rows, to_lane : to_lane + lanes
                        ].astype(F32)
                    continue
                for part in range(2):

                    @pl.when((odd if at % 2 == 0 else 1 - odd) == part)
                    def _(piece=piece, part=part, c=c, out=out, first=first, size=size, blocks=blocks):
                        for row, lane, rows, lanes, to_row, to_lane in blocks:
                            begin = max(to_row, part * size)
                            end = min(to_row + rows, (part + 1) * size)
                            if begin >= end:
                                continue
                            target = pl.multiple_of(c * half + row + begin - to_row, 16)
                            source = first + begin - part * size
                            out[pl.ds(target, end - begin), lane : lane + lanes] = piece[
                                source : source + end - begin, to_lane : to_lane + lanes
                            ].astype(F32)

            copies.append(pltpu.make_async_copy(out, results[index].at[layer], sems.at[slot]))
            copies[-1].start()
            slot += 1
        first += size * (1 if len(pieces) == 4 else 2)
    for copy in copies:
        copy.wait()


def own_kernel(where, little, got, out):
    tid = where[0]
    out[...] = jnp.zeros_like(out)
    for layer in range(LAYERS):
        base, to = 24 * layer, 16 * layer

        def put(rows, row, lane, lanes):
            out[to + rows[0] : to + rows[1], 0:lanes] = (
                little[base + row : base + row + rows[1] - rows[0], lane : lane + lanes]
                + got[base + row : base + row + rows[1] - rows[0], lane : lane + lanes]
            )

        put((0, 4), 0, 0, C)
        put((4, 6), 12, 0, C)
        for r in range(GROUPS):

            @pl.when(tid == r)
            def _(r=r, put=put):
                put((6, 7), 4 + r, 0, C)
                put((7, 8), 8 + r, 0, 2 * LANES)
                put((8, 12), 16 + GHEADS * (r % 2), 2 * LANES * (r // 2), 2 * LANES)


def unpack_kernel(where, little, *outs):
    for layer in range(LAYERS):
        base = 16 * layer
        for out, at in zip(outs[:7], (4, 5, 3, 1, 2, 0, 6)):
            out[layer : layer + 1, :] = little[base + at : base + at + 1, :]
        outs[7][layer : layer + 1, :] = little[base + 7 : base + 8, 0 : 2 * LANES]
        outs[8][layer] = little[base + 8 : base + 12, 0:TABLE]


VM = pl.BlockSpec(memory_space=pltpu.VMEM)
SM = pl.BlockSpec(memory_space=pltpu.SMEM)
ANY = pl.BlockSpec(memory_space=pl.ANY)
VC = pl.BlockSpec(memory_space=pltpu.VMEM)
HB = pl.BlockSpec(memory_space=pltpu.HBM)


def pinned(shape, dtype):
    return pltpu.VMEM(shape, dtype)


def place_operand(spec, value):
    if spec is VC:
        return pltpu.with_memory_space_constraint(value, pltpu.VMEM)
    if spec is HB:
        return pltpu.with_memory_space_constraint(value, pltpu.HBM)
    return value


def call(
    kernel, specs, args, outs, scratch=(), flops=0, out_specs=None, limit=2, moved=4, after=(), aliases=None
):
    count = len(args)
    skip = count + len(after)

    def body(*refs):
        kernel(*refs[:count], *refs[skip:])

    return pl.pallas_call(
        body,
        out_shape=outs,
        in_specs=list(specs) + [ANY] * len(after),
        out_specs=[VM] * len(outs) if out_specs is None else out_specs,
        scratch_shapes=scratch,
        input_output_aliases=aliases or {},
        compiler_params=pltpu.CompilerParams(vmem_limit_bytes=limit << 20),
        cost_estimate=pl.CostEstimate(flops=1, bytes_accessed=1, transcendentals=0),
    )(*[place_operand(spec, arg) for spec, arg in zip(specs, args)], *after)


def struct(shape, dtype):
    return jax.ShapeDtypeStruct(shape, dtype)


DIM_Q, DIM_P, DIM_1, DIM_2 = (C, TRI), (LANES, C), (C, HID), (HID, C)
GF = 1 << 30


def fetch_sems(*dims):
    return [
        pltpu.SemaphoreType.DMA((1 + 6 * (len(PACK_Q) if d == DIM_Q else 1),)) for d in dims
    ]


def chunk_outs(rows):
    return [pinned((2, GROUPS, rows // 2, C), BF16)] * 2


def attn_fwd(layer, batch, where, x, place, ln_g, ln_b, b_qkv, group, bias, w):
    pairs = 2 * batch
    rows = pairs * PAIR
    outs = [
        pinned((rows, C), BF16),
        pinned((GROUPS, rows, TRI), BF16),
        pinned((GROUPS, pairs, PAIR, GHEADS * LANES), BF16),
        pinned((GROUPS, rows, LANES), F32),
        pinned((rows, C), BF16),
        pinned((GROUPS,) + DIM_Q, BF16),
    ]
    if layer == 0:
        outs = [pinned((rows, C), F32)] + outs
    return call(
        functools.partial(attn_fwd_kernel, layer, pairs, w.q_base),
        [SM, VM if layer == 0 else VC] + [VM] * 5 + [VC] + [HB] + [ANY] * 2,
        [where, x, place, ln_g, ln_b, b_qkv, group, bias, *w.qkv],
        outs,
        fetch_sems(DIM_Q),
        flops=8 * GF,
        limit=9,
    )


def mlp_fwd(layer, batch, where, x, ho, b_proj, ln_g, ln_b, b1, b2, place, w):
    pairs = 2 * batch
    rows = pairs * PAIR
    last = layer == LAYERS - 1
    outs = [
        struct((batch, TOK, C), BF16) if last else pinned((rows, C), F32),
        pinned((rows, C), F32),
        pinned((rows, C), BF16),
        pinned((GROUPS, rows, HID), BF16),
        pinned((GROUPS, rows, HID), BF16),
    ] + [pinned((GROUPS,) + dim, BF16) for dim in (DIM_P, DIM_1, DIM_2)]
    return call(
        functools.partial(mlp_fwd_kernel, layer, pairs),
        [SM, VC, VC] + [VM] * 6 + [HB] * 3 + [ANY] * 2,
        [where, x, ho, b_proj, ln_g, ln_b, b1, b2, place, w.own_p, w.own_1, w.own_2, *w.p_m],
        outs,
        fetch_sems(DIM_P, DIM_1, DIM_2)
        + [pltpu.VMEM((rows, C), F32), pltpu.VMEM((rows, HID), F32)],
        flops=8 * GF,
        limit=12,
    )


def mlp_bwd(layer, batch, where, g, place, act, dact, mid, n2, ho, rinv, ln_g, w, after):
    pairs = 2 * batch
    rows = pairs * PAIR
    outs = chunk_outs(M_ROWS) + [
        pinned((rows, C), F32),
        pinned((GROUPS, rows, LANES), BF16),
        pinned((GROUPS, rows, LANES), BF16),
        struct((4, C), F32),
        struct((GROUPS, 1, HID), F32),
    ]
    return call(
        functools.partial(mlp_bwd_kernel, layer, pairs),
        [SM, VM if layer == LAYERS - 1 else VC, VM] + [VC] * 6 + [VM] + [VC] * 3,
        [where, g, place, act, dact, mid, n2, ho, rinv, ln_g, *w],
        outs,
        [
            pltpu.VMEM((rows, C), F32),
            pltpu.VMEM((rows, C), BF16),
            pltpu.VMEM((GROUPS, rows, HID), BF16),
            pltpu.VMEM((rows, C), F32),
            pltpu.VMEM(DIM_1, BF16),
            pltpu.VMEM(DIM_P, BF16),
        ],
        flops=14 * GF,
        limit=18,
        after=after,
    )


def hidden_bwd(layer, batch, where, g, act, dact, w, after):
    pairs = 2 * batch
    rows = pairs * PAIR
    return call(
        functools.partial(hidden_bwd_kernel, layer, pairs),
        [SM] + [VC] * 4,
        [where, g, act, dact, w[2]],
        chunk_outs(TWO_ROWS) + [pinned((GROUPS, rows, HID), BF16)],
        [pltpu.VMEM((rows, C), BF16), pltpu.VMEM(DIM_2, BF16)],
        flops=5 * GF,
        limit=9,
        after=after,
    )


def middle_bwd(layer, batch, where, gp, g, mid, n2, ho, rinv, ln_g, w, after):
    pairs = 2 * batch
    rows = pairs * PAIR
    return call(
        functools.partial(middle_bwd_kernel, layer, pairs),
        [SM] + [VC] * 6 + [VM] + [VC] * 2,
        [where, gp, g, mid, n2, ho, rinv, ln_g, w[0], w[1]],
        chunk_outs(ONE_ROWS)
        + [
            pinned((rows, C), F32),
            pinned((GROUPS, rows, LANES), BF16),
            pinned((GROUPS, rows, LANES), BF16),
            struct((4, C), F32),
            struct((GROUPS, 1, HID), F32),
        ],
        [
            pltpu.VMEM((rows, C), BF16),
            pltpu.VMEM((rows, C), F32),
            pltpu.VMEM(DIM_1, BF16),
            pltpu.VMEM(DIM_P, BF16),
        ],
        flops=9 * GF,
        limit=12,
        after=after,
    )


def attn_bwd(batch, where, dh, u, tri, e, group, after):
    pairs = 2 * batch
    rows = pairs * PAIR
    return call(
        functools.partial(attn_bwd_kernel, pairs),
        [SM] + [VC] * 4 + [VM],
        [where, dh, u, tri, e, group],
        [pinned((GROUPS, rows, TRI), BF16), pinned((HEADS, PAIR, LANES), F32)],
        [pltpu.VMEM((rows, TRI), BF16)],
        flops=12 * GF,
        limit=9,
        after=after,
    )


def qkv_grad(batch, where, n1, dtri, after):
    return call(
        functools.partial(qkv_grad_kernel, 2 * batch),
        [SM] + [VC] * 2,
        [where, n1, dtri],
        chunk_outs(Q_ROWS) + [struct((GROUPS, 1, TRI), F32)],
        [pltpu.VMEM(DIM_Q, BF16)],
        flops=3 * GF,
        limit=6,
        after=after,
    )


def input_bwd(layer, batch, where, gmid, x, dtri, ln_g, place, w, after):
    pairs = 2 * batch
    rows = pairs * PAIR
    return call(
        functools.partial(input_bwd_kernel, layer, pairs),
        [SM, VC, VC, VC, VM, VM, VC],
        [where, gmid, x, dtri, ln_g, place, w],
        [
            struct((batch, TOK, C), BF16) if layer == 0 else pinned((rows, C), F32),
            struct((2, C), F32),
        ],
        [pltpu.VMEM((rows, C), F32)],
        flops=3 * GF,
        limit=9,
        after=after,
    )


def full_bias(qv_rows, heads):
    parts = qv_rows.reshape(LAYERS, heads, 2, HEAD_DIM)
    full = jnp.stack([parts[:, :, 0], jnp.zeros_like(parts[:, :, 0]), parts[:, :, 1]], 2)
    return full.reshape(LAYERS, heads * 3 * HEAD_DIM)


def swap(x, axis, size, bit):
    return lax.ppermute(x, axis, [(i, i ^ bit) for i in range(size)])


class Weights:
    def __init__(self, own, p_q, p_m, q_base=0):
        own_q, self.own_p, self.own_1, self.own_2 = own
        self.q_base = q_base
        self.qkv = [own_q] + p_q
        self.p_m = p_m


class Direct:
    def __init__(self, dp):
        self.dp = dp
        self.t = lax.axis_index("tensor")
        d = lax.axis_index("dp")
        self.where = jnp.stack([self.t, d % 2, d // 2]).astype(jnp.int32)

    def x(self, v):
        return swap(v, "tensor", 4, 1)

    def y(self, v):
        return swap(v, "tensor", 4, 2)

    def diagonal(self, v):
        return swap(v, "tensor", 4, 3)

    def other(self, v):
        return swap(v, "dp", self.dp, 1)

    def level(self, v, k):
        return swap(v, "dp", self.dp, 2 * k)

    def near(self, v):
        return self.x(v), self.y(v), self.diagonal(v)

    def plan(self, parts, first=4):
        plan, outs, halved = [], [], []
        for part in parts:
            at, base = len(outs), 0
            for layer, chunk in part:
                for weight, blocks in (((0, PACK_Q),), ((2, PACK_1), (1, PACK_P), (3, PACK_2)))[chunk]:
                    plan.append((weight, layer, at, moved_down(blocks, base)))
                base += (Q_ROWS, M_ROWS)[chunk]
            outs.append(pinned((base, C), BF16))
            if base == M_ROWS:
                outs.append(pinned((M_ROWS // 2, C), BF16))
                halved.append((at, at + 1))
        return plan, outs, halved

    def pack(self, arrays, parts, after=()):
        plan, outs, halved = self.plan(parts)
        count = sum(len(blocks) for _, _, _, blocks in plan)

        def body(where, *refs):
            pack_start(plan, halved, where, refs[:4], refs[4:-1], refs[-1])()

        return call(
            body, [SM] + [HB] * 4, [self.where, *arrays], outs, [pltpu.SemaphoreType.DMA((count,))],
            after=after,
        )

    def near_halved(self, full, half):
        return self.diagonal(half), self.x(full), self.y(full)

    def merge(self, pieces, arrays=(), parts=(), after=()):
        rows, count = pieces[0].shape[0], len(pieces)
        plan, outs, halved = self.plan(parts, count + 4)
        outs = [pinned((3, rows, C), BF16)] + outs

        def body(where, *refs):
            spare = refs[: count + 4] if parts else refs[:count]
            outs = refs[len(spare) : -2]
            late = pack_start(plan, halved, where, spare[count:], outs[1:], refs[-1]) if parts else None
            merge_kernel(where, *refs[:count], outs[0], refs[-2])
            if parts:
                late()

        moves = sum(len(blocks) for _, _, _, blocks in plan)
        near, *packed = call(
            body, [SM] + [ANY] * count + [HB] * len(arrays), [self.where, *pieces, *arrays], outs,
            [pltpu.SemaphoreType.DMA((4,)), pltpu.SemaphoreType.DMA((max(moves, 1),))], after=after,
            limit=10,
        )
        return [[near, self.other(near)], *packed]

    def merge_halved(self, pieces, far_half, **order):
        half, x, y = pieces
        return self.merge((x, y, half, far_half), **order)

    def step(self, *parts, passing=(), after=()):
        kernels, args, specs, outs, cuts = [], [self.where], [SM], [], []
        for kernel, values, results in parts:
            kernels.append((kernel, len(args) - 1, len(values), len(outs), len(results)))
            args += values
            specs += [VC] * len(values)
            outs += results
        total_in, total_out = len(args) - 1, len(outs)
        aliases = {}
        for value in passing:
            aliases[len(args)] = len(outs)
            args.append(value)
            specs.append(ANY)
            outs.append(struct(value.shape, value.dtype))

        def body(where, *refs):
            refs_in, refs_out = refs[: total_in + len(passing)], refs[total_in + len(passing) :]
            for kernel, at, count, out, results in kernels:
                kernel(where, *refs_in[at : at + count], *refs_out[out : out + results])

        got = call(
            body, specs, args, outs, after=after, aliases=aliases,
            out_specs=[VM] * total_out + [ANY] * len(passing),
        )
        split = []
        for _, _, _, out, results in kernels:
            split.append(got[out : out + results])
        return split + list(got[total_out:])


    def swap_cores(self, keep, send):
        return keep, self.other(send)

    def first_way(self, *states):
        args = [v for state in states for v in state]
        two = pinned((2, sum(keep.shape[2] for keep, _ in states), C), BF16)
        return add_go_kernel, args, [two] * 4

    def send_first(self, done):
        go_a, go_b, stay_a, stay_b = done
        return stay_a, stay_b, self.x(go_a), self.y(go_b)

    def second_way(self, state):
        one = pinned(state[0].shape[1:], BF16)
        return add_next_kernel, list(state), [one] * 4

    def send_second(self, done):
        next_a, next_b, keep_a, keep_b = done
        return keep_a, keep_b, self.y(next_a), self.x(next_b)

    def join(self, state):
        one = pinned(state[0].shape, BF16)
        return add_level_kernel, list(state), [one] * 2

    def join_whole(self, state):
        rows = 2 * state[0].shape[0]
        return add_whole_kernel, list(state), [pinned((rows, C), BF16)]

    def line(self, v, pairs):
        return lax.ppermute(
            v, "dp", [(2 * a + core, 2 * b + core) for a, b in pairs for core in range(2)]
        )

    def choose(self, mine, got):
        return choose_kernel, [mine, got], [pinned(mine.shape, BF16)]

    def send_level(self, state, k):
        mine, send = state
        return mine, self.level(send, k)

    def add(self, state):
        return add_kernel, list(state), [pinned(state[0].shape, BF16)]

    def own_small(self, state):
        return own_kernel, list(state), [pinned((16 * LAYERS, C), F32)]

    def add_small(self, state):
        return add_kernel, list(state), [pinned(state[0].shape, F32)]

    def finish(self, plan, pieces, before=None, after=()):
        dims = (DIM_Q, DIM_P, DIM_1, DIM_2)
        made = len(pieces)
        args, specs = [self.where, *pieces], [SM] + [VC] * made
        aliases = {}
        if before is not None:
            aliases = {1 + made + i: i for i in range(4)}
            args += before[:4]
            specs += [HB] * 4
        scratch = [
            pltpu.VMEM(dims[FINISH[name][0]], F32) for _, _, names in plan for name in names
        ]
        return call(
            functools.partial(finish_kernel, plan, len(args) - 1, made), specs, args,
            [pltpu.HBM((LAYERS,) + dim, F32) for dim in dims] + [pinned((8, LANES), F32)],
            scratch + [pltpu.SemaphoreType.DMA((len(scratch),))],
            out_specs=[HB] * 4 + [VM], limit=6, after=after, aliases=aliases,
        )

    def unpack(self, little, after=()):
        one = struct((LAYERS, C), F32)
        outs = [one] * 7 + [struct((LAYERS, 2 * LANES), F32), struct((LAYERS, GHEADS, TABLE), F32)]
        return call(unpack_kernel, [SM, VC], [self.where, little], outs, after=after)


class Whole:
    def __init__(self):
        self.where = jnp.zeros((3,), jnp.int32)

    def gather(self, arrays, small):
        qkv, proj, w1, w2 = [
            lax.all_gather(v, "tensor", axis=axis, tiled=True) for v, axis in zip(arrays, (2, 1, 2, 1))
        ]
        qkv = qkv.reshape(LAYERS, C, GROUPS, TRI).transpose(0, 2, 1, 3)
        proj = proj.reshape(LAYERS, GROUPS, LANES, C)
        w1 = w1.reshape(LAYERS, C, GROUPS, HID).transpose(0, 2, 1, 3)
        w2 = w2.reshape(LAYERS, GROUPS, HID, C)
        own = [v[:, 0] for v in (qkv, proj, w1, w2)]

        def pack(parts, rows):
            out = jnp.zeros((rows, C), BF16)
            for v, blocks in parts:
                for row, lane, count, lanes, to_row, to_lane in blocks:
                    block = v[row : row + count, lane : lane + lanes]
                    out = out.at[to_row : to_row + count, to_lane : to_lane + lanes].set(block)
            return out

        weights = []
        for layer in range(LAYERS):
            p_q, p_m = [], []
            for side in range(2):
                side_q, side_m = [], []
                for r in range(1, GROUPS):

                    def half(v):
                        size = v.shape[2] // 2
                        return v[layer, r, side * size : (side + 1) * size]

                    side_q.append(pack([(half(qkv), PACK_Q)], Q_ROWS))
                    parts = [(half(w1), PACK_1), (half(proj), PACK_P), (half(w2), PACK_2)]
                    side_m.append(pack(parts, M_ROWS))
                p_q.append(jnp.stack(side_q))
                p_m.append(jnp.stack(side_m))
            weights.append(Weights(own, p_q, p_m))
        return weights, lax.all_gather(small, "tensor", axis=0)

    def sum_small(self, v):
        return lax.psum(v, ("dp", "tensor"))

    def finish(self, chunks):
        full = {}
        for name, chunk, blocks, dim in (
            ("q", 1, PACK_Q, DIM_Q), ("p", 0, PACK_P, DIM_P), ("1", 0, PACK_1, DIM_1), ("2", 0, PACK_2, DIM_2)
        ):
            layers = []
            for layer in range(LAYERS):
                sides = []
                for v in chunks[layer][chunk]:
                    shares = []
                    for r in range(GROUPS):
                        packed = jnp.concatenate(
                            [v[part, ORDERS[part].index(r)] for part in range(2)], 0
                        )
                        out = jnp.zeros((dim[0] // 2, dim[1]), BF16)
                        for row, lane, count, lanes, to_row, to_lane in blocks:
                            block = packed[to_row : to_row + count, to_lane : to_lane + lanes]
                            out = out.at[row : row + count, lane : lane + lanes].set(block)
                        shares.append(out)
                    sides.append(jnp.stack(shares))
                layers.append(jnp.concatenate(sides, 1))
            full[name] = jnp.stack(layers)
        outs = []
        for name, axis in zip("qp12", (2, 1, 2, 1)):
            v = full[name]
            if axis == 2:
                v = v.transpose(0, 2, 1, 3).reshape(LAYERS, C, -1)
            else:
                v = v.reshape(LAYERS, -1, C)
            v = lax.psum_scatter(v, "tensor", scatter_dimension=axis, tiled=True)
            outs.append(lax.psum(v, "dp").astype(F32))
        return outs


def shards(
    tensor, dp, images_in, ln1_gain, ln1_bias, qkv_weight, qv_bias, rel_table, proj_weight,
    proj_bias, ln2_gain, ln2_bias, fc1_weight, fc1_bias, fc2_weight, fc2_bias, rel_index,
    region_ids, out_cot,
):
    batch = images_in.shape[0]
    direct = tensor == 4 and dp == 8
    net = Direct(dp) if direct else Whole()
    where = net.where
    wide = 2 * LANES
    own = (qkv_weight, proj_weight, fc1_weight, fc2_weight)

    heads = rel_table.shape[2]
    table = jnp.pad(rel_table.transpose(2, 0, 1), ((0, 0), (0, 0), (0, wide - TABLE)))
    bias_part = full_bias(qv_bias, heads)
    packed = jnp.concatenate([table.reshape(-1), bias_part.reshape(-1), fc1_bias.reshape(-1)])
    packed = packed.reshape(1, -1)
    if direct:
        (q0,) = net.pack(own, [[(0, 0)]])
        near_q0 = net.near(q0)
        every = jnp.concatenate([packed, net.x(packed)], 0)
        every = jnp.concatenate([every, net.y(every)], 0)
    else:
        weights, every = net.gather(own, packed)
    every = every.reshape(tensor, -1)
    cut1 = heads * LAYERS * wide
    cut2 = cut1 + bias_part.size
    table = every[:, :cut1].reshape(HEADS, LAYERS, wide).transpose(1, 0, 2)
    table = table.reshape(LAYERS * HEADS, 1, wide)
    b_qkv = every[:, cut1:cut2].reshape(tensor, LAYERS, -1).transpose(1, 0, 2)
    b_qkv = b_qkv.reshape(LAYERS, GROUPS, 1, TRI)
    b1 = every[:, cut2:].reshape(tensor, LAYERS, -1).transpose(1, 0, 2)
    b1 = b1.reshape(LAYERS, GROUPS, 1, HID)
    index = jnp.pad(rel_index + 1, ((0, PAIR - WTOK), (0, LANES - WTOK)))
    index = index + jnp.pad(rel_index + 1, ((WTOK, PAIR - 2 * WTOK), (WTOK, LANES - 2 * WTOK))) - 1
    ids = region_ids.astype(BF16)
    ids_col = jnp.broadcast_to(ids[:, None], (TOK, LANES))
    ids_row = jnp.broadcast_to(ids[None, :], (16, TOK))
    lanes_place = np.zeros((2 * LANES, TOK), np.float32)
    for pair in range(2):
        lanes_place[pair * LANES : pair * LANES + PAIR] = PLACE[0][pair * PAIR : (pair + 1) * PAIR]
    place = [jnp.asarray(PLACE[layer], BF16) for layer in range(LAYERS)]
    after = ()
    if direct:
        w_q0, m0 = net.merge(near_q0, own, [[(0, 1), (1, 0)]])
        near_m0 = net.near(m0)
        after = w_q0[:1]

    def bias_of(layer, after=()):
        return call(
            functools.partial(bias_kernel, layer),
            [VM] * 6,
            [table, index, ids_col, ids_row, place[0], jnp.asarray(lanes_place, BF16)],
            [pinned((1 + layer, HEADS, PAIR, LANES), F32)],
            flops=4 * GF,
            after=after,
        )[0]

    bias = [bias_of(0, after), None]
    step01 = jnp.asarray(PLACE[1] @ PLACE[0].T, BF16)
    step10 = jnp.asarray(PLACE[0] @ PLACE[1].T, BF16)
    group = jnp.asarray(GROUP, BF16)

    def row(v, layer):
        return v[layer][None]

    saved, w_q, w_m = [None] * LAYERS, [None] * LAYERS, [None] * LAYERS
    rels, littles = [None] * LAYERS, [None] * LAYERS

    def attn(layer, state, w):
        res = attn_fwd(
            layer, batch, where, state, place[0], row(ln1_gain, layer), row(ln1_bias, layer),
            b_qkv[layer], group, bias[layer], w,
        )
        *res, w_q[layer] = res
        saved[layer] = tuple(res) if layer == 0 else (state,) + tuple(res)

    def mlp(layer, w):
        x, n1, tri, e, rinv, ho = saved[layer]
        state, *rest, wp, w1, w2 = mlp_fwd(
            layer, batch, where, x, ho, row(proj_bias, layer), row(ln2_gain, layer),
            row(ln2_bias, layer), b1[layer], row(fc2_bias, layer), step01 if layer == 0 else place[1],
            w,
        )
        saved[layer] += tuple(rest)
        w_m[layer] = (wp, w1, w2)
        return state

    def mlp_back(layer, grad, after=()):
        x, n1, tri, e, rinv, ho, mid, n2, act, dact = saved[layer]
        keep, send, gmid, dh, u, small2, db1 = mlp_bwd(
            layer, batch, where, grad, place[1], act, dact, mid, n2, ho, rinv,
            row(ln2_gain, layer), w_m[layer], after,
        )
        littles[layer] = {"a": small2, "b": db1}
        return (keep, send), gmid, dh, u

    def hidden_back_0(grad, after):
        act, dact = saved[0][8:]
        keep, send, gp = hidden_bwd(0, batch, where, grad, act, dact, w_m[0], after)
        return (keep, send), gp

    def middle_back_0(gp, grad, after):
        x, n1, tri, e, rinv, ho, mid, n2, act, dact = saved[0]
        keep, send, gmid, dh, u, small2, db1 = middle_bwd(
            0, batch, where, gp, grad, mid, n2, ho, rinv, row(ln2_gain, 0), w_m[0], after
        )
        littles[0] = {"a": small2, "b": db1}
        return (keep, send), gmid, dh, u

    def attn_back(layer, dh, u, after=()):
        dtri, rels[layer] = attn_bwd(
            batch, where, dh, u, saved[layer][2], saved[layer][3], group, after
        )
        return dtri

    def qkv_back(layer, dtri, after=()):
        keep, send, small_q = qkv_grad(batch, where, saved[layer][1], dtri, after)
        littles[layer]["c"] = small_q
        return keep, send

    def input_back(layer, gmid, dtri, after=()):
        grad, small1 = input_bwd(
            layer, batch, where, gmid, saved[layer][0], dtri, row(ln1_gain, layer),
            step10 if layer else place[0], w_q[layer], after,
        )
        littles[layer]["d"] = small1
        return grad

    def small_sums(after=()):
        args = [index.reshape(PAIR, 1, LANES), jnp.asarray(PICK, BF16)]
        for layer in range(LAYERS):
            args += [littles[layer][name] for name in "abcd"] + [rels[layer]]
        specs = [VM] * 2 + ([VM] * 4 + [VC]) * LAYERS
        return call(
            small_kernel, specs, args, [pinned((24 * LAYERS, C), F32)],
            [
                pltpu.VMEM((wide, 2 * LAYERS * HEADS), F32),
                pltpu.VMEM((LAYERS * HEADS * 56, LANES), F32),
            ],
            after=after, limit=4,
        )[0]

    if direct:
        w0 = Weights(own, w_q0, None)
        attn(0, images_in, w0)
        bias[1] = bias_of(1, saved[0][5:6])
        w0.p_m, m1, _ = net.merge(near_m0, own, [[(1, 1)]], after=(bias[1],))
        near_m1 = net.near(m1)
        state = mlp(0, w0)
        w1 = Weights(own, w0.p_m, None, M_ROWS)
        attn(1, state, w1)
        (w1.p_m,) = net.merge(near_m1, after=saved[1][5:6])
        output = mlp(1, w1)

        m1, gmid, dh, u = mlp_back(1, out_cot, after=(output,))
        m1 = net.swap_cores(*m1)
        dtri = attn_back(1, dh, u)
        (g1,) = net.step(net.first_way(m1), after=(dtri,))
        g1 = net.send_first(g1)
        grad = input_back(1, gmid, dtri, after=g1[:1])
        two, gp = hidden_back_0(grad, after=())
        q1 = qkv_back(1, dtri, after=(gp,))
        one, gmid, dh, u = middle_back_0(gp, grad, after=q1[:1])
        g1, send_two, send_q1, send_one = net.step(
            net.second_way(g1), passing=two[1:] + q1[1:] + one[1:], after=(gmid,)
        )
        dtri = attn_back(0, dh, u, after=g1[:1])
        g1 = net.send_second(g1)
        two = net.swap_cores(two[0], send_two)
        q1 = net.swap_cores(q1[0], send_q1)
        one = net.swap_cores(one[0], send_one)
        q0 = qkv_back(0, dtri)
        g1, g2, send = net.step(
            net.join(g1), net.first_way(q1, two), passing=q0[1:], after=q0[:1]
        )
        g1 = net.send_level(g1, 1)
        grad = input_back(0, gmid, dtri, after=g2[:1])
        g2 = net.send_first(g2)
        q0 = net.swap_cores(q0[0], send)
        g3, (g1,) = net.step(net.first_way(one, q0), net.add(g1), after=(grad,))
        g3 = net.send_first(g3)
        g1 = net.send_level((g1, g1), 2)
        (g2,) = net.step(net.second_way(g2), after=g3[:1])
        g2 = net.send_second(g2)
        little = small_sums(after=g2[:1])
        g3, g2, (g1,), little = net.step(
            net.second_way(g3), net.join(g2), net.add(g1), passing=(little,)
        )
        g3 = net.send_second(g3)
        g2 = net.send_level(g2, 1)
        near1 = net.level(g1, 1)
        little = (little, net.other(little))
        g3, (g2,), (little,), side1, near1 = net.step(
            net.join(g3), net.add(g2), net.add_small(little), passing=(g1, near1)
        )
        g3 = net.send_level(g3, 1)
        g2 = net.send_level((g2, g2), 2)
        little = (little, net.x(little))
        g1 = [side1, near1, net.other(side1), net.other(near1)]
        (g3,), (little,) = net.step(net.add(g3), net.add_small(little))
        g3 = net.send_level((g3, g3), 2)
        little = (little, net.y(little))
        (g2,), (little,) = net.step(net.add(g2), net.own_small(little), after=(g3[0],))
        near2, side2 = net.level(g2, 1), net.other(g2)
        little = (little, net.level(little, 1))
        results = net.finish([(M_ROWS, 1, ("1", "p", "2"))], g1)
        (little,), near2 = net.step(net.add_small(little), passing=(near2,), after=results[4:])
        little = (little, net.level(little, 2))
        g2 = [g2, near2, side2, net.other(near2)]
        results = net.finish([(Q_ROWS, 1, ("q",)), (TWO_ROWS, 0, ("two",))], g2, results)
        (g3,), (little,) = net.step(net.add(g3), net.add_small(little), after=results[4:])
        near3, side3 = net.level(g3, 1), net.other(g3)
        small = list(net.unpack(little))
        (near3,) = net.step(passing=(near3,), after=small[7:8])
        dwq, dwp, dw1, dw2, _ = net.finish(
            [(ONE_ROWS, 0, ("1", "p")), (Q_ROWS, 0, ("q",))],
            [g3, near3, side3, net.other(near3)], results,
        )
        small[8] = small[8].transpose(0, 2, 1)
        return (
            output, grad, small[0], small[1], dwq, small[7], small[8], dwp, small[2], small[3],
            small[4], dw1, small[6], dw2, small[5],
        )
    else:
        state = images_in
        bias[1] = bias_of(1)
        for layer in range(LAYERS):
            attn(layer, state, weights[layer])
            state = mlp(layer, weights[layer])
        output = state
        grad = out_cot
        reduced = [None] * LAYERS
        for layer in reversed(range(LAYERS)):
            m, gmid, dh, u = mlp_back(layer, grad)
            dtri = attn_back(layer, dh, u)
            reduced[layer] = (m, qkv_back(layer, dtri))
            grad = input_back(layer, gmid, dtri)
        little = net.sum_small(small_sums())
        dwq, dwp, dw1, dw2 = net.finish(reduced)
    little = little.reshape(LAYERS, 24, C)
    small_q = little[:, 8:12, : 2 * LANES].reshape(LAYERS, -1)
    rel = little[:, 16:].reshape(LAYERS, 8, 2, wide)[..., :TABLE].transpose(0, 3, 2, 1)
    rel = rel.reshape(LAYERS, TABLE, HEADS)
    db1 = little[:, 4:8].reshape(LAYERS, FF)
    mine = lax.axis_index("tensor")

    def share(v, axis):
        size = v.shape[axis] // tensor
        return lax.dynamic_slice_in_dim(v, mine * size, size, axis)

    return (
        output, grad, little[:, 12], little[:, 13], dwq, share(small_q, 1), share(rel, 2), dwp,
        little[:, 3], little[:, 1], little[:, 2], dw1, share(db1, 1), dw2, little[:, 0],
    )


def solution(mesh):
    tokens = P(("dp", "tensor"), None, None)
    cols, rows = P(None, None, "tensor"), P(None, "tensor", None)
    part = P(None, "tensor")
    return jax.shard_map(
        functools.partial(shards, mesh.shape["tensor"], mesh.shape["dp"]),
        mesh=mesh,
        in_specs=(
            tokens, P(), P(), cols, part, cols, rows, P(), P(), P(), cols, part, rows, P(), P(),
            P(), tokens,
        ),
        out_specs=(
            tokens, tokens, P(), P(), cols, part, cols, rows, P(), P(), P(), cols, part, rows, P(),
        ),
        check_vma=False,
    )
```

```python
import functools

import jax
import jax.numpy as jnp
import numpy as np
from jax import lax
from jax.experimental import pallas as pl
from jax.experimental.pallas import tpu as pltpu
from jax.sharding import PartitionSpec as P

C = 512
HEADS = 16
HEAD_DIM = 32
FF = 2048
WIN = 7
GRID = 14
SHIFT = 3
LAYERS = 2
TOK = 196
WTOK = 49
TABLE = 169
PAIR = 112
LANES = 128
GROUPS = 4
GHEADS = HEADS // GROUPS
TRI = 3 * LANES
HID = FF // GROUPS
SCALE = HEAD_DIM ** (-0.5)
NEG = -1e30
F32 = jnp.float32
BF16 = jnp.bfloat16


def window_tokens(offset):
    cells = np.arange(TOK).reshape(GRID, GRID)
    cells = np.roll(cells, (-offset, -offset), (0, 1))
    cells = cells.reshape(2, WIN, 2, WIN).transpose(0, 2, 1, 3)
    return cells.reshape(4, WTOK)


def place_matrix(offset):
    tokens = window_tokens(offset).reshape(2, 2 * WTOK)
    out = np.zeros((2 * PAIR, TOK), np.float32)
    for pair in range(2):
        out[pair * PAIR + np.arange(2 * WTOK), tokens[pair]] = 1.0
    return out


PLACE = [place_matrix(SHIFT if layer % 2 == 1 else 0) for layer in range(LAYERS)]


def group_matrix():
    out = np.zeros((TRI, TRI), np.float32)
    for head in range(GHEADS):
        for part in range(3):
            for pos in range(HEAD_DIM):
                out[
                    (head * 3 + part) * HEAD_DIM + pos, (part * GHEADS + head) * HEAD_DIM + pos
                ] = 1.0
    return out


GROUP = group_matrix()


def pick_matrix():
    out = np.zeros((TRI, 2 * LANES), np.float32)
    for head in range(GHEADS):
        for to, part in enumerate((0, 2)):
            for pos in range(HEAD_DIM):
                out[(head * 3 + part) * HEAD_DIM + pos, (head * 2 + to) * HEAD_DIM + pos] = 1.0
    return out


PICK = pick_matrix()


def mm(a, b):
    return jnp.dot(a, b, preferred_element_type=F32)


def mm_nt(a, b):
    return lax.dot_general(a, b, (((1,), (1,)), ((), ())), preferred_element_type=F32)


def mm_tn(a, b):
    return lax.dot_general(a, b, (((0,), (0,)), ((), ())), preferred_element_type=F32)


def normalize(x):
    centre = x - jnp.mean(x, -1, keepdims=True)
    spread = jnp.mean(centre * centre, -1, keepdims=True)
    rstd = lax.rsqrt(spread + 1e-05)
    return centre * rstd, rstd


def norm_back(x, gain, grad):
    xhat, rstd = normalize(x)
    scaled = grad * gain
    m1 = jnp.mean(scaled, -1, keepdims=True)
    m2 = jnp.mean(scaled * xhat, -1, keepdims=True)
    dx = rstd * (scaled - m1 - xhat * m2)
    return dx, jnp.sum(grad * xhat, 0, keepdims=True), jnp.sum(grad, 0, keepdims=True)


def rows_of(pair):
    return pl.ds(pl.multiple_of(pair * PAIR, 16), PAIR)


def head_mask(head):
    lane = lax.broadcasted_iota(jnp.int32, (PAIR, LANES), 1)
    return (lane // HEAD_DIM) == head


def stack_heads(block, masks):
    zero = jnp.zeros_like(block)
    pad = jnp.zeros((LANES - PAIR, LANES), block.dtype)
    parts = []
    for mask in masks:
        parts += [jnp.where(mask, block, zero), pad]
    return jnp.concatenate(parts, 0)


def split_exact(x):
    high = x.astype(BF16)
    return high, (x - high.astype(F32)).astype(BF16)


def half_rows(core, half):
    mine = pl.ds(pl.multiple_of(core * half, 16), half)
    other = pl.ds(pl.multiple_of((1 - core) * half, 16), half)
    return mine, other


Q_ROWS, M_ROWS = 192, 576
FIRST_ROWS = 224
PACK_Q = [(0, 0, Q_ROWS, TRI, 0, 0)] + [
    (Q_ROWS, j * LANES, 64, LANES, 64 * j, TRI) for j in range(3)
]
PACK_1 = [(0, 0, 256, C, 0, 0)]
PACK_P = [(0, 0, 64, C, 256, 0)]
PACK_2 = [(0, 0, 256, C, 320, 0)]
ONE_ROWS, TWO_ROWS = 320, 256
PACK_TWO = [(0, 0, 256, C, 0, 0)]


def moved_down(blocks, base):
    return [block[:4] + (block[4] + base, block[5]) for block in blocks]


class Fetch:
    def __init__(self, full, layer, pieces, blocks, dest, core, sems):
        half = dest.shape[1] // 2
        self.copies = [[pltpu.make_async_copy(full.at[layer], dest.at[0], sems.at[0])]]
        at = 1
        for r in range(1, GROUPS):
            group = []
            if len(pieces) == 2:
                near, far = pieces[0].at[r - 1], pieces[1].at[r - 1]
            else:
                near, far = pieces[r - 1], pieces[r + 2]
            for side, piece in ((core, near), (1 - core, far)):
                for row, lane, rows, lanes, to_row, to_lane in blocks:
                    target = dest.at[
                        r,
                        pl.ds(pl.multiple_of(side * half + row, 16), rows),
                        pl.ds(lane, lanes),
                    ]
                    source = piece.at[pl.ds(to_row, rows), pl.ds(to_lane, lanes)]
                    group.append(pltpu.make_async_copy(source, target, sems.at[at]))
                    at += 1
            self.copies.append(group)
        for group in self.copies:
            for copy in group:
                copy.start()

    def wait(self, r):
        for copy in self.copies[r]:
            copy.wait()


def bias_kernel(layer, table, index, ids_col, ids_row, place, lanes_place, bias_ref):
    cols = mm(place[...], ids_col[...])
    rows = mm_nt(ids_row[...], lanes_place[...])
    masks = []
    for pair in range(2):
        col = cols[pair * PAIR : (pair + 1) * PAIR]
        row = rows[:1, pair * LANES : (pair + 1) * LANES]
        masks.append(jnp.where(col != row, -100.0, 0.0))
    idx = index[...]
    step = LAYERS * 2 * LANES
    at_low = jnp.clip(idx, 0, LANES - 1)
    at_high = jnp.clip(idx - LANES, 0, LANES - 1)

    def pick(low, high):
        low = jnp.take_along_axis(jnp.broadcast_to(low, (PAIR, LANES)), at_low, axis=1)
        high = jnp.take_along_axis(jnp.broadcast_to(high, (PAIR, LANES)), at_high, axis=1)
        return jnp.where(idx < 0, NEG, jnp.where(idx < LANES, low, high))

    for head in range(HEADS):
        r, lane = head // GHEADS, (head % GHEADS) * step + layer * 2 * LANES
        picked = pick(
            table[r : r + 1, lane : lane + LANES], table[r : r + 1, lane + LANES : lane + 2 * LANES]
        )
        if layer == 0:
            bias_ref[0, head] = picked
        else:
            bias_ref[0, head] = picked + masks[0]
            bias_ref[1, head] = picked + masks[1]


def attn_fwd_kernel(layer, pairs, base, *refs):
    first = layer == 0
    where, x_in, place, ln_g, ln_b, tables, group, bias, full_qkv = refs[:9]
    at = BIAS_AT + layer * TRI
    p_qkv, outs = refs[9:11], refs[11:]
    if first:
        x_ref, outs = outs[0], outs[1:]
    else:
        x_ref = x_in
    n1_ref, tri_ref, e_ref, rinv_ref, ho_ref, w_qkv, sem_q = outs
    qkv = Fetch(full_qkv, layer, p_qkv, moved_down(PACK_Q, base), w_qkv, where[1], sem_q)
    if first:
        for image in range(pairs // 2):
            x_ref[pl.ds(image * 2 * PAIR, 2 * PAIR), :] = mm(place[...], x_in[image])

    def norm_rows(pair, carry):
        rows = rows_of(pair)
        xhat, _ = normalize(x_ref[rows, :])
        n1_ref[rows, :] = (xhat * ln_g[...] + ln_b[...]).astype(BF16)
        return carry

    lax.fori_loop(0, pairs, norm_rows, 0)
    masks = [head_mask(h) for h in range(GHEADS)]
    ones = jnp.ones((PAIR, LANES), BF16)
    for r in range(GROUPS):
        qkv.wait(r)
        tri = (mm(n1_ref[...], w_qkv[r]) + tables[r : r + 1, at : at + TRI]).astype(BF16)
        tri_ref[r] = mm(tri, group[...]).astype(BF16)
        ones_stack = stack_heads(ones, masks)

        def pair_step(pair, carry):
            rows = rows_of(pair)
            q4 = tri_ref[r, rows, 0:LANES]
            k4 = tri_ref[r, rows, LANES : 2 * LANES]
            v4 = tri_ref[r, rows, 2 * LANES : 3 * LANES]
            s4 = mm_nt(q4, stack_heads(k4, masks))
            kind = 0 if first else lax.rem(pair, 2)
            es = []
            for h in range(GHEADS):
                s = s4[:, h * LANES : (h + 1) * LANES] * SCALE + bias[kind, r * GHEADS + h]
                es.append(jnp.exp(s - jnp.max(s, -1, keepdims=True)).astype(BF16))
            e4 = jnp.concatenate(es, 1)
            e_ref[r, pair] = e4
            vm = jnp.concatenate([stack_heads(v4, masks), ones_stack], 1)
            out = mm(e4, vm)
            rinv = 1.0 / out[:, LANES:]
            rinv_ref[r, rows, :] = rinv
            ho_ref[rows, r * LANES : (r + 1) * LANES] = (out[:, :LANES] * rinv).astype(BF16)
            return carry

        lax.fori_loop(0, pairs, pair_step, 0, unroll=True)


def mlp_fwd_kernel(layer, pairs, count, *refs):
    last = layer == LAYERS - 1
    where, x, ho, b_proj, ln_g, ln_b, tables, b2, place = refs[:9]
    at = HIDDEN_AT + layer * HID
    full_p, full_1, full_2 = refs[9:12]
    p_m, refs = refs[12 : 12 + count], refs[12 + count :]
    out_ref, mid, n2_ref, act_ref, dact_ref, wp, w1, w2, sem_p, sem_1, sem_2, acc, pre_ref = refs
    core = where[1]
    f_p = Fetch(full_p, layer, p_m, PACK_P, wp, core, sem_p)
    f_1 = Fetch(full_1, layer, p_m, PACK_1, w1, core, sem_1)
    f_2 = Fetch(full_2, layer, p_m, PACK_2, w2, core, sem_2)
    for r in range(GROUPS):
        f_p.wait(r)
    weight = jnp.concatenate([wp[r] for r in range(GROUPS)], 0)
    mid[...] = x[...] + mm(ho[...], weight) + b_proj[...]

    def norm_rows(pair, carry):
        rows = rows_of(pair)
        xhat, _ = normalize(mid[rows, :])
        n2_ref[rows, :] = (xhat * ln_g[...] + ln_b[...]).astype(BF16)
        return carry

    lax.fori_loop(0, pairs, norm_rows, 0)
    for r in range(GROUPS):
        f_1.wait(r)
        pre_ref[...] = mm(n2_ref[...], w1[r])
        b1_row = tables[r : r + 1, at : at + HID]

        def gelu_rows(step, carry):
            rows = pl.ds(pl.multiple_of(step * 16, 16), 16)
            pre = pre_ref[rows, :] + b1_row
            cdf = 0.5 + 0.5 * lax.erf(pre * (0.5**0.5))
            act_ref[r, rows, :] = (pre * cdf).astype(BF16)
            pdf = jnp.exp(-0.5 * pre * pre) * 0.3989422804014327
            dact_ref[r, rows, :] = (cdf + pre * pdf).astype(BF16)
            return carry

        lax.fori_loop(0, pairs * (PAIR // 16), gelu_rows, 0, unroll=2)
        f_2.wait(r)
        part = mm(act_ref[r], w2[r])
        if r == 0:
            acc[...] = part
        else:
            acc[...] += part
    acc[...] = acc[...] + mid[...] + b2[...]
    for image in range(pairs // 2):
        state = acc[pl.ds(image * 2 * PAIR, 2 * PAIR), :]
        if last:
            out_ref[image] = mm_tn(place[...], state.astype(BF16)).astype(BF16)
        else:
            high, low = split_exact(state)
            out_ref[pl.ds(image * 2 * PAIR, 2 * PAIR), :] = mm(place[...], high) + mm(
                place[...], low
            )


X_FIRST = (0, 2, 1, 3)
Y_FIRST = (0, 1, 2, 3)
ORDERS = (X_FIRST, Y_FIRST)


def give(keep_ref, send_ref, tmp, r, core, blocks):
    half = tmp.shape[0] // 2
    size = keep_ref.shape[2]
    for ref, base in ((keep_ref, core * half), (send_ref, (1 - core) * half)):
        for row, lane, rows, lanes, to_row, to_lane in blocks:
            done = 0
            while done < rows:
                part, at = divmod(to_row + done, size)
                count = min(rows - done, size - at)
                ref[part, ORDERS[part].index(r), at : at + count, to_lane : to_lane + lanes] = tmp[
                    pl.ds(pl.multiple_of(base + row + done, 16), count), lane : lane + lanes
                ]
                done += count


def hidden_back(layer, pairs, where, g_in, place, act, dact, w2, g_ref, gb_ref, gp_ref, tmp, outs, blocks):
    keep, send = outs
    core = where[1]
    if layer == LAYERS - 1:
        for image in range(pairs // 2):
            rows = pl.ds(image * 2 * PAIR, 2 * PAIR)
            g = mm(place[...], g_in[image])
            g_ref[rows, :] = g
            gb_ref[rows, :] = g.astype(BF16)
    else:
        gb_ref[...] = g_ref[...].astype(BF16)
    for r in range(GROUPS):
        tmp[...] = mm_tn(act[r], gb_ref[...]).astype(BF16)
        give(keep, send, tmp, r, core, blocks)
        ga = mm_nt(gb_ref[...], w2[r])
        gp_ref[r] = (ga * dact[r].astype(F32)).astype(BF16)


def middle_back(layer, pairs, where, gp_ref, g_ref, mid, n2, ho, rinv, ln_g, w1, wp, gb_ref, acc, tmp, tmp_p, outs):
    keep, send, gmid_ref, dh_ref, u_ref, small_ref, db1_ref = outs
    tid, core = where[0], where[1]
    small_ref[...] = jnp.zeros_like(small_ref)
    for r in range(GROUPS):
        db1_ref[tid ^ r] = jnp.sum(gp_ref[r].astype(F32), 0, keepdims=True)
        tmp[...] = mm_tn(n2[...], gp_ref[r]).astype(BF16)
        give(keep, send, tmp, r, core, PACK_1)
        part = mm_nt(gp_ref[r], w1[r])
        if r == 0:
            acc[...] = part
        else:
            acc[...] += part

    def back_rows(pair, carry):
        rows = rows_of(pair)
        g_rows = g_ref[rows, :]
        dx, dg, db = norm_back(mid[rows, :], ln_g[...], acc[rows, :])
        gmid = g_rows + dx
        gmid_ref[rows, :] = gmid
        gb_ref[rows, :] = gmid.astype(BF16)
        small_ref[0:1, :] += jnp.sum(g_rows, 0, keepdims=True)
        small_ref[1:2, :] += dg
        small_ref[2:3, :] += db
        small_ref[3:4, :] += jnp.sum(gmid, 0, keepdims=True)
        return carry

    lax.fori_loop(0, pairs, back_rows, 0)
    for r in range(GROUPS):
        lanes = slice(r * LANES, (r + 1) * LANES)
        tmp_p[...] = mm_tn(ho[:, lanes], gb_ref[...]).astype(BF16)
        give(keep, send, tmp_p, r, core, PACK_P)
        gh = mm_nt(gb_ref[...], wp[r]) * rinv[r]
        dh_ref[r] = gh.astype(BF16)
        u_ref[r] = (gh * ho[:, lanes].astype(F32)).astype(BF16)


def mlp_bwd_kernel(layer, pairs, *refs):
    where, g_in, place, act, dact, mid, n2, ho, rinv, ln_g, wp, w1, w2 = refs[:13]
    outs = refs[13:20]
    g_ref, gb_ref, gp_ref, acc, tmp, tmp_p = refs[20:]
    if layer < LAYERS - 1:
        g_ref = g_in
    hidden_back(
        layer, pairs, where, g_in, place, act, dact, w2, g_ref, gb_ref, gp_ref, tmp, outs[:2], PACK_2
    )
    middle_back(
        layer, pairs, where, gp_ref, g_ref, mid, n2, ho, rinv, ln_g, w1, wp, gb_ref, acc, tmp, tmp_p,
        outs,
    )


def hidden_bwd_kernel(layer, pairs, *refs):
    where, g, act, dact, w2 = refs[:5]
    gp_ref, gb_ref, tmp = refs[7:]
    hidden_back(
        layer, pairs, where, g, None, act, dact, w2, g, gb_ref, gp_ref, tmp, refs[5:7], PACK_TWO
    )


def middle_bwd_kernel(layer, pairs, *refs):
    where, gp, g, mid, n2, ho, rinv, ln_g, wp, w1 = refs[:10]
    gb_ref, acc, tmp, tmp_p = refs[17:]
    middle_back(
        layer, pairs, where, gp, g, mid, n2, ho, rinv, ln_g, w1, wp, gb_ref, acc, tmp, tmp_p,
        refs[10:17],
    )


def attn_bwd_kernel(pairs, where, dh, u, tri, e, group, dtri_ref, rel_ref, low_ref):
    tid = where[0]
    masks = [head_mask(h) for h in range(GHEADS)]
    neg_ones = jnp.full((PAIR, LANES), -1.0, BF16)
    for r in range(GROUPS):
        sid = tid ^ r
        neg_stack = stack_heads(neg_ones, masks)

        def pair_step(pair, carry):
            rows = rows_of(pair)
            q4 = tri[r, rows, 0:LANES]
            k4 = tri[r, rows, LANES : 2 * LANES]
            v4 = tri[r, rows, 2 * LANES : 3 * LANES]
            dh4 = dh[r, rows, :]
            left = jnp.concatenate([dh4, u[r, rows, :]], 1)
            right = jnp.concatenate([stack_heads(v4, masks), neg_stack], 1)
            dsp = mm_nt(left, right)
            e4 = e[r, pair]
            ds4 = e4.astype(F32) * dsp
            for h in range(GHEADS):
                part = ds4[:, h * LANES : (h + 1) * LANES]
                head = sid * GHEADS + h
                rel_ref[head] = jnp.where(pair == 0, part, rel_ref[head] + part)
            dsb = (ds4 * SCALE).astype(BF16)
            dq4 = mm(dsb, stack_heads(k4, masks))
            pad = jnp.zeros((LANES - PAIR, GHEADS * LANES), BF16)
            dsb_p = jnp.concatenate([dsb, pad], 0)
            e4_p = jnp.concatenate([e4, pad], 0)

            def flip(block):
                return jnp.concatenate(
                    [block[:, h * LANES : (h + 1) * LANES].T for h in range(GHEADS)], 1
                )[:PAIR]

            dk4 = mm(flip(dsb_p), stack_heads(q4, masks))
            dv4 = mm(flip(e4_p), stack_heads(dh4, masks))
            low_ref[rows, :] = jnp.concatenate([dq4, dk4, dv4], 1).astype(BF16)
            return carry

        lax.fori_loop(0, pairs, pair_step, 0, unroll=True)
        dtri_ref[r] = mm_nt(low_ref[...], group[...]).astype(BF16)


def qkv_grad_kernel(pairs, where, n1, dtri, keep, send, small_ref, tmp):
    tid, core = where[0], where[1]
    for r in range(GROUPS):
        tmp[...] = mm_tn(n1[...], dtri[r]).astype(BF16)
        give(keep, send, tmp, r, core, PACK_Q)
        small_ref[tid ^ r] = jnp.sum(dtri[r].astype(F32), 0, keepdims=True)


def input_bwd_kernel(layer, pairs, where, gmid, x, dtri, ln_g, place, w_qkv, gout_ref, small_ref, acc):
    last = layer == 0
    for r in range(GROUPS):
        part = mm_nt(dtri[r], w_qkv[r])
        if r == 0:
            acc[...] = part
        else:
            acc[...] += part
    small_ref[...] = jnp.zeros_like(small_ref)

    def back_rows(pair, carry):
        rows = rows_of(pair)
        dx, dg, db = norm_back(x[rows, :], ln_g[...], acc[rows, :])
        acc[rows, :] = gmid[rows, :] + dx
        small_ref[0:1, :] += dg
        small_ref[1:2, :] += db
        return carry

    lax.fori_loop(0, pairs, back_rows, 0)
    for image in range(pairs // 2):
        grad = acc[pl.ds(image * 2 * PAIR, 2 * PAIR), :]
        if last:
            gout_ref[:, image, :] = mm_tn(place[...], grad.astype(BF16)).astype(BF16)
        else:
            high, low = split_exact(grad)
            gout_ref[pl.ds(image * 2 * PAIR, 2 * PAIR), :] = mm(place[...], high) + mm(
                place[...], low
            )


def pack_start(plan, where, weights, outs, sems):
    core = where[1]
    moves = []
    for weight, layer, out, blocks in plan:
        weight, out = weights[weight], outs[out]
        half = weight.shape[1] // 2
        for row, lane, rows, lanes, to_row, to_lane in blocks:
            from_row = pl.multiple_of(core * half + row, 16)
            moves.append(
                (
                    weight.at[layer, pl.ds(from_row, rows), pl.ds(lane, lanes)],
                    out.at[pl.ds(to_row, rows), pl.ds(to_lane, lanes)],
                )
            )
    copies = [pltpu.make_async_copy(a, b, sems.at[i]) for i, (a, b) in enumerate(moves)]
    for copy in copies:
        copy.start()

    def end():
        for copy in copies:
            copy.wait()

    return end


def merge_kernel(where, a, b, c, out, sems):
    copies = [pltpu.make_async_copy(v, out.at[i], sems.at[i]) for i, v in enumerate((a, b, c))]
    for copy in copies:
        copy.start()
    for copy in copies:
        copy.wait()


def three_parts(v):
    high = v.astype(BF16)
    rest = v - high.astype(F32)
    mid = rest.astype(BF16)
    return high, mid, (rest - mid.astype(F32)).astype(BF16)


def own_tables(table, qv, b1, out):
    out[...] = jnp.zeros_like(out)
    at = lax.broadcasted_iota(jnp.int32, (2 * LANES, TRI), 0)
    to = lax.broadcasted_iota(jnp.int32, (2 * LANES, TRI), 1)
    same = jnp.logical_and(at // 64 == to // 96, at % HEAD_DIM == to % HEAD_DIM)
    same = jnp.logical_and(same, 2 * ((at // HEAD_DIM) % 2) == (to // HEAD_DIM) % 3)
    spread = jnp.where(same, 1.0, 0.0).astype(BF16)
    for layer in range(LAYERS):
        for head in range(GHEADS):
            lane = (head * LAYERS + layer) * 2 * LANES
            out[:, lane : lane + TABLE] = table[layer, head : head + 1, :]
        lane = BIAS_AT + layer * TRI
        out[:, lane : lane + TRI] = exact_pick(qv[layer : layer + 1, :], spread)
        lane = HIDDEN_AT + layer * HID
        out[:, lane : lane + HID] = b1[layer : layer + 1, :]


def put_tables(tables, out):
    cols = tables.shape[1]
    out[Q_ROWS:, :] = jnp.zeros((out.shape[0] - Q_ROWS, C), BF16)
    for part, v in enumerate(three_parts(tables[...])):
        for row in range(8):
            lanes = min(C, cols - row * C)
            at = Q_ROWS + 8 * part + row
            out[at : at + 1, 0:lanes] = v[:, row * C : row * C + lanes]


def take_tables(tables, near, every):
    cols = tables.shape[1]
    every[0:1, :] = tables[...]
    for r in range(1, GROUPS):
        wide = near[r - 1, Q_ROWS : Q_ROWS + 24, :].astype(F32)
        total = wide[0:8] + wide[8:16] + wide[16:24]
        for row in range(8):
            lanes = min(C, cols - row * C)
            every[r : r + 1, row * C : row * C + lanes] = total[row : row + 1, 0:lanes]


def exact_pick(row, chosen):
    parts = jnp.concatenate([*three_parts(row), jnp.zeros((13, row.shape[1]), BF16)], 0)
    got = mm(parts, chosen)
    return got[0:1] + got[1:2] + got[2:3]


def small_kernel(index, *refs):
    out, acc, folded = refs[-3:]
    out[...] = jnp.zeros_like(out)
    pick = refs[0]
    for layer in range(LAYERS):
        small2, db1, small_q, small1, rel = refs[5 * layer + 1 : 5 * layer + 6]
        base = 24 * layer
        out[base : base + 4, :] = small2[...]
        for r in range(GROUPS):
            out[base + 4 + r : base + 5 + r, :] = db1[r]
            out[base + 8 + r : base + 9 + r, 0 : 2 * LANES] = exact_pick(small_q[r], pick[...])
        out[base + 12 : base + 14, :] = small1[...]

        def fold(head, carry, layer=layer, rel=rel):
            second = pltpu.roll(rel[head, WTOK : 2 * WTOK, :], LANES - WTOK, 1)
            at = pl.multiple_of((layer * HEADS + head) * 56, 8)
            folded[pl.ds(at, WTOK), :] = rel[head, 0:WTOK, :] + second
            return carry

        lax.fori_loop(0, HEADS, fold, 0)
    entry = lax.broadcasted_iota(jnp.int32, (2 * LANES, LANES), 0)
    count = LAYERS * HEADS
    acc[...] = jnp.zeros_like(acc)

    def one_row(i, carry):
        onehot = jnp.where(entry == index[i], 1.0, 0.0).astype(BF16)
        high, low = split_exact(folded[pl.ds(i, count, stride=56), :])
        acc[...] += mm_nt(onehot, jnp.concatenate([high, low], 0))
        return carry

    lax.fori_loop(0, WTOK, one_row, 0, unroll=7)
    total = acc[...].T
    total = total[:count] + total[count:]
    for layer in range(LAYERS):
        for part in range(2):
            at = layer * HEADS + part * 8
            out[24 * layer + 16 : 24 * layer + 24, part * 2 * LANES : (part + 1) * 2 * LANES] = total[
                at : at + 8, :
            ]


def add_go_kernel(where, *refs):
    count = (len(refs) - 4) // 2
    go_a, go_b, stay_a, stay_b = refs[-4:]
    row = 0
    for i in range(count):
        keep, got = refs[2 * i], refs[2 * i + 1]
        size = keep.shape[2]
        rows = slice(row, row + size)
        for part, (stay, go) in enumerate(((stay_a, go_a), (stay_b, go_b))):
            stay[:, rows, :] = keep[part, :2] + got[part, :2]
            go[:, rows, :] = keep[part, 2:] + got[part, 2:]
        row += size


def add_next_kernel(where, stay_a, stay_b, got_a, got_b, next_a, next_b, keep_a, keep_b):
    next_a[...] = stay_a[1] + got_a[1]
    next_b[...] = stay_b[1] + got_b[1]
    keep_a[...] = stay_a[0] + got_a[0]
    keep_b[...] = stay_b[0] + got_b[0]


def add_whole_kernel(where, keep_a, keep_b, got_a, got_b, out):
    size = keep_a.shape[0]
    out[0:size, :] = keep_a[...] + got_a[...]
    out[size:, :] = keep_b[...] + got_b[...]


def choose_kernel(where, mine, got, out):
    end = jnp.logical_or(where[2] == 0, where[2] == 3)
    out[...] = jnp.where(end, got[...], mine[...])


def add_level_kernel(where, keep_a, keep_b, got_a, got_b, mine, send):
    odd = where[2] & 1
    a = keep_a[...] + got_a[...]
    b = keep_b[...] + got_b[...]
    mine[...] = jnp.where(odd == 1, b, a)
    send[...] = jnp.where(odd == 1, a, b)


def add_kernel(where, a, b, out):
    out[...] = a[...] + b[...]


FINISH = {"q": (0, PACK_Q), "p": (1, PACK_P), "1": (2, PACK_1), "2": (3, PACK_2), "two": (3, PACK_TWO)}


def finish_kernel(plan, count, made, where, *refs):
    pieces = refs[:made]
    scratch, sems = refs[count + 5 : -1], refs[-1]
    core, odd = where[1], where[2] & 1
    copies = []
    first, slot = 0, 0
    results = refs[count : count + 4]
    for total, layer, names in plan:
        size = total // 2
        for name in names:
            index, blocks = FINISH[name]
            out = scratch[slot]
            half = out.shape[0] // 2
            for at, piece in enumerate(pieces):
                c = core if at < len(pieces) // 2 else 1 - core
                if len(pieces) == 2:
                    for row, lane, rows, lanes, to_row, to_lane in blocks:
                        target = pl.multiple_of(c * half + row, 16)
                        out[pl.ds(target, rows), lane : lane + lanes] = piece[
                            first + to_row : first + to_row + rows, to_lane : to_lane + lanes
                        ].astype(F32)
                    continue
                for part in range(2):

                    @pl.when((odd if at % 2 == 0 else 1 - odd) == part)
                    def _(piece=piece, part=part, c=c, out=out, first=first, size=size, blocks=blocks):
                        for row, lane, rows, lanes, to_row, to_lane in blocks:
                            begin = max(to_row, part * size)
                            end = min(to_row + rows, (part + 1) * size)
                            if begin >= end:
                                continue
                            target = pl.multiple_of(c * half + row + begin - to_row, 16)
                            source = first + begin - part * size
                            out[pl.ds(target, end - begin), lane : lane + lanes] = piece[
                                source : source + end - begin, to_lane : to_lane + lanes
                            ].astype(F32)

            copies.append(pltpu.make_async_copy(out, results[index].at[layer], sems.at[slot]))
            copies[-1].start()
            slot += 1
        first += size * (1 if len(pieces) == 4 else 2)
    for copy in copies:
        copy.wait()


def own_kernel(where, little, got, out):
    tid = where[0]
    out[...] = jnp.zeros_like(out)
    for layer in range(LAYERS):
        base, to = 24 * layer, 16 * layer

        def put(rows, row, lane, lanes):
            out[to + rows[0] : to + rows[1], 0:lanes] = (
                little[base + row : base + row + rows[1] - rows[0], lane : lane + lanes]
                + got[base + row : base + row + rows[1] - rows[0], lane : lane + lanes]
            )

        put((0, 4), 0, 0, C)
        put((4, 6), 12, 0, C)
        for r in range(GROUPS):

            @pl.when(tid == r)
            def _(r=r, put=put):
                put((6, 7), 4 + r, 0, C)
                put((7, 8), 8 + r, 0, 2 * LANES)
                put((8, 12), 16 + GHEADS * (r % 2), 2 * LANES * (r // 2), 2 * LANES)


def unpack_kernel(where, little, *outs):
    for layer in range(LAYERS):
        base = 16 * layer
        for out, at in zip(outs[:7], (4, 5, 3, 1, 2, 0, 6)):
            out[layer : layer + 1, :] = little[base + at : base + at + 1, :]
        outs[7][layer : layer + 1, :] = little[base + 7 : base + 8, 0 : 2 * LANES]
        outs[8][layer] = little[base + 8 : base + 12, 0:TABLE]


VM = pl.BlockSpec(memory_space=pltpu.VMEM)
SM = pl.BlockSpec(memory_space=pltpu.SMEM)
ANY = pl.BlockSpec(memory_space=pl.ANY)
VC = pl.BlockSpec(memory_space=pltpu.VMEM)
HB = pl.BlockSpec(memory_space=pltpu.HBM)


def pinned(shape, dtype):
    return pltpu.VMEM(shape, dtype)


def place_operand(spec, value):
    if spec is VC:
        return pltpu.with_memory_space_constraint(value, pltpu.VMEM)
    if spec is HB:
        return pltpu.with_memory_space_constraint(value, pltpu.HBM)
    return value


def call(
    kernel, specs, args, outs, scratch=(), flops=0, out_specs=None, limit=2, moved=4, after=(), aliases=None,
    weight=0,
):
    count = len(args)
    skip = count + len(after)

    def body(*refs):
        kernel(*refs[:count], *refs[skip:])

    return pl.pallas_call(
        body,
        out_shape=outs,
        in_specs=list(specs) + [ANY] * len(after),
        out_specs=[VM] * len(outs) if out_specs is None else out_specs,
        scratch_shapes=scratch,
        input_output_aliases=aliases or {},
        compiler_params=pltpu.CompilerParams(vmem_limit_bytes=limit << 20),
        cost_estimate=pl.CostEstimate(flops=1 + weight * GF, bytes_accessed=1, transcendentals=0),
    )(*[place_operand(spec, arg) for spec, arg in zip(specs, args)], *after)


def struct(shape, dtype):
    return jax.ShapeDtypeStruct(shape, dtype)


DIM_Q, DIM_P, DIM_1, DIM_2 = (C, TRI), (LANES, C), (C, HID), (HID, C)
GF = 1 << 30
BIAS_AT = GHEADS * LAYERS * 2 * LANES
HIDDEN_AT = BIAS_AT + LAYERS * TRI


def fetch_sems(*dims):
    return [
        pltpu.SemaphoreType.DMA((1 + 6 * (len(PACK_Q) if d == DIM_Q else 1),)) for d in dims
    ]


def chunk_outs(rows):
    return [pinned((2, GROUPS, rows // 2, C), BF16)] * 2


def attn_fwd(layer, batch, where, x, place, ln_g, ln_b, tables, group, bias, w):
    pairs = 2 * batch
    rows = pairs * PAIR
    outs = [
        pinned((rows, C), BF16),
        pinned((GROUPS, rows, TRI), BF16),
        pinned((GROUPS, pairs, PAIR, GHEADS * LANES), BF16),
        pinned((GROUPS, rows, LANES), F32),
        pinned((rows, C), BF16),
        pinned((GROUPS,) + DIM_Q, BF16),
    ]
    if layer == 0:
        outs = [pinned((rows, C), F32)] + outs
    return call(
        functools.partial(attn_fwd_kernel, layer, pairs, w.q_base),
        [SM, VM if layer == 0 else VC] + [VM] * 5 + [VC] + [HB] + [ANY] * 2,
        [where, x, place, ln_g, ln_b, tables, group, bias, *w.qkv],
        outs,
        fetch_sems(DIM_Q),
        flops=8 * GF,
        limit=9,
    )


def mlp_fwd(layer, batch, where, x, ho, b_proj, ln_g, ln_b, tables, b2, place, w):
    pairs = 2 * batch
    rows = pairs * PAIR
    last = layer == LAYERS - 1
    outs = [
        struct((batch, TOK, C), BF16) if last else pinned((rows, C), F32),
        pinned((rows, C), F32),
        pinned((rows, C), BF16),
        pinned((GROUPS, rows, HID), BF16),
        pinned((GROUPS, rows, HID), BF16),
    ] + [pinned((GROUPS,) + dim, BF16) for dim in (DIM_P, DIM_1, DIM_2)]
    return call(
        functools.partial(mlp_fwd_kernel, layer, pairs, len(w.p_m)),
        [SM, VC, VC] + [VM] * 6 + [HB] * 3 + [ANY] * len(w.p_m),
        [where, x, ho, b_proj, ln_g, ln_b, tables, b2, place, w.own_p, w.own_1, w.own_2, *w.p_m],
        outs,
        fetch_sems(DIM_P, DIM_1, DIM_2)
        + [pltpu.VMEM((rows, C), F32), pltpu.VMEM((rows, HID), F32)],
        flops=8 * GF,
        limit=12,
    )


def mlp_bwd(layer, batch, where, g, place, act, dact, mid, n2, ho, rinv, ln_g, w, after):
    pairs = 2 * batch
    rows = pairs * PAIR
    outs = chunk_outs(M_ROWS) + [
        pinned((rows, C), F32),
        pinned((GROUPS, rows, LANES), BF16),
        pinned((GROUPS, rows, LANES), BF16),
        struct((4, C), F32),
        struct((GROUPS, 1, HID), F32),
    ]
    return call(
        functools.partial(mlp_bwd_kernel, layer, pairs),
        [SM, VM if layer == LAYERS - 1 else VC, VM] + [VC] * 6 + [VM] + [VC] * 3,
        [where, g, place, act, dact, mid, n2, ho, rinv, ln_g, *w],
        outs,
        [
            pltpu.VMEM((rows, C), F32),
            pltpu.VMEM((rows, C), BF16),
            pltpu.VMEM((GROUPS, rows, HID), BF16),
            pltpu.VMEM((rows, C), F32),
            pltpu.VMEM(DIM_1, BF16),
            pltpu.VMEM(DIM_P, BF16),
        ],
        flops=14 * GF,
        limit=18,
        after=after,
    )


def hidden_bwd(layer, batch, where, g, act, dact, w, after):
    pairs = 2 * batch
    rows = pairs * PAIR
    return call(
        functools.partial(hidden_bwd_kernel, layer, pairs),
        [SM] + [VC] * 4,
        [where, g, act, dact, w[2]],
        chunk_outs(TWO_ROWS) + [pinned((GROUPS, rows, HID), BF16)],
        [pltpu.VMEM((rows, C), BF16), pltpu.VMEM(DIM_2, BF16)],
        flops=5 * GF,
        limit=9,
        after=after,
    )


def middle_bwd(layer, batch, where, gp, g, mid, n2, ho, rinv, ln_g, w, after):
    pairs = 2 * batch
    rows = pairs * PAIR
    return call(
        functools.partial(middle_bwd_kernel, layer, pairs),
        [SM] + [VC] * 6 + [VM] + [VC] * 2,
        [where, gp, g, mid, n2, ho, rinv, ln_g, w[0], w[1]],
        chunk_outs(ONE_ROWS)
        + [
            pinned((rows, C), F32),
            pinned((GROUPS, rows, LANES), BF16),
            pinned((GROUPS, rows, LANES), BF16),
            struct((4, C), F32),
            struct((GROUPS, 1, HID), F32),
        ],
        [
            pltpu.VMEM((rows, C), BF16),
            pltpu.VMEM((rows, C), F32),
            pltpu.VMEM(DIM_1, BF16),
            pltpu.VMEM(DIM_P, BF16),
        ],
        flops=9 * GF,
        limit=12,
        after=after,
    )


def attn_bwd(batch, where, dh, u, tri, e, group, after):
    pairs = 2 * batch
    rows = pairs * PAIR
    return call(
        functools.partial(attn_bwd_kernel, pairs),
        [SM] + [VC] * 4 + [VM],
        [where, dh, u, tri, e, group],
        [pinned((GROUPS, rows, TRI), BF16), pinned((HEADS, PAIR, LANES), F32)],
        [pltpu.VMEM((rows, TRI), BF16)],
        flops=12 * GF,
        limit=9,
        after=after,
    )


def qkv_grad(batch, where, n1, dtri, after):
    return call(
        functools.partial(qkv_grad_kernel, 2 * batch),
        [SM] + [VC] * 2,
        [where, n1, dtri],
        chunk_outs(Q_ROWS) + [struct((GROUPS, 1, TRI), F32)],
        [pltpu.VMEM(DIM_Q, BF16)],
        flops=3 * GF,
        limit=6,
        after=after,
    )


def input_bwd(layer, batch, where, gmid, x, dtri, ln_g, place, w, after):
    pairs = 2 * batch
    rows = pairs * PAIR
    return call(
        functools.partial(input_bwd_kernel, layer, pairs),
        [SM, VC, VC, VC, VM, VM, VC],
        [where, gmid, x, dtri, ln_g, place, w],
        [
            struct((TOK, batch, C), BF16) if layer == 0 else pinned((rows, C), F32),
            struct((2, C), F32),
        ],
        [pltpu.VMEM((rows, C), F32)],
        flops=3 * GF,
        limit=9,
        after=after,
    )


def full_bias(qv_rows, heads):
    parts = qv_rows.reshape(LAYERS, heads, 2, HEAD_DIM)
    full = jnp.stack([parts[:, :, 0], jnp.zeros_like(parts[:, :, 0]), parts[:, :, 1]], 2)
    return full.reshape(LAYERS, heads * 3 * HEAD_DIM)


def swap(x, axis, size, bit):
    return lax.ppermute(x, axis, [(i, i ^ bit) for i in range(size)])


class Weights:
    def __init__(self, own, p_q, p_m, q_base=0):
        own_q, self.own_p, self.own_1, self.own_2 = own
        self.q_base = q_base
        self.qkv = [own_q] + p_q
        self.p_m = p_m


class Direct:
    def __init__(self, dp):
        self.dp = dp
        self.t = lax.axis_index("tensor")
        d = lax.axis_index("dp")
        self.where = jnp.stack([self.t, d % 2, d // 2]).astype(jnp.int32)

    def x(self, v):
        return swap(v, "tensor", 4, 1)

    def y(self, v):
        return swap(v, "tensor", 4, 2)

    def diagonal(self, v):
        return swap(v, "tensor", 4, 3)

    def other(self, v):
        return swap(v, "dp", self.dp, 1)

    def level(self, v, k):
        return swap(v, "dp", self.dp, 2 * k)

    def near(self, v):
        return self.x(v), self.y(v), self.diagonal(v)

    def plan(self, parts):
        plan, outs = [], []
        for part in parts:
            at, base = len(outs), 0
            for layer, chunk in part:
                for weight, blocks in (((0, PACK_Q),), ((2, PACK_1), (1, PACK_P), (3, PACK_2)))[chunk]:
                    plan.append((weight, layer, at, moved_down(blocks, base)))
                base += (Q_ROWS, M_ROWS)[chunk]
            outs.append(pinned((base, C), BF16))
        return plan, outs

    def pack(self, arrays, parts, tables=None, after=()):
        plan, outs = self.plan(parts)
        count = sum(len(blocks) for _, _, _, blocks in plan)
        args = [self.where, *arrays]
        scratch = []
        if tables is not None:
            args += tables
            outs[0] = pinned((FIRST_ROWS, C), BF16)
            outs.append(pinned((1, HIDDEN_AT + LAYERS * HID), F32))
            scratch = [pltpu.VMEM(v.shape, F32) for v in tables]
        made = len(outs)

        def body(where, *refs):
            outs = refs[len(args) - 1 : len(args) - 1 + made]
            end = pack_start(plan, where, refs[:4], outs, refs[-1])
            if tables is not None:
                held = refs[len(args) - 1 + made : -1]
                copies = [
                    pltpu.make_async_copy(a, b, refs[-1].at[count + i])
                    for i, (a, b) in enumerate(zip(refs[4:7], held))
                ]
                for copy in copies:
                    copy.start()
                for copy in copies:
                    copy.wait()
                own_tables(*held, outs[-1])
                put_tables(outs[-1], outs[0])
            end()

        return call(
            body, [SM] + [HB] * (len(args) - 1), args, outs,
            scratch + [pltpu.SemaphoreType.DMA((count + 3,))], after=after,
        )

    def merge(self, pieces, arrays=(), parts=(), moved=(), tables=None, after=()):
        rows, count = pieces[0].shape[0], len(pieces)
        plan, packs = self.plan(parts)
        outs = [pinned((3, rows, C), BF16)] + packs + [pinned(v.shape, v.dtype) for v in moved]
        weights = len(arrays)
        small = [] if tables is None else [tables]
        outs += [pinned((GROUPS, v.shape[1]), F32) for v in small]
        given = count + weights + len(moved) + len(small)

        def body(where, *refs):
            spare, outs = refs[:given], refs[given:-2]
            ends = []
            if parts:
                ends.append(pack_start(plan, where, spare[count : count + weights], outs[1:], refs[-1]))
            copies = [
                pltpu.make_async_copy(a, b, refs[-2].at[3 + i])
                for i, (a, b) in enumerate(
                    zip(spare[count + weights : count + weights + len(moved)], outs[1 + len(packs) :])
                )
            ]
            for copy in copies:
                copy.start()
            merge_kernel(where, *refs[:count], outs[0], refs[-2])
            if small:
                take_tables(spare[-1], outs[0], outs[-1])
            for copy in copies:
                copy.wait()
            for end in ends:
                end()

        moves = sum(len(blocks) for _, _, _, blocks in plan)
        near, *others = call(
            body, [SM] + [ANY] * count + [HB] * weights + [ANY] * len(moved) + [VM] * len(small),
            [self.where, *pieces, *arrays, *moved, *small], outs,
            [pltpu.SemaphoreType.DMA((3 + len(moved),)), pltpu.SemaphoreType.DMA((max(moves, 1),))],
            after=after, limit=10,
        )
        return [[near, self.other(near)], *others]

    def step(self, *parts, passing=(), after=(), weight=0):
        kernels, args, specs, outs, cuts = [], [self.where], [SM], [], []
        for kernel, values, results in parts:
            kernels.append((kernel, len(args) - 1, len(values), len(outs), len(results)))
            args += values
            specs += [VC] * len(values)
            outs += results
        total_in, total_out = len(args) - 1, len(outs)
        aliases = {}
        for value in passing:
            aliases[len(args)] = len(outs)
            args.append(value)
            specs.append(ANY)
            outs.append(struct(value.shape, value.dtype))

        def body(where, *refs):
            refs_in, refs_out = refs[: total_in + len(passing)], refs[total_in + len(passing) :]
            for kernel, at, count, out, results in kernels:
                kernel(where, *refs_in[at : at + count], *refs_out[out : out + results])

        got = call(
            body, specs, args, outs, after=after, aliases=aliases, weight=weight,
            out_specs=[VM] * total_out + [ANY] * len(passing),
        )
        split = []
        for _, _, _, out, results in kernels:
            split.append(got[out : out + results])
        return split + list(got[total_out:])


    def swap_cores(self, keep, send):
        return keep, self.other(send)

    def first_way(self, *states):
        args = [v for state in states for v in state]
        two = pinned((2, sum(keep.shape[2] for keep, _ in states), C), BF16)
        return add_go_kernel, args, [two] * 4

    def send_first(self, done):
        go_a, go_b, stay_a, stay_b = done
        return stay_a, stay_b, self.x(go_a), self.y(go_b)

    def second_way(self, state):
        one = pinned(state[0].shape[1:], BF16)
        return add_next_kernel, list(state), [one] * 4

    def send_second(self, done):
        next_a, next_b, keep_a, keep_b = done
        return keep_a, keep_b, self.y(next_a), self.x(next_b)

    def join(self, state):
        one = pinned(state[0].shape, BF16)
        return add_level_kernel, list(state), [one] * 2

    def join_whole(self, state):
        rows = 2 * state[0].shape[0]
        return add_whole_kernel, list(state), [pinned((rows, C), BF16)]

    def line(self, v, pairs):
        return lax.ppermute(
            v, "dp", [(2 * a + core, 2 * b + core) for a, b in pairs for core in range(2)]
        )

    def choose(self, mine, got):
        return choose_kernel, [mine, got], [pinned(mine.shape, BF16)]

    def send_level(self, state, k):
        mine, send = state
        return mine, self.level(send, k)

    def add(self, state):
        return add_kernel, list(state), [pinned(state[0].shape, BF16)]

    def own_small(self, state):
        return own_kernel, list(state), [pinned((16 * LAYERS, C), F32)]

    def add_small(self, state):
        return add_kernel, list(state), [pinned(state[0].shape, F32)]

    def finish(self, plan, pieces, before=None, after=()):
        dims = (DIM_Q, DIM_P, DIM_1, DIM_2)
        made = len(pieces)
        args, specs = [self.where, *pieces], [SM] + [VC] * made
        aliases = {}
        if before is not None:
            aliases = {1 + made + i: i for i in range(4)}
            args += before[:4]
            specs += [HB] * 4
        scratch = [
            pltpu.VMEM(dims[FINISH[name][0]], F32) for _, _, names in plan for name in names
        ]
        return call(
            functools.partial(finish_kernel, plan, len(args) - 1, made), specs, args,
            [pltpu.HBM((LAYERS,) + dim, F32) for dim in dims] + [pinned((8, LANES), F32)],
            scratch + [pltpu.SemaphoreType.DMA((len(scratch),))],
            out_specs=[HB] * 4 + [VM], limit=6, after=after, aliases=aliases,
        )

    def unpack(self, little, after=()):
        one = struct((LAYERS, C), F32)
        outs = [one] * 7 + [struct((LAYERS, 2 * LANES), F32), struct((LAYERS, GHEADS, TABLE), F32)]
        return call(unpack_kernel, [SM, VC], [self.where, little], outs, after=after)


class Whole:
    def __init__(self):
        self.where = jnp.zeros((3,), jnp.int32)

    def gather(self, arrays, small):
        qkv, proj, w1, w2 = [
            lax.all_gather(v, "tensor", axis=axis, tiled=True) for v, axis in zip(arrays, (2, 1, 2, 1))
        ]
        qkv = qkv.reshape(LAYERS, C, GROUPS, TRI).transpose(0, 2, 1, 3)
        proj = proj.reshape(LAYERS, GROUPS, LANES, C)
        w1 = w1.reshape(LAYERS, C, GROUPS, HID).transpose(0, 2, 1, 3)
        w2 = w2.reshape(LAYERS, GROUPS, HID, C)
        own = [v[:, 0] for v in (qkv, proj, w1, w2)]

        def pack(parts, rows):
            out = jnp.zeros((rows, C), BF16)
            for v, blocks in parts:
                for row, lane, count, lanes, to_row, to_lane in blocks:
                    block = v[row : row + count, lane : lane + lanes]
                    out = out.at[to_row : to_row + count, to_lane : to_lane + lanes].set(block)
            return out

        weights = []
        for layer in range(LAYERS):
            p_q, p_m = [], []
            for side in range(2):
                side_q, side_m = [], []
                for r in range(1, GROUPS):

                    def half(v):
                        size = v.shape[2] // 2
                        return v[layer, r, side * size : (side + 1) * size]

                    side_q.append(pack([(half(qkv), PACK_Q)], Q_ROWS))
                    parts = [(half(w1), PACK_1), (half(proj), PACK_P), (half(w2), PACK_2)]
                    side_m.append(pack(parts, M_ROWS))
                p_q.append(jnp.stack(side_q))
                p_m.append(jnp.stack(side_m))
            weights.append(Weights(own, p_q, p_m))
        return weights, lax.all_gather(small, "tensor", axis=0)

    def sum_small(self, v):
        return lax.psum(v, ("dp", "tensor"))

    def finish(self, chunks):
        full = {}
        for name, chunk, blocks, dim in (
            ("q", 1, PACK_Q, DIM_Q), ("p", 0, PACK_P, DIM_P), ("1", 0, PACK_1, DIM_1), ("2", 0, PACK_2, DIM_2)
        ):
            layers = []
            for layer in range(LAYERS):
                sides = []
                for v in chunks[layer][chunk]:
                    shares = []
                    for r in range(GROUPS):
                        packed = jnp.concatenate(
                            [v[part, ORDERS[part].index(r)] for part in range(2)], 0
                        )
                        out = jnp.zeros((dim[0] // 2, dim[1]), BF16)
                        for row, lane, count, lanes, to_row, to_lane in blocks:
                            block = packed[to_row : to_row + count, to_lane : to_lane + lanes]
                            out = out.at[row : row + count, lane : lane + lanes].set(block)
                        shares.append(out)
                    sides.append(jnp.stack(shares))
                layers.append(jnp.concatenate(sides, 1))
            full[name] = jnp.stack(layers)
        outs = []
        for name, axis in zip("qp12", (2, 1, 2, 1)):
            v = full[name]
            if axis == 2:
                v = v.transpose(0, 2, 1, 3).reshape(LAYERS, C, -1)
            else:
                v = v.reshape(LAYERS, -1, C)
            v = lax.psum_scatter(v, "tensor", scatter_dimension=axis, tiled=True)
            outs.append(lax.psum(v, "dp").astype(F32))
        return outs


def shards(
    tensor, dp, images_in, ln1_gain, ln1_bias, qkv_weight, qv_bias, rel_table, proj_weight,
    proj_bias, ln2_gain, ln2_bias, fc1_weight, fc1_bias, fc2_weight, fc2_bias, rel_index,
    region_ids, out_cot,
):
    batch = images_in.shape[0]
    direct = tensor == 4 and dp == 8
    net = Direct(dp) if direct else Whole()
    where = net.where
    wide = 2 * LANES
    own = (qkv_weight, proj_weight, fc1_weight, fc2_weight)

    heads = rel_table.shape[2]
    if direct:
        q0, packed = net.pack(
            own, [[(0, 0)]], tables=[rel_table.transpose(0, 2, 1), qv_bias, fc1_bias]
        )
        near_q0 = net.near(q0)
        w_q0, m0, every = net.merge(near_q0, own, [[(0, 1), (1, 0)]], tables=packed)
        near_m0 = net.near(m0)
    else:
        table = jnp.pad(rel_table.transpose(2, 0, 1), ((0, 0), (0, 0), (0, wide - TABLE)))
        bias_part = full_bias(qv_bias, heads)
        packed = jnp.concatenate([table.reshape(-1), bias_part.reshape(-1), fc1_bias.reshape(-1)])
        packed = packed.reshape(1, -1)
        weights, every = net.gather(own, packed)
    every = every.reshape(tensor, -1)
    if tensor != GROUPS:
        cut1 = heads * LAYERS * wide
        cut2 = cut1 + bias_part.size
        tables = every[:, :cut1].reshape(GROUPS, -1)
        parts = [tables]
        for part in (every[:, cut1:cut2], every[:, cut2:]):
            part = part.reshape(tensor, LAYERS, -1).transpose(1, 0, 2)
            parts.append(part.reshape(LAYERS, GROUPS, -1).transpose(1, 0, 2).reshape(GROUPS, -1))
        every = jnp.concatenate(parts, 1)
    index = jnp.pad(rel_index + 1, ((0, PAIR - WTOK), (0, LANES - WTOK)))
    index = index + jnp.pad(rel_index + 1, ((WTOK, PAIR - 2 * WTOK), (WTOK, LANES - 2 * WTOK))) - 1
    ids = region_ids.astype(BF16)
    ids_col = jnp.broadcast_to(ids[:, None], (TOK, LANES))
    ids_row = jnp.broadcast_to(ids[None, :], (16, TOK))
    lanes_place = np.zeros((2 * LANES, TOK), np.float32)
    for pair in range(2):
        lanes_place[pair * LANES : pair * LANES + PAIR] = PLACE[0][pair * PAIR : (pair + 1) * PAIR]
    place = [jnp.asarray(PLACE[layer], BF16) for layer in range(LAYERS)]
    after = w_q0[:1] if direct else ()

    def bias_of(layer, after=()):
        return call(
            functools.partial(bias_kernel, layer),
            [VM] * 6,
            [every, index, ids_col, ids_row, place[0], jnp.asarray(lanes_place, BF16)],
            [pinned((1 + layer, HEADS, PAIR, LANES), F32)],
            flops=4 * GF,
            after=after,
        )[0]

    bias = [bias_of(0, after), None]
    step01 = jnp.asarray(PLACE[1] @ PLACE[0].T, BF16)
    step10 = jnp.asarray(PLACE[0] @ PLACE[1].T, BF16)
    group = jnp.asarray(GROUP, BF16)

    def row(v, layer):
        return v[layer][None]

    saved, w_q, w_m = [None] * LAYERS, [None] * LAYERS, [None] * LAYERS
    rels, littles = [None] * LAYERS, [None] * LAYERS

    def attn(layer, state, w):
        res = attn_fwd(
            layer, batch, where, state, place[0], row(ln1_gain, layer), row(ln1_bias, layer),
            every, group, bias[layer], w,
        )
        *res, w_q[layer] = res
        saved[layer] = tuple(res) if layer == 0 else (state,) + tuple(res)

    def mlp(layer, w):
        x, n1, tri, e, rinv, ho = saved[layer]
        state, *rest, wp, w1, w2 = mlp_fwd(
            layer, batch, where, x, ho, row(proj_bias, layer), row(ln2_gain, layer),
            row(ln2_bias, layer), every, row(fc2_bias, layer), step01 if layer == 0 else place[1],
            w,
        )
        saved[layer] += tuple(rest)
        w_m[layer] = (wp, w1, w2)
        return state

    def mlp_back(layer, grad, after=()):
        x, n1, tri, e, rinv, ho, mid, n2, act, dact = saved[layer]
        keep, send, gmid, dh, u, small2, db1 = mlp_bwd(
            layer, batch, where, grad, place[1], act, dact, mid, n2, ho, rinv,
            row(ln2_gain, layer), w_m[layer], after,
        )
        littles[layer] = {"a": small2, "b": db1}
        return (keep, send), gmid, dh, u

    def hidden_back_0(grad, after):
        act, dact = saved[0][8:]
        keep, send, gp = hidden_bwd(0, batch, where, grad, act, dact, w_m[0], after)
        return (keep, send), gp

    def middle_back_0(gp, grad, after):
        x, n1, tri, e, rinv, ho, mid, n2, act, dact = saved[0]
        keep, send, gmid, dh, u, small2, db1 = middle_bwd(
            0, batch, where, gp, grad, mid, n2, ho, rinv, row(ln2_gain, 0), w_m[0], after
        )
        littles[0] = {"a": small2, "b": db1}
        return (keep, send), gmid, dh, u

    def attn_back(layer, dh, u, after=()):
        dtri, rels[layer] = attn_bwd(
            batch, where, dh, u, saved[layer][2], saved[layer][3], group, after
        )
        return dtri

    def qkv_back(layer, dtri, after=()):
        keep, send, small_q = qkv_grad(batch, where, saved[layer][1], dtri, after)
        littles[layer]["c"] = small_q
        return keep, send

    def input_back(layer, gmid, dtri, after=()):
        grad, small1 = input_bwd(
            layer, batch, where, gmid, saved[layer][0], dtri, row(ln1_gain, layer),
            step10 if layer else place[0], w_q[layer], after,
        )
        littles[layer]["d"] = small1
        return grad

    def small_sums(after=()):
        args = [index.reshape(PAIR, 1, LANES), jnp.asarray(PICK, BF16)]
        for layer in range(LAYERS):
            args += [littles[layer][name] for name in "abcd"] + [rels[layer]]
        specs = [VM] * 2 + ([VM] * 4 + [VC]) * LAYERS
        return call(
            small_kernel, specs, args, [pinned((24 * LAYERS, C), F32)],
            [
                pltpu.VMEM((wide, 2 * LAYERS * HEADS), F32),
                pltpu.VMEM((LAYERS * HEADS * 56, LANES), F32),
            ],
            after=after, limit=4,
        )[0]

    if direct:
        w0 = Weights(own, w_q0, None)
        attn(0, images_in, w0)
        bias[1] = bias_of(1, saved[0][5:6])
        (m1,) = net.pack(own, [[(1, 1)]], after=(bias[1],))
        w0.p_m, m1 = net.merge(near_m0, moved=(m1,))
        near_m1 = net.near(m1)
        state = mlp(0, w0)
        w1 = Weights(own, w0.p_m, None, M_ROWS)
        attn(1, state, w1)
        near_m1 = net.step(passing=near_m1, after=saved[1][5:6])
        w1.p_m = near_m1 + [net.other(piece) for piece in near_m1]
        output = mlp(1, w1)

        m1, gmid, dh, u = mlp_back(1, out_cot, after=(output,))
        m1 = net.swap_cores(*m1)
        dtri = attn_back(1, dh, u)
        (g1,) = net.step(net.first_way(m1), after=(dtri,))
        g1 = net.send_first(g1)
        grad = input_back(1, gmid, dtri, after=g1[:1])
        two, gp = hidden_back_0(grad, after=())
        q1 = qkv_back(1, dtri, after=(gp,))
        q1, two = net.swap_cores(*q1), net.swap_cores(*two)
        one, gmid, dh, u = middle_back_0(gp, grad, after=q1[:1])
        g1, send = net.step(net.second_way(g1), passing=one[1:], after=(gmid,), weight=40)
        (g2,) = net.step(net.first_way(q1, two), after=g1[:1])
        dtri = attn_back(0, dh, u, after=g2[:1])
        g1, g2 = net.send_second(g1), net.send_first(g2)
        one = net.swap_cores(one[0], send)
        q0 = qkv_back(0, dtri)
        g1, send = net.step(net.join(g1), passing=q0[1:], after=q0[:1])
        g1 = net.send_level(g1, 1)
        q0 = net.swap_cores(q0[0], send)
        (g3,) = net.step(net.first_way(one, q0), after=(g1[0],))
        grad = input_back(0, gmid, dtri, after=g3[:1])
        g3 = net.send_first(g3)
        ((g1,),) = net.step(net.add(g1), after=(grad,))
        g1 = net.send_level((g1, g1), 2)
        little = small_sums(after=(g1[0],))
        g2, little = net.step(net.second_way(g2), passing=(little,))
        order = g2[2:3]
        g2 = net.send_second(g2)
        (g3,) = net.step(net.second_way(g3), after=order)
        order = g3[2:3]
        g3 = net.send_second(g3)
        g2, (g1,), little = net.step(
            net.join(g2), net.add(g1), passing=(little,), after=order
        )
        order = g2[:1]
        g2 = net.send_level(g2, 1)
        near1 = net.level(g1, 1)
        little = (little, net.other(little))
        g3, (little,) = net.step(net.join(g3), net.add_small(little), after=order)
        order = g3[:1]
        g3 = net.send_level(g3, 1)
        little = (little, net.x(little))
        (g2,), (little,), side1, near1 = net.step(
            net.add(g2), net.add_small(little), passing=(g1, near1), after=order
        )
        order = (g2,)
        g2 = net.send_level((g2, g2), 2)
        little = (little, net.y(little))
        g1 = [side1, near1, net.other(side1), net.other(near1)]
        (g3,), (little,) = net.step(net.add(g3), net.own_small(little), after=order)
        order = (g3,)
        g3 = net.send_level((g3, g3), 2)
        little = (little, net.level(little, 1))
        (g2,), (little,) = net.step(net.add(g2), net.add_small(little), after=order)
        near2, side2 = net.level(g2, 1), net.other(g2)
        little = (little, net.level(little, 2))
        results = net.finish([(M_ROWS, 1, ("1", "p", "2"))], g1, after=(g2,))
        (g3,), (little,), near2 = net.step(
            net.add(g3), net.add_small(little), passing=(near2,), after=results[4:]
        )
        near3, side3 = net.level(g3, 1), net.other(g3)
        g2 = [g2, near2, side2, net.other(near2)]
        small = list(net.unpack(little))
        results = net.finish(
            [(Q_ROWS, 1, ("q",)), (TWO_ROWS, 0, ("two",))], g2, results, after=small[7:8]
        )
        (near3,) = net.step(passing=(near3,), after=results[4:])
        dwq, dwp, dw1, dw2, _ = net.finish(
            [(ONE_ROWS, 0, ("1", "p")), (Q_ROWS, 0, ("q",))],
            [g3, near3, side3, net.other(near3)], results,
        )
        small[8] = small[8].transpose(0, 2, 1)
        return (
            output, grad.transpose(1, 0, 2), small[0], small[1], dwq, small[7], small[8], dwp, small[2], small[3],
            small[4], dw1, small[6], dw2, small[5],
        )
    else:
        state = images_in
        bias[1] = bias_of(1)
        for layer in range(LAYERS):
            attn(layer, state, weights[layer])
            state = mlp(layer, weights[layer])
        output = state
        grad = out_cot
        reduced = [None] * LAYERS
        for layer in reversed(range(LAYERS)):
            m, gmid, dh, u = mlp_back(layer, grad)
            dtri = attn_back(layer, dh, u)
            reduced[layer] = (m, qkv_back(layer, dtri))
            grad = input_back(layer, gmid, dtri)
        little = net.sum_small(small_sums())
        dwq, dwp, dw1, dw2 = net.finish(reduced)
    little = little.reshape(LAYERS, 24, C)
    small_q = little[:, 8:12, : 2 * LANES].reshape(LAYERS, -1)
    rel = little[:, 16:].reshape(LAYERS, 8, 2, wide)[..., :TABLE].transpose(0, 3, 2, 1)
    rel = rel.reshape(LAYERS, TABLE, HEADS)
    db1 = little[:, 4:8].reshape(LAYERS, FF)
    mine = lax.axis_index("tensor")

    def share(v, axis):
        size = v.shape[axis] // tensor
        return lax.dynamic_slice_in_dim(v, mine * size, size, axis)

    return (
        output, grad.transpose(1, 0, 2), little[:, 12], little[:, 13], dwq, share(small_q, 1), share(rel, 2), dwp,
        little[:, 3], little[:, 1], little[:, 2], dw1, share(db1, 1), dw2, little[:, 0],
    )


def solution(mesh):
    tokens = P(("dp", "tensor"), None, None)
    cols, rows = P(None, None, "tensor"), P(None, "tensor", None)
    part = P(None, "tensor")
    return jax.shard_map(
        functools.partial(shards, mesh.shape["tensor"], mesh.shape["dp"]),
        mesh=mesh,
        in_specs=(
            tokens, P(), P(), cols, part, cols, rows, P(), P(), P(), cols, part, rows, P(), P(),
            P(), tokens,
        ),
        out_specs=(
            tokens, tokens, P(), P(), cols, part, cols, rows, P(), P(), P(), cols, part, rows, P(),
        ),
        check_vma=False,
    )
```

```python
import functools

import jax
import jax.numpy as jnp
import numpy as np
from jax import lax
from jax.experimental import pallas as pl
from jax.experimental.pallas import tpu as pltpu
from jax.sharding import PartitionSpec as P

C = 512
HEADS = 16
HEAD_DIM = 32
FF = 2048
WIN = 7
GRID = 14
SHIFT = 3
LAYERS = 2
TOK = 196
WTOK = 49
TABLE = 169
PAIR = 112
LANES = 128
GROUPS = 4
GHEADS = HEADS // GROUPS
TRI = 3 * LANES
HID = FF // GROUPS
SCALE = HEAD_DIM ** (-0.5)
NEG = -1e30
F32 = jnp.float32
BF16 = jnp.bfloat16


def window_tokens(offset):
    cells = np.arange(TOK).reshape(GRID, GRID)
    cells = np.roll(cells, (-offset, -offset), (0, 1))
    cells = cells.reshape(2, WIN, 2, WIN).transpose(0, 2, 1, 3)
    return cells.reshape(4, WTOK)


def place_matrix(offset):
    tokens = window_tokens(offset).reshape(2, 2 * WTOK)
    out = np.zeros((2 * PAIR, TOK), np.float32)
    for pair in range(2):
        out[pair * PAIR + np.arange(2 * WTOK), tokens[pair]] = 1.0
    return out


PLACE = [place_matrix(SHIFT if layer % 2 == 1 else 0) for layer in range(LAYERS)]


def group_matrix():
    out = np.zeros((TRI, TRI), np.float32)
    for head in range(GHEADS):
        for part in range(3):
            for pos in range(HEAD_DIM):
                out[
                    (head * 3 + part) * HEAD_DIM + pos, (part * GHEADS + head) * HEAD_DIM + pos
                ] = 1.0
    return out


GROUP = group_matrix()


def pick_matrix():
    out = np.zeros((TRI, 2 * LANES), np.float32)
    for head in range(GHEADS):
        for to, part in enumerate((0, 2)):
            for pos in range(HEAD_DIM):
                out[(head * 3 + part) * HEAD_DIM + pos, (head * 2 + to) * HEAD_DIM + pos] = 1.0
    return out


PICK = pick_matrix()


def mm(a, b):
    return jnp.dot(a, b, preferred_element_type=F32)


def mm_nt(a, b):
    return lax.dot_general(a, b, (((1,), (1,)), ((), ())), preferred_element_type=F32)


def mm_tn(a, b):
    return lax.dot_general(a, b, (((0,), (0,)), ((), ())), preferred_element_type=F32)


def normalize(x):
    centre = x - jnp.mean(x, -1, keepdims=True)
    spread = jnp.mean(centre * centre, -1, keepdims=True)
    rstd = lax.rsqrt(spread + 1e-05)
    return centre * rstd, rstd


def norm_back(xhat, rstd, gain, grad):
    rstd = rstd[:, :1]
    scaled = grad * gain
    m1 = jnp.mean(scaled, -1, keepdims=True)
    m2 = jnp.mean(scaled * xhat, -1, keepdims=True)
    dx = rstd * (scaled - m1 - xhat * m2)
    return dx, jnp.sum(grad * xhat, 0, keepdims=True), jnp.sum(grad, 0, keepdims=True)


def rows_of(pair):
    return pl.ds(pl.multiple_of(pair * PAIR, 16), PAIR)


def head_mask(head):
    lane = lax.broadcasted_iota(jnp.int32, (PAIR, LANES), 1)
    return (lane // HEAD_DIM) == head


def stack_heads(block, masks):
    zero = jnp.zeros_like(block)
    pad = jnp.zeros((LANES - PAIR, LANES), block.dtype)
    parts = []
    for mask in masks:
        parts += [jnp.where(mask, block, zero), pad]
    return jnp.concatenate(parts, 0)


def split_exact(x):
    high = x.astype(BF16)
    return high, (x - high.astype(F32)).astype(BF16)


def half_rows(core, half):
    mine = pl.ds(pl.multiple_of(core * half, 16), half)
    other = pl.ds(pl.multiple_of((1 - core) * half, 16), half)
    return mine, other


Q_ROWS, M_ROWS = 192, 576
FIRST_ROWS = 224
PACK_Q = [(0, 0, Q_ROWS, TRI, 0, 0)] + [
    (Q_ROWS, j * LANES, 64, LANES, 64 * j, TRI) for j in range(3)
]
PACK_1 = [(0, 0, 256, C, 0, 0)]
PACK_P = [(0, 0, 64, C, 256, 0)]
PACK_2 = [(0, 0, 256, C, 320, 0)]
CHUNKS = (
    (((0, PACK_Q),), Q_ROWS),
    (((2, PACK_1), (1, PACK_P), (3, PACK_2)), M_ROWS),
    (((1, [(0, 0, 64, C, 0, 0)]),), 64),
    (((2, PACK_1), (3, [(0, 0, 256, C, 256, 0)])), 512),
)
ONE_ROWS, TWO_ROWS = 320, 256
PACK_TWO = [(0, 0, 256, C, 0, 0)]


def moved_down(blocks, base):
    return [block[:4] + (block[4] + base, block[5]) for block in blocks]


class Fetch:
    def __init__(self, full, layer, pieces, blocks, dest, core, sems):
        half = dest.shape[1] // 2
        self.copies = [[pltpu.make_async_copy(full.at[layer], dest.at[0], sems.at[0])]]
        at = 1
        for r in range(1, GROUPS):
            group = []
            if len(pieces) == 2:
                near, far = pieces[0].at[r - 1], pieces[1].at[r - 1]
            else:
                near, far = pieces[r - 1], pieces[r + 2]
            for side, piece in ((core, near), (1 - core, far)):
                for row, lane, rows, lanes, to_row, to_lane in blocks:
                    target = dest.at[
                        r,
                        pl.ds(pl.multiple_of(side * half + row, 16), rows),
                        pl.ds(lane, lanes),
                    ]
                    source = piece.at[pl.ds(to_row, rows), pl.ds(to_lane, lanes)]
                    group.append(pltpu.make_async_copy(source, target, sems.at[at]))
                    at += 1
            self.copies.append(group)
        for group in self.copies:
            for copy in group:
                copy.start()

    def wait(self, r):
        for copy in self.copies[r]:
            copy.wait()


def bias_kernel(layer, table, index, ids_col, ids_row, place, lanes_place, bias_ref):
    cols = mm(place[...], ids_col[...])
    rows = mm_nt(ids_row[...], lanes_place[...])
    masks = []
    for pair in range(2):
        col = cols[pair * PAIR : (pair + 1) * PAIR]
        row = rows[:1, pair * LANES : (pair + 1) * LANES]
        masks.append(jnp.where(col != row, -100.0, 0.0))
    idx = index[...]
    step = LAYERS * 2 * LANES
    at_low = jnp.clip(idx, 0, LANES - 1)
    at_high = jnp.clip(idx - LANES, 0, LANES - 1)

    def pick(low, high):
        low = jnp.take_along_axis(jnp.broadcast_to(low, (PAIR, LANES)), at_low, axis=1)
        high = jnp.take_along_axis(jnp.broadcast_to(high, (PAIR, LANES)), at_high, axis=1)
        return jnp.where(idx < 0, NEG, jnp.where(idx < LANES, low, high))

    for head in range(HEADS):
        r, lane = head // GHEADS, (head % GHEADS) * step + layer * 2 * LANES
        picked = pick(
            table[r : r + 1, lane : lane + LANES], table[r : r + 1, lane + LANES : lane + 2 * LANES]
        )
        if layer == 0:
            bias_ref[0, head] = picked
        else:
            bias_ref[0, head] = picked + masks[0]
            bias_ref[1, head] = picked + masks[1]


def attn_fwd_kernel(layer, pairs, base, *refs):
    first = layer == 0
    where, x_in, place, ln_g, ln_b, tables, group, bias, full_qkv = refs[:9]
    at = BIAS_AT + layer * TRI
    p_qkv, outs = refs[9:11], refs[11:]
    if first:
        x_ref, outs = outs[0], outs[1:]
    else:
        x_ref = x_in
    xhat_ref, rstd_ref, n1_ref, tri_ref, e_ref, rinv_ref, ho_ref, w_qkv, sem_q = outs
    qkv = Fetch(full_qkv, layer, p_qkv, moved_down(PACK_Q, base), w_qkv, where[1], sem_q)
    if first:
        for image in range(pairs // 2):
            x_ref[pl.ds(image * 2 * PAIR, 2 * PAIR), :] = mm(place[...], x_in[image])

    def norm_rows(pair, carry):
        rows = rows_of(pair)
        xhat, rstd = normalize(x_ref[rows, :])
        xhat_ref[rows, :] = xhat
        rstd_ref[rows, :] = jnp.broadcast_to(rstd, (PAIR, LANES))
        n1_ref[rows, :] = (xhat * ln_g[...] + ln_b[...]).astype(BF16)
        return carry

    lax.fori_loop(0, pairs, norm_rows, 0)
    masks = [head_mask(h) for h in range(GHEADS)]
    ones = jnp.ones((PAIR, LANES), BF16)
    for r in range(GROUPS):
        qkv.wait(r)
        tri = (mm(n1_ref[...], w_qkv[r]) + tables[r : r + 1, at : at + TRI]).astype(BF16)
        tri_ref[r] = mm(tri, group[...]).astype(BF16)
        ones_stack = stack_heads(ones, masks)

        def pair_step(pair, carry):
            rows = rows_of(pair)
            q4 = tri_ref[r, rows, 0:LANES]
            k4 = tri_ref[r, rows, LANES : 2 * LANES]
            v4 = tri_ref[r, rows, 2 * LANES : 3 * LANES]
            s4 = mm_nt(q4, stack_heads(k4, masks))
            kind = 0 if first else lax.rem(pair, 2)
            es = []
            for h in range(GHEADS):
                s = s4[:, h * LANES : (h + 1) * LANES] * SCALE + bias[kind, r * GHEADS + h]
                es.append(jnp.exp(s - jnp.max(s, -1, keepdims=True)).astype(BF16))
            e4 = jnp.concatenate(es, 1)
            e_ref[r, pair] = e4
            vm = jnp.concatenate([stack_heads(v4, masks), ones_stack], 1)
            out = mm(e4, vm)
            rinv = 1.0 / out[:, LANES:]
            rinv_ref[r, rows, :] = rinv
            ho_ref[rows, r * LANES : (r + 1) * LANES] = (out[:, :LANES] * rinv).astype(BF16)
            return carry

        lax.fori_loop(0, pairs, pair_step, 0, unroll=True)


def mlp_fwd_kernel(layer, pairs, count, *refs):
    last = layer == LAYERS - 1
    where, x, ho, b_proj, ln_g, ln_b, tables, b2, place = refs[:9]
    at = HIDDEN_AT + layer * HID
    full_p, full_1, full_2 = refs[9:12]
    p_m, refs = refs[12 : 12 + count], refs[12 + count :]
    out_ref, xhat_ref, rstd_ref, n2_ref, act_ref, dact_ref, wp, w1, w2 = refs[:9]
    sem_p, sem_1, sem_2, acc, pre_ref, mid = refs[9:]
    core = where[1]
    f_p = Fetch(full_p, layer, p_m, PACK_P, wp, core, sem_p)
    f_1 = Fetch(full_1, layer, p_m, PACK_1, w1, core, sem_1)
    f_2 = Fetch(full_2, layer, p_m, PACK_2, w2, core, sem_2)
    for r in range(GROUPS):
        f_p.wait(r)
    weight = jnp.concatenate([wp[r] for r in range(GROUPS)], 0)
    mid[...] = x[...] + mm(ho[...], weight) + b_proj[...]

    def norm_rows(pair, carry):
        rows = rows_of(pair)
        xhat, rstd = normalize(mid[rows, :])
        xhat_ref[rows, :] = xhat
        rstd_ref[rows, :] = jnp.broadcast_to(rstd, (PAIR, LANES))
        n2_ref[rows, :] = (xhat * ln_g[...] + ln_b[...]).astype(BF16)
        return carry

    lax.fori_loop(0, pairs, norm_rows, 0)
    for r in range(GROUPS):
        f_1.wait(r)
        pre_ref[...] = mm(n2_ref[...], w1[r])
        b1_row = tables[r : r + 1, at : at + HID]

        def gelu_rows(step, carry):
            rows = pl.ds(pl.multiple_of(step * 16, 16), 16)
            pre = pre_ref[rows, :] + b1_row
            cdf = 0.5 + 0.5 * lax.erf(pre * (0.5**0.5))
            act_ref[r, rows, :] = (pre * cdf).astype(BF16)
            pdf = jnp.exp(-0.5 * pre * pre) * 0.3989422804014327
            dact_ref[r, rows, :] = (cdf + pre * pdf).astype(BF16)
            return carry

        lax.fori_loop(0, pairs * (PAIR // 16), gelu_rows, 0, unroll=2)
        f_2.wait(r)
        part = mm(act_ref[r], w2[r])
        if r == 0:
            acc[...] = part
        else:
            acc[...] += part
    acc[...] = acc[...] + mid[...] + b2[...]
    for image in range(pairs // 2):
        state = acc[pl.ds(image * 2 * PAIR, 2 * PAIR), :]
        if last:
            out_ref[image] = mm_tn(place[...], state.astype(BF16)).astype(BF16)
        else:
            high, low = split_exact(state)
            out_ref[pl.ds(image * 2 * PAIR, 2 * PAIR), :] = mm(place[...], high) + mm(
                place[...], low
            )


X_FIRST = (0, 2, 1, 3)
Y_FIRST = (0, 1, 2, 3)
ORDERS = (X_FIRST, Y_FIRST)


def give(keep_ref, send_ref, tmp, r, core, blocks, first=0, size=None):
    half = tmp.shape[0] // 2
    size = size or keep_ref.shape[2]
    for ref, base in ((keep_ref, core * half), (send_ref, (1 - core) * half)):
        for row, lane, rows, lanes, to_row, to_lane in blocks:
            done = 0
            while done < rows:
                part, at = divmod(to_row + done, size)
                count = min(rows - done, size - at)
                to = slice(first + at, first + at + count)
                ref[part, ORDERS[part].index(r), to, to_lane : to_lane + lanes] = tmp[
                    pl.ds(pl.multiple_of(base + row + done, 16), count), lane : lane + lanes
                ]
                done += count


class Joined:
    def __init__(self, refs):
        self.refs = refs

    def __getitem__(self, r):
        for ref in self.refs:
            if r < ref.shape[0]:
                return ref[r]
            r -= ref.shape[0]


def gelu_into(pairs, pre_ref, b1_row, act_ref, dact_ref, at):
    def some_rows(step, carry):
        rows = pl.ds(pl.multiple_of(step * 16, 16), 16)
        pre = pre_ref[rows, :] + b1_row
        cdf = 0.5 + 0.5 * lax.erf(pre * (0.5**0.5))
        act_ref[at, rows, :] = (pre * cdf).astype(BF16)
        pdf = jnp.exp(-0.5 * pre * pre) * 0.3989422804014327
        dact_ref[at, rows, :] = (cdf + pre * pdf).astype(BF16)
        return carry

    lax.fori_loop(0, pairs * (PAIR // 16), some_rows, 0, unroll=2)


def mlp_open_kernel(layer, pairs, base, *refs):
    where, x, ho, b_proj, ln_g, ln_b, tables, full_p, full_1, full_2 = refs[:10]
    pieces, refs = refs[10:12], refs[12:]
    mid, xhat_ref, rstd_ref, n2_ref, acc, act_ref, dact_ref, wp, w1, w2, sem_p, sem_w, pre_ref = refs
    f_p = Fetch(full_p, layer, pieces, moved_down(PACK_P, base - 256), wp, where[1], sem_p)
    copies = [
        pltpu.make_async_copy(full.at[layer], w.at[0], sem_w.at[i])
        for i, (full, w) in enumerate(((full_1, w1), (full_2, w2)))
    ]
    for copy in copies:
        copy.start()
    for r in range(GROUPS):
        f_p.wait(r)
    weight = jnp.concatenate([wp[r] for r in range(GROUPS)], 0)
    mid[...] = x[...] + mm(ho[...], weight) + b_proj[...]

    def norm_rows(pair, carry):
        rows = rows_of(pair)
        xhat, rstd = normalize(mid[rows, :])
        xhat_ref[rows, :] = xhat
        rstd_ref[rows, :] = jnp.broadcast_to(rstd, (PAIR, LANES))
        n2_ref[rows, :] = (xhat * ln_g[...] + ln_b[...]).astype(BF16)
        return carry

    lax.fori_loop(0, pairs, norm_rows, 0)
    for copy in copies:
        copy.wait()
    at = HIDDEN_AT + layer * HID
    pre_ref[...] = mm(n2_ref[...], w1[0])
    gelu_into(pairs, pre_ref, tables[0:1, at : at + HID], act_ref, dact_ref, 0)
    acc[...] = mm(act_ref[0], w2[0])


def mlp_more_kernel(layer, pairs, shares, last, *refs):
    where, tables, n2, acc_in = refs[:4]
    count = 2 * len(shares)
    pieces, refs = refs[4 : 4 + count], refs[4 + count :]
    if last:
        mid, b2, place, out_ref, act_ref, dact_ref, w1, w2, sems, pre_ref, acc = refs
    else:
        acc, act_ref, dact_ref, w1, w2, sems, pre_ref = refs
    copies = []
    for i in range(len(shares)):
        group = []
        for side, c in enumerate((where[1], 1 - where[1])):
            for k, w in enumerate((w1, w2)):
                half = w.shape[1] // 2
                target = w.at[i, pl.ds(pl.multiple_of(c * half, 16), half)]
                source = pieces[2 * i + side].at[pl.ds(k * half, half)]
                group.append(pltpu.make_async_copy(source, target, sems.at[4 * i + 2 * side + k]))
        for copy in group:
            copy.start()
        copies.append(group)
    at = HIDDEN_AT + layer * HID
    for i, r in enumerate(shares):
        for copy in copies[i]:
            copy.wait()
        pre_ref[...] = mm(n2[...], w1[i])
        gelu_into(pairs, pre_ref, tables[r : r + 1, at : at + HID], act_ref, dact_ref, i)
        part = mm(act_ref[i], w2[i])
        if i == 0:
            acc[...] = acc_in[...] + part
        else:
            acc[...] += part
    if last:
        for image in range(pairs // 2):
            rows = pl.ds(image * 2 * PAIR, 2 * PAIR)
            state = acc[rows, :] + mid[rows, :] + b2[...]
            out_ref[image] = mm_tn(place[...], state.astype(BF16)).astype(BF16)


def hidden_back(layer, pairs, where, g_in, place, act, dact, w2, g_ref, gb_ref, gp_ref, tmp, outs, blocks, first=0, size=None):
    keep, send = outs
    core = where[1]
    if layer == LAYERS - 1:
        for image in range(pairs // 2):
            rows = pl.ds(image * 2 * PAIR, 2 * PAIR)
            g = mm(place[...], g_in[image])
            g_ref[rows, :] = g
            gb_ref[rows, :] = g.astype(BF16)
    else:
        gb_ref[...] = g_ref[...].astype(BF16)
    for r in range(GROUPS):
        tmp[...] = mm_tn(act[r], gb_ref[...]).astype(BF16)
        give(keep, send, tmp, r, core, blocks, first, size)
        ga = mm_nt(gb_ref[...], w2[r])
        gp_ref[r] = (ga * dact[r].astype(F32)).astype(BF16)


def middle_back(layer, pairs, where, gp_ref, g_ref, mid, n2, ho, rinv, ln_g, w1, wp, gb_ref, acc, tmp, tmp_p, outs):
    keep, send, gmid_ref, dh_ref, u_ref, small_ref, db1_ref = outs
    tid, core = where[0], where[1]
    small_ref[...] = jnp.zeros_like(small_ref)
    for r in range(GROUPS):
        db1_ref[tid ^ r] = jnp.sum(gp_ref[r].astype(F32), 0, keepdims=True)
        tmp[...] = mm_tn(n2[...], gp_ref[r]).astype(BF16)
        give(keep, send, tmp, r, core, PACK_1)
        part = mm_nt(gp_ref[r], w1[r])
        if r == 0:
            acc[...] = part
        else:
            acc[...] += part

    def back_rows(pair, carry):
        rows = rows_of(pair)
        g_rows = g_ref[rows, :]
        dx, dg, db = norm_back(mid[0][rows, :], mid[1][rows, :], ln_g[...], acc[rows, :])
        gmid = g_rows + dx
        gmid_ref[rows, :] = gmid
        gb_ref[rows, :] = gmid.astype(BF16)
        small_ref[0:1, :] += jnp.sum(g_rows, 0, keepdims=True)
        small_ref[1:2, :] += dg
        small_ref[2:3, :] += db
        small_ref[3:4, :] += jnp.sum(gmid, 0, keepdims=True)
        return carry

    lax.fori_loop(0, pairs, back_rows, 0)
    for r in range(GROUPS):
        lanes = slice(r * LANES, (r + 1) * LANES)
        tmp_p[...] = mm_tn(ho[:, lanes], gb_ref[...]).astype(BF16)
        give(keep, send, tmp_p, r, core, PACK_P)
        gh = mm_nt(gb_ref[...], wp[r]) * rinv[r]
        dh_ref[r] = gh.astype(BF16)
        u_ref[r] = (gh * ho[:, lanes].astype(F32)).astype(BF16)


def mlp_bwd_kernel(layer, pairs, count, *refs):
    where, g_in, place = refs[:3]
    act, dact = Joined(refs[3 : 3 + count]), Joined(refs[3 + count : 3 + 2 * count])
    xhat, rstd, n2, ho, rinv, ln_g, wp = refs[3 + 2 * count : 10 + 2 * count]
    mid = (xhat, rstd)
    refs = refs[10 + 2 * count :]
    w1, w2 = Joined(refs[:count]), Joined(refs[count : 2 * count])
    outs = refs[2 * count : 2 * count + 7]
    g_ref, gb_ref, gp_ref, acc, tmp, tmp_p = refs[2 * count + 7 :]
    if layer < LAYERS - 1:
        g_ref = g_in
    hidden_back(
        layer, pairs, where, g_in, place, act, dact, w2, g_ref, gb_ref, gp_ref, tmp, outs[:2], PACK_2
    )
    middle_back(
        layer, pairs, where, gp_ref, g_ref, mid, n2, ho, rinv, ln_g, w1, wp, gb_ref, acc, tmp, tmp_p,
        outs,
    )


def pair_bwd_kernel(layer, pairs, where, g, act, dact, w2, n1, dtri, keep, send, gp_ref, small_ref, gb_ref, tmp, tmp_q):
    hidden_back(
        layer, pairs, where, g, None, act, dact, w2, g, gb_ref, gp_ref, tmp, (keep, send), PACK_TWO,
        Q_ROWS // 2, TWO_ROWS // 2,
    )
    qkv_grad_kernel(pairs, where, n1, dtri, keep, send, small_ref, tmp_q, Q_ROWS // 2)


def middle_bwd_kernel(layer, pairs, *refs):
    where, gp, g, xhat, rstd, n2, ho, rinv, ln_g, wp, w1 = refs[:11]
    mid = (xhat, rstd)
    gb_ref, acc, tmp, tmp_p = refs[18:]
    middle_back(
        layer, pairs, where, gp, g, mid, n2, ho, rinv, ln_g, w1, wp, gb_ref, acc, tmp, tmp_p,
        refs[11:18],
    )


def attn_bwd_kernel(pairs, where, dh, u, tri, e, group, dtri_ref, rel_ref, low_ref):
    tid = where[0]
    masks = [head_mask(h) for h in range(GHEADS)]
    neg_ones = jnp.full((PAIR, LANES), -1.0, BF16)
    for r in range(GROUPS):
        sid = tid ^ r
        neg_stack = stack_heads(neg_ones, masks)

        def pair_step(pair, carry):
            rows = rows_of(pair)
            q4 = tri[r, rows, 0:LANES]
            k4 = tri[r, rows, LANES : 2 * LANES]
            v4 = tri[r, rows, 2 * LANES : 3 * LANES]
            dh4 = dh[r, rows, :]
            left = jnp.concatenate([dh4, u[r, rows, :]], 1)
            right = jnp.concatenate([stack_heads(v4, masks), neg_stack], 1)
            dsp = mm_nt(left, right)
            e4 = e[r, pair]
            ds4 = e4.astype(F32) * dsp
            for h in range(GHEADS):
                part = ds4[:, h * LANES : (h + 1) * LANES]
                head = sid * GHEADS + h
                rel_ref[head] = jnp.where(pair == 0, part, rel_ref[head] + part)
            dsb = (ds4 * SCALE).astype(BF16)
            dq4 = mm(dsb, stack_heads(k4, masks))
            pad = jnp.zeros((LANES - PAIR, GHEADS * LANES), BF16)
            dsb_p = jnp.concatenate([dsb, pad], 0)
            e4_p = jnp.concatenate([e4, pad], 0)

            def flip(block):
                return jnp.concatenate(
                    [block[:, h * LANES : (h + 1) * LANES].T for h in range(GHEADS)], 1
                )[:PAIR]

            dk4 = mm(flip(dsb_p), stack_heads(q4, masks))
            dv4 = mm(flip(e4_p), stack_heads(dh4, masks))
            low_ref[rows, :] = jnp.concatenate([dq4, dk4, dv4], 1).astype(BF16)
            return carry

        lax.fori_loop(0, pairs, pair_step, 0, unroll=True)
        dtri_ref[r] = mm_nt(low_ref[...], group[...]).astype(BF16)


def qkv_grad_kernel(pairs, where, n1, dtri, keep, send, small_ref, tmp, size=None):
    tid, core = where[0], where[1]
    for r in range(GROUPS):
        tmp[...] = mm_tn(n1[...], dtri[r]).astype(BF16)
        give(keep, send, tmp, r, core, PACK_Q, 0, size)
        small_ref[tid ^ r] = jnp.sum(dtri[r].astype(F32), 0, keepdims=True)


def input_bwd_kernel(layer, pairs, where, gmid, xhat, xscale, dtri, ln_g, place, w_qkv, gout_ref, small_ref, acc):
    last = layer == 0
    for r in range(GROUPS):
        part = mm_nt(dtri[r], w_qkv[r])
        if r == 0:
            acc[...] = part
        else:
            acc[...] += part
    small_ref[...] = jnp.zeros_like(small_ref)

    def back_rows(pair, carry):
        rows = rows_of(pair)
        dx, dg, db = norm_back(xhat[rows, :], xscale[rows, :], ln_g[...], acc[rows, :])
        acc[rows, :] = gmid[rows, :] + dx
        small_ref[0:1, :] += dg
        small_ref[1:2, :] += db
        return carry

    lax.fori_loop(0, pairs, back_rows, 0)
    for image in range(pairs // 2):
        grad = acc[pl.ds(image * 2 * PAIR, 2 * PAIR), :]
        if last:
            gout_ref[:, image, :] = mm_tn(place[...], grad.astype(BF16)).astype(BF16)
        else:
            high, low = split_exact(grad)
            gout_ref[pl.ds(image * 2 * PAIR, 2 * PAIR), :] = mm(place[...], high) + mm(
                place[...], low
            )


def pack_start(plan, where, weights, outs, sems):
    core = where[1]
    moves = []
    for weight, layer, out, blocks in plan:
        weight, out = weights[weight], outs[out]
        half = weight.shape[1] // 2
        for row, lane, rows, lanes, to_row, to_lane in blocks:
            from_row = pl.multiple_of(core * half + row, 16)
            moves.append(
                (
                    weight.at[layer, pl.ds(from_row, rows), pl.ds(lane, lanes)],
                    out.at[pl.ds(to_row, rows), pl.ds(to_lane, lanes)],
                )
            )
    copies = [pltpu.make_async_copy(a, b, sems.at[i]) for i, (a, b) in enumerate(moves)]
    for copy in copies:
        copy.start()

    def end():
        for copy in copies:
            copy.wait()

    return end


def merge_kernel(where, a, b, c, out, sems):
    copies = [pltpu.make_async_copy(v, out.at[i], sems.at[i]) for i, v in enumerate((a, b, c))]
    for copy in copies:
        copy.start()
    for copy in copies:
        copy.wait()


def three_parts(v):
    high = v.astype(BF16)
    rest = v - high.astype(F32)
    mid = rest.astype(BF16)
    return high, mid, (rest - mid.astype(F32)).astype(BF16)


def own_tables(table, qv, b1, out):
    out[...] = jnp.zeros_like(out)
    at = lax.broadcasted_iota(jnp.int32, (2 * LANES, TRI), 0)
    to = lax.broadcasted_iota(jnp.int32, (2 * LANES, TRI), 1)
    same = jnp.logical_and(at // 64 == to // 96, at % HEAD_DIM == to % HEAD_DIM)
    same = jnp.logical_and(same, 2 * ((at // HEAD_DIM) % 2) == (to // HEAD_DIM) % 3)
    spread = jnp.where(same, 1.0, 0.0).astype(BF16)
    for layer in range(LAYERS):
        for head in range(GHEADS):
            lane = (head * LAYERS + layer) * 2 * LANES
            out[:, lane : lane + TABLE] = table[layer, head : head + 1, :]
        lane = BIAS_AT + layer * TRI
        out[:, lane : lane + TRI] = exact_pick(qv[layer : layer + 1, :], spread)
        lane = HIDDEN_AT + layer * HID
        out[:, lane : lane + HID] = b1[layer : layer + 1, :]


def put_tables(tables, out):
    cols = tables.shape[1]
    out[Q_ROWS:, :] = jnp.zeros((out.shape[0] - Q_ROWS, C), BF16)
    for part, v in enumerate(three_parts(tables[...])):
        for row in range(8):
            lanes = min(C, cols - row * C)
            at = Q_ROWS + 8 * part + row
            out[at : at + 1, 0:lanes] = v[:, row * C : row * C + lanes]


def take_tables(tables, near, every):
    cols = tables.shape[1]
    every[0:1, :] = tables[...]
    for r in range(1, GROUPS):
        wide = near[r - 1, Q_ROWS : Q_ROWS + 24, :].astype(F32)
        total = wide[0:8] + wide[8:16] + wide[16:24]
        for row in range(8):
            lanes = min(C, cols - row * C)
            every[r : r + 1, row * C : row * C + lanes] = total[row : row + 1, 0:lanes]


def exact_pick(row, chosen):
    parts = jnp.concatenate([*three_parts(row), jnp.zeros((13, row.shape[1]), BF16)], 0)
    got = mm(parts, chosen)
    return got[0:1] + got[1:2] + got[2:3]


def small_kernel(index, *refs):
    out, acc, folded = refs[-3:]
    out[...] = jnp.zeros_like(out)
    pick = refs[0]
    for layer in range(LAYERS):
        small2, db1, small_q, small1, rel = refs[5 * layer + 1 : 5 * layer + 6]
        base = 24 * layer
        out[base : base + 4, :] = small2[...]
        for r in range(GROUPS):
            out[base + 4 + r : base + 5 + r, :] = db1[r]
            out[base + 8 + r : base + 9 + r, 0 : 2 * LANES] = exact_pick(small_q[r], pick[...])
        out[base + 12 : base + 14, :] = small1[...]

        def fold(head, carry, layer=layer, rel=rel):
            second = pltpu.roll(rel[head, WTOK : 2 * WTOK, :], LANES - WTOK, 1)
            at = pl.multiple_of((layer * HEADS + head) * 56, 8)
            folded[pl.ds(at, WTOK), :] = rel[head, 0:WTOK, :] + second
            return carry

        lax.fori_loop(0, HEADS, fold, 0)
    entry = lax.broadcasted_iota(jnp.int32, (2 * LANES, LANES), 0)
    count = LAYERS * HEADS
    acc[...] = jnp.zeros_like(acc)

    def one_row(i, carry):
        onehot = jnp.where(entry == index[i], 1.0, 0.0).astype(BF16)
        high, low = split_exact(folded[pl.ds(i, count, stride=56), :])
        acc[...] += mm_nt(onehot, jnp.concatenate([high, low], 0))
        return carry

    lax.fori_loop(0, WTOK, one_row, 0, unroll=7)
    total = acc[...].T
    total = total[:count] + total[count:]
    for layer in range(LAYERS):
        for part in range(2):
            at = layer * HEADS + part * 8
            out[24 * layer + 16 : 24 * layer + 24, part * 2 * LANES : (part + 1) * 2 * LANES] = total[
                at : at + 8, :
            ]


def add_go_kernel(where, *refs):
    count = (len(refs) - 4) // 2
    go_a, go_b, stay_a, stay_b = refs[-4:]
    row = 0
    for i in range(count):
        keep, got = refs[2 * i], refs[2 * i + 1]
        size = keep.shape[2]
        rows = slice(row, row + size)
        for part, (stay, go) in enumerate(((stay_a, go_a), (stay_b, go_b))):
            stay[:, rows, :] = keep[part, :2] + got[part, :2]
            go[:, rows, :] = keep[part, 2:] + got[part, 2:]
        row += size


def add_next_kernel(where, stay_a, stay_b, got_a, got_b, next_a, next_b, keep_a, keep_b):
    next_a[...] = stay_a[1] + got_a[1]
    next_b[...] = stay_b[1] + got_b[1]
    keep_a[...] = stay_a[0] + got_a[0]
    keep_b[...] = stay_b[0] + got_b[0]


def add_whole_kernel(where, keep_a, keep_b, got_a, got_b, out):
    size = keep_a.shape[0]
    out[0:size, :] = keep_a[...] + got_a[...]
    out[size:, :] = keep_b[...] + got_b[...]


def choose_kernel(where, mine, got, out):
    end = jnp.logical_or(where[2] == 0, where[2] == 3)
    out[...] = jnp.where(end, got[...], mine[...])


def add_level_kernel(where, keep_a, keep_b, got_a, got_b, mine, send):
    odd = where[2] & 1
    a = keep_a[...] + got_a[...]
    b = keep_b[...] + got_b[...]
    mine[...] = jnp.where(odd == 1, b, a)
    send[...] = jnp.where(odd == 1, a, b)


def add_kernel(where, a, b, out):
    out[...] = a[...] + b[...]


FINISH = {"q": (0, PACK_Q), "p": (1, PACK_P), "1": (2, PACK_1), "2": (3, PACK_2), "two": (3, PACK_TWO)}


def finish_kernel(plan, count, made, where, *refs):
    pieces = refs[:made]
    scratch, sems = refs[count + 5 : -1], refs[-1]
    core, odd = where[1], where[2] & 1
    copies = []
    first, slot = 0, 0
    results = refs[count : count + 4]
    for total, layer, names in plan:
        size = total // 2
        for name in names:
            index, blocks = FINISH[name]
            out = scratch[slot]
            half = out.shape[0] // 2
            for at, piece in enumerate(pieces):
                c = core if at < len(pieces) // 2 else 1 - core
                if len(pieces) == 2:
                    for row, lane, rows, lanes, to_row, to_lane in blocks:
                        target = pl.multiple_of(c * half + row, 16)
                        out[pl.ds(target, rows), lane : lane + lanes] = piece[
                            first + to_row : first + to_row + rows, to_lane : to_lane + lanes
                        ].astype(F32)
                    continue
                for part in range(2):

                    @pl.when((odd if at % 2 == 0 else 1 - odd) == part)
                    def _(piece=piece, part=part, c=c, out=out, first=first, size=size, blocks=blocks):
                        for row, lane, rows, lanes, to_row, to_lane in blocks:
                            begin = max(to_row, part * size)
                            end = min(to_row + rows, (part + 1) * size)
                            if begin >= end:
                                continue
                            target = pl.multiple_of(c * half + row + begin - to_row, 16)
                            source = first + begin - part * size
                            out[pl.ds(target, end - begin), lane : lane + lanes] = piece[
                                source : source + end - begin, to_lane : to_lane + lanes
                            ].astype(F32)

            copies.append(pltpu.make_async_copy(out, results[index].at[layer], sems.at[slot]))
            copies[-1].start()
            slot += 1
        first += size * (1 if len(pieces) == 4 else 2)
    for copy in copies:
        copy.wait()


def own_kernel(where, little, got, out):
    tid = where[0]
    out[...] = jnp.zeros_like(out)
    for layer in range(LAYERS):
        base, to = 24 * layer, 16 * layer

        def put(rows, row, lane, lanes):
            out[to + rows[0] : to + rows[1], 0:lanes] = (
                little[base + row : base + row + rows[1] - rows[0], lane : lane + lanes]
                + got[base + row : base + row + rows[1] - rows[0], lane : lane + lanes]
            )

        put((0, 4), 0, 0, C)
        put((4, 6), 12, 0, C)
        for r in range(GROUPS):

            @pl.when(tid == r)
            def _(r=r, put=put):
                put((6, 7), 4 + r, 0, C)
                put((7, 8), 8 + r, 0, 2 * LANES)
                put((8, 12), 16 + GHEADS * (r % 2), 2 * LANES * (r // 2), 2 * LANES)


def unpack_kernel(where, little, *outs):
    for layer in range(LAYERS):
        base = 16 * layer
        for out, at in zip(outs[:7], (4, 5, 3, 1, 2, 0, 6)):
            out[layer : layer + 1, :] = little[base + at : base + at + 1, :]
        outs[7][layer : layer + 1, :] = little[base + 7 : base + 8, 0 : 2 * LANES]
        outs[8][layer] = little[base + 8 : base + 12, 0:TABLE]


VM = pl.BlockSpec(memory_space=pltpu.VMEM)
SM = pl.BlockSpec(memory_space=pltpu.SMEM)
ANY = pl.BlockSpec(memory_space=pl.ANY)
VC = pl.BlockSpec(memory_space=pltpu.VMEM)
HB = pl.BlockSpec(memory_space=pltpu.HBM)


def pinned(shape, dtype):
    return pltpu.VMEM(shape, dtype)


def place_operand(spec, value):
    if spec is VC:
        return pltpu.with_memory_space_constraint(value, pltpu.VMEM)
    if spec is HB:
        return pltpu.with_memory_space_constraint(value, pltpu.HBM)
    return value


def call(
    kernel, specs, args, outs, scratch=(), flops=0, out_specs=None, limit=2, moved=4, after=(), aliases=None,
    weight=0,
):
    count = len(args)
    skip = count + len(after)

    def body(*refs):
        kernel(*refs[:count], *refs[skip:])

    return pl.pallas_call(
        body,
        out_shape=outs,
        in_specs=list(specs) + [ANY] * len(after),
        out_specs=[VM] * len(outs) if out_specs is None else out_specs,
        scratch_shapes=scratch,
        input_output_aliases=aliases or {},
        compiler_params=pltpu.CompilerParams(vmem_limit_bytes=limit << 20),
        cost_estimate=pl.CostEstimate(flops=1 + weight * GF, bytes_accessed=1, transcendentals=0),
    )(*[place_operand(spec, arg) for spec, arg in zip(specs, args)], *after)


def struct(shape, dtype):
    return jax.ShapeDtypeStruct(shape, dtype)


DIM_Q, DIM_P, DIM_1, DIM_2 = (C, TRI), (LANES, C), (C, HID), (HID, C)
GF = 1 << 30
BIAS_AT = GHEADS * LAYERS * 2 * LANES
HIDDEN_AT = BIAS_AT + LAYERS * TRI


def fetch_sems(*dims):
    return [
        pltpu.SemaphoreType.DMA((1 + 6 * (len(PACK_Q) if d == DIM_Q else 1),)) for d in dims
    ]


def chunk_outs(rows):
    return [pinned((2, GROUPS, rows // 2, C), BF16)] * 2


def attn_fwd(layer, batch, where, x, place, ln_g, ln_b, tables, group, bias, w):
    pairs = 2 * batch
    rows = pairs * PAIR
    outs = [
        pinned((rows, C), F32),
        pinned((rows, LANES), F32),
        pinned((rows, C), BF16),
        pinned((GROUPS, rows, TRI), BF16),
        pinned((GROUPS, pairs, PAIR, GHEADS * LANES), BF16),
        pinned((GROUPS, rows, LANES), F32),
        pinned((rows, C), BF16),
        pinned((GROUPS,) + DIM_Q, BF16),
    ]
    if layer == 0:
        outs = [pinned((rows, C), F32)] + outs
    return call(
        functools.partial(attn_fwd_kernel, layer, pairs, w.q_base),
        [SM, VM if layer == 0 else VC] + [VM] * 5 + [VC] + [HB] + [ANY] * 2,
        [where, x, place, ln_g, ln_b, tables, group, bias, *w.qkv],
        outs,
        fetch_sems(DIM_Q),
        flops=8 * GF,
        limit=9,
    )


def mlp_fwd(layer, batch, where, x, ho, b_proj, ln_g, ln_b, tables, b2, place, w):
    pairs = 2 * batch
    rows = pairs * PAIR
    last = layer == LAYERS - 1
    outs = [
        struct((batch, TOK, C), BF16) if last else pinned((rows, C), F32),
        pinned((rows, C), F32),
        pinned((rows, LANES), F32),
        pinned((rows, C), BF16),
        pinned((GROUPS, rows, HID), BF16),
        pinned((GROUPS, rows, HID), BF16),
    ] + [pinned((GROUPS,) + dim, BF16) for dim in (DIM_P, DIM_1, DIM_2)]
    return call(
        functools.partial(mlp_fwd_kernel, layer, pairs, len(w.p_m)),
        [SM, VC, VC] + [VM] * 6 + [HB] * 3 + [ANY] * len(w.p_m),
        [where, x, ho, b_proj, ln_g, ln_b, tables, b2, place, w.own_p, w.own_1, w.own_2, *w.p_m],
        outs,
        fetch_sems(DIM_P, DIM_1, DIM_2)
        + [pltpu.VMEM((rows, C), F32), pltpu.VMEM((rows, HID), F32), pltpu.VMEM((rows, C), F32)],
        flops=8 * GF,
        limit=12,
    )


def mlp_open(layer, batch, where, x, ho, b_proj, ln_g, ln_b, tables, w, base, pieces):
    pairs = 2 * batch
    rows = pairs * PAIR
    return call(
        functools.partial(mlp_open_kernel, layer, pairs, base),
        [SM, VC, VC] + [VM] * 4 + [HB] * 3 + [ANY] * 2,
        [where, x, ho, b_proj, ln_g, ln_b, tables, w.own_p, w.own_1, w.own_2, *pieces],
        [
            pinned((rows, C), F32),
            pinned((rows, C), F32),
            pinned((rows, LANES), F32),
            pinned((rows, C), BF16),
            pinned((rows, C), F32),
            pinned((1, rows, HID), BF16),
            pinned((1, rows, HID), BF16),
            pinned((GROUPS,) + DIM_P, BF16),
            pinned((1,) + DIM_1, BF16),
            pinned((1,) + DIM_2, BF16),
        ],
        fetch_sems(DIM_P) + [pltpu.SemaphoreType.DMA((2,)), pltpu.VMEM((rows, HID), F32)],
        limit=10,
    )


def mlp_more(layer, batch, where, tables, n2, acc, shares, pieces, end=None, after=()):
    pairs = 2 * batch
    rows = pairs * PAIR
    count = len(shares)
    outs = [pinned((count, rows, HID), BF16)] * 2
    outs += [pinned((count,) + dim, BF16) for dim in (DIM_1, DIM_2)]
    scratch = [pltpu.SemaphoreType.DMA((4 * count,)), pltpu.VMEM((rows, HID), F32)]
    if end is None:
        outs = [pinned((rows, C), F32)] + outs
    else:
        outs = [struct((batch, TOK, C), BF16)] + outs
        scratch.append(pltpu.VMEM((rows, C), F32))
    return call(
        functools.partial(mlp_more_kernel, layer, pairs, shares, end is not None),
        [SM, VM, VC, VC] + [ANY] * len(pieces) + ([] if end is None else [VC, VM, VM]),
        [where, tables, n2, acc, *pieces, *(end or ())],
        outs,
        scratch,
        limit=12,
        after=after,
    )


def mlp_bwd(layer, batch, where, g, place, act, dact, mid, n2, ho, rinv, ln_g, w, after):
    pairs = 2 * batch
    rows = pairs * PAIR
    outs = chunk_outs(M_ROWS) + [
        pinned((rows, C), F32),
        pinned((GROUPS, rows, LANES), BF16),
        pinned((GROUPS, rows, LANES), BF16),
        struct((4, C), F32),
        struct((GROUPS, 1, HID), F32),
    ]
    return call(
        functools.partial(mlp_bwd_kernel, layer, pairs, len(act)),
        [SM, VM if layer == LAYERS - 1 else VC, VM]
        + [VC] * (2 * len(act) + 5)
        + [VM]
        + [VC] * (2 * len(act) + 1),
        [where, g, place, *act, *dact, *mid, n2, ho, rinv, ln_g, w[0], *w[1], *w[2]],
        outs,
        [
            pltpu.VMEM((rows, C), F32),
            pltpu.VMEM((rows, C), BF16),
            pltpu.VMEM((GROUPS, rows, HID), BF16),
            pltpu.VMEM((rows, C), F32),
            pltpu.VMEM(DIM_1, BF16),
            pltpu.VMEM(DIM_P, BF16),
        ],
        flops=14 * GF,
        limit=18,
        after=after,
    )


def pair_bwd(layer, batch, where, g, act, dact, w, n1, dtri, after):
    pairs = 2 * batch
    rows = pairs * PAIR
    return call(
        functools.partial(pair_bwd_kernel, layer, pairs),
        [SM] + [VC] * 6,
        [where, g, act[0], dact[0], w[2][0], n1, dtri],
        chunk_outs(TWO_ROWS + Q_ROWS)
        + [pinned((GROUPS, rows, HID), BF16), struct((GROUPS, 1, TRI), F32)],
        [pltpu.VMEM((rows, C), BF16), pltpu.VMEM(DIM_2, BF16), pltpu.VMEM(DIM_Q, BF16)],
        limit=10,
        after=after,
    )


def middle_bwd(layer, batch, where, gp, g, mid, n2, ho, rinv, ln_g, w, after):
    pairs = 2 * batch
    rows = pairs * PAIR
    return call(
        functools.partial(middle_bwd_kernel, layer, pairs),
        [SM] + [VC] * 7 + [VM] + [VC] * 2,
        [where, gp, g, *mid, n2, ho, rinv, ln_g, w[0], w[1][0]],
        chunk_outs(ONE_ROWS)
        + [
            pinned((rows, C), F32),
            pinned((GROUPS, rows, LANES), BF16),
            pinned((GROUPS, rows, LANES), BF16),
            struct((4, C), F32),
            struct((GROUPS, 1, HID), F32),
        ],
        [
            pltpu.VMEM((rows, C), BF16),
            pltpu.VMEM((rows, C), F32),
            pltpu.VMEM(DIM_1, BF16),
            pltpu.VMEM(DIM_P, BF16),
        ],
        flops=9 * GF,
        limit=12,
        after=after,
    )


def attn_bwd(batch, where, dh, u, tri, e, group, after):
    pairs = 2 * batch
    rows = pairs * PAIR
    return call(
        functools.partial(attn_bwd_kernel, pairs),
        [SM] + [VC] * 4 + [VM],
        [where, dh, u, tri, e, group],
        [pinned((GROUPS, rows, TRI), BF16), pinned((HEADS, PAIR, LANES), F32)],
        [pltpu.VMEM((rows, TRI), BF16)],
        flops=12 * GF,
        limit=9,
        after=after,
    )


def qkv_grad(batch, where, n1, dtri, after):
    return call(
        functools.partial(qkv_grad_kernel, 2 * batch),
        [SM] + [VC] * 2,
        [where, n1, dtri],
        chunk_outs(Q_ROWS) + [struct((GROUPS, 1, TRI), F32)],
        [pltpu.VMEM(DIM_Q, BF16)],
        flops=3 * GF,
        limit=6,
        after=after,
    )


def input_bwd(layer, batch, where, gmid, normed, dtri, ln_g, place, w, after):
    pairs = 2 * batch
    rows = pairs * PAIR
    return call(
        functools.partial(input_bwd_kernel, layer, pairs),
        [SM, VC, VC, VC, VC, VM, VM, VC],
        [where, gmid, *normed, dtri, ln_g, place, w],
        [
            struct((TOK, batch, C), BF16) if layer == 0 else pinned((rows, C), F32),
            struct((2, C), F32),
        ],
        [pltpu.VMEM((rows, C), F32)],
        flops=3 * GF,
        limit=9,
        after=after,
    )


def full_bias(qv_rows, heads):
    parts = qv_rows.reshape(LAYERS, heads, 2, HEAD_DIM)
    full = jnp.stack([parts[:, :, 0], jnp.zeros_like(parts[:, :, 0]), parts[:, :, 1]], 2)
    return full.reshape(LAYERS, heads * 3 * HEAD_DIM)


def swap(x, axis, size, bit):
    return lax.ppermute(x, axis, [(i, i ^ bit) for i in range(size)])


class Weights:
    def __init__(self, own, p_q, p_m, q_base=0):
        own_q, self.own_p, self.own_1, self.own_2 = own
        self.q_base = q_base
        self.qkv = [own_q] + p_q
        self.p_m = p_m


class Direct:
    def __init__(self, dp):
        self.dp = dp
        self.t = lax.axis_index("tensor")
        d = lax.axis_index("dp")
        self.where = jnp.stack([self.t, d % 2, d // 2]).astype(jnp.int32)

    def x(self, v):
        return swap(v, "tensor", 4, 1)

    def y(self, v):
        return swap(v, "tensor", 4, 2)

    def diagonal(self, v):
        return swap(v, "tensor", 4, 3)

    def other(self, v):
        return swap(v, "dp", self.dp, 1)

    def level(self, v, k):
        return swap(v, "dp", self.dp, 2 * k)

    def near(self, v):
        return self.x(v), self.y(v), self.diagonal(v)

    def plan(self, parts):
        plan, outs = [], []
        for part in parts:
            at, base = len(outs), 0
            for layer, chunk in part:
                lists, rows = CHUNKS[chunk]
                for weight, blocks in lists:
                    plan.append((weight, layer, at, moved_down(blocks, base)))
                base += rows
            outs.append(pinned((base, C), BF16))
        return plan, outs

    def pack(self, arrays, parts, tables=None, after=()):
        plan, outs = self.plan(parts)
        count = sum(len(blocks) for _, _, _, blocks in plan)
        args = [self.where, *arrays]
        scratch = []
        if tables is not None:
            args += tables
            outs[0] = pinned((FIRST_ROWS, C), BF16)
            outs.append(pinned((1, HIDDEN_AT + LAYERS * HID), F32))
            scratch = [pltpu.VMEM(v.shape, F32) for v in tables]
        made = len(outs)

        def body(where, *refs):
            outs = refs[len(args) - 1 : len(args) - 1 + made]
            end = pack_start(plan, where, refs[:4], outs, refs[-1])
            if tables is not None:
                held = refs[len(args) - 1 + made : -1]
                copies = [
                    pltpu.make_async_copy(a, b, refs[-1].at[count + i])
                    for i, (a, b) in enumerate(zip(refs[4:7], held))
                ]
                for copy in copies:
                    copy.start()
                for copy in copies:
                    copy.wait()
                own_tables(*held, outs[-1])
                put_tables(outs[-1], outs[0])
            end()

        return call(
            body, [SM] + [HB] * (len(args) - 1), args, outs,
            scratch + [pltpu.SemaphoreType.DMA((count + 3,))], after=after,
        )

    def merge(self, pieces, arrays=(), parts=(), moved=(), tables=None, after=()):
        rows, count = pieces[0].shape[0], len(pieces)
        plan, packs = self.plan(parts)
        outs = [pinned((3, rows, C), BF16)] + packs + [pinned(v.shape, v.dtype) for v in moved]
        weights = len(arrays)
        small = [] if tables is None else [tables]
        outs += [pinned((GROUPS, v.shape[1]), F32) for v in small]
        given = count + weights + len(moved) + len(small)

        def body(where, *refs):
            spare, outs = refs[:given], refs[given:-2]
            ends = []
            if parts:
                ends.append(pack_start(plan, where, spare[count : count + weights], outs[1:], refs[-1]))
            copies = [
                pltpu.make_async_copy(a, b, refs[-2].at[3 + i])
                for i, (a, b) in enumerate(
                    zip(spare[count + weights : count + weights + len(moved)], outs[1 + len(packs) :])
                )
            ]
            for copy in copies:
                copy.start()
            merge_kernel(where, *refs[:count], outs[0], refs[-2])
            if small:
                take_tables(spare[-1], outs[0], outs[-1])
            for copy in copies:
                copy.wait()
            for end in ends:
                end()

        moves = sum(len(blocks) for _, _, _, blocks in plan)
        near, *others = call(
            body, [SM] + [ANY] * count + [HB] * weights + [ANY] * len(moved) + [VM] * len(small),
            [self.where, *pieces, *arrays, *moved, *small], outs,
            [pltpu.SemaphoreType.DMA((3 + len(moved),)), pltpu.SemaphoreType.DMA((max(moves, 1),))],
            after=after, limit=10,
        )
        return [[near, self.other(near)], *others]

    def step(self, *parts, passing=(), after=(), weight=0):
        kernels, args, specs, outs, cuts = [], [self.where], [SM], [], []
        for kernel, values, results in parts:
            kernels.append((kernel, len(args) - 1, len(values), len(outs), len(results)))
            args += values
            specs += [VC] * len(values)
            outs += results
        total_in, total_out = len(args) - 1, len(outs)
        aliases = {}
        for value in passing:
            aliases[len(args)] = len(outs)
            args.append(value)
            specs.append(ANY)
            outs.append(struct(value.shape, value.dtype))

        def body(where, *refs):
            refs_in, refs_out = refs[: total_in + len(passing)], refs[total_in + len(passing) :]
            for kernel, at, count, out, results in kernels:
                kernel(where, *refs_in[at : at + count], *refs_out[out : out + results])

        got = call(
            body, specs, args, outs, after=after, aliases=aliases, weight=weight,
            out_specs=[VM] * total_out + [ANY] * len(passing),
        )
        split = []
        for _, _, _, out, results in kernels:
            split.append(got[out : out + results])
        return split + list(got[total_out:])


    def swap_cores(self, keep, send):
        return keep, self.other(send)

    def first_way(self, *states):
        args = [v for state in states for v in state]
        two = pinned((2, sum(keep.shape[2] for keep, _ in states), C), BF16)
        return add_go_kernel, args, [two] * 4

    def send_first(self, done):
        go_a, go_b, stay_a, stay_b = done
        return stay_a, stay_b, self.x(go_a), self.y(go_b)

    def second_way(self, state):
        one = pinned(state[0].shape[1:], BF16)
        return add_next_kernel, list(state), [one] * 4

    def send_second(self, done):
        next_a, next_b, keep_a, keep_b = done
        return keep_a, keep_b, self.y(next_a), self.x(next_b)

    def join(self, state):
        one = pinned(state[0].shape, BF16)
        return add_level_kernel, list(state), [one] * 2

    def join_whole(self, state):
        rows = 2 * state[0].shape[0]
        return add_whole_kernel, list(state), [pinned((rows, C), BF16)]

    def line(self, v, pairs):
        return lax.ppermute(
            v, "dp", [(2 * a + core, 2 * b + core) for a, b in pairs for core in range(2)]
        )

    def choose(self, mine, got):
        return choose_kernel, [mine, got], [pinned(mine.shape, BF16)]

    def send_level(self, state, k):
        mine, send = state
        return mine, self.level(send, k)

    def add(self, state):
        return add_kernel, list(state), [pinned(state[0].shape, BF16)]

    def own_small(self, state):
        return own_kernel, list(state), [pinned((16 * LAYERS, C), F32)]

    def add_small(self, state):
        return add_kernel, list(state), [pinned(state[0].shape, F32)]

    def finish(self, plan, pieces, before=None, after=()):
        dims = (DIM_Q, DIM_P, DIM_1, DIM_2)
        made = len(pieces)
        args, specs = [self.where, *pieces], [SM] + [VC] * made
        aliases = {}
        if before is not None:
            aliases = {1 + made + i: i for i in range(4)}
            args += before[:4]
            specs += [HB] * 4
        scratch = [
            pltpu.VMEM(dims[FINISH[name][0]], F32) for _, _, names in plan for name in names
        ]
        return call(
            functools.partial(finish_kernel, plan, len(args) - 1, made), specs, args,
            [pltpu.HBM((LAYERS,) + dim, F32) for dim in dims] + [pinned((8, LANES), F32)],
            scratch + [pltpu.SemaphoreType.DMA((len(scratch),))],
            out_specs=[HB] * 4 + [VM], limit=6, after=after, aliases=aliases,
        )

    def unpack(self, little, after=()):
        one = struct((LAYERS, C), F32)
        outs = [one] * 7 + [struct((LAYERS, 2 * LANES), F32), struct((LAYERS, GHEADS, TABLE), F32)]
        return call(unpack_kernel, [SM, VC], [self.where, little], outs, after=after)


class Whole:
    def __init__(self):
        self.where = jnp.zeros((3,), jnp.int32)

    def gather(self, arrays, small):
        qkv, proj, w1, w2 = [
            lax.all_gather(v, "tensor", axis=axis, tiled=True) for v, axis in zip(arrays, (2, 1, 2, 1))
        ]
        qkv = qkv.reshape(LAYERS, C, GROUPS, TRI).transpose(0, 2, 1, 3)
        proj = proj.reshape(LAYERS, GROUPS, LANES, C)
        w1 = w1.reshape(LAYERS, C, GROUPS, HID).transpose(0, 2, 1, 3)
        w2 = w2.reshape(LAYERS, GROUPS, HID, C)
        own = [v[:, 0] for v in (qkv, proj, w1, w2)]

        def pack(parts, rows):
            out = jnp.zeros((rows, C), BF16)
            for v, blocks in parts:
                for row, lane, count, lanes, to_row, to_lane in blocks:
                    block = v[row : row + count, lane : lane + lanes]
                    out = out.at[to_row : to_row + count, to_lane : to_lane + lanes].set(block)
            return out

        weights = []
        for layer in range(LAYERS):
            p_q, p_m = [], []
            for side in range(2):
                side_q, side_m = [], []
                for r in range(1, GROUPS):

                    def half(v):
                        size = v.shape[2] // 2
                        return v[layer, r, side * size : (side + 1) * size]

                    side_q.append(pack([(half(qkv), PACK_Q)], Q_ROWS))
                    parts = [(half(w1), PACK_1), (half(proj), PACK_P), (half(w2), PACK_2)]
                    side_m.append(pack(parts, M_ROWS))
                p_q.append(jnp.stack(side_q))
                p_m.append(jnp.stack(side_m))
            weights.append(Weights(own, p_q, p_m))
        return weights, lax.all_gather(small, "tensor", axis=0)

    def sum_small(self, v):
        return lax.psum(v, ("dp", "tensor"))

    def finish(self, chunks):
        full = {}
        for name, chunk, blocks, dim in (
            ("q", 1, PACK_Q, DIM_Q), ("p", 0, PACK_P, DIM_P), ("1", 0, PACK_1, DIM_1), ("2", 0, PACK_2, DIM_2)
        ):
            layers = []
            for layer in range(LAYERS):
                sides = []
                for v in chunks[layer][chunk]:
                    shares = []
                    for r in range(GROUPS):
                        packed = jnp.concatenate(
                            [v[part, ORDERS[part].index(r)] for part in range(2)], 0
                        )
                        out = jnp.zeros((dim[0] // 2, dim[1]), BF16)
                        for row, lane, count, lanes, to_row, to_lane in blocks:
                            block = packed[to_row : to_row + count, to_lane : to_lane + lanes]
                            out = out.at[row : row + count, lane : lane + lanes].set(block)
                        shares.append(out)
                    sides.append(jnp.stack(shares))
                layers.append(jnp.concatenate(sides, 1))
            full[name] = jnp.stack(layers)
        outs = []
        for name, axis in zip("qp12", (2, 1, 2, 1)):
            v = full[name]
            if axis == 2:
                v = v.transpose(0, 2, 1, 3).reshape(LAYERS, C, -1)
            else:
                v = v.reshape(LAYERS, -1, C)
            v = lax.psum_scatter(v, "tensor", scatter_dimension=axis, tiled=True)
            outs.append(lax.psum(v, "dp").astype(F32))
        return outs


def shards(
    tensor, dp, images_in, ln1_gain, ln1_bias, qkv_weight, qv_bias, rel_table, proj_weight,
    proj_bias, ln2_gain, ln2_bias, fc1_weight, fc1_bias, fc2_weight, fc2_bias, rel_index,
    region_ids, out_cot,
):
    batch = images_in.shape[0]
    direct = tensor == 4 and dp == 8
    net = Direct(dp) if direct else Whole()
    where = net.where
    wide = 2 * LANES
    own = (qkv_weight, proj_weight, fc1_weight, fc2_weight)

    heads = rel_table.shape[2]
    if direct:
        q0, packed = net.pack(
            own, [[(0, 0)]], tables=[rel_table.transpose(0, 2, 1), qv_bias, fc1_bias]
        )
        near_q0 = net.near(q0)
        w_q0, m0, every = net.merge(near_q0, own, [[(0, 1), (1, 0), (1, 2)]], tables=packed)
        near_m0 = net.near(m0)
    else:
        table = jnp.pad(rel_table.transpose(2, 0, 1), ((0, 0), (0, 0), (0, wide - TABLE)))
        bias_part = full_bias(qv_bias, heads)
        packed = jnp.concatenate([table.reshape(-1), bias_part.reshape(-1), fc1_bias.reshape(-1)])
        packed = packed.reshape(1, -1)
        weights, every = net.gather(own, packed)
    every = every.reshape(tensor, -1)
    if tensor != GROUPS:
        cut1 = heads * LAYERS * wide
        cut2 = cut1 + bias_part.size
        tables = every[:, :cut1].reshape(GROUPS, -1)
        parts = [tables]
        for part in (every[:, cut1:cut2], every[:, cut2:]):
            part = part.reshape(tensor, LAYERS, -1).transpose(1, 0, 2)
            parts.append(part.reshape(LAYERS, GROUPS, -1).transpose(1, 0, 2).reshape(GROUPS, -1))
        every = jnp.concatenate(parts, 1)
    index = jnp.pad(rel_index + 1, ((0, PAIR - WTOK), (0, LANES - WTOK)))
    index = index + jnp.pad(rel_index + 1, ((WTOK, PAIR - 2 * WTOK), (WTOK, LANES - 2 * WTOK))) - 1
    ids = region_ids.astype(BF16)
    ids_col = jnp.broadcast_to(ids[:, None], (TOK, LANES))
    ids_row = jnp.broadcast_to(ids[None, :], (16, TOK))
    lanes_place = np.zeros((2 * LANES, TOK), np.float32)
    for pair in range(2):
        lanes_place[pair * LANES : pair * LANES + PAIR] = PLACE[0][pair * PAIR : (pair + 1) * PAIR]
    place = [jnp.asarray(PLACE[layer], BF16) for layer in range(LAYERS)]
    after = w_q0[:1] if direct else ()

    def bias_of(layer, after=()):
        return call(
            functools.partial(bias_kernel, layer),
            [VM] * 6,
            [every, index, ids_col, ids_row, place[0], jnp.asarray(lanes_place, BF16)],
            [pinned((1 + layer, HEADS, PAIR, LANES), F32)],
            flops=4 * GF,
            after=after,
        )[0]

    bias = [bias_of(0, after), None]
    step01 = jnp.asarray(PLACE[1] @ PLACE[0].T, BF16)
    step10 = jnp.asarray(PLACE[0] @ PLACE[1].T, BF16)
    group = jnp.asarray(GROUP, BF16)

    def row(v, layer):
        return v[layer][None]

    saved, w_q, w_m = [None] * LAYERS, [None] * LAYERS, [None] * LAYERS
    rels, littles, normed = [None] * LAYERS, [None] * LAYERS, [None] * LAYERS

    def attn(layer, state, w):
        res = attn_fwd(
            layer, batch, where, state, place[0], row(ln1_gain, layer), row(ln1_bias, layer),
            every, group, bias[layer], w,
        )
        *res, w_q[layer] = res
        x, res = (res[0], res[1:]) if layer == 0 else (state, res)
        normed[layer] = res[:2]
        saved[layer] = (x, *res[2:])

    def mlp(layer, w):
        x, n1, tri, e, rinv, ho = saved[layer]
        state, *rest, wp, w1, w2 = mlp_fwd(
            layer, batch, where, x, ho, row(proj_bias, layer), row(ln2_gain, layer),
            row(ln2_bias, layer), every, row(fc2_bias, layer), step01 if layer == 0 else place[1],
            w,
        )
        xhat, rstd, n2, act, dact = rest
        saved[layer] += ((xhat, rstd), n2, (act,), (dact,))
        w_m[layer] = (wp, (w1,), (w2,))
        return state

    def mlp_back(layer, grad, after=()):
        x, n1, tri, e, rinv, ho, mid, n2, act, dact = saved[layer]
        keep, send, gmid, dh, u, small2, db1 = mlp_bwd(
            layer, batch, where, grad, place[1], act, dact, mid, n2, ho, rinv,
            row(ln2_gain, layer), w_m[layer], after,
        )
        littles[layer] = {"a": small2, "b": db1}
        return (keep, send), gmid, dh, u

    def pair_back(grad, dtri, after=()):
        act, dact = saved[0][8:]
        keep, send, gp, littles[1]["c"] = pair_bwd(
            0, batch, where, grad, act, dact, w_m[0], saved[1][1], dtri, after
        )
        return (keep, send), gp

    def middle_back_0(gp, grad, after):
        x, n1, tri, e, rinv, ho, mid, n2, act, dact = saved[0]
        keep, send, gmid, dh, u, small2, db1 = middle_bwd(
            0, batch, where, gp, grad, mid, n2, ho, rinv, row(ln2_gain, 0), w_m[0], after
        )
        littles[0] = {"a": small2, "b": db1}
        return (keep, send), gmid, dh, u

    def attn_back(layer, dh, u, after=()):
        dtri, rels[layer] = attn_bwd(
            batch, where, dh, u, saved[layer][2], saved[layer][3], group, after
        )
        return dtri

    def qkv_back(layer, dtri, after=()):
        keep, send, small_q = qkv_grad(batch, where, saved[layer][1], dtri, after)
        littles[layer]["c"] = small_q
        return keep, send

    def input_back(layer, gmid, dtri, after=()):
        grad, small1 = input_bwd(
            layer, batch, where, gmid, normed[layer], dtri, row(ln1_gain, layer),
            step10 if layer else place[0], w_q[layer], after,
        )
        littles[layer]["d"] = small1
        return grad

    def small_sums(after=()):
        args = [index.reshape(PAIR, 1, LANES), jnp.asarray(PICK, BF16)]
        for layer in range(LAYERS):
            args += [littles[layer][name] for name in "abcd"] + [rels[layer]]
        specs = [VM] * 2 + ([VM] * 4 + [VC]) * LAYERS
        return call(
            small_kernel, specs, args, [pinned((24 * LAYERS, C), F32)],
            [
                pltpu.VMEM((wide, 2 * LAYERS * HEADS), F32),
                pltpu.VMEM((LAYERS * HEADS * 56, LANES), F32),
            ],
            after=after, limit=4,
        )[0]

    if direct:
        w0 = Weights(own, w_q0, None)
        attn(0, images_in, w0)
        bias[1] = bias_of(1, saved[0][5:6])
        (m1,) = net.pack(own, [[(1, 3)]], after=(bias[1],))
        w0.p_m, m1_now = net.merge(near_m0, moved=(m1,))
        m1_x, m1_y = net.x(m1_now), net.y(m1_now)
        state = mlp(0, w0)
        (m1,) = net.step(passing=(m1,), after=(state,))
        m1_d = net.diagonal(m1)
        w1 = Weights(own, w0.p_m, None, M_ROWS)
        attn(1, state, w1)
        x, n1, tri, e, rinv, ho = saved[1]
        m1_x, m1_y = net.step(passing=(m1_x, m1_y), after=(ho,))
        far_x, far_y = net.other(m1_x), net.other(m1_y)
        mid, xhat, rstd, n2, acc, *first = mlp_open(
            1, batch, where, x, ho, row(proj_bias, 1), row(ln2_gain, 1), row(ln2_bias, 1), every,
            w1, M_ROWS + Q_ROWS, w0.p_m,
        )
        (m1_d,) = net.step(passing=(m1_d,), after=(acc,))
        far_d = net.other(m1_d)
        acc, *second = mlp_more(
            1, batch, where, every, n2, acc, (1, 2), (m1_x, far_x, m1_y, far_y), after=(m1_d,)
        )
        output, *third = mlp_more(
            1, batch, where, every, n2, acc, (3,), (m1_d, far_d),
            end=(mid, row(fc2_bias, 1), place[1]),
        )
        act, dact, wp, *w_first = first
        saved[1] += ((xhat, rstd), n2, (act, second[0], third[0]), (dact, second[1], third[1]))
        w_m[1] = (
            wp, (w_first[0], second[2], third[2]), (w_first[1], second[3], third[3])
        )

        m1, gmid, dh, u = mlp_back(1, out_cot, after=(output,))
        m1 = net.swap_cores(*m1)
        dtri = attn_back(1, dh, u)
        (g1,) = net.step(net.first_way(m1), after=(dtri,))
        g1 = net.send_first(g1)
        grad = input_back(1, gmid, dtri, after=g1[:1])
        two, gp = pair_back(grad, dtri)
        two = net.swap_cores(*two)
        one, gmid, dh, u = middle_back_0(gp, grad, after=two[:1])
        g1, send = net.step(net.second_way(g1), passing=one[1:], after=(gmid,), weight=40)
        (g2,) = net.step(net.first_way(two), after=g1[:1])
        dtri = attn_back(0, dh, u, after=g2[:1])
        g1, g2 = net.send_second(g1), net.send_first(g2)
        one = net.swap_cores(one[0], send)
        q0 = qkv_back(0, dtri)
        g1, send = net.step(net.join(g1), passing=q0[1:], after=q0[:1])
        g1 = net.send_level(g1, 1)
        q0 = net.swap_cores(q0[0], send)
        (g3,) = net.step(net.first_way(one, q0), after=(g1[0],))
        grad = input_back(0, gmid, dtri, after=g3[:1])
        g3 = net.send_first(g3)
        ((g1,),) = net.step(net.add(g1), after=(grad,))
        g1 = net.send_level((g1, g1), 2)
        little = small_sums(after=(g1[0],))
        g2, little = net.step(net.second_way(g2), passing=(little,))
        order = g2[2:3]
        g2 = net.send_second(g2)
        (g3,) = net.step(net.second_way(g3), after=order)
        order = g3[2:3]
        g3 = net.send_second(g3)
        g2, (g1,), little = net.step(
            net.join(g2), net.add(g1), passing=(little,), after=order
        )
        order = g2[:1]
        g2 = net.send_level(g2, 1)
        near1 = net.level(g1, 1)
        little = (little, net.other(little))
        g3, (little,) = net.step(net.join(g3), net.add_small(little), after=order)
        order = g3[:1]
        g3 = net.send_level(g3, 1)
        little = (little, net.x(little))
        (g2,), (little,), side1, near1 = net.step(
            net.add(g2), net.add_small(little), passing=(g1, near1), after=order
        )
        order = (g2,)
        g2 = net.send_level((g2, g2), 2)
        little = (little, net.y(little))
        g1 = [side1, near1, net.other(side1), net.other(near1)]
        (g3,), (little,) = net.step(net.add(g3), net.own_small(little), after=order)
        order = (g3,)
        g3 = net.send_level((g3, g3), 2)
        little = (little, net.level(little, 1))
        (g2,), (little,) = net.step(net.add(g2), net.add_small(little), after=order)
        near2, side2 = net.level(g2, 1), net.other(g2)
        little = (little, net.level(little, 2))
        results = net.finish([(M_ROWS, 1, ("1", "p", "2"))], g1, after=(g2,))
        (g3,), (little,), near2 = net.step(
            net.add(g3), net.add_small(little), passing=(near2,), after=results[4:]
        )
        near3, side3 = net.level(g3, 1), net.other(g3)
        g2 = [g2, near2, side2, net.other(near2)]
        small = list(net.unpack(little))
        results = net.finish(
            [(Q_ROWS, 1, ("q",)), (TWO_ROWS, 0, ("two",))], g2, results, after=small[7:8]
        )
        (near3,) = net.step(passing=(near3,), after=results[4:])
        dwq, dwp, dw1, dw2, _ = net.finish(
            [(ONE_ROWS, 0, ("1", "p")), (Q_ROWS, 0, ("q",))],
            [g3, near3, side3, net.other(near3)], results,
        )
        small[8] = small[8].transpose(0, 2, 1)
        return (
            output, grad.transpose(1, 0, 2), small[0], small[1], dwq, small[7], small[8], dwp, small[2], small[3],
            small[4], dw1, small[6], dw2, small[5],
        )
    else:
        state = images_in
        bias[1] = bias_of(1)
        for layer in range(LAYERS):
            attn(layer, state, weights[layer])
            state = mlp(layer, weights[layer])
        output = state
        grad = out_cot
        reduced = [None] * LAYERS
        for layer in reversed(range(LAYERS)):
            m, gmid, dh, u = mlp_back(layer, grad)
            dtri = attn_back(layer, dh, u)
            reduced[layer] = (m, qkv_back(layer, dtri))
            grad = input_back(layer, gmid, dtri)
        little = net.sum_small(small_sums())
        dwq, dwp, dw1, dw2 = net.finish(reduced)
    little = little.reshape(LAYERS, 24, C)
    small_q = little[:, 8:12, : 2 * LANES].reshape(LAYERS, -1)
    rel = little[:, 16:].reshape(LAYERS, 8, 2, wide)[..., :TABLE].transpose(0, 3, 2, 1)
    rel = rel.reshape(LAYERS, TABLE, HEADS)
    db1 = little[:, 4:8].reshape(LAYERS, FF)
    mine = lax.axis_index("tensor")

    def share(v, axis):
        size = v.shape[axis] // tensor
        return lax.dynamic_slice_in_dim(v, mine * size, size, axis)

    return (
        output, grad.transpose(1, 0, 2), little[:, 12], little[:, 13], dwq, share(small_q, 1), share(rel, 2), dwp,
        little[:, 3], little[:, 1], little[:, 2], dw1, share(db1, 1), dw2, little[:, 0],
    )


def solution(mesh):
    tokens = P(("dp", "tensor"), None, None)
    cols, rows = P(None, None, "tensor"), P(None, "tensor", None)
    part = P(None, "tensor")
    return jax.shard_map(
        functools.partial(shards, mesh.shape["tensor"], mesh.shape["dp"]),
        mesh=mesh,
        in_specs=(
            tokens, P(), P(), cols, part, cols, rows, P(), P(), P(), cols, part, rows, P(), P(),
            P(), tokens,
        ),
        out_specs=(
            tokens, tokens, P(), P(), cols, part, cols, rows, P(), P(), P(), cols, part, rows, P(),
        ),
        check_vma=False,
    )
```

```python
import functools

import jax
import jax.numpy as jnp
import numpy as np
from jax import lax
from jax.experimental import pallas as pl
from jax.experimental.pallas import tpu as pltpu
from jax.sharding import PartitionSpec as P

C = 512
HEADS = 16
HEAD_DIM = 32
FF = 2048
WIN = 7
GRID = 14
SHIFT = 3
LAYERS = 2
TOK = 196
WTOK = 49
TABLE = 169
PAIR = 112
LANES = 128
GROUPS = 4
GHEADS = HEADS // GROUPS
TRI = 3 * LANES
HID = FF // GROUPS
SCALE = HEAD_DIM ** (-0.5)
NEG = -1e30
F32 = jnp.float32
BF16 = jnp.bfloat16


def window_tokens(offset):
    cells = np.arange(TOK).reshape(GRID, GRID)
    cells = np.roll(cells, (-offset, -offset), (0, 1))
    cells = cells.reshape(2, WIN, 2, WIN).transpose(0, 2, 1, 3)
    return cells.reshape(4, WTOK)


def place_matrix(offset):
    tokens = window_tokens(offset).reshape(2, 2 * WTOK)
    out = np.zeros((2 * PAIR, TOK), np.float32)
    for pair in range(2):
        out[pair * PAIR + np.arange(2 * WTOK), tokens[pair]] = 1.0
    return out


PLACE = [place_matrix(SHIFT if layer % 2 == 1 else 0) for layer in range(LAYERS)]


def group_matrix():
    out = np.zeros((TRI, TRI), np.float32)
    for head in range(GHEADS):
        for part in range(3):
            for pos in range(HEAD_DIM):
                out[
                    (head * 3 + part) * HEAD_DIM + pos, (part * GHEADS + head) * HEAD_DIM + pos
                ] = 1.0
    return out


GROUP = group_matrix()


def pick_matrix():
    out = np.zeros((TRI, 2 * LANES), np.float32)
    for head in range(GHEADS):
        for to, part in enumerate((0, 2)):
            for pos in range(HEAD_DIM):
                out[(head * 3 + part) * HEAD_DIM + pos, (head * 2 + to) * HEAD_DIM + pos] = 1.0
    return out


PICK = pick_matrix()


def mm(a, b):
    return jnp.dot(a, b, preferred_element_type=F32)


def mm_nt(a, b):
    return lax.dot_general(a, b, (((1,), (1,)), ((), ())), preferred_element_type=F32)


def mm_tn(a, b):
    return lax.dot_general(a, b, (((0,), (0,)), ((), ())), preferred_element_type=F32)


def normalize(x):
    centre = x - jnp.mean(x, -1, keepdims=True)
    spread = jnp.mean(centre * centre, -1, keepdims=True)
    rstd = lax.rsqrt(spread + 1e-05)
    return centre * rstd, rstd


def norm_back(xhat, rstd, gain, grad):
    rstd = rstd[:, :1]
    scaled = grad * gain
    m1 = jnp.mean(scaled, -1, keepdims=True)
    m2 = jnp.mean(scaled * xhat, -1, keepdims=True)
    dx = rstd * (scaled - m1 - xhat * m2)
    return dx, jnp.sum(grad * xhat, 0, keepdims=True), jnp.sum(grad, 0, keepdims=True)


def rows_of(pair):
    return pl.ds(pl.multiple_of(pair * PAIR, 16), PAIR)


def head_mask(head):
    lane = lax.broadcasted_iota(jnp.int32, (PAIR, LANES), 1)
    return (lane // HEAD_DIM) == head


def stack_heads(block, masks):
    zero = jnp.zeros_like(block)
    pad = jnp.zeros((LANES - PAIR, LANES), block.dtype)
    parts = []
    for mask in masks:
        parts += [jnp.where(mask, block, zero), pad]
    return jnp.concatenate(parts, 0)


def split_exact(x):
    high = x.astype(BF16)
    return high, (x - high.astype(F32)).astype(BF16)


def half_rows(core, half):
    mine = pl.ds(pl.multiple_of(core * half, 16), half)
    other = pl.ds(pl.multiple_of((1 - core) * half, 16), half)
    return mine, other


Q_ROWS, M_ROWS = 192, 576
FIRST_ROWS = 224
PACK_Q = [(0, 0, Q_ROWS, TRI, 0, 0)] + [
    (Q_ROWS, j * LANES, 64, LANES, 64 * j, TRI) for j in range(3)
]
PACK_1 = [(0, 0, 256, C, 0, 0)]
PACK_P = [(0, 0, 64, C, 256, 0)]
PACK_2 = [(0, 0, 256, C, 320, 0)]
CHUNKS = (
    (((0, PACK_Q),), Q_ROWS),
    (((2, PACK_1), (1, PACK_P), (3, PACK_2)), M_ROWS),
    (((1, [(0, 0, 64, C, 0, 0)]),), 64),
    (((2, PACK_1), (3, [(0, 0, 256, C, 256, 0)])), 512),
)
ONE_ROWS, TWO_ROWS = 320, 256
PACK_TWO = [(0, 0, 256, C, 0, 0)]


def moved_down(blocks, base):
    return [block[:4] + (block[4] + base, block[5]) for block in blocks]


class Fetch:
    def __init__(self, full, layer, pieces, blocks, dest, core, sems):
        half = dest.shape[1] // 2
        self.copies = [[pltpu.make_async_copy(full.at[layer], dest.at[0], sems.at[0])]]
        at = 1
        for r in range(1, GROUPS):
            group = []
            if len(pieces) == 2:
                near, far = pieces[0].at[r - 1], pieces[1].at[r - 1]
            else:
                near, far = pieces[r - 1], pieces[r + 2]
            for side, piece in ((core, near), (1 - core, far)):
                for row, lane, rows, lanes, to_row, to_lane in blocks:
                    target = dest.at[
                        r,
                        pl.ds(pl.multiple_of(side * half + row, 16), rows),
                        pl.ds(lane, lanes),
                    ]
                    source = piece.at[pl.ds(to_row, rows), pl.ds(to_lane, lanes)]
                    group.append(pltpu.make_async_copy(source, target, sems.at[at]))
                    at += 1
            self.copies.append(group)
        for group in self.copies:
            for copy in group:
                copy.start()

    def wait(self, r):
        for copy in self.copies[r]:
            copy.wait()


def bias_kernel(layer, table, index, ids_col, ids_row, place, lanes_place, bias_ref):
    cols = mm(place[...], ids_col[...])
    rows = mm_nt(ids_row[...], lanes_place[...])
    masks = []
    for pair in range(2):
        col = cols[pair * PAIR : (pair + 1) * PAIR]
        row = rows[:1, pair * LANES : (pair + 1) * LANES]
        masks.append(jnp.where(col != row, -100.0, 0.0))
    idx = index[...]
    step = LAYERS * 2 * LANES
    at_low = jnp.clip(idx, 0, LANES - 1)
    at_high = jnp.clip(idx - LANES, 0, LANES - 1)

    def pick(low, high):
        low = jnp.take_along_axis(jnp.broadcast_to(low, (PAIR, LANES)), at_low, axis=1)
        high = jnp.take_along_axis(jnp.broadcast_to(high, (PAIR, LANES)), at_high, axis=1)
        return jnp.where(idx < 0, NEG, jnp.where(idx < LANES, low, high))

    for head in range(HEADS):
        r, lane = head // GHEADS, (head % GHEADS) * step + layer * 2 * LANES
        picked = pick(
            table[r : r + 1, lane : lane + LANES], table[r : r + 1, lane + LANES : lane + 2 * LANES]
        )
        if layer == 0:
            bias_ref[0, head] = picked
        else:
            bias_ref[0, head] = picked + masks[0]
            bias_ref[1, head] = picked + masks[1]


def attn_fwd_kernel(layer, pairs, base, *refs):
    first = layer == 0
    where, x_in, place, ln_g, ln_b, tables, group, bias, full_qkv = refs[:9]
    at = BIAS_AT + layer * TRI
    p_qkv, outs = refs[9:11], refs[11:]
    if first:
        x_ref, outs = outs[0], outs[1:]
    else:
        x_ref = x_in
    xhat_ref, rstd_ref, n1_ref, tri_ref, e_ref, rinv_ref, ho_ref, w_qkv, sem_q = outs
    qkv = Fetch(full_qkv, layer, p_qkv, moved_down(PACK_Q, base), w_qkv, where[1], sem_q)
    if first:
        for image in range(pairs // 2):
            x_ref[pl.ds(image * 2 * PAIR, 2 * PAIR), :] = mm(place[...], x_in[image])

    def norm_rows(pair, carry):
        rows = rows_of(pair)
        xhat, rstd = normalize(x_ref[rows, :])
        xhat_ref[rows, :] = xhat
        rstd_ref[rows, :] = jnp.broadcast_to(rstd, (PAIR, LANES))
        n1_ref[rows, :] = (xhat * ln_g[...] + ln_b[...]).astype(BF16)
        return carry

    lax.fori_loop(0, pairs, norm_rows, 0)
    masks = [head_mask(h) for h in range(GHEADS)]
    ones = jnp.ones((PAIR, LANES), BF16)
    for r in range(GROUPS):
        qkv.wait(r)
        tri = (mm(n1_ref[...], w_qkv[r]) + tables[r : r + 1, at : at + TRI]).astype(BF16)
        tri_ref[r] = mm(tri, group[...]).astype(BF16)
        ones_stack = stack_heads(ones, masks)

        def pair_step(pair, carry):
            rows = rows_of(pair)
            q4 = tri_ref[r, rows, 0:LANES]
            k4 = tri_ref[r, rows, LANES : 2 * LANES]
            v4 = tri_ref[r, rows, 2 * LANES : 3 * LANES]
            s4 = mm_nt(q4, stack_heads(k4, masks))
            kind = 0 if first else lax.rem(pair, 2)
            es = []
            for h in range(GHEADS):
                s = s4[:, h * LANES : (h + 1) * LANES] * SCALE + bias[kind, r * GHEADS + h]
                es.append(jnp.exp(s - jnp.max(s, -1, keepdims=True)).astype(BF16))
            e4 = jnp.concatenate(es, 1)
            e_ref[r, pair] = e4
            vm = jnp.concatenate([stack_heads(v4, masks), ones_stack], 1)
            out = mm(e4, vm)
            rinv = 1.0 / out[:, LANES:]
            rinv_ref[r, rows, :] = rinv
            ho_ref[rows, r * LANES : (r + 1) * LANES] = (out[:, :LANES] * rinv).astype(BF16)
            return carry

        lax.fori_loop(0, pairs, pair_step, 0, unroll=True)


def mlp_fwd_kernel(layer, pairs, count, *refs):
    last = layer == LAYERS - 1
    where, x, ho, b_proj, ln_g, ln_b, tables, b2, place = refs[:9]
    at = HIDDEN_AT + layer * HID
    full_p, full_1, full_2 = refs[9:12]
    p_m, refs = refs[12 : 12 + count], refs[12 + count :]
    out_ref, xhat_ref, rstd_ref, n2_ref, act_ref, dact_ref, wp, w1, w2 = refs[:9]
    sem_p, sem_1, sem_2, acc, pre_ref, mid = refs[9:]
    core = where[1]
    f_p = Fetch(full_p, layer, p_m, PACK_P, wp, core, sem_p)
    f_1 = Fetch(full_1, layer, p_m, PACK_1, w1, core, sem_1)
    f_2 = Fetch(full_2, layer, p_m, PACK_2, w2, core, sem_2)
    for r in range(GROUPS):
        f_p.wait(r)
    weight = jnp.concatenate([wp[r] for r in range(GROUPS)], 0)
    mid[...] = x[...] + mm(ho[...], weight) + b_proj[...]

    def norm_rows(pair, carry):
        rows = rows_of(pair)
        xhat, rstd = normalize(mid[rows, :])
        xhat_ref[rows, :] = xhat
        rstd_ref[rows, :] = jnp.broadcast_to(rstd, (PAIR, LANES))
        n2_ref[rows, :] = (xhat * ln_g[...] + ln_b[...]).astype(BF16)
        return carry

    lax.fori_loop(0, pairs, norm_rows, 0)
    for r in range(GROUPS):
        f_1.wait(r)
        pre_ref[...] = mm(n2_ref[...], w1[r])
        b1_row = tables[r : r + 1, at : at + HID]

        def gelu_rows(step, carry):
            rows = pl.ds(pl.multiple_of(step * 16, 16), 16)
            pre = pre_ref[rows, :] + b1_row
            cdf = 0.5 + 0.5 * lax.erf(pre * (0.5**0.5))
            act_ref[r, rows, :] = (pre * cdf).astype(BF16)
            pdf = jnp.exp(-0.5 * pre * pre) * 0.3989422804014327
            dact_ref[r, rows, :] = (cdf + pre * pdf).astype(BF16)
            return carry

        lax.fori_loop(0, pairs * (PAIR // 16), gelu_rows, 0, unroll=2)
        f_2.wait(r)
        part = mm(act_ref[r], w2[r])
        if r == 0:
            acc[...] = part
        else:
            acc[...] += part
    acc[...] = acc[...] + mid[...] + b2[...]
    for image in range(pairs // 2):
        state = acc[pl.ds(image * 2 * PAIR, 2 * PAIR), :]
        if last:
            out_ref[image] = mm_tn(place[...], state.astype(BF16)).astype(BF16)
        else:
            high, low = split_exact(state)
            out_ref[pl.ds(image * 2 * PAIR, 2 * PAIR), :] = mm(place[...], high) + mm(
                place[...], low
            )


X_FIRST = (0, 2, 1, 3)
Y_FIRST = (0, 1, 2, 3)
ORDERS = (X_FIRST, Y_FIRST)


def give(keep_ref, send_ref, tmp, r, core, blocks, first=0, size=None):
    half = tmp.shape[0] // 2
    size = size or keep_ref.shape[2]
    for ref, base in ((keep_ref, core * half), (send_ref, (1 - core) * half)):
        for row, lane, rows, lanes, to_row, to_lane in blocks:
            done = 0
            while done < rows:
                part, at = divmod(to_row + done, size)
                count = min(rows - done, size - at)
                to = slice(first + at, first + at + count)
                ref[part, ORDERS[part].index(r), to, to_lane : to_lane + lanes] = tmp[
                    pl.ds(pl.multiple_of(base + row + done, 16), count), lane : lane + lanes
                ]
                done += count


class Joined:
    def __init__(self, refs):
        self.refs = refs

    def __getitem__(self, r):
        for ref in self.refs:
            if r < ref.shape[0]:
                return ref[r]
            r -= ref.shape[0]


def gelu_into(pairs, pre_ref, b1_row, act_ref, dact_ref, at):
    def some_rows(step, carry):
        rows = pl.ds(pl.multiple_of(step * 16, 16), 16)
        pre = pre_ref[rows, :] + b1_row
        cdf = 0.5 + 0.5 * lax.erf(pre * (0.5**0.5))
        act_ref[at, rows, :] = (pre * cdf).astype(BF16)
        pdf = jnp.exp(-0.5 * pre * pre) * 0.3989422804014327
        dact_ref[at, rows, :] = (cdf + pre * pdf).astype(BF16)
        return carry

    lax.fori_loop(0, pairs * (PAIR // 16), some_rows, 0, unroll=2)


def mlp_open_kernel(layer, pairs, base, *refs):
    where, x, ho, b_proj, ln_g, ln_b, tables, full_p, full_1, full_2 = refs[:10]
    pieces, refs = refs[10:12], refs[12:]
    mid, xhat_ref, rstd_ref, n2_ref, acc, act_ref, dact_ref, wp, w1, w2, sem_p, sem_w, pre_ref = refs
    f_p = Fetch(full_p, layer, pieces, moved_down(PACK_P, base - 256), wp, where[1], sem_p)
    copies = [
        pltpu.make_async_copy(full.at[layer], w.at[0], sem_w.at[i])
        for i, (full, w) in enumerate(((full_1, w1), (full_2, w2)))
    ]
    for copy in copies:
        copy.start()
    for r in range(GROUPS):
        f_p.wait(r)
    weight = jnp.concatenate([wp[r] for r in range(GROUPS)], 0)
    mid[...] = x[...] + mm(ho[...], weight) + b_proj[...]

    def norm_rows(pair, carry):
        rows = rows_of(pair)
        xhat, rstd = normalize(mid[rows, :])
        xhat_ref[rows, :] = xhat
        rstd_ref[rows, :] = jnp.broadcast_to(rstd, (PAIR, LANES))
        n2_ref[rows, :] = (xhat * ln_g[...] + ln_b[...]).astype(BF16)
        return carry

    lax.fori_loop(0, pairs, norm_rows, 0)
    for copy in copies:
        copy.wait()
    at = HIDDEN_AT + layer * HID
    pre_ref[...] = mm(n2_ref[...], w1[0])
    gelu_into(pairs, pre_ref, tables[0:1, at : at + HID], act_ref, dact_ref, 0)
    acc[...] = mm(act_ref[0], w2[0])


def mlp_more_kernel(layer, pairs, shares, last, *refs):
    where, tables, n2, acc_in = refs[:4]
    count = 2 * len(shares)
    pieces, refs = refs[4 : 4 + count], refs[4 + count :]
    if last:
        mid, b2, place, out_ref, act_ref, dact_ref, w1, w2, sems, pre_ref, acc = refs
    else:
        acc, act_ref, dact_ref, w1, w2, sems, pre_ref = refs
    copies = []
    for i in range(len(shares)):
        group = []
        for side, c in enumerate((where[1], 1 - where[1])):
            for k, w in enumerate((w1, w2)):
                half = w.shape[1] // 2
                target = w.at[i, pl.ds(pl.multiple_of(c * half, 16), half)]
                source = pieces[2 * i + side].at[pl.ds(k * half, half)]
                group.append(pltpu.make_async_copy(source, target, sems.at[4 * i + 2 * side + k]))
        for copy in group:
            copy.start()
        copies.append(group)
    at = HIDDEN_AT + layer * HID
    for i, r in enumerate(shares):
        for copy in copies[i]:
            copy.wait()
        pre_ref[...] = mm(n2[...], w1[i])
        gelu_into(pairs, pre_ref, tables[r : r + 1, at : at + HID], act_ref, dact_ref, i)
        part = mm(act_ref[i], w2[i])
        if i == 0:
            acc[...] = acc_in[...] + part
        else:
            acc[...] += part
    if last:
        for image in range(pairs // 2):
            rows = pl.ds(image * 2 * PAIR, 2 * PAIR)
            state = acc[rows, :] + mid[rows, :] + b2[...]
            out_ref[image] = mm_tn(place[...], state.astype(BF16)).astype(BF16)


def hidden_back(layer, pairs, where, g_in, place, act, dact, w2, g_ref, gb_ref, gp_ref, tmp, outs, blocks, first=0, size=None):
    keep, send = outs
    core = where[1]
    if layer == LAYERS - 1:
        for image in range(pairs // 2):
            rows = pl.ds(image * 2 * PAIR, 2 * PAIR)
            g = mm(place[...], g_in[image])
            g_ref[rows, :] = g
            gb_ref[rows, :] = g.astype(BF16)
    else:
        gb_ref[...] = g_ref[...].astype(BF16)
    for r in range(GROUPS):
        tmp[...] = mm_tn(act[r], gb_ref[...]).astype(BF16)
        give(keep, send, tmp, r, core, blocks, first, size)
        ga = mm_nt(gb_ref[...], w2[r])
        gp_ref[r] = (ga * dact[r].astype(F32)).astype(BF16)


def middle_back(layer, pairs, where, gp_ref, g_ref, mid, n2, ho, rinv, ln_g, w1, wp, gb_ref, acc, tmp, tmp_p, outs):
    keep, send, gmid_ref, dh_ref, u_ref, small_ref, db1_ref = outs
    tid, core = where[0], where[1]
    small_ref[...] = jnp.zeros_like(small_ref)
    for r in range(GROUPS):
        db1_ref[tid ^ r] = jnp.sum(gp_ref[r].astype(F32), 0, keepdims=True)
        tmp[...] = mm_tn(n2[...], gp_ref[r]).astype(BF16)
        give(keep, send, tmp, r, core, PACK_1)
        part = mm_nt(gp_ref[r], w1[r])
        if r == 0:
            acc[...] = part
        else:
            acc[...] += part

    def back_rows(pair, carry):
        rows = rows_of(pair)
        g_rows = g_ref[rows, :]
        dx, dg, db = norm_back(mid[0][rows, :], mid[1][rows, :], ln_g[...], acc[rows, :])
        gmid = g_rows + dx
        gmid_ref[rows, :] = gmid
        gb_ref[rows, :] = gmid.astype(BF16)
        small_ref[0:1, :] += jnp.sum(g_rows, 0, keepdims=True)
        small_ref[1:2, :] += dg
        small_ref[2:3, :] += db
        small_ref[3:4, :] += jnp.sum(gmid, 0, keepdims=True)
        return carry

    lax.fori_loop(0, pairs, back_rows, 0)
    for r in range(GROUPS):
        lanes = slice(r * LANES, (r + 1) * LANES)
        tmp_p[...] = mm_tn(ho[:, lanes], gb_ref[...]).astype(BF16)
        give(keep, send, tmp_p, r, core, PACK_P)
        gh = mm_nt(gb_ref[...], wp[r]) * rinv[r]
        dh_ref[r] = gh.astype(BF16)
        u_ref[r] = (gh * ho[:, lanes].astype(F32)).astype(BF16)


def mlp_bwd_kernel(layer, pairs, count, *refs):
    where, g_in, place = refs[:3]
    act, dact = Joined(refs[3 : 3 + count]), Joined(refs[3 + count : 3 + 2 * count])
    xhat, rstd, n2, ho, rinv, ln_g, wp = refs[3 + 2 * count : 10 + 2 * count]
    mid = (xhat, rstd)
    refs = refs[10 + 2 * count :]
    w1, w2 = Joined(refs[:count]), Joined(refs[count : 2 * count])
    outs = refs[2 * count : 2 * count + 7]
    g_ref, gb_ref, gp_ref, acc, tmp, tmp_p = refs[2 * count + 7 :]
    if layer < LAYERS - 1:
        g_ref = g_in
    hidden_back(
        layer, pairs, where, g_in, place, act, dact, w2, g_ref, gb_ref, gp_ref, tmp, outs[:2], PACK_2
    )
    middle_back(
        layer, pairs, where, gp_ref, g_ref, mid, n2, ho, rinv, ln_g, w1, wp, gb_ref, acc, tmp, tmp_p,
        outs,
    )


def pair_bwd_kernel(layer, pairs, where, g, act, dact, w2, n1, dtri, keep, send, gp_ref, small_ref, gb_ref, tmp, tmp_q):
    hidden_back(
        layer, pairs, where, g, None, act, dact, w2, g, gb_ref, gp_ref, tmp, (keep, send), PACK_TWO,
        Q_ROWS // 2, TWO_ROWS // 2,
    )
    qkv_grad_kernel(pairs, where, n1, dtri, keep, send, small_ref, tmp_q, Q_ROWS // 2)


def middle_bwd_kernel(layer, pairs, *refs):
    where, gp, g, xhat, rstd, n2, ho, rinv, ln_g, wp, w1 = refs[:11]
    mid = (xhat, rstd)
    gb_ref, acc, tmp, tmp_p = refs[18:]
    middle_back(
        layer, pairs, where, gp, g, mid, n2, ho, rinv, ln_g, w1, wp, gb_ref, acc, tmp, tmp_p,
        refs[11:18],
    )


def attn_bwd_kernel(pairs, where, dh, u, tri, e, group, dtri_ref, rel_ref, low_ref):
    tid = where[0]
    masks = [head_mask(h) for h in range(GHEADS)]
    neg_ones = jnp.full((PAIR, LANES), -1.0, BF16)
    for r in range(GROUPS):
        sid = tid ^ r
        neg_stack = stack_heads(neg_ones, masks)

        def pair_step(pair, carry):
            rows = rows_of(pair)
            q4 = tri[r, rows, 0:LANES]
            k4 = tri[r, rows, LANES : 2 * LANES]
            v4 = tri[r, rows, 2 * LANES : 3 * LANES]
            dh4 = dh[r, rows, :]
            left = jnp.concatenate([dh4, u[r, rows, :]], 1)
            right = jnp.concatenate([stack_heads(v4, masks), neg_stack], 1)
            dsp = mm_nt(left, right)
            e4 = e[r, pair]
            ds4 = e4.astype(F32) * dsp
            for h in range(GHEADS):
                part = ds4[:, h * LANES : (h + 1) * LANES]
                head = sid * GHEADS + h
                rel_ref[head] = jnp.where(pair == 0, part, rel_ref[head] + part)
            dsb = (ds4 * SCALE).astype(BF16)
            dq4 = mm(dsb, stack_heads(k4, masks))
            pad = jnp.zeros((LANES - PAIR, GHEADS * LANES), BF16)
            dsb_p = jnp.concatenate([dsb, pad], 0)
            e4_p = jnp.concatenate([e4, pad], 0)

            def flip(block):
                return jnp.concatenate(
                    [block[:, h * LANES : (h + 1) * LANES].T for h in range(GHEADS)], 1
                )[:PAIR]

            dk4 = mm(flip(dsb_p), stack_heads(q4, masks))
            dv4 = mm(flip(e4_p), stack_heads(dh4, masks))
            low_ref[rows, :] = jnp.concatenate([dq4, dk4, dv4], 1).astype(BF16)
            return carry

        lax.fori_loop(0, pairs, pair_step, 0, unroll=True)
        dtri_ref[r] = mm_nt(low_ref[...], group[...]).astype(BF16)


def qkv_grad_kernel(pairs, where, n1, dtri, keep, send, small_ref, tmp, size=None):
    tid, core = where[0], where[1]
    for r in range(GROUPS):
        tmp[...] = mm_tn(n1[...], dtri[r]).astype(BF16)
        give(keep, send, tmp, r, core, PACK_Q, 0, size)
        small_ref[tid ^ r] = jnp.sum(dtri[r].astype(F32), 0, keepdims=True)


def input_bwd_kernel(layer, pairs, where, gmid, xhat, xscale, dtri, ln_g, place, w_qkv, gout_ref, small_ref, acc):
    last = layer == 0
    for r in range(GROUPS):
        part = mm_nt(dtri[r], w_qkv[r])
        if r == 0:
            acc[...] = part
        else:
            acc[...] += part
    small_ref[...] = jnp.zeros_like(small_ref)

    def back_rows(pair, carry):
        rows = rows_of(pair)
        dx, dg, db = norm_back(xhat[rows, :], xscale[rows, :], ln_g[...], acc[rows, :])
        acc[rows, :] = gmid[rows, :] + dx
        small_ref[0:1, :] += dg
        small_ref[1:2, :] += db
        return carry

    lax.fori_loop(0, pairs, back_rows, 0)
    for image in range(pairs // 2):
        grad = acc[pl.ds(image * 2 * PAIR, 2 * PAIR), :]
        if last:
            gout_ref[:, image, :] = mm_tn(place[...], grad.astype(BF16)).astype(BF16)
        else:
            high, low = split_exact(grad)
            gout_ref[pl.ds(image * 2 * PAIR, 2 * PAIR), :] = mm(place[...], high) + mm(
                place[...], low
            )


def pack_start(plan, where, weights, outs, sems):
    core = where[1]
    moves = []
    for weight, layer, out, blocks in plan:
        weight, out = weights[weight], outs[out]
        half = weight.shape[1] // 2
        for row, lane, rows, lanes, to_row, to_lane in blocks:
            from_row = pl.multiple_of(core * half + row, 16)
            moves.append(
                (
                    weight.at[layer, pl.ds(from_row, rows), pl.ds(lane, lanes)],
                    out.at[pl.ds(to_row, rows), pl.ds(to_lane, lanes)],
                )
            )
    copies = [pltpu.make_async_copy(a, b, sems.at[i]) for i, (a, b) in enumerate(moves)]
    for copy in copies:
        copy.start()

    def end():
        for copy in copies:
            copy.wait()

    return end


def merge_kernel(where, a, b, c, out, sems):
    copies = [pltpu.make_async_copy(v, out.at[i], sems.at[i]) for i, v in enumerate((a, b, c))]
    for copy in copies:
        copy.start()
    for copy in copies:
        copy.wait()


def three_parts(v):
    high = v.astype(BF16)
    rest = v - high.astype(F32)
    mid = rest.astype(BF16)
    return high, mid, (rest - mid.astype(F32)).astype(BF16)


def own_tables(table, qv, b1, out):
    out[...] = jnp.zeros_like(out)
    at = lax.broadcasted_iota(jnp.int32, (2 * LANES, TRI), 0)
    to = lax.broadcasted_iota(jnp.int32, (2 * LANES, TRI), 1)
    same = jnp.logical_and(at // 64 == to // 96, at % HEAD_DIM == to % HEAD_DIM)
    same = jnp.logical_and(same, 2 * ((at // HEAD_DIM) % 2) == (to // HEAD_DIM) % 3)
    spread = jnp.where(same, 1.0, 0.0).astype(BF16)
    for layer in range(LAYERS):
        for head in range(GHEADS):
            lane = (head * LAYERS + layer) * 2 * LANES
            out[:, lane : lane + TABLE] = table[layer, head : head + 1, :]
        lane = BIAS_AT + layer * TRI
        out[:, lane : lane + TRI] = exact_pick(qv[layer : layer + 1, :], spread)
        lane = HIDDEN_AT + layer * HID
        out[:, lane : lane + HID] = b1[layer : layer + 1, :]


def put_tables(tables, out):
    cols = tables.shape[1]
    out[Q_ROWS:, :] = jnp.zeros((out.shape[0] - Q_ROWS, C), BF16)
    for part, v in enumerate(three_parts(tables[...])):
        for row in range(8):
            lanes = min(C, cols - row * C)
            at = Q_ROWS + 8 * part + row
            out[at : at + 1, 0:lanes] = v[:, row * C : row * C + lanes]


def take_tables(tables, near, every):
    cols = tables.shape[1]
    every[0:1, :] = tables[...]
    for r in range(1, GROUPS):
        wide = near[r - 1, Q_ROWS : Q_ROWS + 24, :].astype(F32)
        total = wide[0:8] + wide[8:16] + wide[16:24]
        for row in range(8):
            lanes = min(C, cols - row * C)
            every[r : r + 1, row * C : row * C + lanes] = total[row : row + 1, 0:lanes]


def exact_pick(row, chosen):
    parts = jnp.concatenate([*three_parts(row), jnp.zeros((13, row.shape[1]), BF16)], 0)
    got = mm(parts, chosen)
    return got[0:1] + got[1:2] + got[2:3]


def small_kernel(index, *refs):
    out, acc, folded = refs[-3:]
    out[...] = jnp.zeros_like(out)
    pick = refs[0]
    for layer in range(LAYERS):
        small2, db1, small_q, small1, rel = refs[5 * layer + 1 : 5 * layer + 6]
        base = 24 * layer
        out[base : base + 4, :] = small2[...]
        for r in range(GROUPS):
            out[base + 4 + r : base + 5 + r, :] = db1[r]
            out[base + 8 + r : base + 9 + r, 0 : 2 * LANES] = exact_pick(small_q[r], pick[...])
        out[base + 12 : base + 14, :] = small1[...]

        def fold(head, carry, layer=layer, rel=rel):
            second = pltpu.roll(rel[head, WTOK : 2 * WTOK, :], LANES - WTOK, 1)
            at = pl.multiple_of((layer * HEADS + head) * 56, 8)
            folded[pl.ds(at, WTOK), :] = rel[head, 0:WTOK, :] + second
            return carry

        lax.fori_loop(0, HEADS, fold, 0)
    entry = lax.broadcasted_iota(jnp.int32, (2 * LANES, LANES), 0)
    count = LAYERS * HEADS
    acc[...] = jnp.zeros_like(acc)

    def one_row(i, carry):
        onehot = jnp.where(entry == index[i], 1.0, 0.0).astype(BF16)
        high, low = split_exact(folded[pl.ds(i, count, stride=56), :])
        acc[...] += mm_nt(onehot, jnp.concatenate([high, low], 0))
        return carry

    lax.fori_loop(0, WTOK, one_row, 0, unroll=7)
    total = acc[...].T
    total = total[:count] + total[count:]
    for layer in range(LAYERS):
        for part in range(2):
            at = layer * HEADS + part * 8
            out[24 * layer + 16 : 24 * layer + 24, part * 2 * LANES : (part + 1) * 2 * LANES] = total[
                at : at + 8, :
            ]


def add_go_kernel(where, *refs):
    count = (len(refs) - 4) // 2
    go_a, go_b, stay_a, stay_b = refs[-4:]
    row = 0
    for i in range(count):
        keep, got = refs[2 * i], refs[2 * i + 1]
        size = keep.shape[2]
        rows = slice(row, row + size)
        for part, (stay, go) in enumerate(((stay_a, go_a), (stay_b, go_b))):
            stay[:, rows, :] = keep[part, :2] + got[part, :2]
            go[:, rows, :] = keep[part, 2:] + got[part, 2:]
        row += size


def add_next_kernel(where, stay_a, stay_b, got_a, got_b, next_a, next_b, keep_a, keep_b):
    next_a[...] = stay_a[1] + got_a[1]
    next_b[...] = stay_b[1] + got_b[1]
    keep_a[...] = stay_a[0] + got_a[0]
    keep_b[...] = stay_b[0] + got_b[0]


def add_whole_kernel(where, keep_a, keep_b, got_a, got_b, out):
    size = keep_a.shape[0]
    out[0:size, :] = keep_a[...] + got_a[...]
    out[size:, :] = keep_b[...] + got_b[...]


def choose_kernel(where, mine, got, out):
    end = jnp.logical_or(where[2] == 0, where[2] == 3)
    out[...] = jnp.where(end, got[...], mine[...])


def add_level_kernel(where, keep_a, keep_b, got_a, got_b, mine, send):
    odd = where[2] & 1
    a = keep_a[...] + got_a[...]
    b = keep_b[...] + got_b[...]
    mine[...] = jnp.where(odd == 1, b, a)
    send[...] = jnp.where(odd == 1, a, b)


def add_kernel(where, a, b, out):
    out[...] = a[...] + b[...]


FINISH = {"q": (0, PACK_Q), "p": (1, PACK_P), "1": (2, PACK_1), "2": (3, PACK_2), "two": (3, PACK_TWO)}


def finish_kernel(plan, count, made, where, *refs):
    pieces = refs[:made]
    scratch, sems = refs[count + 5 : -1], refs[-1]
    core, odd = where[1], where[2] & 1
    copies = []
    first, slot = 0, 0
    results = refs[count : count + 4]
    for total, layer, names in plan:
        size = total // 2
        for name in names:
            index, blocks = FINISH[name]
            out = scratch[slot]
            half = out.shape[0] // 2
            for at, piece in enumerate(pieces):
                c = core if at < len(pieces) // 2 else 1 - core
                if len(pieces) == 2:
                    for row, lane, rows, lanes, to_row, to_lane in blocks:
                        target = pl.multiple_of(c * half + row, 16)
                        out[pl.ds(target, rows), lane : lane + lanes] = piece[
                            first + to_row : first + to_row + rows, to_lane : to_lane + lanes
                        ].astype(F32)
                    continue
                for part in range(2):

                    @pl.when((odd if at % 2 == 0 else 1 - odd) == part)
                    def _(piece=piece, part=part, c=c, out=out, first=first, size=size, blocks=blocks):
                        for row, lane, rows, lanes, to_row, to_lane in blocks:
                            begin = max(to_row, part * size)
                            end = min(to_row + rows, (part + 1) * size)
                            if begin >= end:
                                continue
                            target = pl.multiple_of(c * half + row + begin - to_row, 16)
                            source = first + begin - part * size
                            out[pl.ds(target, end - begin), lane : lane + lanes] = piece[
                                source : source + end - begin, to_lane : to_lane + lanes
                            ].astype(F32)

            copies.append(pltpu.make_async_copy(out, results[index].at[layer], sems.at[slot]))
            copies[-1].start()
            slot += 1
        first += size * (1 if len(pieces) == 4 else 2)
    for copy in copies:
        copy.wait()


def own_kernel(where, little, got, out):
    tid = where[0]
    out[...] = jnp.zeros_like(out)
    for layer in range(LAYERS):
        base, to = 24 * layer, 16 * layer

        def put(rows, row, lane, lanes):
            out[to + rows[0] : to + rows[1], 0:lanes] = (
                little[base + row : base + row + rows[1] - rows[0], lane : lane + lanes]
                + got[base + row : base + row + rows[1] - rows[0], lane : lane + lanes]
            )

        put((0, 4), 0, 0, C)
        put((4, 6), 12, 0, C)
        for r in range(GROUPS):

            @pl.when(tid == r)
            def _(r=r, put=put):
                put((6, 7), 4 + r, 0, C)
                put((7, 8), 8 + r, 0, 2 * LANES)
                put((8, 12), 16 + GHEADS * (r % 2), 2 * LANES * (r // 2), 2 * LANES)


def unpack_kernel(where, little, *outs):
    for layer in range(LAYERS):
        base = 16 * layer
        for out, at in zip(outs[:7], (4, 5, 3, 1, 2, 0, 6)):
            out[layer : layer + 1, :] = little[base + at : base + at + 1, :]
        outs[7][layer : layer + 1, :] = little[base + 7 : base + 8, 0 : 2 * LANES]
        outs[8][layer] = little[base + 8 : base + 12, 0:TABLE]


VM = pl.BlockSpec(memory_space=pltpu.VMEM)
SM = pl.BlockSpec(memory_space=pltpu.SMEM)
ANY = pl.BlockSpec(memory_space=pl.ANY)
VC = pl.BlockSpec(memory_space=pltpu.VMEM)
HB = pl.BlockSpec(memory_space=pltpu.HBM)


def pinned(shape, dtype):
    return pltpu.VMEM(shape, dtype)


def place_operand(spec, value):
    if spec is VC:
        return pltpu.with_memory_space_constraint(value, pltpu.VMEM)
    if spec is HB:
        return pltpu.with_memory_space_constraint(value, pltpu.HBM)
    return value


def call(
    kernel, specs, args, outs, scratch=(), flops=0, out_specs=None, limit=2, moved=4, after=(), aliases=None,
    weight=0,
):
    count = len(args)
    skip = count + len(after)

    def body(*refs):
        kernel(*refs[:count], *refs[skip:])

    return pl.pallas_call(
        body,
        out_shape=outs,
        in_specs=list(specs) + [ANY] * len(after),
        out_specs=[VM] * len(outs) if out_specs is None else out_specs,
        scratch_shapes=scratch,
        input_output_aliases=aliases or {},
        compiler_params=pltpu.CompilerParams(vmem_limit_bytes=limit << 20),
        cost_estimate=pl.CostEstimate(flops=1 + weight * GF, bytes_accessed=1, transcendentals=0),
    )(*[place_operand(spec, arg) for spec, arg in zip(specs, args)], *after)


def struct(shape, dtype):
    return jax.ShapeDtypeStruct(shape, dtype)


DIM_Q, DIM_P, DIM_1, DIM_2 = (C, TRI), (LANES, C), (C, HID), (HID, C)
GF = 1 << 30
BIAS_AT = GHEADS * LAYERS * 2 * LANES
HIDDEN_AT = BIAS_AT + LAYERS * TRI


def fetch_sems(*dims):
    return [
        pltpu.SemaphoreType.DMA((1 + 6 * (len(PACK_Q) if d == DIM_Q else 1),)) for d in dims
    ]


def chunk_outs(rows):
    return [pinned((2, GROUPS, rows // 2, C), BF16)] * 2


def attn_fwd(layer, batch, where, x, place, ln_g, ln_b, tables, group, bias, w):
    pairs = 2 * batch
    rows = pairs * PAIR
    outs = [
        pinned((rows, C), F32),
        pinned((rows, LANES), F32),
        pinned((rows, C), BF16),
        pinned((GROUPS, rows, TRI), BF16),
        pinned((GROUPS, pairs, PAIR, GHEADS * LANES), BF16),
        pinned((GROUPS, rows, LANES), F32),
        pinned((rows, C), BF16),
        pinned((GROUPS,) + DIM_Q, BF16),
    ]
    if layer == 0:
        outs = [pinned((rows, C), F32)] + outs
    return call(
        functools.partial(attn_fwd_kernel, layer, pairs, w.q_base),
        [SM, VM if layer == 0 else VC] + [VM] * 5 + [VC] + [HB] + [ANY] * 2,
        [where, x, place, ln_g, ln_b, tables, group, bias, *w.qkv],
        outs,
        fetch_sems(DIM_Q),
        flops=8 * GF,
        limit=9,
    )


def mlp_fwd(layer, batch, where, x, ho, b_proj, ln_g, ln_b, tables, b2, place, w):
    pairs = 2 * batch
    rows = pairs * PAIR
    last = layer == LAYERS - 1
    outs = [
        struct((batch, TOK, C), BF16) if last else pinned((rows, C), F32),
        pinned((rows, C), F32),
        pinned((rows, LANES), F32),
        pinned((rows, C), BF16),
        pinned((GROUPS, rows, HID), BF16),
        pinned((GROUPS, rows, HID), BF16),
    ] + [pinned((GROUPS,) + dim, BF16) for dim in (DIM_P, DIM_1, DIM_2)]
    return call(
        functools.partial(mlp_fwd_kernel, layer, pairs, len(w.p_m)),
        [SM, VC, VC] + [VM] * 6 + [HB] * 3 + [ANY] * len(w.p_m),
        [where, x, ho, b_proj, ln_g, ln_b, tables, b2, place, w.own_p, w.own_1, w.own_2, *w.p_m],
        outs,
        fetch_sems(DIM_P, DIM_1, DIM_2)
        + [pltpu.VMEM((rows, C), F32), pltpu.VMEM((rows, HID), F32), pltpu.VMEM((rows, C), F32)],
        flops=8 * GF,
        limit=12,
    )


def mlp_open(layer, batch, where, x, ho, b_proj, ln_g, ln_b, tables, w, base, pieces):
    pairs = 2 * batch
    rows = pairs * PAIR
    return call(
        functools.partial(mlp_open_kernel, layer, pairs, base),
        [SM, VC, VC] + [VM] * 4 + [HB] * 3 + [ANY] * 2,
        [where, x, ho, b_proj, ln_g, ln_b, tables, w.own_p, w.own_1, w.own_2, *pieces],
        [
            pinned((rows, C), F32),
            pinned((rows, C), F32),
            pinned((rows, LANES), F32),
            pinned((rows, C), BF16),
            pinned((rows, C), F32),
            pinned((1, rows, HID), BF16),
            pinned((1, rows, HID), BF16),
            pinned((GROUPS,) + DIM_P, BF16),
            pinned((1,) + DIM_1, BF16),
            pinned((1,) + DIM_2, BF16),
        ],
        fetch_sems(DIM_P) + [pltpu.SemaphoreType.DMA((2,)), pltpu.VMEM((rows, HID), F32)],
        limit=10,
    )


def mlp_more(layer, batch, where, tables, n2, acc, shares, pieces, end=None, after=()):
    pairs = 2 * batch
    rows = pairs * PAIR
    count = len(shares)
    outs = [pinned((count, rows, HID), BF16)] * 2
    outs += [pinned((count,) + dim, BF16) for dim in (DIM_1, DIM_2)]
    scratch = [pltpu.SemaphoreType.DMA((4 * count,)), pltpu.VMEM((rows, HID), F32)]
    if end is None:
        outs = [pinned((rows, C), F32)] + outs
    else:
        outs = [struct((batch, TOK, C), BF16)] + outs
        scratch.append(pltpu.VMEM((rows, C), F32))
    return call(
        functools.partial(mlp_more_kernel, layer, pairs, shares, end is not None),
        [SM, VM, VC, VC] + [ANY] * len(pieces) + ([] if end is None else [VC, VM, VM]),
        [where, tables, n2, acc, *pieces, *(end or ())],
        outs,
        scratch,
        limit=12,
        after=after,
    )


def mlp_bwd(layer, batch, where, g, place, act, dact, mid, n2, ho, rinv, ln_g, w, after):
    pairs = 2 * batch
    rows = pairs * PAIR
    outs = chunk_outs(M_ROWS) + [
        pinned((rows, C), F32),
        pinned((GROUPS, rows, LANES), BF16),
        pinned((GROUPS, rows, LANES), BF16),
        struct((4, C), F32),
        struct((GROUPS, 1, HID), F32),
    ]
    return call(
        functools.partial(mlp_bwd_kernel, layer, pairs, len(act)),
        [SM, VM if layer == LAYERS - 1 else VC, VM]
        + [VC] * (2 * len(act) + 5)
        + [VM]
        + [VC] * (2 * len(act) + 1),
        [where, g, place, *act, *dact, *mid, n2, ho, rinv, ln_g, w[0], *w[1], *w[2]],
        outs,
        [
            pltpu.VMEM((rows, C), F32),
            pltpu.VMEM((rows, C), BF16),
            pltpu.VMEM((GROUPS, rows, HID), BF16),
            pltpu.VMEM((rows, C), F32),
            pltpu.VMEM(DIM_1, BF16),
            pltpu.VMEM(DIM_P, BF16),
        ],
        flops=14 * GF,
        limit=18,
        after=after,
    )


def pair_bwd(layer, batch, where, g, act, dact, w, n1, dtri, after):
    pairs = 2 * batch
    rows = pairs * PAIR
    return call(
        functools.partial(pair_bwd_kernel, layer, pairs),
        [SM] + [VC] * 6,
        [where, g, act[0], dact[0], w[2][0], n1, dtri],
        chunk_outs(TWO_ROWS + Q_ROWS)
        + [pinned((GROUPS, rows, HID), BF16), struct((GROUPS, 1, TRI), F32)],
        [pltpu.VMEM((rows, C), BF16), pltpu.VMEM(DIM_2, BF16), pltpu.VMEM(DIM_Q, BF16)],
        limit=10,
        after=after,
    )


def middle_bwd(layer, batch, where, gp, g, mid, n2, ho, rinv, ln_g, w, after):
    pairs = 2 * batch
    rows = pairs * PAIR
    return call(
        functools.partial(middle_bwd_kernel, layer, pairs),
        [SM] + [VC] * 7 + [VM] + [VC] * 2,
        [where, gp, g, *mid, n2, ho, rinv, ln_g, w[0], w[1][0]],
        chunk_outs(ONE_ROWS)
        + [
            pinned((rows, C), F32),
            pinned((GROUPS, rows, LANES), BF16),
            pinned((GROUPS, rows, LANES), BF16),
            struct((4, C), F32),
            struct((GROUPS, 1, HID), F32),
        ],
        [
            pltpu.VMEM((rows, C), BF16),
            pltpu.VMEM((rows, C), F32),
            pltpu.VMEM(DIM_1, BF16),
            pltpu.VMEM(DIM_P, BF16),
        ],
        flops=9 * GF,
        limit=12,
        after=after,
    )


def attn_bwd(batch, where, dh, u, tri, e, group, after):
    pairs = 2 * batch
    rows = pairs * PAIR
    return call(
        functools.partial(attn_bwd_kernel, pairs),
        [SM] + [VC] * 4 + [VM],
        [where, dh, u, tri, e, group],
        [pinned((GROUPS, rows, TRI), BF16), pinned((HEADS, PAIR, LANES), F32)],
        [pltpu.VMEM((rows, TRI), BF16)],
        flops=12 * GF,
        limit=9,
        after=after,
    )


def qkv_grad(batch, where, n1, dtri, after):
    return call(
        functools.partial(qkv_grad_kernel, 2 * batch),
        [SM] + [VC] * 2,
        [where, n1, dtri],
        chunk_outs(Q_ROWS) + [struct((GROUPS, 1, TRI), F32)],
        [pltpu.VMEM(DIM_Q, BF16)],
        flops=3 * GF,
        limit=6,
        after=after,
    )


def input_bwd(layer, batch, where, gmid, normed, dtri, ln_g, place, w, after):
    pairs = 2 * batch
    rows = pairs * PAIR
    return call(
        functools.partial(input_bwd_kernel, layer, pairs),
        [SM, VC, VC, VC, VC, VM, VM, VC],
        [where, gmid, *normed, dtri, ln_g, place, w],
        [
            struct((TOK, batch, C), BF16) if layer == 0 else pinned((rows, C), F32),
            pinned((2, C), F32),
        ],
        [pltpu.VMEM((rows, C), F32)],
        flops=3 * GF,
        limit=9,
        after=after,
    )


def full_bias(qv_rows, heads):
    parts = qv_rows.reshape(LAYERS, heads, 2, HEAD_DIM)
    full = jnp.stack([parts[:, :, 0], jnp.zeros_like(parts[:, :, 0]), parts[:, :, 1]], 2)
    return full.reshape(LAYERS, heads * 3 * HEAD_DIM)


def swap(x, axis, size, bit):
    return lax.ppermute(x, axis, [(i, i ^ bit) for i in range(size)])


class Weights:
    def __init__(self, own, p_q, p_m, q_base=0):
        own_q, self.own_p, self.own_1, self.own_2 = own
        self.q_base = q_base
        self.qkv = [own_q] + p_q
        self.p_m = p_m


class Direct:
    def __init__(self, dp):
        self.dp = dp
        self.t = lax.axis_index("tensor")
        d = lax.axis_index("dp")
        self.where = jnp.stack([self.t, d % 2, d // 2]).astype(jnp.int32)

    def x(self, v):
        return swap(v, "tensor", 4, 1)

    def y(self, v):
        return swap(v, "tensor", 4, 2)

    def diagonal(self, v):
        return swap(v, "tensor", 4, 3)

    def other(self, v):
        return swap(v, "dp", self.dp, 1)

    def level(self, v, k):
        return swap(v, "dp", self.dp, 2 * k)

    def near(self, v):
        return self.x(v), self.y(v), self.diagonal(v)

    def plan(self, parts):
        plan, outs = [], []
        for part in parts:
            at, base = len(outs), 0
            for layer, chunk in part:
                lists, rows = CHUNKS[chunk]
                for weight, blocks in lists:
                    plan.append((weight, layer, at, moved_down(blocks, base)))
                base += rows
            outs.append(pinned((base, C), BF16))
        return plan, outs

    def pack(self, arrays, parts, tables=None, after=()):
        plan, outs = self.plan(parts)
        count = sum(len(blocks) for _, _, _, blocks in plan)
        args = [self.where, *arrays]
        scratch = []
        if tables is not None:
            args += tables
            outs[0] = pinned((FIRST_ROWS, C), BF16)
            outs.append(pinned((1, HIDDEN_AT + LAYERS * HID), F32))
            scratch = [pltpu.VMEM(v.shape, F32) for v in tables]
        made = len(outs)

        def body(where, *refs):
            outs = refs[len(args) - 1 : len(args) - 1 + made]
            end = pack_start(plan, where, refs[:4], outs, refs[-1])
            if tables is not None:
                held = refs[len(args) - 1 + made : -1]
                copies = [
                    pltpu.make_async_copy(a, b, refs[-1].at[count + i])
                    for i, (a, b) in enumerate(zip(refs[4:7], held))
                ]
                for copy in copies:
                    copy.start()
                for copy in copies:
                    copy.wait()
                own_tables(*held, outs[-1])
                put_tables(outs[-1], outs[0])
            end()

        return call(
            body, [SM] + [HB] * (len(args) - 1), args, outs,
            scratch + [pltpu.SemaphoreType.DMA((count + 3,))], after=after,
        )

    def merge(self, pieces, arrays=(), parts=(), moved=(), tables=None, after=()):
        rows, count = pieces[0].shape[0], len(pieces)
        plan, packs = self.plan(parts)
        outs = [pinned((3, rows, C), BF16)] + packs + [pinned(v.shape, v.dtype) for v in moved]
        weights = len(arrays)
        small = [] if tables is None else [tables]
        outs += [pinned((GROUPS, v.shape[1]), F32) for v in small]
        given = count + weights + len(moved) + len(small)

        def body(where, *refs):
            spare, outs = refs[:given], refs[given:-2]
            ends = []
            if parts:
                ends.append(pack_start(plan, where, spare[count : count + weights], outs[1:], refs[-1]))
            copies = [
                pltpu.make_async_copy(a, b, refs[-2].at[3 + i])
                for i, (a, b) in enumerate(
                    zip(spare[count + weights : count + weights + len(moved)], outs[1 + len(packs) :])
                )
            ]
            for copy in copies:
                copy.start()
            merge_kernel(where, *refs[:count], outs[0], refs[-2])
            if small:
                take_tables(spare[-1], outs[0], outs[-1])
            for copy in copies:
                copy.wait()
            for end in ends:
                end()

        moves = sum(len(blocks) for _, _, _, blocks in plan)
        near, *others = call(
            body, [SM] + [ANY] * count + [HB] * weights + [ANY] * len(moved) + [VM] * len(small),
            [self.where, *pieces, *arrays, *moved, *small], outs,
            [pltpu.SemaphoreType.DMA((3 + len(moved),)), pltpu.SemaphoreType.DMA((max(moves, 1),))],
            after=after, limit=10,
        )
        return [[near, self.other(near)], *others]

    def step(self, *parts, passing=(), after=(), weight=0):
        kernels, args, specs, outs, cuts = [], [self.where], [SM], [], []
        for kernel, values, results in parts:
            kernels.append((kernel, len(args) - 1, len(values), len(outs), len(results)))
            args += values
            specs += [VC] * len(values)
            outs += results
        total_in, total_out = len(args) - 1, len(outs)
        aliases = {}
        for value in passing:
            aliases[len(args)] = len(outs)
            args.append(value)
            specs.append(ANY)
            outs.append(struct(value.shape, value.dtype))

        def body(where, *refs):
            refs_in, refs_out = refs[: total_in + len(passing)], refs[total_in + len(passing) :]
            for kernel, at, count, out, results in kernels:
                kernel(where, *refs_in[at : at + count], *refs_out[out : out + results])

        got = call(
            body, specs, args, outs, after=after, aliases=aliases, weight=weight,
            out_specs=[VM] * total_out + [ANY] * len(passing),
        )
        split = []
        for _, _, _, out, results in kernels:
            split.append(got[out : out + results])
        return split + list(got[total_out:])


    def swap_cores(self, keep, send):
        return keep, self.other(send)

    def first_way(self, *states):
        args = [v for state in states for v in state]
        two = pinned((2, sum(keep.shape[2] for keep, _ in states), C), BF16)
        return add_go_kernel, args, [two] * 4

    def send_first(self, done):
        go_a, go_b, stay_a, stay_b = done
        return stay_a, stay_b, self.x(go_a), self.y(go_b)

    def second_way(self, state):
        one = pinned(state[0].shape[1:], BF16)
        return add_next_kernel, list(state), [one] * 4

    def send_second(self, done):
        next_a, next_b, keep_a, keep_b = done
        return keep_a, keep_b, self.y(next_a), self.x(next_b)

    def join(self, state):
        one = pinned(state[0].shape, BF16)
        return add_level_kernel, list(state), [one] * 2

    def join_whole(self, state):
        rows = 2 * state[0].shape[0]
        return add_whole_kernel, list(state), [pinned((rows, C), BF16)]

    def line(self, v, pairs):
        return lax.ppermute(
            v, "dp", [(2 * a + core, 2 * b + core) for a, b in pairs for core in range(2)]
        )

    def choose(self, mine, got):
        return choose_kernel, [mine, got], [pinned(mine.shape, BF16)]

    def send_level(self, state, k):
        mine, send = state
        return mine, self.level(send, k)

    def add(self, state):
        return add_kernel, list(state), [pinned(state[0].shape, BF16)]

    def own_small(self, state):
        return own_kernel, list(state), [pinned((16 * LAYERS, C), F32)]

    def add_small(self, state):
        return add_kernel, list(state), [pinned(state[0].shape, F32)]

    def finish(self, plan, pieces, before=None, after=()):
        dims = (DIM_Q, DIM_P, DIM_1, DIM_2)
        made = len(pieces)
        args, specs = [self.where, *pieces], [SM] + [VC] * made
        aliases = {}
        if before is not None:
            aliases = {1 + made + i: i for i in range(4)}
            args += before[:4]
            specs += [HB] * 4
        scratch = [
            pltpu.VMEM(dims[FINISH[name][0]], F32) for _, _, names in plan for name in names
        ]
        return call(
            functools.partial(finish_kernel, plan, len(args) - 1, made), specs, args,
            [pltpu.HBM((LAYERS,) + dim, F32) for dim in dims] + [pinned((8, LANES), F32)],
            scratch + [pltpu.SemaphoreType.DMA((len(scratch),))],
            out_specs=[HB] * 4 + [VM], limit=6, after=after, aliases=aliases,
        )

    def unpack(self, little, after=()):
        one = struct((LAYERS, C), F32)
        outs = [one] * 7 + [struct((LAYERS, 2 * LANES), F32), struct((LAYERS, GHEADS, TABLE), F32)]
        outs.append(pinned((8, LANES), F32))
        return call(unpack_kernel, [SM, VC], [self.where, little], outs, after=after)


class Whole:
    def __init__(self):
        self.where = jnp.zeros((3,), jnp.int32)

    def gather(self, arrays, small):
        qkv, proj, w1, w2 = [
            lax.all_gather(v, "tensor", axis=axis, tiled=True) for v, axis in zip(arrays, (2, 1, 2, 1))
        ]
        qkv = qkv.reshape(LAYERS, C, GROUPS, TRI).transpose(0, 2, 1, 3)
        proj = proj.reshape(LAYERS, GROUPS, LANES, C)
        w1 = w1.reshape(LAYERS, C, GROUPS, HID).transpose(0, 2, 1, 3)
        w2 = w2.reshape(LAYERS, GROUPS, HID, C)
        own = [v[:, 0] for v in (qkv, proj, w1, w2)]

        def pack(parts, rows):
            out = jnp.zeros((rows, C), BF16)
            for v, blocks in parts:
                for row, lane, count, lanes, to_row, to_lane in blocks:
                    block = v[row : row + count, lane : lane + lanes]
                    out = out.at[to_row : to_row + count, to_lane : to_lane + lanes].set(block)
            return out

        weights = []
        for layer in range(LAYERS):
            p_q, p_m = [], []
            for side in range(2):
                side_q, side_m = [], []
                for r in range(1, GROUPS):

                    def half(v):
                        size = v.shape[2] // 2
                        return v[layer, r, side * size : (side + 1) * size]

                    side_q.append(pack([(half(qkv), PACK_Q)], Q_ROWS))
                    parts = [(half(w1), PACK_1), (half(proj), PACK_P), (half(w2), PACK_2)]
                    side_m.append(pack(parts, M_ROWS))
                p_q.append(jnp.stack(side_q))
                p_m.append(jnp.stack(side_m))
            weights.append(Weights(own, p_q, p_m))
        return weights, lax.all_gather(small, "tensor", axis=0)

    def sum_small(self, v):
        return lax.psum(v, ("dp", "tensor"))

    def finish(self, chunks):
        full = {}
        for name, chunk, blocks, dim in (
            ("q", 1, PACK_Q, DIM_Q), ("p", 0, PACK_P, DIM_P), ("1", 0, PACK_1, DIM_1), ("2", 0, PACK_2, DIM_2)
        ):
            layers = []
            for layer in range(LAYERS):
                sides = []
                for v in chunks[layer][chunk]:
                    shares = []
                    for r in range(GROUPS):
                        packed = jnp.concatenate(
                            [v[part, ORDERS[part].index(r)] for part in range(2)], 0
                        )
                        out = jnp.zeros((dim[0] // 2, dim[1]), BF16)
                        for row, lane, count, lanes, to_row, to_lane in blocks:
                            block = packed[to_row : to_row + count, to_lane : to_lane + lanes]
                            out = out.at[row : row + count, lane : lane + lanes].set(block)
                        shares.append(out)
                    sides.append(jnp.stack(shares))
                layers.append(jnp.concatenate(sides, 1))
            full[name] = jnp.stack(layers)
        outs = []
        for name, axis in zip("qp12", (2, 1, 2, 1)):
            v = full[name]
            if axis == 2:
                v = v.transpose(0, 2, 1, 3).reshape(LAYERS, C, -1)
            else:
                v = v.reshape(LAYERS, -1, C)
            v = lax.psum_scatter(v, "tensor", scatter_dimension=axis, tiled=True)
            outs.append(lax.psum(v, "dp").astype(F32))
        return outs


def shards(
    tensor, dp, images_in, ln1_gain, ln1_bias, qkv_weight, qv_bias, rel_table, proj_weight,
    proj_bias, ln2_gain, ln2_bias, fc1_weight, fc1_bias, fc2_weight, fc2_bias, rel_index,
    region_ids, out_cot,
):
    batch = images_in.shape[0]
    direct = tensor == 4 and dp == 8
    net = Direct(dp) if direct else Whole()
    where = net.where
    wide = 2 * LANES
    own = (qkv_weight, proj_weight, fc1_weight, fc2_weight)

    heads = rel_table.shape[2]
    if direct:
        q0, packed = net.pack(
            own, [[(0, 0)]], tables=[rel_table.transpose(0, 2, 1), qv_bias, fc1_bias]
        )
        near_q0 = net.near(q0)
        w_q0, m0, every = net.merge(near_q0, own, [[(0, 1), (1, 0), (1, 2)]], tables=packed)
        near_m0 = net.near(m0)
    else:
        table = jnp.pad(rel_table.transpose(2, 0, 1), ((0, 0), (0, 0), (0, wide - TABLE)))
        bias_part = full_bias(qv_bias, heads)
        packed = jnp.concatenate([table.reshape(-1), bias_part.reshape(-1), fc1_bias.reshape(-1)])
        packed = packed.reshape(1, -1)
        weights, every = net.gather(own, packed)
    every = every.reshape(tensor, -1)
    if tensor != GROUPS:
        cut1 = heads * LAYERS * wide
        cut2 = cut1 + bias_part.size
        tables = every[:, :cut1].reshape(GROUPS, -1)
        parts = [tables]
        for part in (every[:, cut1:cut2], every[:, cut2:]):
            part = part.reshape(tensor, LAYERS, -1).transpose(1, 0, 2)
            parts.append(part.reshape(LAYERS, GROUPS, -1).transpose(1, 0, 2).reshape(GROUPS, -1))
        every = jnp.concatenate(parts, 1)
    index = jnp.pad(rel_index + 1, ((0, PAIR - WTOK), (0, LANES - WTOK)))
    index = index + jnp.pad(rel_index + 1, ((WTOK, PAIR - 2 * WTOK), (WTOK, LANES - 2 * WTOK))) - 1
    ids = region_ids.astype(BF16)
    ids_col = jnp.broadcast_to(ids[:, None], (TOK, LANES))
    ids_row = jnp.broadcast_to(ids[None, :], (16, TOK))
    lanes_place = np.zeros((2 * LANES, TOK), np.float32)
    for pair in range(2):
        lanes_place[pair * LANES : pair * LANES + PAIR] = PLACE[0][pair * PAIR : (pair + 1) * PAIR]
    place = [jnp.asarray(PLACE[layer], BF16) for layer in range(LAYERS)]
    after = w_q0[:1] if direct else ()

    def bias_of(layer, after=()):
        return call(
            functools.partial(bias_kernel, layer),
            [VM] * 6,
            [every, index, ids_col, ids_row, place[0], jnp.asarray(lanes_place, BF16)],
            [pinned((1 + layer, HEADS, PAIR, LANES), F32)],
            flops=4 * GF,
            after=after,
        )[0]

    bias = [bias_of(0, after), None]
    step01 = jnp.asarray(PLACE[1] @ PLACE[0].T, BF16)
    step10 = jnp.asarray(PLACE[0] @ PLACE[1].T, BF16)
    group = jnp.asarray(GROUP, BF16)

    def row(v, layer):
        return v[layer][None]

    saved, w_q, w_m = [None] * LAYERS, [None] * LAYERS, [None] * LAYERS
    rels, littles, normed = [None] * LAYERS, [None] * LAYERS, [None] * LAYERS

    def attn(layer, state, w):
        res = attn_fwd(
            layer, batch, where, state, place[0], row(ln1_gain, layer), row(ln1_bias, layer),
            every, group, bias[layer], w,
        )
        *res, w_q[layer] = res
        x, res = (res[0], res[1:]) if layer == 0 else (state, res)
        normed[layer] = res[:2]
        saved[layer] = (x, *res[2:])

    def mlp(layer, w):
        x, n1, tri, e, rinv, ho = saved[layer]
        state, *rest, wp, w1, w2 = mlp_fwd(
            layer, batch, where, x, ho, row(proj_bias, layer), row(ln2_gain, layer),
            row(ln2_bias, layer), every, row(fc2_bias, layer), step01 if layer == 0 else place[1],
            w,
        )
        xhat, rstd, n2, act, dact = rest
        saved[layer] += ((xhat, rstd), n2, (act,), (dact,))
        w_m[layer] = (wp, (w1,), (w2,))
        return state

    def mlp_back(layer, grad, after=()):
        x, n1, tri, e, rinv, ho, mid, n2, act, dact = saved[layer]
        keep, send, gmid, dh, u, small2, db1 = mlp_bwd(
            layer, batch, where, grad, place[1], act, dact, mid, n2, ho, rinv,
            row(ln2_gain, layer), w_m[layer], after,
        )
        littles[layer] = {"a": small2, "b": db1}
        return (keep, send), gmid, dh, u

    def pair_back(grad, dtri, after=()):
        act, dact = saved[0][8:]
        keep, send, gp, littles[1]["c"] = pair_bwd(
            0, batch, where, grad, act, dact, w_m[0], saved[1][1], dtri, after
        )
        return (keep, send), gp

    def middle_back_0(gp, grad, after):
        x, n1, tri, e, rinv, ho, mid, n2, act, dact = saved[0]
        keep, send, gmid, dh, u, small2, db1 = middle_bwd(
            0, batch, where, gp, grad, mid, n2, ho, rinv, row(ln2_gain, 0), w_m[0], after
        )
        littles[0] = {"a": small2, "b": db1}
        return (keep, send), gmid, dh, u

    def attn_back(layer, dh, u, after=()):
        dtri, rels[layer] = attn_bwd(
            batch, where, dh, u, saved[layer][2], saved[layer][3], group, after
        )
        return dtri

    def qkv_back(layer, dtri, after=()):
        keep, send, small_q = qkv_grad(batch, where, saved[layer][1], dtri, after)
        littles[layer]["c"] = small_q
        return keep, send

    def input_back(layer, gmid, dtri, after=()):
        grad, small1 = input_bwd(
            layer, batch, where, gmid, normed[layer], dtri, row(ln1_gain, layer),
            step10 if layer else place[0], w_q[layer], after,
        )
        littles[layer]["d"] = small1
        return grad, small1

    def small_sums(after=()):
        args = [index.reshape(PAIR, 1, LANES), jnp.asarray(PICK, BF16)]
        for layer in range(LAYERS):
            args += [littles[layer][name] for name in "abcd"] + [rels[layer]]
        specs = [VM] * 2 + ([VM] * 4 + [VC]) * LAYERS
        return call(
            small_kernel, specs, args, [pinned((24 * LAYERS, C), F32)],
            [
                pltpu.VMEM((wide, 2 * LAYERS * HEADS), F32),
                pltpu.VMEM((LAYERS * HEADS * 56, LANES), F32),
            ],
            after=after, limit=4,
        )[0]

    if direct:
        w0 = Weights(own, w_q0, None)
        attn(0, images_in, w0)
        bias[1] = bias_of(1, saved[0][5:6])
        (m1,) = net.pack(own, [[(1, 3)]], after=(bias[1],))
        w0.p_m, m1_now = net.merge(near_m0, moved=(m1,))
        m1_x, m1_y = net.x(m1_now), net.y(m1_now)
        state = mlp(0, w0)
        (m1,) = net.step(passing=(m1,), after=(state,))
        m1_d = net.diagonal(m1)
        w1 = Weights(own, w0.p_m, None, M_ROWS)
        attn(1, state, w1)
        x, n1, tri, e, rinv, ho = saved[1]
        m1_x, m1_y = net.step(passing=(m1_x, m1_y), after=(ho,))
        far_x, far_y = net.other(m1_x), net.other(m1_y)
        mid, xhat, rstd, n2, acc, *first = mlp_open(
            1, batch, where, x, ho, row(proj_bias, 1), row(ln2_gain, 1), row(ln2_bias, 1), every,
            w1, M_ROWS + Q_ROWS, w0.p_m,
        )
        (m1_d,) = net.step(passing=(m1_d,), after=(acc,))
        far_d = net.other(m1_d)
        acc, *second = mlp_more(
            1, batch, where, every, n2, acc, (1, 2), (m1_x, far_x, m1_y, far_y), after=(m1_d,)
        )
        output, *third = mlp_more(
            1, batch, where, every, n2, acc, (3,), (m1_d, far_d),
            end=(mid, row(fc2_bias, 1), place[1]),
        )
        act, dact, wp, *w_first = first
        saved[1] += ((xhat, rstd), n2, (act, second[0], third[0]), (dact, second[1], third[1]))
        w_m[1] = (
            wp, (w_first[0], second[2], third[2]), (w_first[1], second[3], third[3])
        )

        m1, gmid, dh, u = mlp_back(1, out_cot, after=(output,))
        m1 = net.swap_cores(*m1)
        dtri = attn_back(1, dh, u)
        (g1,) = net.step(net.first_way(m1), after=(dtri,))
        g1 = net.send_first(g1)
        grad, _ = input_back(1, gmid, dtri, after=g1[:1])
        two, gp = pair_back(grad, dtri)
        two = net.swap_cores(*two)
        one, gmid, dh, u = middle_back_0(gp, grad, after=two[:1])
        g1, send = net.step(net.second_way(g1), passing=one[1:], after=(gmid,), weight=40)
        (g2,) = net.step(net.first_way(two), after=g1[:1])
        dtri = attn_back(0, dh, u, after=g2[:1])
        g1, g2 = net.send_second(g1), net.send_first(g2)
        one = net.swap_cores(one[0], send)
        q0 = qkv_back(0, dtri)
        g1, send = net.step(net.join(g1), passing=q0[1:], after=q0[:1])
        g1 = net.send_level(g1, 1)
        q0 = net.swap_cores(q0[0], send)
        (g3,) = net.step(net.first_way(one, q0), after=(g1[0],))
        grad, done = input_back(0, gmid, dtri, after=g3[:1])
        g3 = net.send_first(g3)
        ((g1,),) = net.step(net.add(g1), after=(done,))
        g1 = net.send_level((g1, g1), 2)
        little = small_sums(after=(g1[0],))
        g2, little = net.step(net.second_way(g2), passing=(little,))
        order = g2[2:3]
        g2 = net.send_second(g2)
        (g3,) = net.step(net.second_way(g3), after=order)
        order = g3[2:3]
        g3 = net.send_second(g3)
        g2, (g1,), little = net.step(
            net.join(g2), net.add(g1), passing=(little,), after=order
        )
        order = g2[:1]
        g2 = net.send_level(g2, 1)
        near1 = net.level(g1, 1)
        little = (little, net.other(little))
        g3, (little,) = net.step(net.join(g3), net.add_small(little), after=order)
        order = g3[:1]
        g3 = net.send_level(g3, 1)
        little = (little, net.x(little))
        (g2,), (little,), side1, near1 = net.step(
            net.add(g2), net.add_small(little), passing=(g1, near1), after=order
        )
        order = (g2,)
        g2 = net.send_level((g2, g2), 2)
        little = (little, net.y(little))
        g1 = [side1, near1, net.other(side1), net.other(near1)]
        (g3,), (little,) = net.step(net.add(g3), net.own_small(little), after=order)
        order = (g3,)
        g3 = net.send_level((g3, g3), 2)
        little = (little, net.level(little, 1))
        (g2,), (little,) = net.step(net.add(g2), net.add_small(little), after=order)
        near2, side2 = net.level(g2, 1), net.other(g2)
        little = (little, net.level(little, 2))
        results = net.finish([(M_ROWS, 1, ("1", "p", "2"))], g1, after=(g2,))
        (g3,), (little,), near2 = net.step(
            net.add(g3), net.add_small(little), passing=(near2,), after=results[4:]
        )
        near3, side3 = net.level(g3, 1), net.other(g3)
        g2 = [g2, near2, side2, net.other(near2)]
        small = list(net.unpack(little))
        results = net.finish(
            [(Q_ROWS, 1, ("q",)), (TWO_ROWS, 0, ("two",))], g2, results, after=small[9:]
        )
        (near3,) = net.step(passing=(near3,), after=results[4:])
        dwq, dwp, dw1, dw2, _ = net.finish(
            [(ONE_ROWS, 0, ("1", "p")), (Q_ROWS, 0, ("q",))],
            [g3, near3, side3, net.other(near3)], results,
        )
        small[8] = small[8].transpose(0, 2, 1)
        return (
            output, grad.transpose(1, 0, 2), small[0], small[1], dwq, small[7], small[8], dwp, small[2], small[3],
            small[4], dw1, small[6], dw2, small[5],
        )
    else:
        state = images_in
        bias[1] = bias_of(1)
        for layer in range(LAYERS):
            attn(layer, state, weights[layer])
            state = mlp(layer, weights[layer])
        output = state
        grad = out_cot
        reduced = [None] * LAYERS
        for layer in reversed(range(LAYERS)):
            m, gmid, dh, u = mlp_back(layer, grad)
            dtri = attn_back(layer, dh, u)
            reduced[layer] = (m, qkv_back(layer, dtri))
            grad, _ = input_back(layer, gmid, dtri)
        little = net.sum_small(small_sums())
        dwq, dwp, dw1, dw2 = net.finish(reduced)
    little = little.reshape(LAYERS, 24, C)
    small_q = little[:, 8:12, : 2 * LANES].reshape(LAYERS, -1)
    rel = little[:, 16:].reshape(LAYERS, 8, 2, wide)[..., :TABLE].transpose(0, 3, 2, 1)
    rel = rel.reshape(LAYERS, TABLE, HEADS)
    db1 = little[:, 4:8].reshape(LAYERS, FF)
    mine = lax.axis_index("tensor")

    def share(v, axis):
        size = v.shape[axis] // tensor
        return lax.dynamic_slice_in_dim(v, mine * size, size, axis)

    return (
        output, grad.transpose(1, 0, 2), little[:, 12], little[:, 13], dwq, share(small_q, 1), share(rel, 2), dwp,
        little[:, 3], little[:, 1], little[:, 2], dw1, share(db1, 1), dw2, little[:, 0],
    )


def solution(mesh):
    tokens = P(("dp", "tensor"), None, None)
    cols, rows = P(None, None, "tensor"), P(None, "tensor", None)
    part = P(None, "tensor")
    return jax.shard_map(
        functools.partial(shards, mesh.shape["tensor"], mesh.shape["dp"]),
        mesh=mesh,
        in_specs=(
            tokens, P(), P(), cols, part, cols, rows, P(), P(), P(), cols, part, rows, P(), P(),
            P(), tokens,
        ),
        out_specs=(
            tokens, tokens, P(), P(), cols, part, cols, rows, P(), P(), P(), cols, part, rows, P(),
        ),
        check_vma=False,
    )
```

```python
import functools

import jax
import jax.numpy as jnp
import numpy as np
from jax import lax
from jax.experimental import pallas as pl
from jax.experimental.pallas import tpu as pltpu
from jax.sharding import PartitionSpec as P

C = 512
HEADS = 16
HEAD_DIM = 32
FF = 2048
WIN = 7
GRID = 14
SHIFT = 3
LAYERS = 2
TOK = 196
WTOK = 49
TABLE = 169
PAIR = 112
LANES = 128
GROUPS = 4
GHEADS = HEADS // GROUPS
TRI = 3 * LANES
HID = FF // GROUPS
SCALE = HEAD_DIM ** (-0.5)
NEG = -1e30
F32 = jnp.float32
BF16 = jnp.bfloat16


def window_tokens(offset):
    cells = np.arange(TOK).reshape(GRID, GRID)
    cells = np.roll(cells, (-offset, -offset), (0, 1))
    cells = cells.reshape(2, WIN, 2, WIN).transpose(0, 2, 1, 3)
    return cells.reshape(4, WTOK)


def place_matrix(offset):
    tokens = window_tokens(offset).reshape(2, 2 * WTOK)
    out = np.zeros((2 * PAIR, TOK), np.float32)
    for pair in range(2):
        out[pair * PAIR + np.arange(2 * WTOK), tokens[pair]] = 1.0
    return out


PLACE = [place_matrix(SHIFT if layer % 2 == 1 else 0) for layer in range(LAYERS)]


def group_matrix():
    out = np.zeros((TRI, TRI), np.float32)
    for head in range(GHEADS):
        for part in range(3):
            for pos in range(HEAD_DIM):
                out[
                    (head * 3 + part) * HEAD_DIM + pos, (part * GHEADS + head) * HEAD_DIM + pos
                ] = 1.0
    return out


GROUP = group_matrix()


def pick_matrix():
    out = np.zeros((TRI, 2 * LANES), np.float32)
    for head in range(GHEADS):
        for to, part in enumerate((0, 2)):
            for pos in range(HEAD_DIM):
                out[(head * 3 + part) * HEAD_DIM + pos, (head * 2 + to) * HEAD_DIM + pos] = 1.0
    return out


PICK = pick_matrix()


def mm(a, b):
    return jnp.dot(a, b, preferred_element_type=F32)


def mm_nt(a, b):
    return lax.dot_general(a, b, (((1,), (1,)), ((), ())), preferred_element_type=F32)


def mm_tn(a, b):
    return lax.dot_general(a, b, (((0,), (0,)), ((), ())), preferred_element_type=F32)


def normalize(x):
    centre = x - jnp.mean(x, -1, keepdims=True)
    spread = jnp.mean(centre * centre, -1, keepdims=True)
    rstd = lax.rsqrt(spread + 1e-05)
    return centre * rstd, rstd


def norm_back(xhat, rstd, gain, grad):
    rstd = rstd[:, :1]
    scaled = grad * gain
    m1 = jnp.mean(scaled, -1, keepdims=True)
    m2 = jnp.mean(scaled * xhat, -1, keepdims=True)
    dx = rstd * (scaled - m1 - xhat * m2)
    return dx, jnp.sum(grad * xhat, 0, keepdims=True), jnp.sum(grad, 0, keepdims=True)


def rows_of(pair):
    return pl.ds(pl.multiple_of(pair * PAIR, 16), PAIR)


def head_mask(head):
    lane = lax.broadcasted_iota(jnp.int32, (PAIR, LANES), 1)
    return (lane // HEAD_DIM) == head


def stack_heads(block, masks):
    zero = jnp.zeros_like(block)
    pad = jnp.zeros((LANES - PAIR, LANES), block.dtype)
    parts = []
    for mask in masks:
        parts += [jnp.where(mask, block, zero), pad]
    return jnp.concatenate(parts, 0)


def split_exact(x):
    high = x.astype(BF16)
    return high, (x - high.astype(F32)).astype(BF16)


def half_rows(core, half):
    mine = pl.ds(pl.multiple_of(core * half, 16), half)
    other = pl.ds(pl.multiple_of((1 - core) * half, 16), half)
    return mine, other


Q_ROWS, M_ROWS = 192, 576
FIRST_ROWS = 224
PACK_Q = [(0, 0, Q_ROWS, TRI, 0, 0)] + [
    (Q_ROWS, j * LANES, 64, LANES, 64 * j, TRI) for j in range(3)
]
PACK_1 = [(0, 0, 256, C, 0, 0)]
PACK_P = [(0, 0, 64, C, 256, 0)]
PACK_2 = [(0, 0, 256, C, 320, 0)]
CHUNKS = (
    (((0, PACK_Q),), Q_ROWS),
    (((2, PACK_1), (1, PACK_P), (3, PACK_2)), M_ROWS),
    (((1, [(0, 0, 64, C, 0, 0)]),), 64),
    (((2, PACK_1), (3, [(0, 0, 256, C, 256, 0)])), 512),
)
ONE_ROWS, TWO_ROWS = 320, 256
PACK_TWO = [(0, 0, 256, C, 0, 0)]


def moved_down(blocks, base):
    return [block[:4] + (block[4] + base, block[5]) for block in blocks]


class Fetch:
    def __init__(self, full, layer, pieces, blocks, dest, core, sems):
        half = dest.shape[1] // 2
        self.copies = [[pltpu.make_async_copy(full.at[layer], dest.at[0], sems.at[0])]]
        at = 1
        for r in range(1, GROUPS):
            group = []
            if len(pieces) == 2:
                near, far = pieces[0].at[r - 1], pieces[1].at[r - 1]
            else:
                near, far = pieces[r - 1], pieces[r + 2]
            for side, piece in ((core, near), (1 - core, far)):
                for row, lane, rows, lanes, to_row, to_lane in blocks:
                    target = dest.at[
                        r,
                        pl.ds(pl.multiple_of(side * half + row, 16), rows),
                        pl.ds(lane, lanes),
                    ]
                    source = piece.at[pl.ds(to_row, rows), pl.ds(to_lane, lanes)]
                    group.append(pltpu.make_async_copy(source, target, sems.at[at]))
                    at += 1
            self.copies.append(group)
        for group in self.copies:
            for copy in group:
                copy.start()

    def wait(self, r):
        for copy in self.copies[r]:
            copy.wait()


def bias_kernel(layer, table, index, ids_col, ids_row, place, lanes_place, bias_ref):
    cols = mm(place[...], ids_col[...])
    rows = mm_nt(ids_row[...], lanes_place[...])
    masks = []
    for pair in range(2):
        col = cols[pair * PAIR : (pair + 1) * PAIR]
        row = rows[:1, pair * LANES : (pair + 1) * LANES]
        masks.append(jnp.where(col != row, -100.0, 0.0))
    idx = index[...]
    step = LAYERS * 2 * LANES
    at_low = jnp.clip(idx, 0, LANES - 1)
    at_high = jnp.clip(idx - LANES, 0, LANES - 1)

    def pick(low, high):
        low = jnp.take_along_axis(jnp.broadcast_to(low, (PAIR, LANES)), at_low, axis=1)
        high = jnp.take_along_axis(jnp.broadcast_to(high, (PAIR, LANES)), at_high, axis=1)
        return jnp.where(idx < 0, NEG, jnp.where(idx < LANES, low, high))

    for head in range(HEADS):
        r, lane = head // GHEADS, (head % GHEADS) * step + layer * 2 * LANES
        picked = pick(
            table[r : r + 1, lane : lane + LANES], table[r : r + 1, lane + LANES : lane + 2 * LANES]
        )
        if layer == 0:
            bias_ref[0, head] = picked
        else:
            bias_ref[0, head] = picked + masks[0]
            bias_ref[1, head] = picked + masks[1]


def attn_fwd_kernel(layer, pairs, base, *refs):
    first = layer == 0
    where, x_in, place, ln_g, ln_b, tables, group, bias, full_qkv = refs[:9]
    at = BIAS_AT + layer * TRI
    p_qkv, outs = refs[9:11], refs[11:]
    if first:
        x_ref, outs = outs[0], outs[1:]
    else:
        x_ref = x_in
    xhat_ref, rstd_ref, n1_ref, tri_ref, e_ref, rinv_ref, ho_ref, w_qkv, sem_q = outs
    qkv = Fetch(full_qkv, layer, p_qkv, moved_down(PACK_Q, base), w_qkv, where[1], sem_q)
    if first:
        for image in range(pairs // 2):
            x_ref[pl.ds(image * 2 * PAIR, 2 * PAIR), :] = mm(place[...], x_in[image])

    def norm_rows(pair, carry):
        rows = rows_of(pair)
        xhat, rstd = normalize(x_ref[rows, :])
        xhat_ref[rows, :] = xhat
        rstd_ref[rows, :] = jnp.broadcast_to(rstd, (PAIR, LANES))
        n1_ref[rows, :] = (xhat * ln_g[...] + ln_b[...]).astype(BF16)
        return carry

    lax.fori_loop(0, pairs, norm_rows, 0, unroll=True)
    masks = [head_mask(h) for h in range(GHEADS)]
    ones = jnp.ones((PAIR, LANES), BF16)
    for r in range(GROUPS):
        qkv.wait(r)
        tri = (mm(n1_ref[...], w_qkv[r]) + tables[r : r + 1, at : at + TRI]).astype(BF16)
        tri_ref[r] = mm(tri, group[...]).astype(BF16)
        ones_stack = stack_heads(ones, masks)

        def pair_step(pair, carry):
            rows = rows_of(pair)
            q4 = tri_ref[r, rows, 0:LANES]
            k4 = tri_ref[r, rows, LANES : 2 * LANES]
            v4 = tri_ref[r, rows, 2 * LANES : 3 * LANES]
            s4 = mm_nt(q4, stack_heads(k4, masks))
            kind = 0 if first else lax.rem(pair, 2)
            es = []
            for h in range(GHEADS):
                s = s4[:, h * LANES : (h + 1) * LANES] * SCALE + bias[kind, r * GHEADS + h]
                es.append(jnp.exp(s - jnp.max(s, -1, keepdims=True)).astype(BF16))
            e4 = jnp.concatenate(es, 1)
            e_ref[r, pair] = e4
            vm = jnp.concatenate([stack_heads(v4, masks), ones_stack], 1)
            out = mm(e4, vm)
            rinv = 1.0 / out[:, LANES:]
            rinv_ref[r, rows, :] = rinv
            ho_ref[rows, r * LANES : (r + 1) * LANES] = (out[:, :LANES] * rinv).astype(BF16)
            return carry

        lax.fori_loop(0, pairs, pair_step, 0, unroll=True)


def mlp_fwd_kernel(layer, pairs, count, *refs):
    last = layer == LAYERS - 1
    where, x, ho, b_proj, ln_g, ln_b, tables, b2, place = refs[:9]
    at = HIDDEN_AT + layer * HID
    full_p, full_1, full_2 = refs[9:12]
    p_m, refs = refs[12 : 12 + count], refs[12 + count :]
    out_ref, xhat_ref, rstd_ref, n2_ref, act_ref, dact_ref, wp, w1, w2 = refs[:9]
    sem_p, sem_1, sem_2, acc, pre_ref, mid = refs[9:]
    core = where[1]
    f_p = Fetch(full_p, layer, p_m, PACK_P, wp, core, sem_p)
    f_1 = Fetch(full_1, layer, p_m, PACK_1, w1, core, sem_1)
    f_2 = Fetch(full_2, layer, p_m, PACK_2, w2, core, sem_2)
    for r in range(GROUPS):
        f_p.wait(r)
    weight = jnp.concatenate([wp[r] for r in range(GROUPS)], 0)
    mid[...] = x[...] + mm(ho[...], weight) + b_proj[...]

    def norm_rows(pair, carry):
        rows = rows_of(pair)
        xhat, rstd = normalize(mid[rows, :])
        xhat_ref[rows, :] = xhat
        rstd_ref[rows, :] = jnp.broadcast_to(rstd, (PAIR, LANES))
        n2_ref[rows, :] = (xhat * ln_g[...] + ln_b[...]).astype(BF16)
        return carry

    lax.fori_loop(0, pairs, norm_rows, 0, unroll=True)
    for r in range(GROUPS):
        f_1.wait(r)
        pre_ref[...] = mm(n2_ref[...], w1[r])
        b1_row = tables[r : r + 1, at : at + HID]

        def gelu_rows(step, carry):
            rows = pl.ds(pl.multiple_of(step * 16, 16), 16)
            pre = pre_ref[rows, :] + b1_row
            cdf = 0.5 + 0.5 * lax.erf(pre * (0.5**0.5))
            act_ref[r, rows, :] = (pre * cdf).astype(BF16)
            pdf = jnp.exp(-0.5 * pre * pre) * 0.3989422804014327
            dact_ref[r, rows, :] = (cdf + pre * pdf).astype(BF16)
            return carry

        lax.fori_loop(0, pairs * (PAIR // 16), gelu_rows, 0, unroll=4)
        f_2.wait(r)
        part = mm(act_ref[r], w2[r])
        if r == 0:
            acc[...] = part
        else:
            acc[...] += part
    acc[...] = acc[...] + mid[...] + b2[...]
    for image in range(pairs // 2):
        state = acc[pl.ds(image * 2 * PAIR, 2 * PAIR), :]
        if last:
            out_ref[image] = mm_tn(place[...], state.astype(BF16)).astype(BF16)
        else:
            high, low = split_exact(state)
            out_ref[pl.ds(image * 2 * PAIR, 2 * PAIR), :] = mm(place[...], high) + mm(
                place[...], low
            )


X_FIRST = (0, 2, 1, 3)
Y_FIRST = (0, 1, 2, 3)
ORDERS = (X_FIRST, Y_FIRST)


def give(keep_ref, send_ref, tmp, r, core, blocks, first=0, size=None):
    half = tmp.shape[0] // 2
    size = size or keep_ref.shape[2]
    for ref, base in ((keep_ref, core * half), (send_ref, (1 - core) * half)):
        for row, lane, rows, lanes, to_row, to_lane in blocks:
            done = 0
            while done < rows:
                part, at = divmod(to_row + done, size)
                count = min(rows - done, size - at)
                to = slice(first + at, first + at + count)
                ref[part, ORDERS[part].index(r), to, to_lane : to_lane + lanes] = tmp[
                    pl.ds(pl.multiple_of(base + row + done, 16), count), lane : lane + lanes
                ]
                done += count


class Joined:
    def __init__(self, refs):
        self.refs = refs

    def __getitem__(self, r):
        for ref in self.refs:
            if r < ref.shape[0]:
                return ref[r]
            r -= ref.shape[0]


def gelu_into(pairs, pre_ref, b1_row, act_ref, dact_ref, at):
    def some_rows(step, carry):
        rows = pl.ds(pl.multiple_of(step * 16, 16), 16)
        pre = pre_ref[rows, :] + b1_row
        cdf = 0.5 + 0.5 * lax.erf(pre * (0.5**0.5))
        act_ref[at, rows, :] = (pre * cdf).astype(BF16)
        pdf = jnp.exp(-0.5 * pre * pre) * 0.3989422804014327
        dact_ref[at, rows, :] = (cdf + pre * pdf).astype(BF16)
        return carry

    lax.fori_loop(0, pairs * (PAIR // 16), some_rows, 0, unroll=4)


def mlp_open_kernel(layer, pairs, base, *refs):
    where, x, ho, b_proj, ln_g, ln_b, tables, full_p, full_1, full_2 = refs[:10]
    pieces, refs = refs[10:12], refs[12:]
    mid, xhat_ref, rstd_ref, n2_ref, acc, act_ref, dact_ref, wp, w1, w2, sem_p, sem_w, pre_ref = refs
    f_p = Fetch(full_p, layer, pieces, moved_down(PACK_P, base - 256), wp, where[1], sem_p)
    copies = [
        pltpu.make_async_copy(full.at[layer], w.at[0], sem_w.at[i])
        for i, (full, w) in enumerate(((full_1, w1), (full_2, w2)))
    ]
    for copy in copies:
        copy.start()
    for r in range(GROUPS):
        f_p.wait(r)
    weight = jnp.concatenate([wp[r] for r in range(GROUPS)], 0)
    mid[...] = x[...] + mm(ho[...], weight) + b_proj[...]

    def norm_rows(pair, carry):
        rows = rows_of(pair)
        xhat, rstd = normalize(mid[rows, :])
        xhat_ref[rows, :] = xhat
        rstd_ref[rows, :] = jnp.broadcast_to(rstd, (PAIR, LANES))
        n2_ref[rows, :] = (xhat * ln_g[...] + ln_b[...]).astype(BF16)
        return carry

    lax.fori_loop(0, pairs, norm_rows, 0, unroll=True)
    for copy in copies:
        copy.wait()
    at = HIDDEN_AT + layer * HID
    pre_ref[...] = mm(n2_ref[...], w1[0])
    gelu_into(pairs, pre_ref, tables[0:1, at : at + HID], act_ref, dact_ref, 0)
    acc[...] = mm(act_ref[0], w2[0])


def mlp_more_kernel(layer, pairs, shares, last, *refs):
    where, tables, n2, acc_in = refs[:4]
    count = 2 * len(shares)
    pieces, refs = refs[4 : 4 + count], refs[4 + count :]
    if last:
        mid, b2, place, out_ref, act_ref, dact_ref, w1, w2, sems, pre_ref, acc = refs
    else:
        acc, act_ref, dact_ref, w1, w2, sems, pre_ref = refs
    copies = []
    for i in range(len(shares)):
        group = []
        for side, c in enumerate((where[1], 1 - where[1])):
            for k, w in enumerate((w1, w2)):
                half = w.shape[1] // 2
                target = w.at[i, pl.ds(pl.multiple_of(c * half, 16), half)]
                source = pieces[2 * i + side].at[pl.ds(k * half, half)]
                group.append(pltpu.make_async_copy(source, target, sems.at[4 * i + 2 * side + k]))
        for copy in group:
            copy.start()
        copies.append(group)
    at = HIDDEN_AT + layer * HID
    for i, r in enumerate(shares):
        for copy in copies[i]:
            copy.wait()
        pre_ref[...] = mm(n2[...], w1[i])
        gelu_into(pairs, pre_ref, tables[r : r + 1, at : at + HID], act_ref, dact_ref, i)
        part = mm(act_ref[i], w2[i])
        if i == 0:
            acc[...] = acc_in[...] + part
        else:
            acc[...] += part
    if last:
        for image in range(pairs // 2):
            rows = pl.ds(image * 2 * PAIR, 2 * PAIR)
            state = acc[rows, :] + mid[rows, :] + b2[...]
            out_ref[image] = mm_tn(place[...], state.astype(BF16)).astype(BF16)


def hidden_back(layer, pairs, where, g_in, place, act, dact, w2, g_ref, gb_ref, gp_ref, tmp, outs, blocks, first=0, size=None):
    keep, send = outs
    core = where[1]
    if layer == LAYERS - 1:
        for image in range(pairs // 2):
            rows = pl.ds(image * 2 * PAIR, 2 * PAIR)
            g = mm(place[...], g_in[image])
            g_ref[rows, :] = g
            gb_ref[rows, :] = g.astype(BF16)
    else:
        gb_ref[...] = g_ref[...].astype(BF16)
    for r in range(GROUPS):
        tmp[...] = mm_tn(act[r], gb_ref[...]).astype(BF16)
        give(keep, send, tmp, r, core, blocks, first, size)
        ga = mm_nt(gb_ref[...], w2[r])
        gp_ref[r] = (ga * dact[r].astype(F32)).astype(BF16)


def middle_back(layer, pairs, where, gp_ref, g_ref, mid, n2, ho, rinv, ln_g, w1, wp, gb_ref, acc, tmp, tmp_p, outs):
    keep, send, gmid_ref, dh_ref, u_ref, small_ref, db1_ref = outs
    tid, core = where[0], where[1]
    small_ref[...] = jnp.zeros_like(small_ref)
    for r in range(GROUPS):
        db1_ref[tid ^ r] = jnp.sum(gp_ref[r].astype(F32), 0, keepdims=True)
        tmp[...] = mm_tn(n2[...], gp_ref[r]).astype(BF16)
        give(keep, send, tmp, r, core, PACK_1)
        part = mm_nt(gp_ref[r], w1[r])
        if r == 0:
            acc[...] = part
        else:
            acc[...] += part

    def back_rows(pair, carry):
        rows = rows_of(pair)
        g_rows = g_ref[rows, :]
        dx, dg, db = norm_back(mid[0][rows, :], mid[1][rows, :], ln_g[...], acc[rows, :])
        gmid = g_rows + dx
        gmid_ref[rows, :] = gmid
        gb_ref[rows, :] = gmid.astype(BF16)
        small_ref[0:1, :] += jnp.sum(g_rows, 0, keepdims=True)
        small_ref[1:2, :] += dg
        small_ref[2:3, :] += db
        small_ref[3:4, :] += jnp.sum(gmid, 0, keepdims=True)
        return carry

    lax.fori_loop(0, pairs, back_rows, 0, unroll=True)
    for r in range(GROUPS):
        lanes = slice(r * LANES, (r + 1) * LANES)
        tmp_p[...] = mm_tn(ho[:, lanes], gb_ref[...]).astype(BF16)
        give(keep, send, tmp_p, r, core, PACK_P)
        gh = mm_nt(gb_ref[...], wp[r]) * rinv[r]
        dh_ref[r] = gh.astype(BF16)
        u_ref[r] = (gh * ho[:, lanes].astype(F32)).astype(BF16)


def mlp_bwd_kernel(layer, pairs, count, *refs):
    where, g_in, place = refs[:3]
    act, dact = Joined(refs[3 : 3 + count]), Joined(refs[3 + count : 3 + 2 * count])
    xhat, rstd, n2, ho, rinv, ln_g, wp = refs[3 + 2 * count : 10 + 2 * count]
    mid = (xhat, rstd)
    refs = refs[10 + 2 * count :]
    w1, w2 = Joined(refs[:count]), Joined(refs[count : 2 * count])
    outs = refs[2 * count : 2 * count + 7]
    g_ref, gb_ref, gp_ref, acc, tmp, tmp_p = refs[2 * count + 7 :]
    if layer < LAYERS - 1:
        g_ref = g_in
    hidden_back(
        layer, pairs, where, g_in, place, act, dact, w2, g_ref, gb_ref, gp_ref, tmp, outs[:2], PACK_2
    )
    middle_back(
        layer, pairs, where, gp_ref, g_ref, mid, n2, ho, rinv, ln_g, w1, wp, gb_ref, acc, tmp, tmp_p,
        outs,
    )


def pair_bwd_kernel(layer, pairs, where, g, act, dact, w2, n1, dtri, keep, send, gp_ref, small_ref, gb_ref, tmp, tmp_q):
    hidden_back(
        layer, pairs, where, g, None, act, dact, w2, g, gb_ref, gp_ref, tmp, (keep, send), PACK_TWO,
        Q_ROWS // 2, TWO_ROWS // 2,
    )
    qkv_grad_kernel(pairs, where, n1, dtri, keep, send, small_ref, tmp_q, Q_ROWS // 2)


def middle_bwd_kernel(layer, pairs, *refs):
    where, gp, g, xhat, rstd, n2, ho, rinv, ln_g, wp, w1 = refs[:11]
    mid = (xhat, rstd)
    gb_ref, acc, tmp, tmp_p = refs[18:]
    middle_back(
        layer, pairs, where, gp, g, mid, n2, ho, rinv, ln_g, w1, wp, gb_ref, acc, tmp, tmp_p,
        refs[11:18],
    )


def attn_bwd_kernel(pairs, where, dh, u, tri, e, group, dtri_ref, rel_ref, low_ref):
    tid = where[0]
    masks = [head_mask(h) for h in range(GHEADS)]
    neg_ones = jnp.full((PAIR, LANES), -1.0, BF16)
    for r in range(GROUPS):
        sid = tid ^ r
        neg_stack = stack_heads(neg_ones, masks)

        def pair_step(pair, carry):
            rows = rows_of(pair)
            q4 = tri[r, rows, 0:LANES]
            k4 = tri[r, rows, LANES : 2 * LANES]
            v4 = tri[r, rows, 2 * LANES : 3 * LANES]
            dh4 = dh[r, rows, :]
            left = jnp.concatenate([dh4, u[r, rows, :]], 1)
            right = jnp.concatenate([stack_heads(v4, masks), neg_stack], 1)
            dsp = mm_nt(left, right)
            e4 = e[r, pair]
            ds4 = e4.astype(F32) * dsp
            for h in range(GHEADS):
                part = ds4[:, h * LANES : (h + 1) * LANES]
                head = sid * GHEADS + h
                rel_ref[head] = jnp.where(pair == 0, part, rel_ref[head] + part)
            dsb = (ds4 * SCALE).astype(BF16)
            dq4 = mm(dsb, stack_heads(k4, masks))
            pad = jnp.zeros((LANES - PAIR, GHEADS * LANES), BF16)
            dsb_p = jnp.concatenate([dsb, pad], 0)
            e4_p = jnp.concatenate([e4, pad], 0)

            def flip(block):
                return jnp.concatenate(
                    [block[:, h * LANES : (h + 1) * LANES].T for h in range(GHEADS)], 1
                )[:PAIR]

            dk4 = mm(flip(dsb_p), stack_heads(q4, masks))
            dv4 = mm(flip(e4_p), stack_heads(dh4, masks))
            low_ref[rows, :] = jnp.concatenate([dq4, dk4, dv4], 1).astype(BF16)
            return carry

        lax.fori_loop(0, pairs, pair_step, 0, unroll=True)
        dtri_ref[r] = mm_nt(low_ref[...], group[...]).astype(BF16)


def qkv_grad_kernel(pairs, where, n1, dtri, keep, send, small_ref, tmp, size=None):
    tid, core = where[0], where[1]
    for r in range(GROUPS):
        tmp[...] = mm_tn(n1[...], dtri[r]).astype(BF16)
        give(keep, send, tmp, r, core, PACK_Q, 0, size)
        small_ref[tid ^ r] = jnp.sum(dtri[r].astype(F32), 0, keepdims=True)


def input_bwd_kernel(layer, pairs, where, gmid, xhat, xscale, dtri, ln_g, place, w_qkv, gout_ref, small_ref, acc):
    last = layer == 0
    for r in range(GROUPS):
        part = mm_nt(dtri[r], w_qkv[r])
        if r == 0:
            acc[...] = part
        else:
            acc[...] += part
    small_ref[...] = jnp.zeros_like(small_ref)

    def back_rows(pair, carry):
        rows = rows_of(pair)
        dx, dg, db = norm_back(xhat[rows, :], xscale[rows, :], ln_g[...], acc[rows, :])
        acc[rows, :] = gmid[rows, :] + dx
        small_ref[0:1, :] += dg
        small_ref[1:2, :] += db
        return carry

    lax.fori_loop(0, pairs, back_rows, 0, unroll=True)
    for image in range(pairs // 2):
        grad = acc[pl.ds(image * 2 * PAIR, 2 * PAIR), :]
        if last:
            gout_ref[:, image, :] = mm_tn(place[...], grad.astype(BF16)).astype(BF16)
        else:
            high, low = split_exact(grad)
            gout_ref[pl.ds(image * 2 * PAIR, 2 * PAIR), :] = mm(place[...], high) + mm(
                place[...], low
            )


def pack_start(plan, where, weights, outs, sems):
    core = where[1]
    moves = []
    for weight, layer, out, blocks in plan:
        weight, out = weights[weight], outs[out]
        half = weight.shape[1] // 2
        for row, lane, rows, lanes, to_row, to_lane in blocks:
            from_row = pl.multiple_of(core * half + row, 16)
            moves.append(
                (
                    weight.at[layer, pl.ds(from_row, rows), pl.ds(lane, lanes)],
                    out.at[pl.ds(to_row, rows), pl.ds(to_lane, lanes)],
                )
            )
    copies = [pltpu.make_async_copy(a, b, sems.at[i]) for i, (a, b) in enumerate(moves)]
    for copy in copies:
        copy.start()

    def end():
        for copy in copies:
            copy.wait()

    return end


def merge_kernel(where, a, b, c, out, sems):
    copies = [pltpu.make_async_copy(v, out.at[i], sems.at[i]) for i, v in enumerate((a, b, c))]
    for copy in copies:
        copy.start()
    for copy in copies:
        copy.wait()


def three_parts(v):
    high = v.astype(BF16)
    rest = v - high.astype(F32)
    mid = rest.astype(BF16)
    return high, mid, (rest - mid.astype(F32)).astype(BF16)


def own_tables(table, qv, b1, out):
    out[...] = jnp.zeros_like(out)
    at = lax.broadcasted_iota(jnp.int32, (2 * LANES, TRI), 0)
    to = lax.broadcasted_iota(jnp.int32, (2 * LANES, TRI), 1)
    same = jnp.logical_and(at // 64 == to // 96, at % HEAD_DIM == to % HEAD_DIM)
    same = jnp.logical_and(same, 2 * ((at // HEAD_DIM) % 2) == (to // HEAD_DIM) % 3)
    spread = jnp.where(same, 1.0, 0.0).astype(BF16)
    for layer in range(LAYERS):
        for head in range(GHEADS):
            lane = (head * LAYERS + layer) * 2 * LANES
            out[:, lane : lane + TABLE] = table[layer, head : head + 1, :]
        lane = BIAS_AT + layer * TRI
        out[:, lane : lane + TRI] = exact_pick(qv[layer : layer + 1, :], spread)
        lane = HIDDEN_AT + layer * HID
        out[:, lane : lane + HID] = b1[layer : layer + 1, :]


def put_tables(tables, out):
    cols = tables.shape[1]
    out[Q_ROWS:, :] = jnp.zeros((out.shape[0] - Q_ROWS, C), BF16)
    for part, v in enumerate(three_parts(tables[...])):
        for row in range(8):
            lanes = min(C, cols - row * C)
            at = Q_ROWS + 8 * part + row
            out[at : at + 1, 0:lanes] = v[:, row * C : row * C + lanes]


def take_tables(tables, near, every):
    cols = tables.shape[1]
    every[0:1, :] = tables[...]
    for r in range(1, GROUPS):
        wide = near[r - 1, Q_ROWS : Q_ROWS + 24, :].astype(F32)
        total = wide[0:8] + wide[8:16] + wide[16:24]
        for row in range(8):
            lanes = min(C, cols - row * C)
            every[r : r + 1, row * C : row * C + lanes] = total[row : row + 1, 0:lanes]


def exact_pick(row, chosen):
    parts = jnp.concatenate([*three_parts(row), jnp.zeros((13, row.shape[1]), BF16)], 0)
    got = mm(parts, chosen)
    return got[0:1] + got[1:2] + got[2:3]


def small_kernel(index, *refs):
    out, acc, folded = refs[-3:]
    out[...] = jnp.zeros_like(out)
    pick = refs[0]
    for layer in range(LAYERS):
        small2, db1, small_q, small1, rel = refs[5 * layer + 1 : 5 * layer + 6]
        base = 24 * layer
        out[base : base + 4, :] = small2[...]
        for r in range(GROUPS):
            out[base + 4 + r : base + 5 + r, :] = db1[r]
            out[base + 8 + r : base + 9 + r, 0 : 2 * LANES] = exact_pick(small_q[r], pick[...])
        out[base + 12 : base + 14, :] = small1[...]

        def fold(head, carry, layer=layer, rel=rel):
            second = pltpu.roll(rel[head, WTOK : 2 * WTOK, :], LANES - WTOK, 1)
            at = pl.multiple_of((layer * HEADS + head) * 56, 8)
            folded[pl.ds(at, WTOK), :] = rel[head, 0:WTOK, :] + second
            return carry

        lax.fori_loop(0, HEADS, fold, 0)
    entry = lax.broadcasted_iota(jnp.int32, (2 * LANES, LANES), 0)
    count = LAYERS * HEADS
    acc[...] = jnp.zeros_like(acc)

    def one_row(i, carry):
        onehot = jnp.where(entry == index[i], 1.0, 0.0).astype(BF16)
        high, low = split_exact(folded[pl.ds(i, count, stride=56), :])
        acc[...] += mm_nt(onehot, jnp.concatenate([high, low], 0))
        return carry

    lax.fori_loop(0, WTOK, one_row, 0, unroll=7)
    total = acc[...].T
    total = total[:count] + total[count:]
    for layer in range(LAYERS):
        for part in range(2):
            at = layer * HEADS + part * 8
            out[24 * layer + 16 : 24 * layer + 24, part * 2 * LANES : (part + 1) * 2 * LANES] = total[
                at : at + 8, :
            ]


def add_go_kernel(where, *refs):
    count = (len(refs) - 4) // 2
    go_a, go_b, stay_a, stay_b = refs[-4:]
    row = 0
    for i in range(count):
        keep, got = refs[2 * i], refs[2 * i + 1]
        size = keep.shape[2]
        rows = slice(row, row + size)
        for part, (stay, go) in enumerate(((stay_a, go_a), (stay_b, go_b))):
            stay[:, rows, :] = keep[part, :2] + got[part, :2]
            go[:, rows, :] = keep[part, 2:] + got[part, 2:]
        row += size


def add_next_kernel(where, stay_a, stay_b, got_a, got_b, next_a, next_b, keep_a, keep_b):
    next_a[...] = stay_a[1] + got_a[1]
    next_b[...] = stay_b[1] + got_b[1]
    keep_a[...] = stay_a[0] + got_a[0]
    keep_b[...] = stay_b[0] + got_b[0]


def add_whole_kernel(where, keep_a, keep_b, got_a, got_b, out):
    size = keep_a.shape[0]
    out[0:size, :] = keep_a[...] + got_a[...]
    out[size:, :] = keep_b[...] + got_b[...]


def choose_kernel(where, mine, got, out):
    end = jnp.logical_or(where[2] == 0, where[2] == 3)
    out[...] = jnp.where(end, got[...], mine[...])


def add_level_kernel(where, keep_a, keep_b, got_a, got_b, mine, send):
    odd = where[2] & 1
    a = keep_a[...] + got_a[...]
    b = keep_b[...] + got_b[...]
    mine[...] = jnp.where(odd == 1, b, a)
    send[...] = jnp.where(odd == 1, a, b)


def add_kernel(where, a, b, out):
    out[...] = a[...] + b[...]


FINISH = {"q": (0, PACK_Q), "p": (1, PACK_P), "1": (2, PACK_1), "2": (3, PACK_2), "two": (3, PACK_TWO)}


def finish_kernel(plan, count, made, where, *refs):
    pieces = refs[:made]
    scratch, sems = refs[count + 5 : -1], refs[-1]
    core, odd = where[1], where[2] & 1
    copies = []
    first, slot = 0, 0
    results = refs[count : count + 4]
    for total, layer, names in plan:
        size = total // 2
        for name in names:
            index, blocks = FINISH[name]
            out = scratch[slot]
            half = out.shape[0] // 2
            for at, piece in enumerate(pieces):
                c = core if at < len(pieces) // 2 else 1 - core
                if len(pieces) == 2:
                    for row, lane, rows, lanes, to_row, to_lane in blocks:
                        target = pl.multiple_of(c * half + row, 16)
                        out[pl.ds(target, rows), lane : lane + lanes] = piece[
                            first + to_row : first + to_row + rows, to_lane : to_lane + lanes
                        ].astype(F32)
                    continue
                for part in range(2):

                    @pl.when((odd if at % 2 == 0 else 1 - odd) == part)
                    def _(piece=piece, part=part, c=c, out=out, first=first, size=size, blocks=blocks):
                        for row, lane, rows, lanes, to_row, to_lane in blocks:
                            begin = max(to_row, part * size)
                            end = min(to_row + rows, (part + 1) * size)
                            if begin >= end:
                                continue
                            target = pl.multiple_of(c * half + row + begin - to_row, 16)
                            source = first + begin - part * size
                            out[pl.ds(target, end - begin), lane : lane + lanes] = piece[
                                source : source + end - begin, to_lane : to_lane + lanes
                            ].astype(F32)

            copies.append(pltpu.make_async_copy(out, results[index].at[layer], sems.at[slot]))
            copies[-1].start()
            slot += 1
        first += size * (1 if len(pieces) == 4 else 2)
    for copy in copies:
        copy.wait()


def own_kernel(where, little, got, out):
    tid = where[0]
    out[...] = jnp.zeros_like(out)
    for layer in range(LAYERS):
        base, to = 24 * layer, 16 * layer

        def put(rows, row, lane, lanes):
            out[to + rows[0] : to + rows[1], 0:lanes] = (
                little[base + row : base + row + rows[1] - rows[0], lane : lane + lanes]
                + got[base + row : base + row + rows[1] - rows[0], lane : lane + lanes]
            )

        put((0, 4), 0, 0, C)
        put((4, 6), 12, 0, C)
        for r in range(GROUPS):

            @pl.when(tid == r)
            def _(r=r, put=put):
                put((6, 7), 4 + r, 0, C)
                put((7, 8), 8 + r, 0, 2 * LANES)
                put((8, 12), 16 + GHEADS * (r % 2), 2 * LANES * (r // 2), 2 * LANES)


def unpack_kernel(where, little, *outs):
    for layer in range(LAYERS):
        base = 16 * layer
        for out, at in zip(outs[:7], (4, 5, 3, 1, 2, 0, 6)):
            out[layer : layer + 1, :] = little[base + at : base + at + 1, :]
        outs[7][layer : layer + 1, :] = little[base + 7 : base + 8, 0 : 2 * LANES]
        outs[8][layer] = little[base + 8 : base + 12, 0:TABLE]


VM = pl.BlockSpec(memory_space=pltpu.VMEM)
SM = pl.BlockSpec(memory_space=pltpu.SMEM)
ANY = pl.BlockSpec(memory_space=pl.ANY)
VC = pl.BlockSpec(memory_space=pltpu.VMEM)
HB = pl.BlockSpec(memory_space=pltpu.HBM)


def pinned(shape, dtype):
    return pltpu.VMEM(shape, dtype)


def place_operand(spec, value):
    if spec is VC:
        return pltpu.with_memory_space_constraint(value, pltpu.VMEM)
    if spec is HB:
        return pltpu.with_memory_space_constraint(value, pltpu.HBM)
    return value


def call(
    kernel, specs, args, outs, scratch=(), flops=0, out_specs=None, limit=2, moved=4, after=(), aliases=None,
    weight=0,
):
    count = len(args)
    skip = count + len(after)

    def body(*refs):
        kernel(*refs[:count], *refs[skip:])

    return pl.pallas_call(
        body,
        out_shape=outs,
        in_specs=list(specs) + [ANY] * len(after),
        out_specs=[VM] * len(outs) if out_specs is None else out_specs,
        scratch_shapes=scratch,
        input_output_aliases=aliases or {},
        compiler_params=pltpu.CompilerParams(vmem_limit_bytes=limit << 20),
        cost_estimate=pl.CostEstimate(flops=1 + weight * GF, bytes_accessed=1, transcendentals=0),
    )(*[place_operand(spec, arg) for spec, arg in zip(specs, args)], *after)


def struct(shape, dtype):
    return jax.ShapeDtypeStruct(shape, dtype)


DIM_Q, DIM_P, DIM_1, DIM_2 = (C, TRI), (LANES, C), (C, HID), (HID, C)
GF = 1 << 30
BIAS_AT = GHEADS * LAYERS * 2 * LANES
HIDDEN_AT = BIAS_AT + LAYERS * TRI


def fetch_sems(*dims):
    return [
        pltpu.SemaphoreType.DMA((1 + 6 * (len(PACK_Q) if d == DIM_Q else 1),)) for d in dims
    ]


def chunk_outs(rows):
    return [pinned((2, GROUPS, rows // 2, C), BF16)] * 2


def attn_fwd(layer, batch, where, x, place, ln_g, ln_b, tables, group, bias, w):
    pairs = 2 * batch
    rows = pairs * PAIR
    outs = [
        pinned((rows, C), F32),
        pinned((rows, LANES), F32),
        pinned((rows, C), BF16),
        pinned((GROUPS, rows, TRI), BF16),
        pinned((GROUPS, pairs, PAIR, GHEADS * LANES), BF16),
        pinned((GROUPS, rows, LANES), F32),
        pinned((rows, C), BF16),
        pinned((GROUPS,) + DIM_Q, BF16),
    ]
    if layer == 0:
        outs = [pinned((rows, C), F32)] + outs
    return call(
        functools.partial(attn_fwd_kernel, layer, pairs, w.q_base),
        [SM, VM if layer == 0 else VC] + [VM] * 5 + [VC] + [HB] + [ANY] * 2,
        [where, x, place, ln_g, ln_b, tables, group, bias, *w.qkv],
        outs,
        fetch_sems(DIM_Q),
        flops=8 * GF,
        limit=9,
    )


def mlp_fwd(layer, batch, where, x, ho, b_proj, ln_g, ln_b, tables, b2, place, w):
    pairs = 2 * batch
    rows = pairs * PAIR
    last = layer == LAYERS - 1
    outs = [
        struct((batch, TOK, C), BF16) if last else pinned((rows, C), F32),
        pinned((rows, C), F32),
        pinned((rows, LANES), F32),
        pinned((rows, C), BF16),
        pinned((GROUPS, rows, HID), BF16),
        pinned((GROUPS, rows, HID), BF16),
    ] + [pinned((GROUPS,) + dim, BF16) for dim in (DIM_P, DIM_1, DIM_2)]
    return call(
        functools.partial(mlp_fwd_kernel, layer, pairs, len(w.p_m)),
        [SM, VC, VC] + [VM] * 6 + [HB] * 3 + [ANY] * len(w.p_m),
        [where, x, ho, b_proj, ln_g, ln_b, tables, b2, place, w.own_p, w.own_1, w.own_2, *w.p_m],
        outs,
        fetch_sems(DIM_P, DIM_1, DIM_2)
        + [pltpu.VMEM((rows, C), F32), pltpu.VMEM((rows, HID), F32), pltpu.VMEM((rows, C), F32)],
        flops=8 * GF,
        limit=12,
    )


def mlp_open(layer, batch, where, x, ho, b_proj, ln_g, ln_b, tables, w, base, pieces):
    pairs = 2 * batch
    rows = pairs * PAIR
    return call(
        functools.partial(mlp_open_kernel, layer, pairs, base),
        [SM, VC, VC] + [VM] * 4 + [HB] * 3 + [ANY] * 2,
        [where, x, ho, b_proj, ln_g, ln_b, tables, w.own_p, w.own_1, w.own_2, *pieces],
        [
            pinned((rows, C), F32),
            pinned((rows, C), F32),
            pinned((rows, LANES), F32),
            pinned((rows, C), BF16),
            pinned((rows, C), F32),
            pinned((1, rows, HID), BF16),
            pinned((1, rows, HID), BF16),
            pinned((GROUPS,) + DIM_P, BF16),
            pinned((1,) + DIM_1, BF16),
            pinned((1,) + DIM_2, BF16),
        ],
        fetch_sems(DIM_P) + [pltpu.SemaphoreType.DMA((2,)), pltpu.VMEM((rows, HID), F32)],
        limit=10,
    )


def mlp_more(layer, batch, where, tables, n2, acc, shares, pieces, end=None, after=()):
    pairs = 2 * batch
    rows = pairs * PAIR
    count = len(shares)
    outs = [pinned((count, rows, HID), BF16)] * 2
    outs += [pinned((count,) + dim, BF16) for dim in (DIM_1, DIM_2)]
    scratch = [pltpu.SemaphoreType.DMA((4 * count,)), pltpu.VMEM((rows, HID), F32)]
    if end is None:
        outs = [pinned((rows, C), F32)] + outs
    else:
        outs = [struct((batch, TOK, C), BF16)] + outs
        scratch.append(pltpu.VMEM((rows, C), F32))
    return call(
        functools.partial(mlp_more_kernel, layer, pairs, shares, end is not None),
        [SM, VM, VC, VC] + [ANY] * len(pieces) + ([] if end is None else [VC, VM, VM]),
        [where, tables, n2, acc, *pieces, *(end or ())],
        outs,
        scratch,
        limit=12,
        after=after,
    )


def mlp_bwd(layer, batch, where, g, place, act, dact, mid, n2, ho, rinv, ln_g, w, after):
    pairs = 2 * batch
    rows = pairs * PAIR
    outs = chunk_outs(M_ROWS) + [
        pinned((rows, C), F32),
        pinned((GROUPS, rows, LANES), BF16),
        pinned((GROUPS, rows, LANES), BF16),
        struct((4, C), F32),
        struct((GROUPS, 1, HID), F32),
    ]
    return call(
        functools.partial(mlp_bwd_kernel, layer, pairs, len(act)),
        [SM, VM if layer == LAYERS - 1 else VC, VM]
        + [VC] * (2 * len(act) + 5)
        + [VM]
        + [VC] * (2 * len(act) + 1),
        [where, g, place, *act, *dact, *mid, n2, ho, rinv, ln_g, w[0], *w[1], *w[2]],
        outs,
        [
            pltpu.VMEM((rows, C), F32),
            pltpu.VMEM((rows, C), BF16),
            pltpu.VMEM((GROUPS, rows, HID), BF16),
            pltpu.VMEM((rows, C), F32),
            pltpu.VMEM(DIM_1, BF16),
            pltpu.VMEM(DIM_P, BF16),
        ],
        flops=14 * GF,
        limit=18,
        after=after,
    )


def pair_bwd(layer, batch, where, g, act, dact, w, n1, dtri, after):
    pairs = 2 * batch
    rows = pairs * PAIR
    return call(
        functools.partial(pair_bwd_kernel, layer, pairs),
        [SM] + [VC] * 6,
        [where, g, act[0], dact[0], w[2][0], n1, dtri],
        chunk_outs(TWO_ROWS + Q_ROWS)
        + [pinned((GROUPS, rows, HID), BF16), struct((GROUPS, 1, TRI), F32)],
        [pltpu.VMEM((rows, C), BF16), pltpu.VMEM(DIM_2, BF16), pltpu.VMEM(DIM_Q, BF16)],
        limit=10,
        after=after,
    )


def middle_bwd(layer, batch, where, gp, g, mid, n2, ho, rinv, ln_g, w, after):
    pairs = 2 * batch
    rows = pairs * PAIR
    return call(
        functools.partial(middle_bwd_kernel, layer, pairs),
        [SM] + [VC] * 7 + [VM] + [VC] * 2,
        [where, gp, g, *mid, n2, ho, rinv, ln_g, w[0], w[1][0]],
        chunk_outs(ONE_ROWS)
        + [
            pinned((rows, C), F32),
            pinned((GROUPS, rows, LANES), BF16),
            pinned((GROUPS, rows, LANES), BF16),
            struct((4, C), F32),
            struct((GROUPS, 1, HID), F32),
        ],
        [
            pltpu.VMEM((rows, C), BF16),
            pltpu.VMEM((rows, C), F32),
            pltpu.VMEM(DIM_1, BF16),
            pltpu.VMEM(DIM_P, BF16),
        ],
        flops=9 * GF,
        limit=12,
        after=after,
    )


def attn_bwd(batch, where, dh, u, tri, e, group, after):
    pairs = 2 * batch
    rows = pairs * PAIR
    return call(
        functools.partial(attn_bwd_kernel, pairs),
        [SM] + [VC] * 4 + [VM],
        [where, dh, u, tri, e, group],
        [pinned((GROUPS, rows, TRI), BF16), pinned((HEADS, PAIR, LANES), F32)],
        [pltpu.VMEM((rows, TRI), BF16)],
        flops=12 * GF,
        limit=9,
        after=after,
    )


def qkv_grad(batch, where, n1, dtri, after):
    return call(
        functools.partial(qkv_grad_kernel, 2 * batch),
        [SM] + [VC] * 2,
        [where, n1, dtri],
        chunk_outs(Q_ROWS) + [struct((GROUPS, 1, TRI), F32)],
        [pltpu.VMEM(DIM_Q, BF16)],
        flops=3 * GF,
        limit=6,
        after=after,
    )


def input_bwd(layer, batch, where, gmid, normed, dtri, ln_g, place, w, after):
    pairs = 2 * batch
    rows = pairs * PAIR
    return call(
        functools.partial(input_bwd_kernel, layer, pairs),
        [SM, VC, VC, VC, VC, VM, VM, VC],
        [where, gmid, *normed, dtri, ln_g, place, w],
        [
            struct((TOK, batch, C), BF16) if layer == 0 else pinned((rows, C), F32),
            pinned((2, C), F32),
        ],
        [pltpu.VMEM((rows, C), F32)],
        flops=3 * GF,
        limit=9,
        after=after,
    )


def full_bias(qv_rows, heads):
    parts = qv_rows.reshape(LAYERS, heads, 2, HEAD_DIM)
    full = jnp.stack([parts[:, :, 0], jnp.zeros_like(parts[:, :, 0]), parts[:, :, 1]], 2)
    return full.reshape(LAYERS, heads * 3 * HEAD_DIM)


def swap(x, axis, size, bit):
    return lax.ppermute(x, axis, [(i, i ^ bit) for i in range(size)])


class Weights:
    def __init__(self, own, p_q, p_m, q_base=0):
        own_q, self.own_p, self.own_1, self.own_2 = own
        self.q_base = q_base
        self.qkv = [own_q] + p_q
        self.p_m = p_m


class Direct:
    def __init__(self, dp):
        self.dp = dp
        self.t = lax.axis_index("tensor")
        d = lax.axis_index("dp")
        self.where = jnp.stack([self.t, d % 2, d // 2]).astype(jnp.int32)

    def x(self, v):
        return swap(v, "tensor", 4, 1)

    def y(self, v):
        return swap(v, "tensor", 4, 2)

    def diagonal(self, v):
        return swap(v, "tensor", 4, 3)

    def other(self, v):
        return swap(v, "dp", self.dp, 1)

    def level(self, v, k):
        return swap(v, "dp", self.dp, 2 * k)

    def near(self, v):
        return self.x(v), self.y(v), self.diagonal(v)

    def plan(self, parts):
        plan, outs = [], []
        for part in parts:
            at, base = len(outs), 0
            for layer, chunk in part:
                lists, rows = CHUNKS[chunk]
                for weight, blocks in lists:
                    plan.append((weight, layer, at, moved_down(blocks, base)))
                base += rows
            outs.append(pinned((base, C), BF16))
        return plan, outs

    def pack(self, arrays, parts, tables=None, after=()):
        plan, outs = self.plan(parts)
        count = sum(len(blocks) for _, _, _, blocks in plan)
        args = [self.where, *arrays]
        scratch = []
        if tables is not None:
            args += tables
            outs[0] = pinned((FIRST_ROWS, C), BF16)
            outs.append(pinned((1, HIDDEN_AT + LAYERS * HID), F32))
            scratch = [pltpu.VMEM(v.shape, F32) for v in tables]
        made = len(outs)

        def body(where, *refs):
            outs = refs[len(args) - 1 : len(args) - 1 + made]
            end = pack_start(plan, where, refs[:4], outs, refs[-1])
            if tables is not None:
                held = refs[len(args) - 1 + made : -1]
                copies = [
                    pltpu.make_async_copy(a, b, refs[-1].at[count + i])
                    for i, (a, b) in enumerate(zip(refs[4:7], held))
                ]
                for copy in copies:
                    copy.start()
                for copy in copies:
                    copy.wait()
                own_tables(*held, outs[-1])
                put_tables(outs[-1], outs[0])
            end()

        return call(
            body, [SM] + [HB] * (len(args) - 1), args, outs,
            scratch + [pltpu.SemaphoreType.DMA((count + 3,))], after=after,
        )

    def merge(self, pieces, arrays=(), parts=(), moved=(), tables=None, after=()):
        rows, count = pieces[0].shape[0], len(pieces)
        plan, packs = self.plan(parts)
        outs = [pinned((3, rows, C), BF16)] + packs + [pinned(v.shape, v.dtype) for v in moved]
        weights = len(arrays)
        small = [] if tables is None else [tables]
        outs += [pinned((GROUPS, v.shape[1]), F32) for v in small]
        given = count + weights + len(moved) + len(small)

        def body(where, *refs):
            spare, outs = refs[:given], refs[given:-2]
            ends = []
            if parts:
                ends.append(pack_start(plan, where, spare[count : count + weights], outs[1:], refs[-1]))
            copies = [
                pltpu.make_async_copy(a, b, refs[-2].at[3 + i])
                for i, (a, b) in enumerate(
                    zip(spare[count + weights : count + weights + len(moved)], outs[1 + len(packs) :])
                )
            ]
            for copy in copies:
                copy.start()
            merge_kernel(where, *refs[:count], outs[0], refs[-2])
            if small:
                take_tables(spare[-1], outs[0], outs[-1])
            for copy in copies:
                copy.wait()
            for end in ends:
                end()

        moves = sum(len(blocks) for _, _, _, blocks in plan)
        near, *others = call(
            body, [SM] + [ANY] * count + [HB] * weights + [ANY] * len(moved) + [VM] * len(small),
            [self.where, *pieces, *arrays, *moved, *small], outs,
            [pltpu.SemaphoreType.DMA((3 + len(moved),)), pltpu.SemaphoreType.DMA((max(moves, 1),))],
            after=after, limit=10,
        )
        return [[near, self.other(near)], *others]

    def step(self, *parts, passing=(), after=(), weight=0):
        kernels, args, specs, outs, cuts = [], [self.where], [SM], [], []
        for kernel, values, results in parts:
            kernels.append((kernel, len(args) - 1, len(values), len(outs), len(results)))
            args += values
            specs += [VC] * len(values)
            outs += results
        total_in, total_out = len(args) - 1, len(outs)
        aliases = {}
        for value in passing:
            aliases[len(args)] = len(outs)
            args.append(value)
            specs.append(ANY)
            outs.append(struct(value.shape, value.dtype))

        def body(where, *refs):
            refs_in, refs_out = refs[: total_in + len(passing)], refs[total_in + len(passing) :]
            for kernel, at, count, out, results in kernels:
                kernel(where, *refs_in[at : at + count], *refs_out[out : out + results])

        got = call(
            body, specs, args, outs, after=after, aliases=aliases, weight=weight,
            out_specs=[VM] * total_out + [ANY] * len(passing),
        )
        split = []
        for _, _, _, out, results in kernels:
            split.append(got[out : out + results])
        return split + list(got[total_out:])


    def swap_cores(self, keep, send):
        return keep, self.other(send)

    def first_way(self, *states):
        args = [v for state in states for v in state]
        two = pinned((2, sum(keep.shape[2] for keep, _ in states), C), BF16)
        return add_go_kernel, args, [two] * 4

    def send_first(self, done):
        go_a, go_b, stay_a, stay_b = done
        return stay_a, stay_b, self.x(go_a), self.y(go_b)

    def second_way(self, state):
        one = pinned(state[0].shape[1:], BF16)
        return add_next_kernel, list(state), [one] * 4

    def send_second(self, done):
        next_a, next_b, keep_a, keep_b = done
        return keep_a, keep_b, self.y(next_a), self.x(next_b)

    def join(self, state):
        one = pinned(state[0].shape, BF16)
        return add_level_kernel, list(state), [one] * 2

    def join_whole(self, state):
        rows = 2 * state[0].shape[0]
        return add_whole_kernel, list(state), [pinned((rows, C), BF16)]

    def line(self, v, pairs):
        return lax.ppermute(
            v, "dp", [(2 * a + core, 2 * b + core) for a, b in pairs for core in range(2)]
        )

    def choose(self, mine, got):
        return choose_kernel, [mine, got], [pinned(mine.shape, BF16)]

    def send_level(self, state, k):
        mine, send = state
        return mine, self.level(send, k)

    def add(self, state):
        return add_kernel, list(state), [pinned(state[0].shape, BF16)]

    def own_small(self, state):
        return own_kernel, list(state), [pinned((16 * LAYERS, C), F32)]

    def add_small(self, state):
        return add_kernel, list(state), [pinned(state[0].shape, F32)]

    def finish(self, plan, pieces, before=None, after=()):
        dims = (DIM_Q, DIM_P, DIM_1, DIM_2)
        made = len(pieces)
        args, specs = [self.where, *pieces], [SM] + [VC] * made
        aliases = {}
        if before is not None:
            aliases = {1 + made + i: i for i in range(4)}
            args += before[:4]
            specs += [HB] * 4
        scratch = [
            pltpu.VMEM(dims[FINISH[name][0]], F32) for _, _, names in plan for name in names
        ]
        return call(
            functools.partial(finish_kernel, plan, len(args) - 1, made), specs, args,
            [pltpu.HBM((LAYERS,) + dim, F32) for dim in dims] + [pinned((8, LANES), F32)],
            scratch + [pltpu.SemaphoreType.DMA((len(scratch),))],
            out_specs=[HB] * 4 + [VM], limit=6, after=after, aliases=aliases,
        )

    def unpack(self, little, after=()):
        one = struct((LAYERS, C), F32)
        outs = [one] * 7 + [struct((LAYERS, 2 * LANES), F32), struct((LAYERS, GHEADS, TABLE), F32)]
        outs.append(pinned((8, LANES), F32))
        return call(unpack_kernel, [SM, VC], [self.where, little], outs, after=after)


class Whole:
    def __init__(self):
        self.where = jnp.zeros((3,), jnp.int32)

    def gather(self, arrays, small):
        qkv, proj, w1, w2 = [
            lax.all_gather(v, "tensor", axis=axis, tiled=True) for v, axis in zip(arrays, (2, 1, 2, 1))
        ]
        qkv = qkv.reshape(LAYERS, C, GROUPS, TRI).transpose(0, 2, 1, 3)
        proj = proj.reshape(LAYERS, GROUPS, LANES, C)
        w1 = w1.reshape(LAYERS, C, GROUPS, HID).transpose(0, 2, 1, 3)
        w2 = w2.reshape(LAYERS, GROUPS, HID, C)
        own = [v[:, 0] for v in (qkv, proj, w1, w2)]

        def pack(parts, rows):
            out = jnp.zeros((rows, C), BF16)
            for v, blocks in parts:
                for row, lane, count, lanes, to_row, to_lane in blocks:
                    block = v[row : row + count, lane : lane + lanes]
                    out = out.at[to_row : to_row + count, to_lane : to_lane + lanes].set(block)
            return out

        weights = []
        for layer in range(LAYERS):
            p_q, p_m = [], []
            for side in range(2):
                side_q, side_m = [], []
                for r in range(1, GROUPS):

                    def half(v):
                        size = v.shape[2] // 2
                        return v[layer, r, side * size : (side + 1) * size]

                    side_q.append(pack([(half(qkv), PACK_Q)], Q_ROWS))
                    parts = [(half(w1), PACK_1), (half(proj), PACK_P), (half(w2), PACK_2)]
                    side_m.append(pack(parts, M_ROWS))
                p_q.append(jnp.stack(side_q))
                p_m.append(jnp.stack(side_m))
            weights.append(Weights(own, p_q, p_m))
        return weights, lax.all_gather(small, "tensor", axis=0)

    def sum_small(self, v):
        return lax.psum(v, ("dp", "tensor"))

    def finish(self, chunks):
        full = {}
        for name, chunk, blocks, dim in (
            ("q", 1, PACK_Q, DIM_Q), ("p", 0, PACK_P, DIM_P), ("1", 0, PACK_1, DIM_1), ("2", 0, PACK_2, DIM_2)
        ):
            layers = []
            for layer in range(LAYERS):
                sides = []
                for v in chunks[layer][chunk]:
                    shares = []
                    for r in range(GROUPS):
                        packed = jnp.concatenate(
                            [v[part, ORDERS[part].index(r)] for part in range(2)], 0
                        )
                        out = jnp.zeros((dim[0] // 2, dim[1]), BF16)
                        for row, lane, count, lanes, to_row, to_lane in blocks:
                            block = packed[to_row : to_row + count, to_lane : to_lane + lanes]
                            out = out.at[row : row + count, lane : lane + lanes].set(block)
                        shares.append(out)
                    sides.append(jnp.stack(shares))
                layers.append(jnp.concatenate(sides, 1))
            full[name] = jnp.stack(layers)
        outs = []
        for name, axis in zip("qp12", (2, 1, 2, 1)):
            v = full[name]
            if axis == 2:
                v = v.transpose(0, 2, 1, 3).reshape(LAYERS, C, -1)
            else:
                v = v.reshape(LAYERS, -1, C)
            v = lax.psum_scatter(v, "tensor", scatter_dimension=axis, tiled=True)
            outs.append(lax.psum(v, "dp").astype(F32))
        return outs


def shards(
    tensor, dp, images_in, ln1_gain, ln1_bias, qkv_weight, qv_bias, rel_table, proj_weight,
    proj_bias, ln2_gain, ln2_bias, fc1_weight, fc1_bias, fc2_weight, fc2_bias, rel_index,
    region_ids, out_cot,
):
    batch = images_in.shape[0]
    direct = tensor == 4 and dp == 8
    net = Direct(dp) if direct else Whole()
    where = net.where
    wide = 2 * LANES
    own = (qkv_weight, proj_weight, fc1_weight, fc2_weight)

    heads = rel_table.shape[2]
    if direct:
        q0, packed = net.pack(
            own, [[(0, 0)]], tables=[rel_table.transpose(0, 2, 1), qv_bias, fc1_bias]
        )
        near_q0 = net.near(q0)
        w_q0, m0, every = net.merge(near_q0, own, [[(0, 1), (1, 0), (1, 2)]], tables=packed)
        near_m0 = net.near(m0)
    else:
        table = jnp.pad(rel_table.transpose(2, 0, 1), ((0, 0), (0, 0), (0, wide - TABLE)))
        bias_part = full_bias(qv_bias, heads)
        packed = jnp.concatenate([table.reshape(-1), bias_part.reshape(-1), fc1_bias.reshape(-1)])
        packed = packed.reshape(1, -1)
        weights, every = net.gather(own, packed)
    every = every.reshape(tensor, -1)
    if tensor != GROUPS:
        cut1 = heads * LAYERS * wide
        cut2 = cut1 + bias_part.size
        tables = every[:, :cut1].reshape(GROUPS, -1)
        parts = [tables]
        for part in (every[:, cut1:cut2], every[:, cut2:]):
            part = part.reshape(tensor, LAYERS, -1).transpose(1, 0, 2)
            parts.append(part.reshape(LAYERS, GROUPS, -1).transpose(1, 0, 2).reshape(GROUPS, -1))
        every = jnp.concatenate(parts, 1)
    index = jnp.pad(rel_index + 1, ((0, PAIR - WTOK), (0, LANES - WTOK)))
    index = index + jnp.pad(rel_index + 1, ((WTOK, PAIR - 2 * WTOK), (WTOK, LANES - 2 * WTOK))) - 1
    ids = region_ids.astype(BF16)
    ids_col = jnp.broadcast_to(ids[:, None], (TOK, LANES))
    ids_row = jnp.broadcast_to(ids[None, :], (16, TOK))
    lanes_place = np.zeros((2 * LANES, TOK), np.float32)
    for pair in range(2):
        lanes_place[pair * LANES : pair * LANES + PAIR] = PLACE[0][pair * PAIR : (pair + 1) * PAIR]
    place = [jnp.asarray(PLACE[layer], BF16) for layer in range(LAYERS)]
    after = w_q0[:1] if direct else ()

    def bias_of(layer, after=()):
        return call(
            functools.partial(bias_kernel, layer),
            [VM] * 6,
            [every, index, ids_col, ids_row, place[0], jnp.asarray(lanes_place, BF16)],
            [pinned((1 + layer, HEADS, PAIR, LANES), F32)],
            flops=4 * GF,
            after=after,
        )[0]

    bias = [bias_of(0, after), None]
    step01 = jnp.asarray(PLACE[1] @ PLACE[0].T, BF16)
    step10 = jnp.asarray(PLACE[0] @ PLACE[1].T, BF16)
    group = jnp.asarray(GROUP, BF16)

    def row(v, layer):
        return v[layer][None]

    saved, w_q, w_m = [None] * LAYERS, [None] * LAYERS, [None] * LAYERS
    rels, littles, normed = [None] * LAYERS, [None] * LAYERS, [None] * LAYERS

    def attn(layer, state, w):
        res = attn_fwd(
            layer, batch, where, state, place[0], row(ln1_gain, layer), row(ln1_bias, layer),
            every, group, bias[layer], w,
        )
        *res, w_q[layer] = res
        x, res = (res[0], res[1:]) if layer == 0 else (state, res)
        normed[layer] = res[:2]
        saved[layer] = (x, *res[2:])

    def mlp(layer, w):
        x, n1, tri, e, rinv, ho = saved[layer]
        state, *rest, wp, w1, w2 = mlp_fwd(
            layer, batch, where, x, ho, row(proj_bias, layer), row(ln2_gain, layer),
            row(ln2_bias, layer), every, row(fc2_bias, layer), step01 if layer == 0 else place[1],
            w,
        )
        xhat, rstd, n2, act, dact = rest
        saved[layer] += ((xhat, rstd), n2, (act,), (dact,))
        w_m[layer] = (wp, (w1,), (w2,))
        return state

    def mlp_back(layer, grad, after=()):
        x, n1, tri, e, rinv, ho, mid, n2, act, dact = saved[layer]
        keep, send, gmid, dh, u, small2, db1 = mlp_bwd(
            layer, batch, where, grad, place[1], act, dact, mid, n2, ho, rinv,
            row(ln2_gain, layer), w_m[layer], after,
        )
        littles[layer] = {"a": small2, "b": db1}
        return (keep, send), gmid, dh, u

    def pair_back(grad, dtri, after=()):
        act, dact = saved[0][8:]
        keep, send, gp, littles[1]["c"] = pair_bwd(
            0, batch, where, grad, act, dact, w_m[0], saved[1][1], dtri, after
        )
        return (keep, send), gp

    def middle_back_0(gp, grad, after):
        x, n1, tri, e, rinv, ho, mid, n2, act, dact = saved[0]
        keep, send, gmid, dh, u, small2, db1 = middle_bwd(
            0, batch, where, gp, grad, mid, n2, ho, rinv, row(ln2_gain, 0), w_m[0], after
        )
        littles[0] = {"a": small2, "b": db1}
        return (keep, send), gmid, dh, u

    def attn_back(layer, dh, u, after=()):
        dtri, rels[layer] = attn_bwd(
            batch, where, dh, u, saved[layer][2], saved[layer][3], group, after
        )
        return dtri

    def qkv_back(layer, dtri, after=()):
        keep, send, small_q = qkv_grad(batch, where, saved[layer][1], dtri, after)
        littles[layer]["c"] = small_q
        return keep, send

    def input_back(layer, gmid, dtri, after=()):
        grad, small1 = input_bwd(
            layer, batch, where, gmid, normed[layer], dtri, row(ln1_gain, layer),
            step10 if layer else place[0], w_q[layer], after,
        )
        littles[layer]["d"] = small1
        return grad, small1

    def small_sums(after=()):
        args = [index.reshape(PAIR, 1, LANES), jnp.asarray(PICK, BF16)]
        for layer in range(LAYERS):
            args += [littles[layer][name] for name in "abcd"] + [rels[layer]]
        specs = [VM] * 2 + ([VM] * 4 + [VC]) * LAYERS
        return call(
            small_kernel, specs, args, [pinned((24 * LAYERS, C), F32)],
            [
                pltpu.VMEM((wide, 2 * LAYERS * HEADS), F32),
                pltpu.VMEM((LAYERS * HEADS * 56, LANES), F32),
            ],
            after=after, limit=4,
        )[0]

    if direct:
        w0 = Weights(own, w_q0, None)
        attn(0, images_in, w0)
        bias[1] = bias_of(1, saved[0][5:6])
        (m1,) = net.pack(own, [[(1, 3)]], after=(bias[1],))
        w0.p_m, m1_now = net.merge(near_m0, moved=(m1,))
        m1_x, m1_y = net.x(m1_now), net.y(m1_now)
        state = mlp(0, w0)
        (m1,) = net.step(passing=(m1,), after=(state,))
        m1_d = net.diagonal(m1)
        w1 = Weights(own, w0.p_m, None, M_ROWS)
        attn(1, state, w1)
        x, n1, tri, e, rinv, ho = saved[1]
        m1_x, m1_y = net.step(passing=(m1_x, m1_y), after=(ho,))
        far_x, far_y = net.other(m1_x), net.other(m1_y)
        mid, xhat, rstd, n2, acc, *first = mlp_open(
            1, batch, where, x, ho, row(proj_bias, 1), row(ln2_gain, 1), row(ln2_bias, 1), every,
            w1, M_ROWS + Q_ROWS, w0.p_m,
        )
        (m1_d,) = net.step(passing=(m1_d,), after=(acc,))
        far_d = net.other(m1_d)
        acc, *second = mlp_more(
            1, batch, where, every, n2, acc, (1, 2), (m1_x, far_x, m1_y, far_y), after=(m1_d,)
        )
        output, *third = mlp_more(
            1, batch, where, every, n2, acc, (3,), (m1_d, far_d),
            end=(mid, row(fc2_bias, 1), place[1]),
        )
        act, dact, wp, *w_first = first
        saved[1] += ((xhat, rstd), n2, (act, second[0], third[0]), (dact, second[1], third[1]))
        w_m[1] = (
            wp, (w_first[0], second[2], third[2]), (w_first[1], second[3], third[3])
        )

        m1, gmid, dh, u = mlp_back(1, out_cot, after=(output,))
        m1 = net.swap_cores(*m1)
        dtri = attn_back(1, dh, u)
        (g1,) = net.step(net.first_way(m1), after=(dtri,))
        g1 = net.send_first(g1)
        grad, _ = input_back(1, gmid, dtri, after=g1[:1])
        two, gp = pair_back(grad, dtri)
        two = net.swap_cores(*two)
        one, gmid, dh, u = middle_back_0(gp, grad, after=two[:1])
        g1, send = net.step(net.second_way(g1), passing=one[1:], after=(gmid,), weight=40)
        (g2,) = net.step(net.first_way(two), after=g1[:1])
        dtri = attn_back(0, dh, u, after=g2[:1])
        g1, g2 = net.send_second(g1), net.send_first(g2)
        one = net.swap_cores(one[0], send)
        q0 = qkv_back(0, dtri)
        g1, send = net.step(net.join(g1), passing=q0[1:], after=q0[:1])
        g1 = net.send_level(g1, 1)
        q0 = net.swap_cores(q0[0], send)
        (g3,) = net.step(net.first_way(one, q0), after=(g1[0],))
        grad, done = input_back(0, gmid, dtri, after=g3[:1])
        g3 = net.send_first(g3)
        ((g1,),) = net.step(net.add(g1), after=(done,))
        g1 = net.send_level((g1, g1), 2)
        little = small_sums(after=(g1[0],))
        g2, little = net.step(net.second_way(g2), passing=(little,))
        order = g2[2:3]
        g2 = net.send_second(g2)
        (g3,) = net.step(net.second_way(g3), after=order)
        order = g3[2:3]
        g3 = net.send_second(g3)
        g2, (g1,), little = net.step(
            net.join(g2), net.add(g1), passing=(little,), after=order
        )
        order = g2[:1]
        g2 = net.send_level(g2, 1)
        near1 = net.level(g1, 1)
        little = (little, net.other(little))
        g3, (little,) = net.step(net.join(g3), net.add_small(little), after=order)
        order = g3[:1]
        g3 = net.send_level(g3, 1)
        little = (little, net.x(little))
        (g2,), (little,), side1, near1 = net.step(
            net.add(g2), net.add_small(little), passing=(g1, near1), after=order
        )
        order = (g2,)
        g2 = net.send_level((g2, g2), 2)
        little = (little, net.y(little))
        g1 = [side1, near1, net.other(side1), net.other(near1)]
        (g3,), (little,) = net.step(net.add(g3), net.own_small(little), after=order)
        order = (g3,)
        g3 = net.send_level((g3, g3), 2)
        little = (little, net.level(little, 1))
        (g2,), (little,) = net.step(net.add(g2), net.add_small(little), after=order)
        near2, side2 = net.level(g2, 1), net.other(g2)
        little = (little, net.level(little, 2))
        results = net.finish([(M_ROWS, 1, ("1", "p", "2"))], g1, after=(g2,))
        (g3,), (little,), near2 = net.step(
            net.add(g3), net.add_small(little), passing=(near2,), after=results[4:]
        )
        near3, side3 = net.level(g3, 1), net.other(g3)
        g2 = [g2, near2, side2, net.other(near2)]
        small = list(net.unpack(little))
        results = net.finish(
            [(Q_ROWS, 1, ("q",)), (TWO_ROWS, 0, ("two",))], g2, results, after=small[9:]
        )
        (near3,) = net.step(passing=(near3,), after=results[4:])
        dwq, dwp, dw1, dw2, _ = net.finish(
            [(ONE_ROWS, 0, ("1", "p")), (Q_ROWS, 0, ("q",))],
            [g3, near3, side3, net.other(near3)], results,
        )
        small[8] = small[8].transpose(0, 2, 1)
        return (
            output, grad.transpose(1, 0, 2), small[0], small[1], dwq, small[7], small[8], dwp, small[2], small[3],
            small[4], dw1, small[6], dw2, small[5],
        )
    else:
        state = images_in
        bias[1] = bias_of(1)
        for layer in range(LAYERS):
            attn(layer, state, weights[layer])
            state = mlp(layer, weights[layer])
        output = state
        grad = out_cot
        reduced = [None] * LAYERS
        for layer in reversed(range(LAYERS)):
            m, gmid, dh, u = mlp_back(layer, grad)
            dtri = attn_back(layer, dh, u)
            reduced[layer] = (m, qkv_back(layer, dtri))
            grad, _ = input_back(layer, gmid, dtri)
        little = net.sum_small(small_sums())
        dwq, dwp, dw1, dw2 = net.finish(reduced)
    little = little.reshape(LAYERS, 24, C)
    small_q = little[:, 8:12, : 2 * LANES].reshape(LAYERS, -1)
    rel = little[:, 16:].reshape(LAYERS, 8, 2, wide)[..., :TABLE].transpose(0, 3, 2, 1)
    rel = rel.reshape(LAYERS, TABLE, HEADS)
    db1 = little[:, 4:8].reshape(LAYERS, FF)
    mine = lax.axis_index("tensor")

    def share(v, axis):
        size = v.shape[axis] // tensor
        return lax.dynamic_slice_in_dim(v, mine * size, size, axis)

    return (
        output, grad.transpose(1, 0, 2), little[:, 12], little[:, 13], dwq, share(small_q, 1), share(rel, 2), dwp,
        little[:, 3], little[:, 1], little[:, 2], dw1, share(db1, 1), dw2, little[:, 0],
    )


def solution(mesh):
    tokens = P(("dp", "tensor"), None, None)
    cols, rows = P(None, None, "tensor"), P(None, "tensor", None)
    part = P(None, "tensor")
    return jax.shard_map(
        functools.partial(shards, mesh.shape["tensor"], mesh.shape["dp"]),
        mesh=mesh,
        in_specs=(
            tokens, P(), P(), cols, part, cols, rows, P(), P(), P(), cols, part, rows, P(), P(),
            P(), tokens,
        ),
        out_specs=(
            tokens, tokens, P(), P(), cols, part, cols, rows, P(), P(), P(), cols, part, rows, P(),
        ),
        check_vma=False,
    )
```

```python
import functools

import jax
import jax.numpy as jnp
import numpy as np
from jax import lax
from jax.experimental import pallas as pl
from jax.experimental.pallas import tpu as pltpu
from jax.sharding import PartitionSpec as P

C = 512
HEADS = 16
HEAD_DIM = 32
FF = 2048
WIN = 7
GRID = 14
SHIFT = 3
LAYERS = 2
TOK = 196
WTOK = 49
TABLE = 169
PAIR = 112
LANES = 128
GROUPS = 4
GHEADS = HEADS // GROUPS
TRI = 3 * LANES
HID = FF // GROUPS
SCALE = HEAD_DIM ** (-0.5)
NEG = -1e30
F32 = jnp.float32
BF16 = jnp.bfloat16


def window_tokens(offset):
    cells = np.arange(TOK).reshape(GRID, GRID)
    cells = np.roll(cells, (-offset, -offset), (0, 1))
    cells = cells.reshape(2, WIN, 2, WIN).transpose(0, 2, 1, 3)
    return cells.reshape(4, WTOK)


def place_matrix(offset):
    tokens = window_tokens(offset).reshape(2, 2 * WTOK)
    out = np.zeros((2 * PAIR, TOK), np.float32)
    for pair in range(2):
        out[pair * PAIR + np.arange(2 * WTOK), tokens[pair]] = 1.0
    return out


PLACE = [place_matrix(SHIFT if layer % 2 == 1 else 0) for layer in range(LAYERS)]


def group_matrix():
    out = np.zeros((TRI, TRI), np.float32)
    for head in range(GHEADS):
        for part in range(3):
            for pos in range(HEAD_DIM):
                out[
                    (head * 3 + part) * HEAD_DIM + pos, (part * GHEADS + head) * HEAD_DIM + pos
                ] = 1.0
    return out


GROUP = group_matrix()


def pick_matrix():
    out = np.zeros((TRI, 2 * LANES), np.float32)
    for head in range(GHEADS):
        for to, part in enumerate((0, 2)):
            for pos in range(HEAD_DIM):
                out[(head * 3 + part) * HEAD_DIM + pos, (head * 2 + to) * HEAD_DIM + pos] = 1.0
    return out


PICK = pick_matrix()


def mm(a, b):
    return jnp.dot(a, b, preferred_element_type=F32)


def mm_nt(a, b):
    return lax.dot_general(a, b, (((1,), (1,)), ((), ())), preferred_element_type=F32)


def mm_tn(a, b):
    return lax.dot_general(a, b, (((0,), (0,)), ((), ())), preferred_element_type=F32)


def normalize(x):
    centre = x - jnp.mean(x, -1, keepdims=True)
    spread = jnp.mean(centre * centre, -1, keepdims=True)
    rstd = lax.rsqrt(spread + 1e-05)
    return centre * rstd, rstd


def norm_back(xhat, rstd, gain, grad):
    rstd = rstd[:, :1]
    scaled = grad * gain
    m1 = jnp.mean(scaled, -1, keepdims=True)
    m2 = jnp.mean(scaled * xhat, -1, keepdims=True)
    dx = rstd * (scaled - m1 - xhat * m2)
    return dx, jnp.sum(grad * xhat, 0, keepdims=True), jnp.sum(grad, 0, keepdims=True)


def rows_of(pair):
    return pl.ds(pl.multiple_of(pair * PAIR, 16), PAIR)


def head_mask(head):
    lane = lax.broadcasted_iota(jnp.int32, (PAIR, LANES), 1)
    return (lane // HEAD_DIM) == head


def stack_heads(block, masks):
    zero = jnp.zeros_like(block)
    pad = jnp.zeros((LANES - PAIR, LANES), block.dtype)
    parts = []
    for mask in masks:
        parts += [jnp.where(mask, block, zero), pad]
    return jnp.concatenate(parts, 0)


def split_exact(x):
    high = x.astype(BF16)
    return high, (x - high.astype(F32)).astype(BF16)


def half_rows(core, half):
    mine = pl.ds(pl.multiple_of(core * half, 16), half)
    other = pl.ds(pl.multiple_of((1 - core) * half, 16), half)
    return mine, other


Q_ROWS, M_ROWS = 192, 576
FIRST_ROWS = 224
PACK_Q = [(0, 0, Q_ROWS, TRI, 0, 0)] + [
    (Q_ROWS, j * LANES, 64, LANES, 64 * j, TRI) for j in range(3)
]
PACK_1 = [(0, 0, 256, C, 0, 0)]
PACK_P = [(0, 0, 64, C, 256, 0)]
PACK_2 = [(0, 0, 256, C, 320, 0)]
CHUNKS = (
    (((0, PACK_Q),), Q_ROWS),
    (((2, PACK_1), (1, PACK_P), (3, PACK_2)), M_ROWS),
    (((1, [(0, 0, 64, C, 0, 0)]),), 64),
    (((2, PACK_1), (3, [(0, 0, 256, C, 256, 0)])), 512),
)
ONE_ROWS, TWO_ROWS = 320, 256
PACK_TWO = [(0, 0, 256, C, 0, 0)]


def moved_down(blocks, base):
    return [block[:4] + (block[4] + base, block[5]) for block in blocks]


class Fetch:
    def __init__(self, full, layer, pieces, blocks, dest, core, sems):
        half = dest.shape[1] // 2
        self.copies = [[pltpu.make_async_copy(full.at[layer], dest.at[0], sems.at[0])]]
        at = 1
        for r in range(1, GROUPS):
            group = []
            if len(pieces) == 2:
                near, far = pieces[0].at[r - 1], pieces[1].at[r - 1]
            else:
                near, far = pieces[r - 1], pieces[r + 2]
            for side, piece in ((core, near), (1 - core, far)):
                for row, lane, rows, lanes, to_row, to_lane in blocks:
                    target = dest.at[
                        r,
                        pl.ds(pl.multiple_of(side * half + row, 16), rows),
                        pl.ds(lane, lanes),
                    ]
                    source = piece.at[pl.ds(to_row, rows), pl.ds(to_lane, lanes)]
                    group.append(pltpu.make_async_copy(source, target, sems.at[at]))
                    at += 1
            self.copies.append(group)
        for group in self.copies:
            for copy in group:
                copy.start()

    def wait(self, r):
        for copy in self.copies[r]:
            copy.wait()


def bias_kernel(layer, table, index, ids_col, ids_row, place, lanes_place, bias_ref):
    cols = mm(place[...], ids_col[...])
    rows = mm_nt(ids_row[...], lanes_place[...])
    masks = []
    for pair in range(2):
        col = cols[pair * PAIR : (pair + 1) * PAIR]
        row = rows[:1, pair * LANES : (pair + 1) * LANES]
        masks.append(jnp.where(col != row, -100.0, 0.0))
    idx = index[...]
    step = LAYERS * 2 * LANES
    at_low = jnp.clip(idx, 0, LANES - 1)
    at_high = jnp.clip(idx - LANES, 0, LANES - 1)

    def pick(low, high):
        low = jnp.take_along_axis(jnp.broadcast_to(low, (PAIR, LANES)), at_low, axis=1)
        high = jnp.take_along_axis(jnp.broadcast_to(high, (PAIR, LANES)), at_high, axis=1)
        return jnp.where(idx < 0, NEG, jnp.where(idx < LANES, low, high))

    for head in range(HEADS):
        r, lane = head // GHEADS, (head % GHEADS) * step + layer * 2 * LANES
        picked = pick(
            table[r : r + 1, lane : lane + LANES], table[r : r + 1, lane + LANES : lane + 2 * LANES]
        )
        if layer == 0:
            bias_ref[0, head] = picked
        else:
            bias_ref[0, head] = picked + masks[0]
            bias_ref[1, head] = picked + masks[1]


def attn_fwd_kernel(layer, pairs, base, *refs):
    first = layer == 0
    where, x_in, place, ln_g, ln_b, tables, group, bias, full_qkv = refs[:9]
    at = BIAS_AT + layer * TRI
    p_qkv, outs = refs[9:11], refs[11:]
    if first:
        x_ref, outs = outs[0], outs[1:]
    else:
        x_ref = x_in
    xhat_ref, rstd_ref, n1_ref, tri_ref, e_ref, rinv_ref, ho_ref, w_qkv, sem_q = outs
    qkv = Fetch(full_qkv, layer, p_qkv, moved_down(PACK_Q, base), w_qkv, where[1], sem_q)
    if first:
        for image in range(pairs // 2):
            x_ref[pl.ds(image * 2 * PAIR, 2 * PAIR), :] = mm(place[...], x_in[image])

    def norm_rows(pair, carry):
        rows = rows_of(pair)
        xhat, rstd = normalize(x_ref[rows, :])
        xhat_ref[rows, :] = xhat
        rstd_ref[rows, :] = jnp.broadcast_to(rstd, (PAIR, LANES))
        n1_ref[rows, :] = (xhat * ln_g[...] + ln_b[...]).astype(BF16)
        return carry

    lax.fori_loop(0, pairs, norm_rows, 0, unroll=True)
    masks = [head_mask(h) for h in range(GHEADS)]
    ones = jnp.ones((PAIR, LANES), BF16)
    for r in range(GROUPS):
        qkv.wait(r)
        tri = (mm(n1_ref[...], w_qkv[r]) + tables[r : r + 1, at : at + TRI]).astype(BF16)
        tri_ref[r] = mm(tri, group[...]).astype(BF16)
        ones_stack = stack_heads(ones, masks)

        def pair_step(pair, carry):
            rows = rows_of(pair)
            q4 = tri_ref[r, rows, 0:LANES]
            k4 = tri_ref[r, rows, LANES : 2 * LANES]
            v4 = tri_ref[r, rows, 2 * LANES : 3 * LANES]
            s4 = mm_nt(q4, stack_heads(k4, masks))
            kind = 0 if first else lax.rem(pair, 2)
            es = []
            for h in range(GHEADS):
                s = s4[:, h * LANES : (h + 1) * LANES] * SCALE + bias[kind, r * GHEADS + h]
                es.append(jnp.exp(s - jnp.max(s, -1, keepdims=True)).astype(BF16))
            e4 = jnp.concatenate(es, 1)
            e_ref[r, pair] = e4
            vm = jnp.concatenate([stack_heads(v4, masks), ones_stack], 1)
            out = mm(e4, vm)
            rinv = 1.0 / out[:, LANES:]
            rinv_ref[r, rows, :] = rinv
            ho_ref[rows, r * LANES : (r + 1) * LANES] = (out[:, :LANES] * rinv).astype(BF16)
            return carry

        lax.fori_loop(0, pairs, pair_step, 0, unroll=True)


def mlp_fwd_kernel(layer, pairs, count, *refs):
    last = layer == LAYERS - 1
    where, x, ho, b_proj, ln_g, ln_b, tables, b2, place = refs[:9]
    at = HIDDEN_AT + layer * HID
    full_p, full_1, full_2 = refs[9:12]
    p_m, refs = refs[12 : 12 + count], refs[12 + count :]
    out_ref, xhat_ref, rstd_ref, n2_ref, act_ref, dact_ref, wp, w1, w2 = refs[:9]
    sem_p, sem_1, sem_2, acc, pre_ref, mid = refs[9:]
    core = where[1]
    f_p = Fetch(full_p, layer, p_m, PACK_P, wp, core, sem_p)
    f_1 = Fetch(full_1, layer, p_m, PACK_1, w1, core, sem_1)
    f_2 = Fetch(full_2, layer, p_m, PACK_2, w2, core, sem_2)
    for r in range(GROUPS):
        f_p.wait(r)
    weight = jnp.concatenate([wp[r] for r in range(GROUPS)], 0)
    mid[...] = x[...] + mm(ho[...], weight) + b_proj[...]

    def norm_rows(pair, carry):
        rows = rows_of(pair)
        xhat, rstd = normalize(mid[rows, :])
        xhat_ref[rows, :] = xhat
        rstd_ref[rows, :] = jnp.broadcast_to(rstd, (PAIR, LANES))
        n2_ref[rows, :] = (xhat * ln_g[...] + ln_b[...]).astype(BF16)
        return carry

    lax.fori_loop(0, pairs, norm_rows, 0, unroll=True)
    for r in range(GROUPS):
        f_1.wait(r)
        pre_ref[...] = mm(n2_ref[...], w1[r])
        b1_row = tables[r : r + 1, at : at + HID]

        def gelu_rows(step, carry):
            rows = pl.ds(pl.multiple_of(step * 16, 16), 16)
            pre = pre_ref[rows, :] + b1_row
            cdf = 0.5 + 0.5 * lax.erf(pre * (0.5**0.5))
            act_ref[r, rows, :] = (pre * cdf).astype(BF16)
            pdf = jnp.exp(-0.5 * pre * pre) * 0.3989422804014327
            dact_ref[r, rows, :] = (cdf + pre * pdf).astype(BF16)
            return carry

        lax.fori_loop(0, pairs * (PAIR // 16), gelu_rows, 0, unroll=4)
        f_2.wait(r)
        part = mm(act_ref[r], w2[r])
        if r == 0:
            acc[...] = part
        else:
            acc[...] += part
    acc[...] = acc[...] + mid[...] + b2[...]
    for image in range(pairs // 2):
        state = acc[pl.ds(image * 2 * PAIR, 2 * PAIR), :]
        if last:
            out_ref[image] = mm_tn(place[...], state.astype(BF16)).astype(BF16)
        else:
            high, low = split_exact(state)
            out_ref[pl.ds(image * 2 * PAIR, 2 * PAIR), :] = mm(place[...], high) + mm(
                place[...], low
            )


X_FIRST = (0, 2, 1, 3)
Y_FIRST = (0, 1, 2, 3)
ORDERS = (X_FIRST, Y_FIRST)


def give(keep_ref, send_ref, tmp, r, core, blocks, first=0, size=None):
    half = tmp.shape[0] // 2
    size = size or keep_ref.shape[2]
    for ref, base in ((keep_ref, core * half), (send_ref, (1 - core) * half)):
        for row, lane, rows, lanes, to_row, to_lane in blocks:
            done = 0
            while done < rows:
                part, at = divmod(to_row + done, size)
                count = min(rows - done, size - at)
                to = slice(first + at, first + at + count)
                ref[part, ORDERS[part].index(r), to, to_lane : to_lane + lanes] = tmp[
                    pl.ds(pl.multiple_of(base + row + done, 16), count), lane : lane + lanes
                ]
                done += count


class Joined:
    def __init__(self, refs):
        self.refs = refs

    def __getitem__(self, r):
        for ref in self.refs:
            if r < ref.shape[0]:
                return ref[r]
            r -= ref.shape[0]


def gelu_into(pairs, pre_ref, b1_row, act_ref, dact_ref, at):
    def some_rows(step, carry):
        rows = pl.ds(pl.multiple_of(step * 16, 16), 16)
        pre = pre_ref[rows, :] + b1_row
        cdf = 0.5 + 0.5 * lax.erf(pre * (0.5**0.5))
        act_ref[at, rows, :] = (pre * cdf).astype(BF16)
        pdf = jnp.exp(-0.5 * pre * pre) * 0.3989422804014327
        dact_ref[at, rows, :] = (cdf + pre * pdf).astype(BF16)
        return carry

    lax.fori_loop(0, pairs * (PAIR // 16), some_rows, 0, unroll=4)


def mlp_open_kernel(layer, pairs, base, *refs):
    where, x, ho, b_proj, ln_g, ln_b, tables, full_p, full_1, full_2 = refs[:10]
    pieces, refs = refs[10:12], refs[12:]
    mid, xhat_ref, rstd_ref, n2_ref, acc, act_ref, dact_ref, wp, w1, w2, sem_p, sem_w, pre_ref = refs
    f_p = Fetch(full_p, layer, pieces, moved_down(PACK_P, base - 256), wp, where[1], sem_p)
    copies = [
        pltpu.make_async_copy(full.at[layer], w.at[0], sem_w.at[i])
        for i, (full, w) in enumerate(((full_1, w1), (full_2, w2)))
    ]
    for copy in copies:
        copy.start()
    for r in range(GROUPS):
        f_p.wait(r)
    weight = jnp.concatenate([wp[r] for r in range(GROUPS)], 0)
    mid[...] = x[...] + mm(ho[...], weight) + b_proj[...]

    def norm_rows(pair, carry):
        rows = rows_of(pair)
        xhat, rstd = normalize(mid[rows, :])
        xhat_ref[rows, :] = xhat
        rstd_ref[rows, :] = jnp.broadcast_to(rstd, (PAIR, LANES))
        n2_ref[rows, :] = (xhat * ln_g[...] + ln_b[...]).astype(BF16)
        return carry

    lax.fori_loop(0, pairs, norm_rows, 0, unroll=True)
    for copy in copies:
        copy.wait()
    at = HIDDEN_AT + layer * HID
    pre_ref[...] = mm(n2_ref[...], w1[0])
    gelu_into(pairs, pre_ref, tables[0:1, at : at + HID], act_ref, dact_ref, 0)
    acc[...] = mm(act_ref[0], w2[0])


def mlp_more_kernel(layer, pairs, shares, last, *refs):
    where, tables, n2, acc_in = refs[:4]
    count = 2 * len(shares)
    pieces, refs = refs[4 : 4 + count], refs[4 + count :]
    if last:
        mid, b2, place, out_ref, act_ref, dact_ref, w1, w2, sems, pre_ref, acc = refs
    else:
        acc, act_ref, dact_ref, w1, w2, sems, pre_ref = refs
    copies = []
    for i in range(len(shares)):
        group = []
        for side, c in enumerate((where[1], 1 - where[1])):
            for k, w in enumerate((w1, w2)):
                half = w.shape[1] // 2
                target = w.at[i, pl.ds(pl.multiple_of(c * half, 16), half)]
                source = pieces[2 * i + side].at[pl.ds(k * half, half)]
                group.append(pltpu.make_async_copy(source, target, sems.at[4 * i + 2 * side + k]))
        for copy in group:
            copy.start()
        copies.append(group)
    at = HIDDEN_AT + layer * HID
    for i, r in enumerate(shares):
        for copy in copies[i]:
            copy.wait()
        pre_ref[...] = mm(n2[...], w1[i])
        gelu_into(pairs, pre_ref, tables[r : r + 1, at : at + HID], act_ref, dact_ref, i)
        part = mm(act_ref[i], w2[i])
        if i == 0:
            acc[...] = acc_in[...] + part
        else:
            acc[...] += part
    if last:
        for image in range(pairs // 2):
            rows = pl.ds(image * 2 * PAIR, 2 * PAIR)
            state = acc[rows, :] + mid[rows, :] + b2[...]
            out_ref[image] = mm_tn(place[...], state.astype(BF16)).astype(BF16)


def hidden_back(layer, pairs, where, g_in, place, act, dact, w2, g_ref, gb_ref, gp_ref, tmp, outs, blocks, first=0, size=None):
    keep, send = outs
    core = where[1]
    if layer == LAYERS - 1:
        for image in range(pairs // 2):
            rows = pl.ds(image * 2 * PAIR, 2 * PAIR)
            g = mm(place[...], g_in[image])
            g_ref[rows, :] = g
            gb_ref[rows, :] = g.astype(BF16)
    else:
        gb_ref[...] = g_ref[...].astype(BF16)
    for r in range(GROUPS):
        tmp[...] = mm_tn(act[r], gb_ref[...]).astype(BF16)
        give(keep, send, tmp, r, core, blocks, first, size)
        ga = mm_nt(gb_ref[...], w2[r])
        gp_ref[r] = (ga * dact[r].astype(F32)).astype(BF16)


def middle_back(layer, pairs, where, gp_ref, g_ref, mid, n2, ho, rinv, ln_g, w1, wp, gb_ref, acc, tmp, tmp_p, outs):
    keep, send, gmid_ref, dh_ref, u_ref, small_ref, db1_ref = outs
    tid, core = where[0], where[1]
    small_ref[...] = jnp.zeros_like(small_ref)
    for r in range(GROUPS):
        db1_ref[tid ^ r] = jnp.sum(gp_ref[r].astype(F32), 0, keepdims=True)
        tmp[...] = mm_tn(n2[...], gp_ref[r]).astype(BF16)
        give(keep, send, tmp, r, core, PACK_1)
        part = mm_nt(gp_ref[r], w1[r])
        if r == 0:
            acc[...] = part
        else:
            acc[...] += part

    def back_rows(pair, carry):
        rows = rows_of(pair)
        g_rows = g_ref[rows, :]
        dx, dg, db = norm_back(mid[0][rows, :], mid[1][rows, :], ln_g[...], acc[rows, :])
        gmid = g_rows + dx
        gmid_ref[rows, :] = gmid
        gb_ref[rows, :] = gmid.astype(BF16)
        small_ref[0:1, :] += jnp.sum(g_rows, 0, keepdims=True)
        small_ref[1:2, :] += dg
        small_ref[2:3, :] += db
        small_ref[3:4, :] += jnp.sum(gmid, 0, keepdims=True)
        return carry

    lax.fori_loop(0, pairs, back_rows, 0, unroll=True)
    for r in range(GROUPS):
        lanes = slice(r * LANES, (r + 1) * LANES)
        tmp_p[...] = mm_tn(ho[:, lanes], gb_ref[...]).astype(BF16)
        give(keep, send, tmp_p, r, core, PACK_P)
        gh = mm_nt(gb_ref[...], wp[r]) * rinv[r]
        dh_ref[r] = gh.astype(BF16)
        u_ref[r] = (gh * ho[:, lanes].astype(F32)).astype(BF16)


def mlp_bwd_kernel(layer, pairs, count, *refs):
    where, g_in, place = refs[:3]
    act, dact = Joined(refs[3 : 3 + count]), Joined(refs[3 + count : 3 + 2 * count])
    xhat, rstd, n2, ho, rinv, ln_g, wp = refs[3 + 2 * count : 10 + 2 * count]
    mid = (xhat, rstd)
    refs = refs[10 + 2 * count :]
    w1, w2 = Joined(refs[:count]), Joined(refs[count : 2 * count])
    outs = refs[2 * count : 2 * count + 7]
    g_ref, gb_ref, gp_ref, acc, tmp, tmp_p = refs[2 * count + 7 :]
    if layer < LAYERS - 1:
        g_ref = g_in
    hidden_back(
        layer, pairs, where, g_in, place, act, dact, w2, g_ref, gb_ref, gp_ref, tmp, outs[:2], PACK_2
    )
    middle_back(
        layer, pairs, where, gp_ref, g_ref, mid, n2, ho, rinv, ln_g, w1, wp, gb_ref, acc, tmp, tmp_p,
        outs,
    )


def pair_bwd_kernel(layer, pairs, where, g, act, dact, w2, n1, dtri, keep, send, gp_ref, small_ref, gb_ref, tmp, tmp_q):
    hidden_back(
        layer, pairs, where, g, None, act, dact, w2, g, gb_ref, gp_ref, tmp, (keep, send), PACK_TWO,
        Q_ROWS // 2, TWO_ROWS // 2,
    )
    qkv_grad_kernel(pairs, where, n1, dtri, keep, send, small_ref, tmp_q, Q_ROWS // 2)


def middle_bwd_kernel(layer, pairs, *refs):
    where, gp, g, xhat, rstd, n2, ho, rinv, ln_g, wp, w1 = refs[:11]
    mid = (xhat, rstd)
    gb_ref, acc, tmp, tmp_p = refs[18:]
    middle_back(
        layer, pairs, where, gp, g, mid, n2, ho, rinv, ln_g, w1, wp, gb_ref, acc, tmp, tmp_p,
        refs[11:18],
    )


def attn_bwd_kernel(pairs, where, dh, u, tri, e, group, dtri_ref, rel_ref, low_ref):
    tid = where[0]
    masks = [head_mask(h) for h in range(GHEADS)]
    neg_ones = jnp.full((PAIR, LANES), -1.0, BF16)
    for r in range(GROUPS):
        sid = tid ^ r
        neg_stack = stack_heads(neg_ones, masks)

        def pair_step(pair, carry):
            rows = rows_of(pair)
            q4 = tri[r, rows, 0:LANES]
            k4 = tri[r, rows, LANES : 2 * LANES]
            v4 = tri[r, rows, 2 * LANES : 3 * LANES]
            dh4 = dh[r, rows, :]
            left = jnp.concatenate([dh4, u[r, rows, :]], 1)
            right = jnp.concatenate([stack_heads(v4, masks), neg_stack], 1)
            dsp = mm_nt(left, right)
            e4 = e[r, pair]
            ds4 = e4.astype(F32) * dsp
            for h in range(GHEADS):
                part = ds4[:, h * LANES : (h + 1) * LANES]
                head = sid * GHEADS + h
                rel_ref[head] = jnp.where(pair == 0, part, rel_ref[head] + part)
            dsb = (ds4 * SCALE).astype(BF16)
            dq4 = mm(dsb, stack_heads(k4, masks))
            pad = jnp.zeros((LANES - PAIR, GHEADS * LANES), BF16)
            dsb_p = jnp.concatenate([dsb, pad], 0)
            e4_p = jnp.concatenate([e4, pad], 0)

            def flip(block):
                return jnp.concatenate(
                    [block[:, h * LANES : (h + 1) * LANES].T for h in range(GHEADS)], 1
                )[:PAIR]

            dk4 = mm(flip(dsb_p), stack_heads(q4, masks))
            dv4 = mm(flip(e4_p), stack_heads(dh4, masks))
            low_ref[rows, :] = jnp.concatenate([dq4, dk4, dv4], 1).astype(BF16)
            return carry

        lax.fori_loop(0, pairs, pair_step, 0, unroll=True)
        dtri_ref[r] = mm_nt(low_ref[...], group[...]).astype(BF16)


def qkv_grad_kernel(pairs, where, n1, dtri, keep, send, small_ref, tmp, size=None):
    tid, core = where[0], where[1]
    for r in range(GROUPS):
        tmp[...] = mm_tn(n1[...], dtri[r]).astype(BF16)
        give(keep, send, tmp, r, core, PACK_Q, 0, size)
        small_ref[tid ^ r] = jnp.sum(dtri[r].astype(F32), 0, keepdims=True)


def input_bwd_kernel(layer, pairs, where, gmid, xhat, xscale, dtri, ln_g, place, w_qkv, gout_ref, small_ref, acc):
    last = layer == 0
    for r in range(GROUPS):
        part = mm_nt(dtri[r], w_qkv[r])
        if r == 0:
            acc[...] = part
        else:
            acc[...] += part
    small_ref[...] = jnp.zeros_like(small_ref)

    def back_rows(pair, carry):
        rows = rows_of(pair)
        dx, dg, db = norm_back(xhat[rows, :], xscale[rows, :], ln_g[...], acc[rows, :])
        acc[rows, :] = gmid[rows, :] + dx
        small_ref[0:1, :] += dg
        small_ref[1:2, :] += db
        return carry

    lax.fori_loop(0, pairs, back_rows, 0, unroll=True)
    for image in range(pairs // 2):
        grad = acc[pl.ds(image * 2 * PAIR, 2 * PAIR), :]
        if last:
            gout_ref[:, image, :] = mm_tn(place[...], grad.astype(BF16)).astype(BF16)
        else:
            high, low = split_exact(grad)
            gout_ref[pl.ds(image * 2 * PAIR, 2 * PAIR), :] = mm(place[...], high) + mm(
                place[...], low
            )


def pack_start(plan, where, weights, outs, sems):
    core = where[1]
    moves = []
    for weight, layer, out, blocks in plan:
        weight, out = weights[weight], outs[out]
        half = weight.shape[1] // 2
        for row, lane, rows, lanes, to_row, to_lane in blocks:
            from_row = pl.multiple_of(core * half + row, 16)
            moves.append(
                (
                    weight.at[layer, pl.ds(from_row, rows), pl.ds(lane, lanes)],
                    out.at[pl.ds(to_row, rows), pl.ds(to_lane, lanes)],
                )
            )
    copies = [pltpu.make_async_copy(a, b, sems.at[i]) for i, (a, b) in enumerate(moves)]
    for copy in copies:
        copy.start()

    def end():
        for copy in copies:
            copy.wait()

    return end


def merge_kernel(where, a, b, c, out, sems):
    copies = [pltpu.make_async_copy(v, out.at[i], sems.at[i]) for i, v in enumerate((a, b, c))]
    for copy in copies:
        copy.start()
    for copy in copies:
        copy.wait()


def three_parts(v):
    high = v.astype(BF16)
    rest = v - high.astype(F32)
    mid = rest.astype(BF16)
    return high, mid, (rest - mid.astype(F32)).astype(BF16)


def own_tables(table, qv, b1, out):
    out[...] = jnp.zeros_like(out)
    at = lax.broadcasted_iota(jnp.int32, (2 * LANES, TRI), 0)
    to = lax.broadcasted_iota(jnp.int32, (2 * LANES, TRI), 1)
    same = jnp.logical_and(at // 64 == to // 96, at % HEAD_DIM == to % HEAD_DIM)
    same = jnp.logical_and(same, 2 * ((at // HEAD_DIM) % 2) == (to // HEAD_DIM) % 3)
    spread = jnp.where(same, 1.0, 0.0).astype(BF16)
    for layer in range(LAYERS):
        for head in range(GHEADS):
            lane = (head * LAYERS + layer) * 2 * LANES
            out[:, lane : lane + TABLE] = table[layer, head : head + 1, :]
        lane = BIAS_AT + layer * TRI
        out[:, lane : lane + TRI] = exact_pick(qv[layer : layer + 1, :], spread)
        lane = HIDDEN_AT + layer * HID
        out[:, lane : lane + HID] = b1[layer : layer + 1, :]


def put_tables(tables, out):
    cols = tables.shape[1]
    out[Q_ROWS:, :] = jnp.zeros((out.shape[0] - Q_ROWS, C), BF16)
    for part, v in enumerate(three_parts(tables[...])):
        for row in range(8):
            lanes = min(C, cols - row * C)
            at = Q_ROWS + 8 * part + row
            out[at : at + 1, 0:lanes] = v[:, row * C : row * C + lanes]


def take_tables(tables, near, every):
    cols = tables.shape[1]
    every[0:1, :] = tables[...]
    for r in range(1, GROUPS):
        wide = near[r - 1, Q_ROWS : Q_ROWS + 24, :].astype(F32)
        total = wide[0:8] + wide[8:16] + wide[16:24]
        for row in range(8):
            lanes = min(C, cols - row * C)
            every[r : r + 1, row * C : row * C + lanes] = total[row : row + 1, 0:lanes]


def exact_pick(row, chosen):
    parts = jnp.concatenate([*three_parts(row), jnp.zeros((13, row.shape[1]), BF16)], 0)
    got = mm(parts, chosen)
    return got[0:1] + got[1:2] + got[2:3]


def small_kernel(index, *refs):
    out, acc, folded = refs[-3:]
    out[...] = jnp.zeros_like(out)
    folded[...] = jnp.zeros_like(folded)
    pick = refs[0]
    for layer in range(LAYERS):
        small2, db1, small_q, small1, rel = refs[5 * layer + 1 : 5 * layer + 6]
        base = 24 * layer
        out[base : base + 4, :] = small2[...]
        for r in range(GROUPS):
            out[base + 4 + r : base + 5 + r, :] = db1[r]
            out[base + 8 + r : base + 9 + r, 0 : 2 * LANES] = exact_pick(small_q[r], pick[...])
        out[base + 12 : base + 14, :] = small1[...]

        def fold(head, carry, layer=layer, rel=rel):
            second = pltpu.roll(rel[head, WTOK : 2 * WTOK, :], LANES - WTOK, 1)
            at = pl.multiple_of((layer * HEADS + head) * 56, 8)
            folded[pl.ds(at, WTOK), :] = rel[head, 0:WTOK, :] + second
            return carry

        lax.fori_loop(0, HEADS, fold, 0)
    entry = lax.broadcasted_iota(jnp.int32, (2 * LANES, LANES), 0)
    count = LAYERS * HEADS
    acc[...] = jnp.zeros_like(acc)

    def two_rows(step, carry):
        hots, parts = [], []
        for i in (2 * step, 2 * step + 1):
            hots.append(jnp.where(entry == index[i], 1.0, 0.0).astype(BF16))
            high, low = split_exact(folded[pl.ds(i, count, stride=56), :])
            parts.append(jnp.concatenate([high, low], 0))
        acc[...] += mm_nt(jnp.concatenate(hots, 1), jnp.concatenate(parts, 1))
        return carry

    lax.fori_loop(0, (WTOK + 1) // 2, two_rows, 0, unroll=5)
    total = acc[...].T
    total = total[:count] + total[count:]
    for layer in range(LAYERS):
        for part in range(2):
            at = layer * HEADS + part * 8
            out[24 * layer + 16 : 24 * layer + 24, part * 2 * LANES : (part + 1) * 2 * LANES] = total[
                at : at + 8, :
            ]


def add_go_kernel(where, *refs):
    count = (len(refs) - 4) // 2
    go_a, go_b, stay_a, stay_b = refs[-4:]
    row = 0
    for i in range(count):
        keep, got = refs[2 * i], refs[2 * i + 1]
        size = keep.shape[2]
        rows = slice(row, row + size)
        for part, (stay, go) in enumerate(((stay_a, go_a), (stay_b, go_b))):
            stay[:, rows, :] = keep[part, :2] + got[part, :2]
            go[:, rows, :] = keep[part, 2:] + got[part, 2:]
        row += size


def add_next_kernel(where, stay_a, stay_b, got_a, got_b, next_a, next_b, keep_a, keep_b):
    next_a[...] = stay_a[1] + got_a[1]
    next_b[...] = stay_b[1] + got_b[1]
    keep_a[...] = stay_a[0] + got_a[0]
    keep_b[...] = stay_b[0] + got_b[0]


def add_whole_kernel(where, keep_a, keep_b, got_a, got_b, out):
    size = keep_a.shape[0]
    out[0:size, :] = keep_a[...] + got_a[...]
    out[size:, :] = keep_b[...] + got_b[...]


def choose_kernel(where, mine, got, out):
    end = jnp.logical_or(where[2] == 0, where[2] == 3)
    out[...] = jnp.where(end, got[...], mine[...])


def add_level_kernel(where, keep_a, keep_b, got_a, got_b, mine, send):
    odd = where[2] & 1
    a = keep_a[...] + got_a[...]
    b = keep_b[...] + got_b[...]
    mine[...] = jnp.where(odd == 1, b, a)
    send[...] = jnp.where(odd == 1, a, b)


def add_kernel(where, a, b, out):
    out[...] = a[...] + b[...]


FINISH = {"q": (0, PACK_Q), "p": (1, PACK_P), "1": (2, PACK_1), "2": (3, PACK_2), "two": (3, PACK_TWO)}


def finish_kernel(plan, count, made, where, *refs):
    pieces = refs[:made]
    scratch, sems = refs[count + 5 : -1], refs[-1]
    core, odd = where[1], where[2] & 1
    copies = []
    first, slot = 0, 0
    results = refs[count : count + 4]
    for total, layer, names in plan:
        size = total // 2
        for name in names:
            index, blocks = FINISH[name]
            out = scratch[slot]
            half = out.shape[0] // 2
            for at, piece in enumerate(pieces):
                c = core if at < len(pieces) // 2 else 1 - core
                if len(pieces) == 2:
                    for row, lane, rows, lanes, to_row, to_lane in blocks:
                        target = pl.multiple_of(c * half + row, 16)
                        out[pl.ds(target, rows), lane : lane + lanes] = piece[
                            first + to_row : first + to_row + rows, to_lane : to_lane + lanes
                        ].astype(F32)
                    continue
                for part in range(2):

                    @pl.when((odd if at % 2 == 0 else 1 - odd) == part)
                    def _(piece=piece, part=part, c=c, out=out, first=first, size=size, blocks=blocks):
                        for row, lane, rows, lanes, to_row, to_lane in blocks:
                            begin = max(to_row, part * size)
                            end = min(to_row + rows, (part + 1) * size)
                            if begin >= end:
                                continue
                            target = pl.multiple_of(c * half + row + begin - to_row, 16)
                            source = first + begin - part * size
                            out[pl.ds(target, end - begin), lane : lane + lanes] = piece[
                                source : source + end - begin, to_lane : to_lane + lanes
                            ].astype(F32)

            copies.append(pltpu.make_async_copy(out, results[index].at[layer], sems.at[slot]))
            copies[-1].start()
            slot += 1
        first += size * (1 if len(pieces) == 4 else 2)
    for copy in copies:
        copy.wait()


def own_kernel(where, little, got, out):
    tid = where[0]
    out[...] = jnp.zeros_like(out)
    for layer in range(LAYERS):
        base, to = 24 * layer, 16 * layer

        def put(rows, row, lane, lanes):
            out[to + rows[0] : to + rows[1], 0:lanes] = (
                little[base + row : base + row + rows[1] - rows[0], lane : lane + lanes]
                + got[base + row : base + row + rows[1] - rows[0], lane : lane + lanes]
            )

        put((0, 4), 0, 0, C)
        put((4, 6), 12, 0, C)
        for r in range(GROUPS):

            @pl.when(tid == r)
            def _(r=r, put=put):
                put((6, 7), 4 + r, 0, C)
                put((7, 8), 8 + r, 0, 2 * LANES)
                put((8, 12), 16 + GHEADS * (r % 2), 2 * LANES * (r // 2), 2 * LANES)


def unpack_kernel(where, little, *outs):
    for layer in range(LAYERS):
        base = 16 * layer
        for out, at in zip(outs[:7], (4, 5, 3, 1, 2, 0, 6)):
            out[layer : layer + 1, :] = little[base + at : base + at + 1, :]
        outs[7][layer : layer + 1, :] = little[base + 7 : base + 8, 0 : 2 * LANES]
        outs[8][layer] = little[base + 8 : base + 12, 0:TABLE]


VM = pl.BlockSpec(memory_space=pltpu.VMEM)
SM = pl.BlockSpec(memory_space=pltpu.SMEM)
ANY = pl.BlockSpec(memory_space=pl.ANY)
VC = pl.BlockSpec(memory_space=pltpu.VMEM)
HB = pl.BlockSpec(memory_space=pltpu.HBM)


def pinned(shape, dtype):
    return pltpu.VMEM(shape, dtype)


def place_operand(spec, value):
    if spec is VC:
        return pltpu.with_memory_space_constraint(value, pltpu.VMEM)
    if spec is HB:
        return pltpu.with_memory_space_constraint(value, pltpu.HBM)
    return value


def call(
    kernel, specs, args, outs, scratch=(), flops=0, out_specs=None, limit=2, moved=4, after=(), aliases=None,
    weight=0,
):
    count = len(args)
    skip = count + len(after)

    def body(*refs):
        kernel(*refs[:count], *refs[skip:])

    return pl.pallas_call(
        body,
        out_shape=outs,
        in_specs=list(specs) + [ANY] * len(after),
        out_specs=[VM] * len(outs) if out_specs is None else out_specs,
        scratch_shapes=scratch,
        input_output_aliases=aliases or {},
        compiler_params=pltpu.CompilerParams(vmem_limit_bytes=limit << 20),
        cost_estimate=pl.CostEstimate(flops=1 + weight * GF, bytes_accessed=1, transcendentals=0),
    )(*[place_operand(spec, arg) for spec, arg in zip(specs, args)], *after)


def struct(shape, dtype):
    return jax.ShapeDtypeStruct(shape, dtype)


DIM_Q, DIM_P, DIM_1, DIM_2 = (C, TRI), (LANES, C), (C, HID), (HID, C)
GF = 1 << 30
BIAS_AT = GHEADS * LAYERS * 2 * LANES
HIDDEN_AT = BIAS_AT + LAYERS * TRI


def fetch_sems(*dims):
    return [
        pltpu.SemaphoreType.DMA((1 + 6 * (len(PACK_Q) if d == DIM_Q else 1),)) for d in dims
    ]


def chunk_outs(rows):
    return [pinned((2, GROUPS, rows // 2, C), BF16)] * 2


def attn_fwd(layer, batch, where, x, place, ln_g, ln_b, tables, group, bias, w):
    pairs = 2 * batch
    rows = pairs * PAIR
    outs = [
        pinned((rows, C), F32),
        pinned((rows, LANES), F32),
        pinned((rows, C), BF16),
        pinned((GROUPS, rows, TRI), BF16),
        pinned((GROUPS, pairs, PAIR, GHEADS * LANES), BF16),
        pinned((GROUPS, rows, LANES), F32),
        pinned((rows, C), BF16),
        pinned((GROUPS,) + DIM_Q, BF16),
    ]
    if layer == 0:
        outs = [pinned((rows, C), F32)] + outs
    return call(
        functools.partial(attn_fwd_kernel, layer, pairs, w.q_base),
        [SM, VM if layer == 0 else VC] + [VM] * 5 + [VC] + [HB] + [ANY] * 2,
        [where, x, place, ln_g, ln_b, tables, group, bias, *w.qkv],
        outs,
        fetch_sems(DIM_Q),
        flops=8 * GF,
        limit=9,
    )


def mlp_fwd(layer, batch, where, x, ho, b_proj, ln_g, ln_b, tables, b2, place, w):
    pairs = 2 * batch
    rows = pairs * PAIR
    last = layer == LAYERS - 1
    outs = [
        struct((batch, TOK, C), BF16) if last else pinned((rows, C), F32),
        pinned((rows, C), F32),
        pinned((rows, LANES), F32),
        pinned((rows, C), BF16),
        pinned((GROUPS, rows, HID), BF16),
        pinned((GROUPS, rows, HID), BF16),
    ] + [pinned((GROUPS,) + dim, BF16) for dim in (DIM_P, DIM_1, DIM_2)]
    return call(
        functools.partial(mlp_fwd_kernel, layer, pairs, len(w.p_m)),
        [SM, VC, VC] + [VM] * 6 + [HB] * 3 + [ANY] * len(w.p_m),
        [where, x, ho, b_proj, ln_g, ln_b, tables, b2, place, w.own_p, w.own_1, w.own_2, *w.p_m],
        outs,
        fetch_sems(DIM_P, DIM_1, DIM_2)
        + [pltpu.VMEM((rows, C), F32), pltpu.VMEM((rows, HID), F32), pltpu.VMEM((rows, C), F32)],
        flops=8 * GF,
        limit=12,
    )


def mlp_open(layer, batch, where, x, ho, b_proj, ln_g, ln_b, tables, w, base, pieces):
    pairs = 2 * batch
    rows = pairs * PAIR
    return call(
        functools.partial(mlp_open_kernel, layer, pairs, base),
        [SM, VC, VC] + [VM] * 4 + [HB] * 3 + [ANY] * 2,
        [where, x, ho, b_proj, ln_g, ln_b, tables, w.own_p, w.own_1, w.own_2, *pieces],
        [
            pinned((rows, C), F32),
            pinned((rows, C), F32),
            pinned((rows, LANES), F32),
            pinned((rows, C), BF16),
            pinned((rows, C), F32),
            pinned((1, rows, HID), BF16),
            pinned((1, rows, HID), BF16),
            pinned((GROUPS,) + DIM_P, BF16),
            pinned((1,) + DIM_1, BF16),
            pinned((1,) + DIM_2, BF16),
        ],
        fetch_sems(DIM_P) + [pltpu.SemaphoreType.DMA((2,)), pltpu.VMEM((rows, HID), F32)],
        limit=10,
    )


def mlp_more(layer, batch, where, tables, n2, acc, shares, pieces, end=None, after=()):
    pairs = 2 * batch
    rows = pairs * PAIR
    count = len(shares)
    outs = [pinned((count, rows, HID), BF16)] * 2
    outs += [pinned((count,) + dim, BF16) for dim in (DIM_1, DIM_2)]
    scratch = [pltpu.SemaphoreType.DMA((4 * count,)), pltpu.VMEM((rows, HID), F32)]
    if end is None:
        outs = [pinned((rows, C), F32)] + outs
    else:
        outs = [struct((batch, TOK, C), BF16)] + outs
        scratch.append(pltpu.VMEM((rows, C), F32))
    return call(
        functools.partial(mlp_more_kernel, layer, pairs, shares, end is not None),
        [SM, VM, VC, VC] + [ANY] * len(pieces) + ([] if end is None else [VC, VM, VM]),
        [where, tables, n2, acc, *pieces, *(end or ())],
        outs,
        scratch,
        limit=12,
        after=after,
    )


def mlp_bwd(layer, batch, where, g, place, act, dact, mid, n2, ho, rinv, ln_g, w, after):
    pairs = 2 * batch
    rows = pairs * PAIR
    outs = chunk_outs(M_ROWS) + [
        pinned((rows, C), F32),
        pinned((GROUPS, rows, LANES), BF16),
        pinned((GROUPS, rows, LANES), BF16),
        struct((4, C), F32),
        struct((GROUPS, 1, HID), F32),
    ]
    return call(
        functools.partial(mlp_bwd_kernel, layer, pairs, len(act)),
        [SM, VM if layer == LAYERS - 1 else VC, VM]
        + [VC] * (2 * len(act) + 5)
        + [VM]
        + [VC] * (2 * len(act) + 1),
        [where, g, place, *act, *dact, *mid, n2, ho, rinv, ln_g, w[0], *w[1], *w[2]],
        outs,
        [
            pltpu.VMEM((rows, C), F32),
            pltpu.VMEM((rows, C), BF16),
            pltpu.VMEM((GROUPS, rows, HID), BF16),
            pltpu.VMEM((rows, C), F32),
            pltpu.VMEM(DIM_1, BF16),
            pltpu.VMEM(DIM_P, BF16),
        ],
        flops=14 * GF,
        limit=18,
        after=after,
    )


def pair_bwd(layer, batch, where, g, act, dact, w, n1, dtri, after):
    pairs = 2 * batch
    rows = pairs * PAIR
    return call(
        functools.partial(pair_bwd_kernel, layer, pairs),
        [SM] + [VC] * 6,
        [where, g, act[0], dact[0], w[2][0], n1, dtri],
        chunk_outs(TWO_ROWS + Q_ROWS)
        + [pinned((GROUPS, rows, HID), BF16), struct((GROUPS, 1, TRI), F32)],
        [pltpu.VMEM((rows, C), BF16), pltpu.VMEM(DIM_2, BF16), pltpu.VMEM(DIM_Q, BF16)],
        limit=10,
        after=after,
    )


def middle_bwd(layer, batch, where, gp, g, mid, n2, ho, rinv, ln_g, w, after):
    pairs = 2 * batch
    rows = pairs * PAIR
    return call(
        functools.partial(middle_bwd_kernel, layer, pairs),
        [SM] + [VC] * 7 + [VM] + [VC] * 2,
        [where, gp, g, *mid, n2, ho, rinv, ln_g, w[0], w[1][0]],
        chunk_outs(ONE_ROWS)
        + [
            pinned((rows, C), F32),
            pinned((GROUPS, rows, LANES), BF16),
            pinned((GROUPS, rows, LANES), BF16),
            struct((4, C), F32),
            struct((GROUPS, 1, HID), F32),
        ],
        [
            pltpu.VMEM((rows, C), BF16),
            pltpu.VMEM((rows, C), F32),
            pltpu.VMEM(DIM_1, BF16),
            pltpu.VMEM(DIM_P, BF16),
        ],
        flops=9 * GF,
        limit=12,
        after=after,
    )


def attn_bwd(batch, where, dh, u, tri, e, group, after):
    pairs = 2 * batch
    rows = pairs * PAIR
    return call(
        functools.partial(attn_bwd_kernel, pairs),
        [SM] + [VC] * 4 + [VM],
        [where, dh, u, tri, e, group],
        [pinned((GROUPS, rows, TRI), BF16), pinned((HEADS, PAIR, LANES), F32)],
        [pltpu.VMEM((rows, TRI), BF16)],
        flops=12 * GF,
        limit=9,
        after=after,
    )


def qkv_grad(batch, where, n1, dtri, after):
    return call(
        functools.partial(qkv_grad_kernel, 2 * batch),
        [SM] + [VC] * 2,
        [where, n1, dtri],
        chunk_outs(Q_ROWS) + [struct((GROUPS, 1, TRI), F32)],
        [pltpu.VMEM(DIM_Q, BF16)],
        flops=3 * GF,
        limit=6,
        after=after,
    )


def input_bwd(layer, batch, where, gmid, normed, dtri, ln_g, place, w, after):
    pairs = 2 * batch
    rows = pairs * PAIR
    return call(
        functools.partial(input_bwd_kernel, layer, pairs),
        [SM, VC, VC, VC, VC, VM, VM, VC],
        [where, gmid, *normed, dtri, ln_g, place, w],
        [
            struct((TOK, batch, C), BF16) if layer == 0 else pinned((rows, C), F32),
            pinned((2, C), F32),
        ],
        [pltpu.VMEM((rows, C), F32)],
        flops=3 * GF,
        limit=9,
        after=after,
    )


def full_bias(qv_rows, heads):
    parts = qv_rows.reshape(LAYERS, heads, 2, HEAD_DIM)
    full = jnp.stack([parts[:, :, 0], jnp.zeros_like(parts[:, :, 0]), parts[:, :, 1]], 2)
    return full.reshape(LAYERS, heads * 3 * HEAD_DIM)


def swap(x, axis, size, bit):
    return lax.ppermute(x, axis, [(i, i ^ bit) for i in range(size)])


class Weights:
    def __init__(self, own, p_q, p_m, q_base=0):
        own_q, self.own_p, self.own_1, self.own_2 = own
        self.q_base = q_base
        self.qkv = [own_q] + p_q
        self.p_m = p_m


class Direct:
    def __init__(self, dp):
        self.dp = dp
        self.t = lax.axis_index("tensor")
        d = lax.axis_index("dp")
        self.where = jnp.stack([self.t, d % 2, d // 2]).astype(jnp.int32)

    def x(self, v):
        return swap(v, "tensor", 4, 1)

    def y(self, v):
        return swap(v, "tensor", 4, 2)

    def diagonal(self, v):
        return swap(v, "tensor", 4, 3)

    def other(self, v):
        return swap(v, "dp", self.dp, 1)

    def level(self, v, k):
        return swap(v, "dp", self.dp, 2 * k)

    def near(self, v):
        return self.x(v), self.y(v), self.diagonal(v)

    def plan(self, parts):
        plan, outs = [], []
        for part in parts:
            at, base = len(outs), 0
            for layer, chunk in part:
                lists, rows = CHUNKS[chunk]
                for weight, blocks in lists:
                    plan.append((weight, layer, at, moved_down(blocks, base)))
                base += rows
            outs.append(pinned((base, C), BF16))
        return plan, outs

    def pack(self, arrays, parts, tables=None, after=()):
        plan, outs = self.plan(parts)
        count = sum(len(blocks) for _, _, _, blocks in plan)
        args = [self.where, *arrays]
        scratch = []
        if tables is not None:
            args += tables
            outs[0] = pinned((FIRST_ROWS, C), BF16)
            outs.append(pinned((1, HIDDEN_AT + LAYERS * HID), F32))
            scratch = [pltpu.VMEM(v.shape, F32) for v in tables]
        made = len(outs)

        def body(where, *refs):
            outs = refs[len(args) - 1 : len(args) - 1 + made]
            end = pack_start(plan, where, refs[:4], outs, refs[-1])
            if tables is not None:
                held = refs[len(args) - 1 + made : -1]
                copies = [
                    pltpu.make_async_copy(a, b, refs[-1].at[count + i])
                    for i, (a, b) in enumerate(zip(refs[4:7], held))
                ]
                for copy in copies:
                    copy.start()
                for copy in copies:
                    copy.wait()
                own_tables(*held, outs[-1])
                put_tables(outs[-1], outs[0])
            end()

        return call(
            body, [SM] + [HB] * (len(args) - 1), args, outs,
            scratch + [pltpu.SemaphoreType.DMA((count + 3,))], after=after,
        )

    def merge(self, pieces, arrays=(), parts=(), moved=(), tables=None, after=()):
        rows, count = pieces[0].shape[0], len(pieces)
        plan, packs = self.plan(parts)
        outs = [pinned((3, rows, C), BF16)] + packs + [pinned(v.shape, v.dtype) for v in moved]
        weights = len(arrays)
        small = [] if tables is None else [tables]
        outs += [pinned((GROUPS, v.shape[1]), F32) for v in small]
        given = count + weights + len(moved) + len(small)

        def body(where, *refs):
            spare, outs = refs[:given], refs[given:-2]
            ends = []
            if parts:
                ends.append(pack_start(plan, where, spare[count : count + weights], outs[1:], refs[-1]))
            copies = [
                pltpu.make_async_copy(a, b, refs[-2].at[3 + i])
                for i, (a, b) in enumerate(
                    zip(spare[count + weights : count + weights + len(moved)], outs[1 + len(packs) :])
                )
            ]
            for copy in copies:
                copy.start()
            merge_kernel(where, *refs[:count], outs[0], refs[-2])
            if small:
                take_tables(spare[-1], outs[0], outs[-1])
            for copy in copies:
                copy.wait()
            for end in ends:
                end()

        moves = sum(len(blocks) for _, _, _, blocks in plan)
        near, *others = call(
            body, [SM] + [ANY] * count + [HB] * weights + [ANY] * len(moved) + [VM] * len(small),
            [self.where, *pieces, *arrays, *moved, *small], outs,
            [pltpu.SemaphoreType.DMA((3 + len(moved),)), pltpu.SemaphoreType.DMA((max(moves, 1),))],
            after=after, limit=10,
        )
        return [[near, self.other(near)], *others]

    def step(self, *parts, passing=(), after=(), weight=0):
        kernels, args, specs, outs, cuts = [], [self.where], [SM], [], []
        for kernel, values, results in parts:
            kernels.append((kernel, len(args) - 1, len(values), len(outs), len(results)))
            args += values
            specs += [VC] * len(values)
            outs += results
        total_in, total_out = len(args) - 1, len(outs)
        aliases = {}
        for value in passing:
            aliases[len(args)] = len(outs)
            args.append(value)
            specs.append(ANY)
            outs.append(struct(value.shape, value.dtype))

        def body(where, *refs):
            refs_in, refs_out = refs[: total_in + len(passing)], refs[total_in + len(passing) :]
            for kernel, at, count, out, results in kernels:
                kernel(where, *refs_in[at : at + count], *refs_out[out : out + results])

        got = call(
            body, specs, args, outs, after=after, aliases=aliases, weight=weight,
            out_specs=[VM] * total_out + [ANY] * len(passing),
        )
        split = []
        for _, _, _, out, results in kernels:
            split.append(got[out : out + results])
        return split + list(got[total_out:])


    def swap_cores(self, keep, send):
        return keep, self.other(send)

    def first_way(self, *states):
        args = [v for state in states for v in state]
        two = pinned((2, sum(keep.shape[2] for keep, _ in states), C), BF16)
        return add_go_kernel, args, [two] * 4

    def send_first(self, done):
        go_a, go_b, stay_a, stay_b = done
        return stay_a, stay_b, self.x(go_a), self.y(go_b)

    def second_way(self, state):
        one = pinned(state[0].shape[1:], BF16)
        return add_next_kernel, list(state), [one] * 4

    def send_second(self, done):
        next_a, next_b, keep_a, keep_b = done
        return keep_a, keep_b, self.y(next_a), self.x(next_b)

    def join(self, state):
        one = pinned(state[0].shape, BF16)
        return add_level_kernel, list(state), [one] * 2

    def join_whole(self, state):
        rows = 2 * state[0].shape[0]
        return add_whole_kernel, list(state), [pinned((rows, C), BF16)]

    def line(self, v, pairs):
        return lax.ppermute(
            v, "dp", [(2 * a + core, 2 * b + core) for a, b in pairs for core in range(2)]
        )

    def choose(self, mine, got):
        return choose_kernel, [mine, got], [pinned(mine.shape, BF16)]

    def send_level(self, state, k):
        mine, send = state
        return mine, self.level(send, k)

    def add(self, state):
        return add_kernel, list(state), [pinned(state[0].shape, BF16)]

    def own_small(self, state):
        return own_kernel, list(state), [pinned((16 * LAYERS, C), F32)]

    def add_small(self, state):
        return add_kernel, list(state), [pinned(state[0].shape, F32)]

    def finish(self, plan, pieces, before=None, after=()):
        dims = (DIM_Q, DIM_P, DIM_1, DIM_2)
        made = len(pieces)
        args, specs = [self.where, *pieces], [SM] + [VC] * made
        aliases = {}
        if before is not None:
            aliases = {1 + made + i: i for i in range(4)}
            args += before[:4]
            specs += [HB] * 4
        scratch = [
            pltpu.VMEM(dims[FINISH[name][0]], F32) for _, _, names in plan for name in names
        ]
        return call(
            functools.partial(finish_kernel, plan, len(args) - 1, made), specs, args,
            [pltpu.HBM((LAYERS,) + dim, F32) for dim in dims] + [pinned((8, LANES), F32)],
            scratch + [pltpu.SemaphoreType.DMA((len(scratch),))],
            out_specs=[HB] * 4 + [VM], limit=6, after=after, aliases=aliases,
        )

    def unpack(self, little, after=()):
        one = struct((LAYERS, C), F32)
        outs = [one] * 7 + [struct((LAYERS, 2 * LANES), F32), struct((LAYERS, GHEADS, TABLE), F32)]
        outs.append(pinned((8, LANES), F32))
        return call(unpack_kernel, [SM, VC], [self.where, little], outs, after=after)


class Whole:
    def __init__(self):
        self.where = jnp.zeros((3,), jnp.int32)

    def gather(self, arrays, small):
        qkv, proj, w1, w2 = [
            lax.all_gather(v, "tensor", axis=axis, tiled=True) for v, axis in zip(arrays, (2, 1, 2, 1))
        ]
        qkv = qkv.reshape(LAYERS, C, GROUPS, TRI).transpose(0, 2, 1, 3)
        proj = proj.reshape(LAYERS, GROUPS, LANES, C)
        w1 = w1.reshape(LAYERS, C, GROUPS, HID).transpose(0, 2, 1, 3)
        w2 = w2.reshape(LAYERS, GROUPS, HID, C)
        own = [v[:, 0] for v in (qkv, proj, w1, w2)]

        def pack(parts, rows):
            out = jnp.zeros((rows, C), BF16)
            for v, blocks in parts:
                for row, lane, count, lanes, to_row, to_lane in blocks:
                    block = v[row : row + count, lane : lane + lanes]
                    out = out.at[to_row : to_row + count, to_lane : to_lane + lanes].set(block)
            return out

        weights = []
        for layer in range(LAYERS):
            p_q, p_m = [], []
            for side in range(2):
                side_q, side_m = [], []
                for r in range(1, GROUPS):

                    def half(v):
                        size = v.shape[2] // 2
                        return v[layer, r, side * size : (side + 1) * size]

                    side_q.append(pack([(half(qkv), PACK_Q)], Q_ROWS))
                    parts = [(half(w1), PACK_1), (half(proj), PACK_P), (half(w2), PACK_2)]
                    side_m.append(pack(parts, M_ROWS))
                p_q.append(jnp.stack(side_q))
                p_m.append(jnp.stack(side_m))
            weights.append(Weights(own, p_q, p_m))
        return weights, lax.all_gather(small, "tensor", axis=0)

    def sum_small(self, v):
        return lax.psum(v, ("dp", "tensor"))

    def finish(self, chunks):
        full = {}
        for name, chunk, blocks, dim in (
            ("q", 1, PACK_Q, DIM_Q), ("p", 0, PACK_P, DIM_P), ("1", 0, PACK_1, DIM_1), ("2", 0, PACK_2, DIM_2)
        ):
            layers = []
            for layer in range(LAYERS):
                sides = []
                for v in chunks[layer][chunk]:
                    shares = []
                    for r in range(GROUPS):
                        packed = jnp.concatenate(
                            [v[part, ORDERS[part].index(r)] for part in range(2)], 0
                        )
                        out = jnp.zeros((dim[0] // 2, dim[1]), BF16)
                        for row, lane, count, lanes, to_row, to_lane in blocks:
                            block = packed[to_row : to_row + count, to_lane : to_lane + lanes]
                            out = out.at[row : row + count, lane : lane + lanes].set(block)
                        shares.append(out)
                    sides.append(jnp.stack(shares))
                layers.append(jnp.concatenate(sides, 1))
            full[name] = jnp.stack(layers)
        outs = []
        for name, axis in zip("qp12", (2, 1, 2, 1)):
            v = full[name]
            if axis == 2:
                v = v.transpose(0, 2, 1, 3).reshape(LAYERS, C, -1)
            else:
                v = v.reshape(LAYERS, -1, C)
            v = lax.psum_scatter(v, "tensor", scatter_dimension=axis, tiled=True)
            outs.append(lax.psum(v, "dp").astype(F32))
        return outs


def shards(
    tensor, dp, images_in, ln1_gain, ln1_bias, qkv_weight, qv_bias, rel_table, proj_weight,
    proj_bias, ln2_gain, ln2_bias, fc1_weight, fc1_bias, fc2_weight, fc2_bias, rel_index,
    region_ids, out_cot,
):
    batch = images_in.shape[0]
    direct = tensor == 4 and dp == 8
    net = Direct(dp) if direct else Whole()
    where = net.where
    wide = 2 * LANES
    own = (qkv_weight, proj_weight, fc1_weight, fc2_weight)

    heads = rel_table.shape[2]
    if direct:
        q0, packed = net.pack(
            own, [[(0, 0)]], tables=[rel_table.transpose(0, 2, 1), qv_bias, fc1_bias]
        )
        near_q0 = net.near(q0)
        w_q0, m0, every = net.merge(near_q0, own, [[(0, 1), (1, 0), (1, 2)]], tables=packed)
        near_m0 = net.near(m0)
    else:
        table = jnp.pad(rel_table.transpose(2, 0, 1), ((0, 0), (0, 0), (0, wide - TABLE)))
        bias_part = full_bias(qv_bias, heads)
        packed = jnp.concatenate([table.reshape(-1), bias_part.reshape(-1), fc1_bias.reshape(-1)])
        packed = packed.reshape(1, -1)
        weights, every = net.gather(own, packed)
    every = every.reshape(tensor, -1)
    if tensor != GROUPS:
        cut1 = heads * LAYERS * wide
        cut2 = cut1 + bias_part.size
        tables = every[:, :cut1].reshape(GROUPS, -1)
        parts = [tables]
        for part in (every[:, cut1:cut2], every[:, cut2:]):
            part = part.reshape(tensor, LAYERS, -1).transpose(1, 0, 2)
            parts.append(part.reshape(LAYERS, GROUPS, -1).transpose(1, 0, 2).reshape(GROUPS, -1))
        every = jnp.concatenate(parts, 1)
    index = jnp.pad(rel_index + 1, ((0, PAIR - WTOK), (0, LANES - WTOK)))
    index = index + jnp.pad(rel_index + 1, ((WTOK, PAIR - 2 * WTOK), (WTOK, LANES - 2 * WTOK))) - 1
    ids = region_ids.astype(BF16)
    ids_col = jnp.broadcast_to(ids[:, None], (TOK, LANES))
    ids_row = jnp.broadcast_to(ids[None, :], (16, TOK))
    lanes_place = np.zeros((2 * LANES, TOK), np.float32)
    for pair in range(2):
        lanes_place[pair * LANES : pair * LANES + PAIR] = PLACE[0][pair * PAIR : (pair + 1) * PAIR]
    place = [jnp.asarray(PLACE[layer], BF16) for layer in range(LAYERS)]
    after = w_q0[:1] if direct else ()

    def bias_of(layer, after=()):
        return call(
            functools.partial(bias_kernel, layer),
            [VM] * 6,
            [every, index, ids_col, ids_row, place[0], jnp.asarray(lanes_place, BF16)],
            [pinned((1 + layer, HEADS, PAIR, LANES), F32)],
            flops=4 * GF,
            after=after,
        )[0]

    bias = [bias_of(0, after), None]
    step01 = jnp.asarray(PLACE[1] @ PLACE[0].T, BF16)
    step10 = jnp.asarray(PLACE[0] @ PLACE[1].T, BF16)
    group = jnp.asarray(GROUP, BF16)

    def row(v, layer):
        return v[layer][None]

    saved, w_q, w_m = [None] * LAYERS, [None] * LAYERS, [None] * LAYERS
    rels, littles, normed = [None] * LAYERS, [None] * LAYERS, [None] * LAYERS

    def attn(layer, state, w):
        res = attn_fwd(
            layer, batch, where, state, place[0], row(ln1_gain, layer), row(ln1_bias, layer),
            every, group, bias[layer], w,
        )
        *res, w_q[layer] = res
        x, res = (res[0], res[1:]) if layer == 0 else (state, res)
        normed[layer] = res[:2]
        saved[layer] = (x, *res[2:])

    def mlp(layer, w):
        x, n1, tri, e, rinv, ho = saved[layer]
        state, *rest, wp, w1, w2 = mlp_fwd(
            layer, batch, where, x, ho, row(proj_bias, layer), row(ln2_gain, layer),
            row(ln2_bias, layer), every, row(fc2_bias, layer), step01 if layer == 0 else place[1],
            w,
        )
        xhat, rstd, n2, act, dact = rest
        saved[layer] += ((xhat, rstd), n2, (act,), (dact,))
        w_m[layer] = (wp, (w1,), (w2,))
        return state

    def mlp_back(layer, grad, after=()):
        x, n1, tri, e, rinv, ho, mid, n2, act, dact = saved[layer]
        keep, send, gmid, dh, u, small2, db1 = mlp_bwd(
            layer, batch, where, grad, place[1], act, dact, mid, n2, ho, rinv,
            row(ln2_gain, layer), w_m[layer], after,
        )
        littles[layer] = {"a": small2, "b": db1}
        return (keep, send), gmid, dh, u

    def pair_back(grad, dtri, after=()):
        act, dact = saved[0][8:]
        keep, send, gp, littles[1]["c"] = pair_bwd(
            0, batch, where, grad, act, dact, w_m[0], saved[1][1], dtri, after
        )
        return (keep, send), gp

    def middle_back_0(gp, grad, after):
        x, n1, tri, e, rinv, ho, mid, n2, act, dact = saved[0]
        keep, send, gmid, dh, u, small2, db1 = middle_bwd(
            0, batch, where, gp, grad, mid, n2, ho, rinv, row(ln2_gain, 0), w_m[0], after
        )
        littles[0] = {"a": small2, "b": db1}
        return (keep, send), gmid, dh, u

    def attn_back(layer, dh, u, after=()):
        dtri, rels[layer] = attn_bwd(
            batch, where, dh, u, saved[layer][2], saved[layer][3], group, after
        )
        return dtri

    def qkv_back(layer, dtri, after=()):
        keep, send, small_q = qkv_grad(batch, where, saved[layer][1], dtri, after)
        littles[layer]["c"] = small_q
        return keep, send

    def input_back(layer, gmid, dtri, after=()):
        grad, small1 = input_bwd(
            layer, batch, where, gmid, normed[layer], dtri, row(ln1_gain, layer),
            step10 if layer else place[0], w_q[layer], after,
        )
        littles[layer]["d"] = small1
        return grad, small1

    def small_sums(after=()):
        args = [index.reshape(PAIR, 1, LANES), jnp.asarray(PICK, BF16)]
        for layer in range(LAYERS):
            args += [littles[layer][name] for name in "abcd"] + [rels[layer]]
        specs = [VM] * 2 + ([VM] * 4 + [VC]) * LAYERS
        return call(
            small_kernel, specs, args, [pinned((24 * LAYERS, C), F32)],
            [
                pltpu.VMEM((wide, 2 * LAYERS * HEADS), F32),
                pltpu.VMEM((LAYERS * HEADS * 56, LANES), F32),
            ],
            after=after, limit=4,
        )[0]

    if direct:
        w0 = Weights(own, w_q0, None)
        attn(0, images_in, w0)
        bias[1] = bias_of(1, saved[0][5:6])
        (m1,) = net.pack(own, [[(1, 3)]], after=(bias[1],))
        w0.p_m, m1_now = net.merge(near_m0, moved=(m1,))
        m1_x, m1_y = net.x(m1_now), net.y(m1_now)
        state = mlp(0, w0)
        (m1,) = net.step(passing=(m1,), after=(state,))
        m1_d = net.diagonal(m1)
        w1 = Weights(own, w0.p_m, None, M_ROWS)
        attn(1, state, w1)
        x, n1, tri, e, rinv, ho = saved[1]
        m1_x, m1_y = net.step(passing=(m1_x, m1_y), after=(ho,))
        far_x, far_y = net.other(m1_x), net.other(m1_y)
        mid, xhat, rstd, n2, acc, *first = mlp_open(
            1, batch, where, x, ho, row(proj_bias, 1), row(ln2_gain, 1), row(ln2_bias, 1), every,
            w1, M_ROWS + Q_ROWS, w0.p_m,
        )
        (m1_d,) = net.step(passing=(m1_d,), after=(acc,))
        far_d = net.other(m1_d)
        acc, *second = mlp_more(
            1, batch, where, every, n2, acc, (1, 2), (m1_x, far_x, m1_y, far_y), after=(m1_d,)
        )
        output, *third = mlp_more(
            1, batch, where, every, n2, acc, (3,), (m1_d, far_d),
            end=(mid, row(fc2_bias, 1), place[1]),
        )
        act, dact, wp, *w_first = first
        saved[1] += ((xhat, rstd), n2, (act, second[0], third[0]), (dact, second[1], third[1]))
        w_m[1] = (
            wp, (w_first[0], second[2], third[2]), (w_first[1], second[3], third[3])
        )

        m1, gmid, dh, u = mlp_back(1, out_cot, after=(output,))
        m1 = net.swap_cores(*m1)
        dtri = attn_back(1, dh, u)
        (g1,) = net.step(net.first_way(m1), after=(dtri,))
        g1 = net.send_first(g1)
        grad, _ = input_back(1, gmid, dtri, after=g1[:1])
        two, gp = pair_back(grad, dtri)
        two = net.swap_cores(*two)
        one, gmid, dh, u = middle_back_0(gp, grad, after=two[:1])
        g1, send = net.step(net.second_way(g1), passing=one[1:], after=(gmid,), weight=40)
        (g2,) = net.step(net.first_way(two), after=g1[:1])
        dtri = attn_back(0, dh, u, after=g2[:1])
        g1, g2 = net.send_second(g1), net.send_first(g2)
        one = net.swap_cores(one[0], send)
        q0 = qkv_back(0, dtri)
        g1, send = net.step(net.join(g1), passing=q0[1:], after=q0[:1])
        g1 = net.send_level(g1, 1)
        q0 = net.swap_cores(q0[0], send)
        (g3,) = net.step(net.first_way(one, q0), after=(g1[0],))
        grad, done = input_back(0, gmid, dtri, after=g3[:1])
        g3 = net.send_first(g3)
        ((g1,),) = net.step(net.add(g1), after=(done,))
        g1 = net.send_level((g1, g1), 2)
        little = small_sums(after=(g1[0],))
        g2, little = net.step(net.second_way(g2), passing=(little,))
        order = g2[2:3]
        g2 = net.send_second(g2)
        (g3,) = net.step(net.second_way(g3), after=order)
        order = g3[2:3]
        g3 = net.send_second(g3)
        g2, (g1,), little = net.step(
            net.join(g2), net.add(g1), passing=(little,), after=order
        )
        order = g2[:1]
        g2 = net.send_level(g2, 1)
        near1 = net.level(g1, 1)
        little = (little, net.other(little))
        g3, (little,) = net.step(net.join(g3), net.add_small(little), after=order)
        order = g3[:1]
        g3 = net.send_level(g3, 1)
        little = (little, net.x(little))
        (g2,), (little,), side1, near1 = net.step(
            net.add(g2), net.add_small(little), passing=(g1, near1), after=order
        )
        order = (g2,)
        g2 = net.send_level((g2, g2), 2)
        little = (little, net.y(little))
        g1 = [side1, near1, net.other(side1), net.other(near1)]
        (g3,), (little,) = net.step(net.add(g3), net.own_small(little), after=order)
        order = (g3,)
        g3 = net.send_level((g3, g3), 2)
        little = (little, net.level(little, 1))
        (g2,), (little,) = net.step(net.add(g2), net.add_small(little), after=order)
        near2, side2 = net.level(g2, 1), net.other(g2)
        little = (little, net.level(little, 2))
        results = net.finish([(M_ROWS, 1, ("1", "p", "2"))], g1, after=(g2,))
        (g3,), (little,), near2 = net.step(
            net.add(g3), net.add_small(little), passing=(near2,), after=results[4:]
        )
        near3, side3 = net.level(g3, 1), net.other(g3)
        g2 = [g2, near2, side2, net.other(near2)]
        small = list(net.unpack(little))
        results = net.finish(
            [(Q_ROWS, 1, ("q",)), (TWO_ROWS, 0, ("two",))], g2, results, after=small[9:]
        )
        (near3,) = net.step(passing=(near3,), after=results[4:])
        dwq, dwp, dw1, dw2, _ = net.finish(
            [(ONE_ROWS, 0, ("1", "p")), (Q_ROWS, 0, ("q",))],
            [g3, near3, side3, net.other(near3)], results,
        )
        small[8] = small[8].transpose(0, 2, 1)
        return (
            output, grad.transpose(1, 0, 2), small[0], small[1], dwq, small[7], small[8], dwp, small[2], small[3],
            small[4], dw1, small[6], dw2, small[5],
        )
    else:
        state = images_in
        bias[1] = bias_of(1)
        for layer in range(LAYERS):
            attn(layer, state, weights[layer])
            state = mlp(layer, weights[layer])
        output = state
        grad = out_cot
        reduced = [None] * LAYERS
        for layer in reversed(range(LAYERS)):
            m, gmid, dh, u = mlp_back(layer, grad)
            dtri = attn_back(layer, dh, u)
            reduced[layer] = (m, qkv_back(layer, dtri))
            grad, _ = input_back(layer, gmid, dtri)
        little = net.sum_small(small_sums())
        dwq, dwp, dw1, dw2 = net.finish(reduced)
    little = little.reshape(LAYERS, 24, C)
    small_q = little[:, 8:12, : 2 * LANES].reshape(LAYERS, -1)
    rel = little[:, 16:].reshape(LAYERS, 8, 2, wide)[..., :TABLE].transpose(0, 3, 2, 1)
    rel = rel.reshape(LAYERS, TABLE, HEADS)
    db1 = little[:, 4:8].reshape(LAYERS, FF)
    mine = lax.axis_index("tensor")

    def share(v, axis):
        size = v.shape[axis] // tensor
        return lax.dynamic_slice_in_dim(v, mine * size, size, axis)

    return (
        output, grad.transpose(1, 0, 2), little[:, 12], little[:, 13], dwq, share(small_q, 1), share(rel, 2), dwp,
        little[:, 3], little[:, 1], little[:, 2], dw1, share(db1, 1), dw2, little[:, 0],
    )


def solution(mesh):
    tokens = P(("dp", "tensor"), None, None)
    cols, rows = P(None, None, "tensor"), P(None, "tensor", None)
    part = P(None, "tensor")
    return jax.shard_map(
        functools.partial(shards, mesh.shape["tensor"], mesh.shape["dp"]),
        mesh=mesh,
        in_specs=(
            tokens, P(), P(), cols, part, cols, rows, P(), P(), P(), cols, part, rows, P(), P(),
            P(), tokens,
        ),
        out_specs=(
            tokens, tokens, P(), P(), cols, part, cols, rows, P(), P(), P(), cols, part, rows, P(),
        ),
        check_vma=False,
    )
```
